32 devices in a mesh: fsdp: 4 (over y, x), ctx: 8 (over z, core).
Axes of the slice: x: 2, y: 2, z: 4, core: 2. Of those that a mesh axis runs over, the one named last changes fastest.
Arguments:
- tokens: bfloat16 [4, 1024, 1600], P('fsdp', 'ctx'), may hold values from -6 to 6
- block_order: int32 [16], replicated, may hold values from 0 to 15, each once
- cotangent: bfloat16 [4, 1024, 1600], P('fsdp', 'ctx'), may hold values from -6 to 6
- pre_attn_gain: bfloat16 [1600], P('ctx'), may hold values from 0.5 to 1.5
- pre_attn_bias: bfloat16 [1600], P('ctx'), may hold values from -1.25 to 1.25
- qkv_weight: bfloat16 [1600, 4800], P('fsdp', 'ctx'), may hold values from -0.21875 to 0.21875
- query_bias: bfloat16 [1600], P('ctx'), may hold values from -1.75 to 1.75
- value_bias: bfloat16 [1600], P('ctx'), may hold values from -1.75 to 1.75
- out_weight: bfloat16 [1600, 1600], P('fsdp', 'ctx'), may hold values from -0.875 to 0.875
- out_bias: bfloat16 [1600], P('ctx'), may hold values from -1.75 to 1.75
- pre_mlp_gain: bfloat16 [1600], P('ctx'), may hold values from 0.5 to 1.5
- pre_mlp_bias: bfloat16 [1600], P('ctx'), may hold values from -1.25 to 1.25
- fc_weight: bfloat16 [1600, 6400], P('fsdp', 'ctx'), may hold values from -0.15625 to 0.15625
- fc_bias: bfloat16 [6400], P('ctx'), may hold values from -1.75 to 1.75
- proj_weight: bfloat16 [6400, 1600], P('fsdp', 'ctx'), may hold values from -0.15625 to 0.15625
- proj_bias: bfloat16 [1600], P('ctx'), may hold values from -1.75 to 1.75
Outputs:
- output: bfloat16 [4, 1024, 1600], P('fsdp', 'ctx')
- input_grad: float32 [4, 1024, 1600], P('fsdp', 'ctx')
- pre_attn_gain_grad: float32 [1600], P('ctx')
- pre_attn_bias_grad: float32 [1600], P('ctx')
- qkv_weight_grad: float32 [1600, 4800], P('fsdp', 'ctx')
- query_bias_grad: float32 [1600], P('ctx')
- value_bias_grad: float32 [1600], P('ctx')
- out_weight_grad: float32 [1600, 1600], P('fsdp', 'ctx')
- out_bias_grad: float32 [1600], P('ctx')
- pre_mlp_gain_grad: float32 [1600], P('ctx')
- pre_mlp_bias_grad: float32 [1600], P('ctx')
- fc_weight_grad: float32 [1600, 6400], P('fsdp', 'ctx')
- fc_bias_grad: float32 [6400], P('ctx')
- proj_weight_grad: float32 [6400, 1600], P('fsdp', 'ctx')
- proj_bias_grad: float32 [1600], P('ctx')
The draws below stay inside these ranges and needn't reach their ends.
Inputs may be any that keep to these rules, and one draw needn't show every extreme that they name: `block_order`: each stored block holds one position block; every value appears once.
All inputs are finite; a program needn't handle non-finite values.
Results may differ from the reference program's by a relative error of at most 0.022.
Values may be sent and summed in bfloat16 or wider, within the bound.
A program may use at most 320 MiB of HBM per device.

```python
import math
import jax
import jax.numpy as jnp
from jax import lax

D = 1600
H = 25
HD = 64
FF = 6400
BLK = 64
SEQS = 4
SLOTS = 16
LENGTH = 1024


def level_of(stream_key, dims, cuts, low, largest):
    def one(position, shards_of):
        steps = jax.random.uniform(jax.random.fold_in(jax.random.fold_in(stream_key, 6), position), (shards_of,), jnp.float32, low / len(cuts), largest / len(cuts))
        return jnp.repeat(jnp.exp(steps), dims[position] // shards_of).reshape((-1,) + (1,) * (len(dims) - position - 1))

    level = one(*cuts[0])
    for cut in cuts[1:]:
        level = level * one(*cut)
    return level


def noise(own_key, extent, width, limit, shards=(), kind=jnp.bfloat16):
    drawn = jax.random.normal(own_key, extent, jnp.float32) * width
    if len(shards) > 0:
        drawn = level_of(own_key, extent, shards, -0.22, 0.18) * drawn
    return jnp.clip(drawn, min=-limit, max=limit).astype(kind)


def setup_inputs(seed: int = 0) -> dict:
    keys = jax.random.split(jax.random.key(seed), 17)
    tokens = noise(keys[0], (SEQS, LENGTH, D), 1.0, 6.0, ((0, 4), (1, 8)))
    block_order = jax.random.permutation(keys[1], SLOTS).astype(jnp.int32)
    cotangent = noise(keys[2], (SEQS, LENGTH, D), 1.0, 6.0, ((0, 4), (1, 8)))
    pre_attn_gain = jnp.clip(1.0 + 0.1 * jax.random.normal(keys[3], (D,), jnp.float32), 0.5, 1.5).astype(jnp.bfloat16)
    pre_attn_bias = noise(keys[4], (D,), 0.2, 1.25, ((0, 8),))
    qkv_weight = noise(keys[5], (D, 3 * D), (D // 2) ** -0.5, 0.21875, ((0, 4), (1, 8)))
    query_bias = noise(keys[6], (D,), 0.3, 1.75, ((0, 8),))
    value_bias = noise(keys[7], (D,), 0.3, 1.75, ((0, 8),))
    out_weight = noise(keys[8], (D, D), (D // 32) ** -0.5, 0.875, ((0, 4), (1, 8)))
    out_bias = noise(keys[9], (D,), 0.3, 1.75, ((0, 8),))
    pre_mlp_gain = jnp.clip(1.0 + 0.1 * jax.random.normal(keys[10], (D,), jnp.float32), 0.5, 1.5).astype(jnp.bfloat16)
    pre_mlp_bias = noise(keys[11], (D,), 0.2, 1.25, ((0, 8),))
    fc_weight = noise(keys[12], (D, FF), D ** -0.5, 0.15625, ((0, 4), (1, 8)))
    fc_bias = noise(keys[13], (FF,), 0.3, 1.75, ((0, 8),))
    proj_weight = noise(keys[14], (FF, D), (FF // 4) ** -0.5, 0.15625, ((0, 4), (1, 8)))
    proj_bias = noise(keys[15], (D,), 0.3, 1.75, ((0, 8),))
    return dict(tokens=tokens, block_order=block_order, cotangent=cotangent, pre_attn_gain=pre_attn_gain, pre_attn_bias=pre_attn_bias, qkv_weight=qkv_weight, query_bias=query_bias, value_bias=value_bias, out_weight=out_weight, out_bias=out_bias, pre_mlp_gain=pre_mlp_gain, pre_mlp_bias=pre_mlp_bias, fc_weight=fc_weight, fc_bias=fc_bias, proj_weight=proj_weight, proj_bias=proj_bias)


@jax.custom_vjp
def low(v):
    return lax.optimization_barrier(v.astype(jnp.bfloat16)).astype(jnp.float32)

@jax.custom_vjp
def low_back(v):
    return v

def low_keep(v):
    return (low(v), None)

def low_pass(kept, grad):
    return (grad,)

def back_keep(v):
    return (v, None)

def back_low(kept, grad):
    return (low(grad),)
low.defvjp(low_keep, low_pass)
low_back.defvjp(back_keep, back_low)

def layer_norm(values, gain, shift):
    centred = values - lax.optimization_barrier(jnp.mean(values, axis=-1, keepdims=True))
    spread = lax.optimization_barrier(jnp.mean(centred * centred, axis=-1, keepdims=True))
    return centred * lax.rsqrt(spread + 1e-05) * gain + shift

def positions(block_order):
    stored = jnp.arange(LENGTH, dtype=jnp.int32)
    return block_order[stored // BLK].astype(jnp.int32) * BLK + stored % BLK

def attention(queries, key_rows, value_rows, pos):
    rows_each = math.gcd(LENGTH, 512)
    scale = HD ** (-0.5)
    hi = lax.Precision.HIGHEST

    def one_block(query_block, query_pos, key_rows, value_rows, pos):
        scores = jnp.einsum('qhd,khd->hqk', query_block, key_rows, precision=hi) * scale
        scores = low_back(scores)
        allowed = pos[None, None, :] <= query_pos[None, :, None]
        scores = jnp.where(allowed, scores, -1e+30)
        top = lax.optimization_barrier(jnp.max(scores, axis=2, keepdims=True))
        weights = jnp.exp(scores - top)
        probs = low(weights / lax.optimization_barrier(jnp.sum(weights, axis=2, keepdims=True)))
        return jnp.einsum('hqk,khd->qhd', probs, value_rows, precision=hi)
    step = jax.checkpoint(one_block)
    query_blocks = queries.reshape(LENGTH // rows_each, rows_each, H, HD)
    pos_blocks = pos.reshape(LENGTH // rows_each, rows_each)
    result = lax.map(lambda pair: step(pair[0], pair[1], key_rows, value_rows, pos), (query_blocks, pos_blocks))
    return result.reshape(LENGTH, D)

def layer(values, params, pos):
    hi = lax.Precision.HIGHEST
    attention_gain_vector, attention_shift_vector, qkv_weight, query_bias, value_bias, out_weight, out_bias, feedforward_gain, feedforward_shift, fc_weight, fc_bias, proj_weight, proj_bias = params
    hidden_one = low(layer_norm(values, attention_gain_vector, attention_shift_vector))
    shift_row = jnp.concatenate([query_bias, jnp.zeros((D,), jnp.float32), value_bias])
    projected = jnp.dot(hidden_one, qkv_weight, precision=hi) + shift_row
    projected = low_back(low(projected))
    queries = projected[:, :D].reshape(LENGTH, H, HD)
    key_rows = projected[:, D:2 * D].reshape(LENGTH, H, HD)
    value_rows = projected[:, 2 * D:].reshape(LENGTH, H, HD)
    attended = low_back(low(attention(queries, key_rows, value_rows, pos)))
    branch = low_back(jnp.dot(attended, out_weight, precision=hi) + out_bias)
    middle_rows = values + branch
    hidden_two = low(layer_norm(middle_rows, feedforward_gain, feedforward_shift))
    before = low_back(jnp.dot(hidden_two, fc_weight, precision=hi) + fc_bias)
    activated = low(jax.nn.gelu(before, approximate=True))
    feed = low_back(jnp.dot(activated, proj_weight, precision=hi) + proj_bias)
    return middle_rows + feed

def reference(tokens, block_order, cotangent, pre_attn_gain, pre_attn_bias, qkv_weight, query_bias, value_bias, out_weight, out_bias, pre_mlp_gain, pre_mlp_bias, fc_weight, fc_bias, proj_weight, proj_bias):
    params = tuple((p.astype(jnp.float32) for p in (pre_attn_gain, pre_attn_bias, qkv_weight, query_bias, value_bias, out_weight, out_bias, pre_mlp_gain, pre_mlp_bias, fc_weight, fc_bias, proj_weight, proj_bias)))
    pos = positions(block_order)

    def one_sequence(totals, pair):
        sequence, upstream = pair
        result, back = jax.vjp(lambda values, weights: layer(values, weights, pos), sequence.astype(jnp.float32), params)
        grad_in, grad_params = back(upstream.astype(jnp.float32))
        totals = jax.tree.map(jnp.add, totals, grad_params)
        return (totals, (result.astype(jnp.bfloat16), grad_in))
    zeros = tuple((jnp.zeros_like(p) for p in params))
    totals, (outputs, input_grads) = lax.scan(one_sequence, zeros, (tokens, cotangent))
    return (outputs, input_grads, totals[0], totals[1], totals[2], totals[3], totals[4], totals[5], totals[6], totals[7], totals[8], totals[9], totals[10], totals[11], totals[12])
```

```python
from functools import partial
import math

import jax
import jax.numpy as jnp
from jax import lax
from jax.experimental import pallas as pl
from jax.experimental.pallas import tpu as pltpu
from jax.sharding import Mesh
from jax.sharding import PartitionSpec as P

HD = 64
EPS = 1e-05
FLOOR = -1e30
BF = jnp.bfloat16
F32 = jnp.float32
CTX = ("z", "core")


def dot(a, b):
    return jnp.dot(a, b, preferred_element_type=F32)


def dot_nt(a, b):
    return lax.dot_general(a, b, (((1,), (1,)), ((), ())), preferred_element_type=F32)


def dot_tn(a, b):
    return lax.dot_general(a, b, (((0,), (0,)), ((), ())), preferred_element_type=F32)


def norm_rows(rows):
    centred = rows - jnp.mean(rows, axis=-1, keepdims=True)
    rstd = lax.rsqrt(jnp.mean(centred * centred, axis=-1, keepdims=True) + EPS)
    return centred * rstd, rstd


def norm_back(upstream, xhat, rstd, gain):
    inner = upstream * gain
    return rstd * (
        inner
        - jnp.mean(inner, axis=-1, keepdims=True)
        - xhat * jnp.mean(inner * xhat, axis=-1, keepdims=True)
    )


def positions(order_table, rows, block_rows):
    stored = jnp.arange(rows, dtype=jnp.int32)
    picked = jnp.repeat(order_table, block_rows, total_repeat_length=rows)
    return picked * block_rows + stored % block_rows


def attend_kernel(heads, q_block, qkv_ref, pos_col_ref, pos_row_ref, out_ref, lse_ref):
    rows = qkv_ref.shape[0]
    width = heads * HD
    for h in range(heads):
        k = qkv_ref[:, width + h * HD : width + (h + 1) * HD]
        v = qkv_ref[:, 2 * width + h * HD : 2 * width + (h + 1) * HD]
        for b in range(rows // q_block):
            at = slice(b * q_block, (b + 1) * q_block)
            q = qkv_ref[at, h * HD : (h + 1) * HD] * BF(HD**-0.5)
            s = dot_nt(k, q)
            s = jnp.where(pos_col_ref[...] <= pos_row_ref[:, at], s, FLOOR)
            top = jnp.max(s, axis=0, keepdims=True)
            p = jnp.exp(s - top)
            total = jnp.sum(p, axis=0, keepdims=True)
            o = dot_tn(v, p.astype(BF)) * (1.0 / total)
            out_ref[at, h * HD : (h + 1) * HD] = o.T.astype(BF)
            lse_ref[h : h + 1, at] = top + jnp.log(total)


def attend(qkv, pos, heads):
    rows = qkv.shape[0]
    return pl.pallas_call(
        partial(attend_kernel, heads, min(256, rows)),
        out_shape=(
            jax.ShapeDtypeStruct((rows, heads * HD), BF),
            jax.ShapeDtypeStruct((heads, rows), F32),
        ),
        name="attend",
        compiler_params=pltpu.CompilerParams(vmem_limit_bytes=48 * 2**20),
    )(qkv, pos[:, None], pos[None, :])


def attend_back_kernel(
    heads, q_block, qkv_ref, pos_col_ref, pos_row_ref, out_ref, lse_ref, dout_ref, dqkv_ref, acc_ref
):
    rows = qkv_ref.shape[0]
    width = heads * HD
    for h in range(heads):
        k = qkv_ref[:, width + h * HD : width + (h + 1) * HD]
        v = qkv_ref[:, 2 * width + h * HD : 2 * width + (h + 1) * HD]
        for b in range(rows // q_block):
            at = slice(b * q_block, (b + 1) * q_block)
            q = qkv_ref[at, h * HD : (h + 1) * HD] * BF(HD**-0.5)
            do = dout_ref[at, h * HD : (h + 1) * HD]
            o = out_ref[at, h * HD : (h + 1) * HD]
            delta = jnp.sum(do.astype(F32).T * o.astype(F32).T, axis=0, keepdims=True)
            s = dot_nt(k, q)
            p = jnp.where(
                pos_col_ref[...] <= pos_row_ref[:, at], jnp.exp(s - lse_ref[h : h + 1, at]), 0.0
            )
            dp = dot_nt(v, do)
            ds = (p * (dp - delta)).astype(BF)
            dq = dot_tn(k, ds) * (HD**-0.5)
            dqkv_ref[at, h * HD : (h + 1) * HD] = dq.T.astype(BF)
            dk = dot(ds, q)
            dv = dot(p.astype(BF), do)
            if b == 0:
                acc_ref[:, :HD] = dk
                acc_ref[:, HD:] = dv
            else:
                acc_ref[:, :HD] += dk
                acc_ref[:, HD:] += dv
        dqkv_ref[:, width + h * HD : width + (h + 1) * HD] = acc_ref[:, :HD].astype(BF)
        dqkv_ref[:, 2 * width + h * HD : 2 * width + (h + 1) * HD] = acc_ref[:, HD:].astype(BF)


def attend_back(qkv, pos, out, lse, dout, heads):
    rows = qkv.shape[0]
    return pl.pallas_call(
        partial(attend_back_kernel, heads, min(256, rows)),
        out_shape=jax.ShapeDtypeStruct((rows, 3 * heads * HD), BF),
        scratch_shapes=[pltpu.VMEM((rows, 2 * HD), F32)],
        name="attend_back",
        compiler_params=pltpu.CompilerParams(vmem_limit_bytes=48 * 2**20),
    )(qkv, pos[:, None], pos[None, :], out, lse, dout)


MESH = pl.DeviceIdType.MESH


def remote(src, dst, send, recv, **to):
    return pltpu.make_async_remote_copy(
        src_ref=src, dst_ref=dst, send_sem=send, recv_sem=recv, device_id=to, device_id_type=MESH
    )


def lane_cuts(lanes, parts):
    tiles = -(-lanes // 128)
    return [min(lanes, (i * tiles + parts // 2) // parts * 128) for i in range(parts + 1)]


def column_segments(ranks, d, width, grain):
    own = 3 * d // ranks
    runs = []
    for src in range(ranks):
        for part in range(3):
            for dst in range(ranks):
                low = part * d + dst * width
                first = max(src * own, low)
                last = min((src + 1) * own, low + width, (part + 1) * d)
                if first < last:
                    at = part * width + first - low
                    runs.append(
                        (src, (first - src * own) // grain, dst, at // grain, (last - first) // grain)
                    )
    return runs


def meet(peers):
    barrier = pltpu.get_barrier_semaphore()
    for peer in peers:
        pl.semaphore_signal(barrier, inc=1, device_id=peer, device_id_type=MESH)
    pl.semaphore_wait(barrier, len(peers))


class Line:
    def __init__(self, buf, size, sems):
        self.buf, self.size = buf, size
        self.right, self.left, self.recv = sems
        self.z = lax.axis_index("z")

    def copy(self, block, way):
        send = (self.right if way > 0 else self.left).at[block]
        at = self.buf(block)
        return remote(at, at, send, self.recv.at[block], z=self.z + way)

    def start(self):
        @pl.when(self.z < self.size - 1)
        def _():
            self.copy(self.z, 1).start()

        @pl.when(self.z > 0)
        def _():
            self.copy(self.z, -1).start()

    def step(self, s, then=None):
        @pl.when(self.z >= s)
        def _():
            block = self.z - s
            self.copy(block, 1).wait_recv()

            @pl.when(self.z < self.size - 1)
            def _():
                self.copy(block, 1).start()

            if then is not None:
                then(block)

        @pl.when(self.z + s < self.size)
        def _():
            block = self.z + s
            self.copy(block, -1).wait_recv()

            @pl.when(self.z > 0)
            def _():
                self.copy(block, -1).start()

            if then is not None:
                then(block)

    def finish(self):
        for s in range(self.size):

            @pl.when((self.z >= s) & (self.z < self.size - 1))
            def _():
                self.copy(self.z - s, 1).wait_send()

            @pl.when((self.z + s < self.size) & (self.z > 0))
            def _():
                self.copy(self.z + s, -1).wait_send()


def start_kernel(
    cfg,
    tok,
    wq,
    small,
    pj,
    pos_col,
    pos_row,
    h1,
    w,
    qkv,
    att,
    lse,
    smalls,
    p2,
    toks,
    p1,
    vecs,
    small_send,
    small_recv,
    q_send,
    q_recv,
    q_local,
    x_send,
    x_recv,
    t_right,
    t_left,
    t_recv,
    c_send,
    c_recv,
    p1_send,
    p1_recv,
    p2_send,
    p2_recv,
    p_local,
):
    fs, nz, d, heads = cfg
    cs = 2 * nz
    f, z, core = lax.axis_index("fsdp"), lax.axis_index("z"), lax.axis_index("core")
    rank = 2 * z + core
    rows, lanes = tok.shape[0], wq.shape[2]
    width = heads * HD
    grain = wq.shape[1]
    own_rows = d // fs
    part = d // cs
    my_lanes = pl.ds(pl.multiple_of(f * lanes, 128), lanes)
    runs = column_segments(cs, d, width, grain)
    cuts = lane_cuts(pj.shape[1], fs)

    w[:, :, my_lanes] = jnp.zeros((w.shape[0], grain, lanes), BF)
    ranks = [lax.rem(rank + i, cs) for i in range(1, cs)]
    planes = [lax.rem(f + i, fs) for i in range(1, fs)]
    meet([dict(z=r // 2, core=lax.rem(r, 2)) for r in ranks] + [dict(fsdp=p) for p in planes])

    def run_copy(n):
        src, first, dst, at, count = runs[n]
        here, there = wq.at[pl.ds(first, count)], w.at[pl.ds(at, count), :, my_lanes]
        return remote(here, there, q_send.at[n], q_recv.at[n], z=dst // 2, core=dst % 2)

    for n, (src, first, dst, at, count) in enumerate(runs):

        @pl.when(rank == src)
        def _():
            if src == dst:
                here, there = wq.at[pl.ds(first, count)], w.at[pl.ds(at, count), :, my_lanes]
                pltpu.make_async_copy(here, there, q_local.at[n]).start()
            else:
                run_copy(n).start()

    def small_copy(i):
        r = ranks[i]
        at = smalls.at[rank]
        return remote(small, at, small_send.at[i], small_recv.at[rank], z=r // 2, core=lax.rem(r, 2))

    for i in range(cs - 1):
        small_copy(i).start()

    def p1_copy(g):
        at = pl.ds(cuts[g], cuts[g + 1] - cuts[g])
        to = p1.at[f, :, pl.ds(0, cuts[g + 1] - cuts[g])]
        return remote(pj.at[:, at], to, p1_send.at[g], p1_recv.at[f], fsdp=g)

    def p1_arrival(g, src):
        to = p1.at[src, :, pl.ds(0, cuts[g + 1] - cuts[g])]
        return remote(to, to, p1_send.at[g], p1_recv.at[src], fsdp=src)

    def p1_local(g):
        at = pl.ds(cuts[g], cuts[g + 1] - cuts[g])
        to = p1.at[f, :, pl.ds(0, cuts[g + 1] - cuts[g])]
        return pltpu.make_async_copy(pj.at[:, at], to, p_local.at[0])

    for g in range(fs):
        if cuts[g] == cuts[g + 1]:
            continue

        @pl.when(f == g)
        def _():
            p1_local(g).start()

        @pl.when(f != g)
        def _():
            p1_copy(g).start()

    for n, (src, first, dst, at, count) in enumerate(runs):

        @pl.when(rank == dst)
        def _():
            if src == dst:
                here, there = wq.at[pl.ds(first, count)], w.at[pl.ds(at, count), :, my_lanes]
                pltpu.make_async_copy(here, there, q_local.at[n]).wait()
            else:
                run_copy(n).wait_recv()

    def x_copy(i, peer):
        at = w.at[:, :, my_lanes]
        return remote(at, at, x_send.at[i], x_recv.at[f], fsdp=peer)

    def x_arrival(peer):
        at = w.at[:, :, pl.ds(pl.multiple_of(peer * lanes, 128), lanes)]
        return remote(at, at, x_send.at[0], x_recv.at[peer], fsdp=peer)

    for i, peer in enumerate(planes):
        x_copy(i, peer).start()

    pltpu.sync_copy(tok, toks.at[rank])
    line = Line(lambda b: toks.at[2 * b + core], nz, (t_right, t_left, t_recv))

    def pass_on(block):
        at = toks.at[2 * block + core]
        return remote(at, at, c_send.at[block], c_recv.at[block], core=1 - core)

    def arrival(block):
        at = toks.at[2 * block + 1 - core]
        return remote(at, at, c_send.at[block], c_recv.at[block], core=1 - core)

    line.start()
    pass_on(z).start()

    smalls[rank] = small[...]
    vecs[...] = jnp.zeros(vecs.shape, F32)
    for i, r in enumerate(ranks):
        back = lax.rem(rank + cs - 1 - i, cs)
        remote(small, smalls.at[back], small_send.at[i], small_recv.at[back], z=z).wait_recv()
    for r in range(cs):
        vecs[:, part * r : part * (r + 1)] = smalls[r, 0:8, 0:part]
    for g in range(fs):
        h1[:, lanes * g + own_rows : lanes * (g + 1)] = jnp.zeros(
            (h1.shape[0], lanes - own_rows), BF
        )

    for s in range(1, nz):
        line.step(s, lambda b: pass_on(b).start())

    def p1_wait(src):
        for g in range(fs):
            if cuts[g] < cuts[g + 1]:

                @pl.when(f == g)
                def _():
                    p1_arrival(g, src).wait_recv()

    def p2_copy(plane):
        return remote(
            p1.at[plane], p2.at[z], p2_send.at[plane], p2_recv.at[z], z=plane
        )

    for g in range(fs):
        if cuts[g] < cuts[g + 1]:

            @pl.when(f == g)
            def _():
                p1_local(g).wait()

    for i in range(1, fs):
        p1_wait(lax.rem(f + fs - i, fs))
    for plane in range(nz):

        @pl.when(z == plane)
        def _():
            pltpu.make_async_copy(p1.at[plane], p2.at[z], p_local.at[1]).start()

        @pl.when(z != plane)
        def _():
            p2_copy(plane).start()

    for b in range(nz):
        arrival(b).wait_recv()

    step = 32

    def norm_chunk(i, _):
        block, at = i // (rows // step), lax.rem(i, rows // step) * step
        x = toks[block, pl.ds(at, step), :].astype(F32)
        xhat, _ = norm_rows(x)
        h = (xhat * vecs[0:1, 0:d] + vecs[1:2, 0:d]).astype(BF)
        to = pl.ds(pl.multiple_of(i * step, step), step)
        for g in range(fs):
            h1[to, lanes * g : lanes * g + own_rows] = h[:, own_rows * g : own_rows * (g + 1)]
        return 0

    lax.fori_loop(0, cs * rows // step, norm_chunk, 0)

    for i in range(1, fs):
        x_arrival(lax.rem(f + fs - i, fs)).wait_recv()

    tall = min(256, cs * rows)
    head_lanes = pl.ds(pl.multiple_of(rank * width, 128), width)

    def project(i, _):
        at = pl.ds(pl.multiple_of(i * tall, tall), tall)
        full = dot_nt(h1[at, :], w[...].reshape(3 * width, fs * lanes))
        qkv[at, 0:width] = (full[:, 0:width] + vecs[2:3, head_lanes]).astype(BF)
        qkv[at, width : 2 * width] = full[:, width : 2 * width].astype(BF)
        qkv[at, 2 * width :] = (full[:, 2 * width :] + vecs[3:4, head_lanes]).astype(BF)
        return 0

    lax.fori_loop(0, cs * rows // tall, project, 0)
    attend_kernel(heads, tall, qkv, pos_col, pos_row, att, lse)

    for n, (src, first, dst, at, count) in enumerate(runs):
        if src != dst:

            @pl.when(rank == src)
            def _():
                run_copy(n).wait_send()

    for i in range(cs - 1):
        small_copy(i).wait_send()
    for i, peer in enumerate(planes):
        x_copy(i, peer).wait_send()
    line.finish()
    for b in range(nz):
        pass_on(b).wait_send()
    for g in range(fs):
        if cuts[g] < cuts[g + 1]:

            @pl.when(f != g)
            def _():
                p1_copy(g).wait_send()

    for plane in range(nz):

        @pl.when(z == plane)
        def _():
            pltpu.make_async_copy(p1.at[plane], p2.at[z], p_local.at[1]).wait()

        @pl.when(z != plane)
        def _():
            p2_copy(plane).wait_send()
            remote(p1.at[plane], p2.at[plane], p2_send.at[plane], p2_recv.at[plane], z=plane).wait_recv()


def start(cfg, tok, wq, small, pj, pos):
    fs, nz, d, heads = cfg
    cs = 2 * nz
    rows, lanes = tok.shape[0], wq.shape[2]
    width, length = heads * HD, rows * cs
    cuts = lane_cuts(pj.shape[1], fs)
    slab = max(b - a for a, b in zip(cuts, cuts[1:]))
    runs = len(column_segments(cs, d, width, wq.shape[1]))
    vmem = pl.BlockSpec(memory_space=pltpu.VMEM)
    hbm = pl.BlockSpec(memory_space=pl.ANY)
    sem = lambda n: pltpu.SemaphoreType.DMA((n,))
    return pl.pallas_call(
        partial(start_kernel, cfg),
        out_shape=(
            jax.ShapeDtypeStruct((length, fs * lanes), BF),
            jax.ShapeDtypeStruct((3 * width // wq.shape[1], wq.shape[1], fs * lanes), BF),
            jax.ShapeDtypeStruct((length, 3 * width), BF),
            jax.ShapeDtypeStruct((length, width), BF),
            jax.ShapeDtypeStruct((heads, length), F32),
            jax.ShapeDtypeStruct((cs,) + small.shape, F32),
            jax.ShapeDtypeStruct((nz, pj.shape[0], slab), BF),
        ),
        in_specs=[vmem, vmem, vmem, hbm, vmem, vmem],
        out_specs=(vmem, vmem, vmem, vmem, vmem, vmem, hbm),
        scratch_shapes=[
            pltpu.VMEM((cs, rows, d), BF),
            pltpu.VMEM((fs, pj.shape[0], slab), BF),
            pltpu.VMEM((8, width * cs), F32),
            sem(cs),
            sem(cs),
            sem(runs),
            sem(runs),
            sem(runs),
            sem(fs),
            sem(fs),
            sem(nz),
            sem(nz),
            sem(nz),
            sem(nz),
            sem(nz),
            sem(fs),
            sem(fs),
            sem(nz),
            sem(nz),
            sem(2),
        ],
        name="start",
        compiler_params=pltpu.CompilerParams(
            collective_id=0, has_side_effects=True, vmem_limit_bytes=56 * 2**20
        ),
    )(tok, wq, small, pj, pos[:, None], pos[None, :])


def body(
    tokens,
    block_order,
    cotangent,
    pre_attn_gain,
    pre_attn_bias,
    qkv_weight,
    query_bias,
    value_bias,
    out_weight,
    out_bias,
    pre_mlp_gain,
    pre_mlp_bias,
    fc_weight,
    fc_bias,
    proj_weight,
    proj_bias,
):
    fs, nz = lax.axis_size("fsdp"), lax.axis_size("z")
    cs = nz * 2
    rank = lax.axis_index("z") * 2 + lax.axis_index("core")
    rows, d = tokens.shape[1], tokens.shape[2]
    length = rows * cs
    heads_all = d // HD
    heads = -(-heads_all // cs)
    width = heads * HD
    padded = width * cs
    ff_chip = fc_weight.shape[1] * 2

    part, own_rows = d // cs, d // fs
    up = lambda n: -(-n // 128) * 128
    small = jnp.concatenate(
        [
            pre_attn_gain,
            pre_attn_bias,
            query_bias,
            value_bias,
            out_bias,
            pre_mlp_gain,
            pre_mlp_bias,
            proj_bias,
            fc_bias,
        ]
    ).astype(F32)
    small = jnp.pad(small.reshape(-1, part), ((0, 0), (0, up(part) - part)))
    lanes = up(own_rows)
    wq = jnp.pad(qkv_weight.T, ((0, 0), (0, lanes - own_rows)))
    grain = math.gcd(math.gcd(wq.shape[0], HD), 8)
    wq = wq.reshape(-1, grain, lanes)
    pj = jnp.pad(proj_weight.T, ((0, 0), (0, up(ff_chip) - ff_chip)))
    pos = positions(block_order, length, length // block_order.shape[0])
    h1, w, qkv, att, lse, smalls, p2 = start((fs, nz, d, heads), tokens[0], wq, small, pj, pos)
    vec = lambda i: smalls[:, i, :part].reshape(d)
    gain1, ob, gain2, shift2, pb = vec(0), vec(4), vec(5), vec(6), vec(7)
    fb = smalls[:, 8:, :part].reshape(cs, -1)
    fb_chip = lax.dynamic_slice_in_dim(fb, lax.axis_index("z") * 2, 2, 0).reshape(ff_chip)
    w = w.reshape(3 * width, fs * lanes)

    w_out = lax.all_gather(
        lax.all_gather(out_weight, CTX, axis=1, tiled=True), "fsdp", axis=0, tiled=True
    )
    fc = lax.all_gather(fc_weight, "fsdp", axis=0, tiled=True)
    fc = lax.all_gather(fc, "core", axis=1, tiled=True)
    cuts = lane_cuts(pj.shape[1], fs)
    pj_all = lax.all_gather(p2, "fsdp", axis=0)
    pj_all = jnp.concatenate([pj_all[g, :, :, : cuts[g + 1] - cuts[g]] for g in range(fs)], axis=2)
    pj_all = lax.all_gather(pj_all, "core", axis=1).reshape(d, -1)[:, :ff_chip]

    own = tokens[0].astype(F32)
    att_own = lax.all_to_all(att, CTX, split_axis=0, concat_axis=1, tiled=True)[:, :d]
    middle = own + dot(att_own, w_out) + ob

    xhat2, rstd2 = norm_rows(middle)
    h2_own = (xhat2 * gain2 + shift2).astype(BF)
    h2 = lax.all_gather(h2_own, "z", axis=0, tiled=True)
    ct = lax.all_gather(cotangent[0], "z", axis=0, tiled=True)
    before = dot(h2, fc) + fb_chip
    act, gelu_back = jax.vjp(partial(jax.nn.gelu, approximate=True), before)
    act = act.astype(BF)
    d_before = gelu_back(dot(ct, pj_all))[0].astype(BF)
    out_part = dot_nt(act, pj_all).astype(BF)
    dh2_part = dot_nt(d_before, fc).astype(BF)
    out_rows = lax.psum_scatter(out_part, "z", scatter_dimension=0, tiled=True)
    output = (middle + out_rows.astype(F32) + pb).astype(BF)
    dh2 = lax.psum_scatter(dh2_part, "z", scatter_dimension=0, tiled=True).astype(F32)

    fc_grad = lax.psum_scatter(
        dot_tn(h2, d_before).astype(BF), "core", scatter_dimension=1, tiled=True
    )
    fc_grad = lax.psum_scatter(fc_grad, "fsdp", scatter_dimension=0, tiled=True)
    proj_grad = dot_tn(act, ct).astype(BF)
    full = jnp.zeros((ff_chip * nz, d), BF)
    full = lax.dynamic_update_slice_in_dim(full, proj_grad, lax.axis_index("z") * ff_chip, 0)
    proj_grad = lax.psum_scatter(full, "fsdp", scatter_dimension=0, tiled=True)
    proj_grad = lax.psum_scatter(proj_grad, CTX, scatter_dimension=1, tiled=True)

    ct_own = cotangent[0].astype(F32)
    d_middle = ct_own + norm_back(dh2, xhat2, rstd2, gain2)
    d_branch = d_middle.astype(BF)
    out_grad = dot_tn(att_own, d_branch).astype(BF)
    out_grad = lax.psum_scatter(out_grad, CTX, scatter_dimension=1, tiled=True)
    out_grad = lax.psum_scatter(out_grad, "fsdp", scatter_dimension=0, tiled=True)
    d_att_own = dot_nt(d_branch, w_out).astype(BF)
    d_att_own = jnp.pad(d_att_own, ((0, 0), (0, padded - d)))
    d_att = lax.all_to_all(d_att_own, CTX, split_axis=1, concat_axis=0, tiled=True)
    d_qkv = attend_back(qkv, pos, att, lse, d_att, heads)
    dh1_part = dot(d_qkv, w).astype(BF).reshape(length, fs, lanes)
    dh1_part = dh1_part[:, :, :own_rows].reshape(length, d)
    dh1 = lax.psum_scatter(dh1_part, CTX, scatter_dimension=0, tiled=True).astype(F32)
    xhat1, rstd1 = norm_rows(own)
    input_grad = d_middle + norm_back(dh1, xhat1, rstd1, gain1)

    qkv_grad = dot_tn(h1, d_qkv).astype(BF).reshape(fs, lanes, 3 * width)
    qkv_grad = qkv_grad[:, :own_rows].reshape(d, 3 * width)
    qkv_grad = lax.psum_scatter(qkv_grad, "fsdp", scatter_dimension=0, tiled=True)
    full = jnp.zeros((qkv_grad.shape[0], 3, padded), BF)
    full = lax.dynamic_update_slice_in_dim(
        full, qkv_grad.reshape(-1, 3, width), rank * width, 2
    )
    qkv_grad = lax.psum_scatter(
        full[:, :, :d].reshape(-1, 3 * d), CTX, scatter_dimension=1, tiled=True
    )

    bias_cols = jnp.sum(d_qkv.astype(F32), axis=0).reshape(3, width)
    bias_full = jnp.zeros((3, padded), F32)
    bias_full = lax.dynamic_update_slice_in_dim(bias_full, bias_cols, rank * width, 1)[:, :d]
    fb_full = jnp.zeros((nz, ff_chip), F32)
    fb_full = lax.dynamic_update_slice_in_dim(
        fb_full, jnp.sum(d_before.astype(F32), axis=0)[None], lax.axis_index("z"), 0
    )
    stack = jnp.stack(
        [
            jnp.sum(dh1 * xhat1, axis=0),
            jnp.sum(dh1, axis=0),
            bias_full[0],
            bias_full[2],
            jnp.sum(d_branch.astype(F32), axis=0),
            jnp.sum(dh2 * xhat2, axis=0),
            jnp.sum(dh2, axis=0),
            jnp.sum(ct_own, axis=0),
        ]
    )
    stack = jnp.concatenate(
        [stack.reshape(8, cs, part).transpose(1, 0, 2).reshape(cs, -1), fb_full.reshape(cs, -1)],
        axis=1,
    )
    stack = lax.psum(lax.psum_scatter(stack, CTX, scatter_dimension=0, tiled=True), "fsdp")[0]
    g = [stack[i * part : (i + 1) * part] for i in range(8)]
    fb_grad = stack[8 * part :]
    return (
        output[None],
        input_grad[None],
        g[0],
        g[1],
        qkv_grad.astype(F32),
        g[2],
        g[3],
        out_grad.astype(F32),
        g[4],
        g[5],
        g[6],
        fc_grad.astype(F32),
        fb_grad,
        proj_grad.astype(F32),
        g[7],
    )


def solution(mesh):
    fs, cs = mesh.shape["fsdp"], mesh.shape["ctx"]
    split = Mesh(mesh.devices.reshape(fs, cs // 2, 2), ("fsdp", "z", "core"))
    rows = P("fsdp", CTX, None)
    weight = P("fsdp", CTX)
    vector = P(CTX)
    in_specs = (
        rows,
        P(),
        rows,
        vector,
        vector,
        weight,
        vector,
        vector,
        weight,
        vector,
        vector,
        vector,
        weight,
        vector,
        weight,
        vector,
    )
    out_specs = (
        rows,
        rows,
        vector,
        vector,
        weight,
        vector,
        vector,
        weight,
        vector,
        vector,
        vector,
        weight,
        vector,
        weight,
        vector,
    )
    return jax.shard_map(body, mesh=split, in_specs=in_specs, out_specs=out_specs, check_vma=False)
```

```python
from functools import partial
import math

import jax
import jax.numpy as jnp
from jax import lax
from jax.experimental import pallas as pl
from jax.experimental.pallas import tpu as pltpu
from jax.sharding import Mesh
from jax.sharding import PartitionSpec as P

HD = 64
EPS = 1e-05
FLOOR = -1e30
BF = jnp.bfloat16
F32 = jnp.float32
CTX = ("z", "core")
MESH = pl.DeviceIdType.MESH
VMEM = pl.BlockSpec(memory_space=pltpu.VMEM)
HBM = pl.BlockSpec(memory_space=pl.ANY)
GELU_A = math.sqrt(2.0 / math.pi)
GELU_B = 0.044715


def up(n):
    return -(-n // 128) * 128


def sems(*counts):
    return [pltpu.SemaphoreType.DMA(c if isinstance(c, tuple) else (c,)) for c in counts]


def shape(dims, kind=BF):
    return jax.ShapeDtypeStruct(dims, kind)


def dot(a, b):
    return jnp.dot(a, b, preferred_element_type=F32)


def dot_nt(a, b):
    return lax.dot_general(a, b, (((1,), (1,)), ((), ())), preferred_element_type=F32)


def dot_tn(a, b):
    return lax.dot_general(a, b, (((0,), (0,)), ((), ())), preferred_element_type=F32)


def norm_rows(rows):
    centred = rows - jnp.mean(rows, axis=-1, keepdims=True)
    rstd = lax.rsqrt(jnp.mean(centred * centred, axis=-1, keepdims=True) + EPS)
    return centred * rstd, rstd


def norm_back(upstream, xhat, rstd, gain):
    inner = upstream * gain
    return rstd * (
        inner
        - jnp.mean(inner, axis=-1, keepdims=True)
        - xhat * jnp.mean(inner * xhat, axis=-1, keepdims=True)
    )


def gelu_pair(v):
    sq = v * v
    t = jnp.tanh(GELU_A * v * (1.0 + GELU_B * sq))
    half = 0.5 * (1.0 + t)
    slope = half + 0.5 * v * (1.0 - t * t) * (GELU_A * (1.0 + 3.0 * GELU_B * sq))
    return v * half, slope


def positions(order_table, rows):
    block = rows // order_table.shape[0]
    return (order_table[:, None] * block + jnp.arange(block, dtype=jnp.int32)[None]).reshape(rows)


def remote(src, dst, send, recv, **to):
    return pltpu.make_async_remote_copy(
        src_ref=src, dst_ref=dst, send_sem=send, recv_sem=recv, device_id=to, device_id_type=MESH
    )


def column_segments(ranks, d, width, grain):
    own = 3 * d // ranks
    runs = []
    for src in range(ranks):
        for part in range(3):
            for dst in range(ranks):
                low = part * d + dst * width
                first = max(src * own, low)
                last = min((src + 1) * own, low + width, (part + 1) * d)
                if first < last:
                    at = part * width + first - low
                    runs.append(
                        (src, (first - src * own) // grain, dst, at // grain, (last - first) // grain)
                    )
    return runs


def meet(peers):
    barrier = pltpu.get_barrier_semaphore()
    for peer in peers:
        pl.semaphore_signal(barrier, inc=1, device_id=peer, device_id_type=MESH)
    pl.semaphore_wait(barrier, len(peers))


class Line:
    def __init__(self, at, size, sems):
        self.at, self.size = at, size
        self.right, self.left, self.recv = sems
        self.z = lax.axis_index("z")

    def copy(self, block, way):
        send = (self.right if way > 0 else self.left).at[block]
        at = self.at(block)
        return remote(at, at, send, self.recv.at[block], z=self.z + way)

    def start(self):
        @pl.when(self.z < self.size - 1)
        def _():
            self.copy(self.z, 1).start()

        @pl.when(self.z > 0)
        def _():
            self.copy(self.z, -1).start()

    def step(self, s, then=None):
        @pl.when(self.z >= s)
        def _():
            block = self.z - s
            self.copy(block, 1).wait_recv()

            @pl.when(self.z < self.size - 1)
            def _():
                self.copy(block, 1).start()

            if then is not None:
                then(block)

        @pl.when(self.z + s < self.size)
        def _():
            block = self.z + s
            self.copy(block, -1).wait_recv()

            @pl.when(self.z > 0)
            def _():
                self.copy(block, -1).start()

            if then is not None:
                then(block)

    def finish(self):
        for s in range(self.size):

            @pl.when((self.z >= s) & (self.z < self.size - 1))
            def _():
                self.copy(self.z - s, 1).wait_send()

            @pl.when((self.z + s < self.size) & (self.z > 0))
            def _():
                self.copy(self.z + s, -1).wait_send()


class LineSum:
    def __init__(self, parts, from_left, from_right, size, sems):
        self.parts, self.ins, self.size = parts, (from_left, from_right), size
        self.send, self.recv_left, self.recv_right = sems
        self.z = lax.axis_index("z")

    def copy(self, block, way):
        recv = self.recv_left if way > 0 else self.recv_right
        there = self.ins[0 if way > 0 else 1].at[block]
        return remote(
            self.parts.at[block], there, self.send.at[block], recv.at[block], z=self.z + way
        )

    def first(self):
        for way, edge in ((1, 0), (-1, self.size - 1)):

            @pl.when(self.z == edge)
            def _():
                for hop in range(self.size - 1, 0, -1):
                    self.copy(self.z + way * hop, way).start()

    def add_on(self, block, way):
        self.copy(block, way).wait_recv()
        came = self.ins[0 if way > 0 else 1]
        self.parts[block] = (
            self.parts[block].astype(F32) + came[block].astype(F32)
        ).astype(self.parts.dtype)
        self.copy(block, way).start()

    def step(self, s):
        right, left = self.z + self.size - 1 - s, s - (self.size - 1 - self.z)

        @pl.when((self.z > 0) & (right < self.size) & (right > self.z))
        def _():
            self.add_on(right, 1)

        @pl.when((self.z < self.size - 1) & (left >= 0) & (left < self.z))
        def _():
            self.add_on(left, -1)

    def finish(self):
        @pl.when(self.z > 0)
        def _():
            self.copy(self.z, 1).wait_recv()

        @pl.when(self.z == 0)
        def _():
            self.ins[0][self.z] = jnp.zeros(self.parts.shape[1:], self.parts.dtype)

        @pl.when(self.z < self.size - 1)
        def _():
            self.copy(self.z, -1).wait_recv()

        @pl.when(self.z == self.size - 1)
        def _():
            self.ins[1][self.z] = jnp.zeros(self.parts.shape[1:], self.parts.dtype)

    def sent(self):
        for block in range(self.size):

            @pl.when(self.z < block)
            def _():
                self.copy(block, 1).wait_send()

            @pl.when(self.z > block)
            def _():
                self.copy(block, -1).wait_send()


def halves(n):
    return ((0, n // 2), (n // 2, n - n // 2))


class Plane:
    def __init__(self, size):
        self.size, self.f = size, lax.axis_index("fsdp")
        self.square = size == 4
        f = self.f
        self.peers = [lax.rem(f + i, size) for i in range(1, size)]
        if self.square:
            self.x, self.y, self.far = f + 1 - 2 * lax.rem(f, 2), lax.rem(f + 2, 4), 3 - f
            self.peers = [self.x, self.y, self.far]


class PlaneGather:
    def __init__(self, plane, at, sems):
        self.p, self.at = plane, at
        self.send, self.recv = sems
        f = plane.f
        if plane.square:
            x, y = plane.x, plane.y
            self.early = [(f, 0, x), (f, 1, y), (f, 0, y), (f, 1, x)]
            self.late = [(x, 0, y), (y, 1, x)]
        else:
            self.early = [(f, h, g) for g in plane.peers for h in range(2)]
            self.late = []

    def copy(self, n, move):
        g, half, to = move
        at = self.at(g, half)
        return remote(at, at, self.send.at[n], self.recv.at[g, half], fsdp=to)

    def arrive(self, g, half):
        at = self.at(g, half)
        remote(at, at, self.send.at[0], self.recv.at[g, half], fsdp=g).wait_recv()

    def start(self):
        for n, move in enumerate(self.early):
            self.copy(n, move).start()

    def mid(self):
        for n, move in enumerate(self.late):
            self.arrive(move[0], move[1])
            self.copy(len(self.early) + n, move).start()

    def end(self):
        known = [(m[0], m[1]) for m in self.late]
        for g in self.p.peers:
            for half in range(2):
                if not any(g is a and half == b for a, b in known):
                    self.arrive(g, half)

    def sent(self):
        for n, move in enumerate(self.early + self.late):
            self.copy(n, move).wait_send()


class PlaneSum:
    def __init__(self, plane, at, came, sems):
        self.p, self.at, self.came = plane, at, came
        self.send, self.recv = sems
        if plane.square:
            x, y, far = plane.x, plane.y, plane.far
            self.early = [(far, 0, x, 0), (far, 1, y, 1), (x, 0, x, 2), (y, 1, y, 3)]
            self.late = [(y, 0, y, 4), (x, 1, x, 5)]
            self.mine = [[2, 4], [3, 5]]
        else:
            n = plane.size
            self.early = [
                (g, h, g, 2 * i + h) for i, g in enumerate(plane.peers) for h in range(2)
            ]
            self.late = []
            self.mine = [[2 * i + h for i in range(n - 1)] for h in range(2)]

    def copy(self, move):
        g, half, to, slot = move
        return remote(
            self.at(g, half), self.came(slot, half), self.send.at[slot], self.recv.at[slot], fsdp=to
        )

    def arrive(self, slot, half):
        there = self.came(slot, half)
        remote(
            there, there, self.send.at[slot], self.recv.at[slot], fsdp=self.p.peers[0]
        ).wait_recv()

    def start(self):
        for move in self.early:
            self.copy(move).start()

    def mid(self):
        for slot, move in enumerate(self.late):
            self.arrive(slot, move[1])
            at, came = self.at(move[0], move[1]), self.came(slot, move[1])
            at[...] = (at[...].astype(F32) + came[...].astype(F32)).astype(at.dtype)
            self.copy(move).start()

    def end(self):
        for half in range(2):
            for slot in self.mine[half]:
                self.arrive(slot, half)

    def total(self, half):
        out = self.at(self.p.f, half)[...].astype(F32)
        for slot in self.mine[half]:
            out += self.came(slot, half)[...].astype(F32)
        return out

    def sent(self):
        for move in self.early + self.late:
            self.copy(move).wait_send()


def query_block(length):
    return max(128, min(256, length, 256 * 1024 // length))


def attend_head(h, width, q_block, qkv, pos_col, pos_row, out, lse):
    rows = qkv.shape[0]
    k = qkv[:, width + h * HD : width + (h + 1) * HD]
    v = qkv[:, 2 * width + h * HD : 2 * width + (h + 1) * HD]
    for b in range(rows // q_block):
        at = slice(b * q_block, (b + 1) * q_block)
        q = qkv[at, h * HD : (h + 1) * HD] * BF(HD**-0.5)
        s = dot_nt(k, q)
        s = jnp.where(pos_col[...] <= pos_row[:, at], s, FLOOR)
        top = jnp.max(s, axis=0, keepdims=True)
        p = jnp.exp(s - top)
        total = jnp.sum(p, axis=0, keepdims=True)
        o = dot_tn(v, p.astype(BF)) * (1.0 / total)
        out[at, h * HD : (h + 1) * HD] = o.T.astype(BF)
        lse[h : h + 1, at] = top + jnp.log(total)


def attend_back_head(h, width, q_block, qkv, pos_col, pos_row, out, lse, dout, dqkv, acc):
    rows = qkv.shape[0]
    k = qkv[:, width + h * HD : width + (h + 1) * HD]
    v = qkv[:, 2 * width + h * HD : 2 * width + (h + 1) * HD]
    for b in range(rows // q_block):
        at = slice(b * q_block, (b + 1) * q_block)
        q = qkv[at, h * HD : (h + 1) * HD] * BF(HD**-0.5)
        do = dout[at, h * HD : (h + 1) * HD]
        o = out[at, h * HD : (h + 1) * HD]
        delta = jnp.sum(do.astype(F32).T * o.astype(F32).T, axis=0, keepdims=True)
        s = dot_nt(k, q)
        p = jnp.where(pos_col[...] <= pos_row[:, at], jnp.exp(s - lse[h : h + 1, at]), 0.0)
        dp = dot_nt(v, do)
        ds = (p * (dp - delta)).astype(BF)
        dq = dot_tn(k, ds) * (HD**-0.5)
        dqkv[at, h * HD : (h + 1) * HD] = dq.T.astype(BF)
        dk = dot(ds, q)
        dv = dot(p.astype(BF), do)
        if b == 0:
            acc[:, :HD] = dk
            acc[:, HD:] = dv
        else:
            acc[:, :HD] += dk
            acc[:, HD:] += dv
    dqkv[:, width + h * HD : width + (h + 1) * HD] = acc[:, :HD].astype(BF)
    dqkv[:, 2 * width + h * HD : 2 * width + (h + 1) * HD] = acc[:, HD:].astype(BF)


def start_kernel(
    cfg,
    tok,
    wq,
    small,
    pj,
    ot,
    pos_col,
    pos_row,
    h1,
    w,
    qkv,
    att,
    lse,
    smalls,
    p1,
    o_all,
    a_own,
    toks,
    vecs,
    small_send,
    small_recv,
    q_send,
    q_recv,
    q_local,
    x_send,
    x_recv,
    t_right,
    t_left,
    t_recv,
    c_send,
    c_recv,
    p1_send,
    p1_recv,
    p_local,
    a_send,
    a_recv,
    o_right,
    o_left,
    o_recv,
    ox_send,
    ox_recv,
    oc_send,
    oc_recv,
):
    fs, nz, d, heads = cfg
    cs = 2 * nz
    f, z, core = lax.axis_index("fsdp"), lax.axis_index("z"), lax.axis_index("core")
    rank = 2 * z + core
    rows, lanes = tok.shape[0], wq.shape[2]
    width = heads * HD
    grain = wq.shape[1]
    own_rows = d // fs
    part = d // cs
    lanes_of = lambda g: pl.ds(pl.multiple_of(g * lanes, 128), lanes)
    runs = column_segments(cs, d, width, grain)
    plane = Plane(fs)
    planes = plane.peers

    w[:, :, lanes_of(f)] = jnp.zeros((w.shape[0], grain, lanes), BF)
    own_out = o_all.at[rank, :, :, lanes_of(f)]
    pltpu.sync_copy(ot, own_out)
    ranks = [lax.rem(rank + i, cs) for i in range(1, cs)]
    meet([dict(z=r // 2, core=lax.rem(r, 2)) for r in ranks] + [dict(fsdp=p) for p in planes])

    def run_copy(n):
        src, first, dst, at, count = runs[n]
        here, there = wq.at[pl.ds(first, count)], w.at[pl.ds(at, count), :, lanes_of(f)]
        if src == dst:
            return pltpu.make_async_copy(here, there, q_local.at[n])
        return remote(here, there, q_send.at[n], q_recv.at[n], z=dst // 2, core=dst % 2)

    for n, run in enumerate(runs):

        @pl.when(rank == run[0])
        def _():
            run_copy(n).start()

    def small_copy(i):
        r = ranks[i]
        to = smalls.at[rank]
        return remote(small, to, small_send.at[i], small_recv.at[rank], z=r // 2, core=lax.rem(r, 2))

    for i in range(cs - 1):
        small_copy(i).start()

    share = p1.shape[1]

    def p1_copy(i):
        here = pj.at[pl.ds(planes[i] * share, share)]
        return remote(here, p1.at[f], p1_send.at[i], p1_recv.at[f], fsdp=planes[i])

    p1_local = pltpu.make_async_copy(pj.at[pl.ds(f * share, share)], p1.at[f], p_local.at[0])
    p1_local.start()
    for i in range(fs - 1):
        p1_copy(i).start()

    def ox_copy(i, block):
        at = o_all.at[2 * block + core, :, :, lanes_of(f)]
        return remote(at, at, ox_send.at[i, block], ox_recv.at[f, block], fsdp=planes[i])

    def ox_arrival(g, block):
        at = o_all.at[2 * block + core, :, :, lanes_of(g)]
        return remote(at, at, ox_send.at[0, block], ox_recv.at[g, block], fsdp=g)

    def oc_copy(g, block):
        at = o_all.at[2 * block + core, :, :, lanes_of(g)]
        return remote(at, at, oc_send.at[g, block], oc_recv.at[g, block], core=1 - core)

    def oc_arrival(g, block):
        at = o_all.at[2 * block + 1 - core, :, :, lanes_of(g)]
        return remote(at, at, oc_send.at[g, block], oc_recv.at[g, block], core=1 - core)

    def out_block(block):
        for i in range(fs - 1):
            ox_copy(i, block).start()
        oc_copy(f, block).start()

    out_block(z)

    for n, run in enumerate(runs):

        @pl.when(rank == run[2])
        def _():
            if run[0] == run[2]:
                run_copy(n).wait()
            else:
                run_copy(n).wait_recv()

    gather = PlaneGather(
        plane, lambda g, h: w.at[pl.ds(*halves(w.shape[0])[h]), :, lanes_of(g)], (x_send, x_recv)
    )
    gather.start()

    pltpu.sync_copy(tok, toks.at[rank])
    line = Line(lambda b: toks.at[2 * b + core], nz, (t_right, t_left, t_recv))

    def pass_on(block):
        at = toks.at[2 * block + core]
        return remote(at, at, c_send.at[block], c_recv.at[block], core=1 - core)

    def arrival(block):
        at = toks.at[2 * block + 1 - core]
        return remote(at, at, c_send.at[block], c_recv.at[block], core=1 - core)

    line.start()
    pass_on(z).start()

    smalls[rank] = small[...]
    vecs[...] = jnp.zeros(vecs.shape, F32)
    for i in range(1, cs):
        back = lax.rem(rank + cs - i, cs)
        remote(small, smalls.at[back], small_send.at[i - 1], small_recv.at[back], z=z).wait_recv()
    for r in range(cs):
        vecs[:, part * r : part * (r + 1)] = smalls[r, 0:8, 0:part]
    for g in range(fs):
        h1[:, lanes * g + own_rows : lanes * (g + 1)] = jnp.zeros(
            (h1.shape[0], lanes - own_rows), BF
        )

    for s in range(1, nz):
        line.step(s, lambda b: pass_on(b).start())

    out_line = Line(
        lambda b: o_all.at[2 * b + core, :, :, lanes_of(f)], nz, (o_right, o_left, o_recv)
    )
    out_line.start()
    gather.mid()
    for b in range(nz):
        arrival(b).wait_recv()

    step = min(32, rows)

    def norm_chunk(i, _):
        block, at = i // (rows // step), lax.rem(i, rows // step) * step
        xhat, _ = norm_rows(toks[block, pl.ds(at, step), :].astype(F32))
        h = (xhat * vecs[0:1, 0:d] + vecs[1:2, 0:d]).astype(BF)
        to = pl.ds(pl.multiple_of(i * step, step), step)
        for g in range(fs):
            h1[to, lanes * g : lanes * g + own_rows] = h[:, own_rows * g : own_rows * (g + 1)]
        return 0

    lax.fori_loop(0, cs * rows // step, norm_chunk, 0)
    out_line.step(1, out_block)
    gather.end()

    tall = min(256, cs * rows)
    head_lanes = pl.ds(pl.multiple_of(rank * width, 128), width)

    def project(i, _):
        at = pl.ds(pl.multiple_of(i * tall, tall), tall)
        full = dot_nt(h1[at, :], w[...].reshape(3 * width, fs * lanes))
        qkv[at, 0:width] = (full[:, 0:width] + vecs[2:3, head_lanes]).astype(BF)
        qkv[at, width : 2 * width] = full[:, width : 2 * width].astype(BF)
        qkv[at, 2 * width :] = (full[:, 2 * width :] + vecs[3:4, head_lanes]).astype(BF)
        return 0

    lax.fori_loop(0, cs * rows // tall, project, 0)
    for s in range(2, nz):
        out_line.step(s, out_block)
    for h in range(heads):
        attend_head(h, width, query_block(cs * rows), qkv, pos_col, pos_row, att, lse)

    def a_copy(i):
        r = ranks[i]
        here = att.at[pl.ds(pl.multiple_of(r * rows, rows), rows)]
        there = a_own.at[:, head_lanes]
        return remote(here, there, a_send.at[i], a_recv.at[rank], z=r // 2, core=lax.rem(r, 2))

    for i in range(cs - 1):
        a_copy(i).start()
    a_own[:, head_lanes] = att[pl.ds(pl.multiple_of(rank * rows, rows), rows), :]

    for g in planes:
        for b in range(nz):
            ox_arrival(g, b).wait_recv()
            oc_copy(g, b).start()
    for i in range(1, cs):
        back = lax.rem(rank + cs - i, cs)
        to = a_own.at[:, pl.ds(pl.multiple_of(back * width, 128), width)]
        remote(to, to, a_send.at[0], a_recv.at[back], z=z).wait_recv()
    p1_local.wait()
    for g in planes:
        remote(p1.at[g], p1.at[g], p1_send.at[0], p1_recv.at[g], fsdp=g).wait_recv()
    for g in range(fs):
        for b in range(nz):
            oc_arrival(g, b).wait_recv()

    for n, run in enumerate(runs):
        if run[0] != run[2]:

            @pl.when(rank == run[0])
            def _():
                run_copy(n).wait_send()

    for i in range(cs - 1):
        small_copy(i).wait_send()
        a_copy(i).wait_send()
    gather.sent()
    for i in range(fs - 1):
        p1_copy(i).wait_send()
        for b in range(nz):
            ox_copy(i, b).wait_send()
    for g in range(fs):
        for b in range(nz):
            oc_copy(g, b).wait_send()
    line.finish()
    out_line.finish()
    for b in range(nz):
        pass_on(b).wait_send()


def start(cfg, tok, wq, small, pj, ot, pos):
    fs, nz, d, heads = cfg
    cs = 2 * nz
    rows, lanes = tok.shape[0], wq.shape[2]
    width, length = heads * HD, rows * cs
    runs = len(column_segments(cs, d, width, wq.shape[1]))
    return pl.pallas_call(
        partial(start_kernel, cfg),
        out_shape=(
            shape((length, fs * lanes)),
            shape((3 * width // wq.shape[1], wq.shape[1], fs * lanes)),
            shape((length, 3 * width)),
            shape((length, width)),
            shape((heads, length), F32),
            shape((cs,) + small.shape, F32),
            shape((fs, pj.shape[0] // fs) + pj.shape[1:]),
            shape((cs,) + ot.shape[:2] + (fs * lanes,)),
            shape((rows, cs * width)),
        ),
        in_specs=[VMEM, VMEM, VMEM, HBM, HBM, VMEM, VMEM],
        out_specs=(VMEM, VMEM, VMEM, VMEM, VMEM, VMEM, HBM, HBM, VMEM),
        scratch_shapes=[
            pltpu.VMEM((cs, rows, d), BF),
            pltpu.VMEM((8, width * cs), F32),
        ]
        + sems(cs, cs, runs, runs, runs, 2 * fs, (fs, 2), nz, nz, nz, nz, nz, fs, fs, 1, cs, cs)
        + sems(nz, nz, nz, (fs, nz), (fs, nz), (fs, nz), (fs, nz)),
        name="start",
        compiler_params=pltpu.CompilerParams(
            collective_id=0, has_side_effects=True, vmem_limit_bytes=56 * 2**20
        ),
    )(tok, wq, small, pj, ot, pos[:, None], pos[None, :])


def middle_kernel(
    cfg,
    a_own,
    tok,
    ct,
    ct_split,
    vec,
    fb,
    o_all,
    p1,
    fc,
    middle,
    d_middle,
    d_att,
    out_part,
    fc_grad,
    p_sum,
    og,
    sums,
    a_pad,
    ov,
    fcv,
    pjv,
    p2,
    ctb,
    cto,
    h2b,
    actb,
    dbo,
    dbp,
    dh,
    in_left,
    in_right,
    own_dh,
    da,
    dsp,
    pg,
    pr,
    stage,
    local,
    p2_send,
    p2_recv,
    p3_send,
    p3_recv,
    pc_send,
    pc_recv,
    f_send,
    f_recv,
    fc_send,
    fc_recv,
    c_right,
    c_left,
    c_recv,
    h_right,
    h_left,
    h_recv,
    e_send,
    e_recv,
    r_send,
    r_left,
    r_right,
    d_send,
    d_recv,
    g_send,
    g_recv,
):
    fs, nz, d, heads = cfg
    cs = 2 * nz
    f, z, core = lax.axis_index("fsdp"), lax.axis_index("z"), lax.axis_index("core")
    rank = 2 * z + core
    rows = tok.shape[0]
    width = heads * HD
    lanes = o_all.shape[3] // fs
    own_rows, part = d // fs, d // cs
    share, grain = p1.shape[1], p1.shape[2]
    he, hf = ct_split.shape[1] // 2, fc.shape[2]
    slot = he // nz
    ff = 2 * hf
    fc_rows = fc.shape[0]
    tall = nz * rows
    step = min(32, rows)
    plane = Plane(fs)
    ranks = [lax.rem(rank + i, cs) for i in range(1, cs)]
    half_at = lambda k: pl.ds(pl.multiple_of(k * hf, 128), hf)
    e_at = lambda k: pl.ds(pl.multiple_of(k * he, 128), he)

    load_out = pltpu.make_async_copy(o_all, ov, local.at[0])
    fc_at = lambda g, k, h: fcv.at[
        pl.ds(g * fc_rows + halves(fc_rows)[h][0], halves(fc_rows)[h][1]), :, half_at(k)
    ]
    load_fc = [
        pltpu.make_async_copy(fc.at[pl.ds(*halves(fc_rows)[h])], fc_at(f, core, h), local.at[1 + h])
        for h in range(2)
    ]
    load_p2 = pltpu.make_async_copy(p1.at[z], p2.at[z], local.at[3])
    load_out.start()
    for copy in load_fc:
        copy.start()
    load_p2.start()
    meet(
        [dict(z=r // 2, core=lax.rem(r, 2)) for r in ranks] + [dict(fsdp=p) for p in plane.peers]
    )

    def swap(n, here, there):
        return remote(here, there, e_send.at[n], e_recv.at[n], core=1 - core)

    def p2_copy(i):
        to = lax.rem(z + i, nz)
        return remote(p1.at[to], p2.at[z], p2_send.at[to], p2_recv.at[z], z=to)

    for i in range(1, nz):
        p2_copy(i).start()

    for copy in load_fc:
        copy.wait()
    fc_gather = PlaneGather(plane, lambda g, h: fc_at(g, core, h), (f_send, f_recv))
    fc_gather.start()

    def fc_pass(g):
        at = fcv.at[pl.ds(g * fc_rows, fc_rows), :, half_at(core)]
        return remote(at, at, fc_send.at[g], fc_recv.at[g], core=1 - core)

    def fc_came(g):
        at = fcv.at[pl.ds(g * fc_rows, fc_rows), :, half_at(1 - core)]
        return remote(at, at, fc_send.at[g], fc_recv.at[g], core=1 - core)

    fc_pass(f).start()

    ctb[z] = ct_split[...]
    c_line = Line(lambda b: ctb.at[b], nz, (c_right, c_left, c_recv))
    c_line.start()

    for g in range(fs):
        a_pad[core, :, lanes * g : lanes * g + own_rows] = a_own[
            :, own_rows * g : own_rows * (g + 1)
        ]
        a_pad[core, :, lanes * g + own_rows : lanes * (g + 1)] = jnp.zeros(
            (rows, lanes - own_rows), BF
        )
    swap_a = swap(4, a_pad.at[core], a_pad.at[core])
    swap_a.start()
    load_out.wait()
    branch = dot_nt(a_pad[core], ov[...].reshape(d, fs * lanes))
    middle[...] = tok[...].astype(F32) + branch + vec[0:1, :]

    def norm_chunk(i, _):
        at = pl.ds(pl.multiple_of(i * step, step), step)
        xhat, _ = norm_rows(middle[at, :])
        h2b[core, z, at, :] = (xhat * vec[1:2, :] + vec[2:3, :]).astype(BF)
        return 0

    lax.fori_loop(0, rows // step, norm_chunk, 0)
    h_line = Line(lambda b: h2b.at[core, b], nz, (h_right, h_left, h_recv))
    h_line.start()
    c_line.step(1)
    fc_gather.mid()
    h_line.step(1)

    load_p2.wait()
    for i in range(1, nz):
        back = lax.rem(z + nz - i, nz)
        remote(p2.at[back], p2.at[back], p2_send.at[0], p2_recv.at[back], z=back).wait_recv()
    half_z = lambda h: pl.ds(*halves(nz)[h])
    pjv[core, :, f] = p2[...]
    p_gather = PlaneGather(plane, lambda g, h: pjv.at[core, half_z(h), g], (p3_send, p3_recv))
    p_gather.start()

    def p_pass(g):
        at = pjv.at[core, :, g]
        return remote(at, at, pc_send.at[g], pc_recv.at[g], core=1 - core)

    def p_came(g):
        at = pjv.at[1 - core, :, g]
        return remote(at, at, pc_send.at[g], pc_recv.at[g], core=1 - core)

    p_pass(f).start()
    for s in range(2, nz):
        c_line.step(s)
        h_line.step(s)
    swap_ct = swap(0, ctb.at[:, :, e_at(1 - core)], cto)
    swap_h2 = swap(1, h2b.at[core], h2b.at[core])
    swap_h2.start()
    swap_ct.start()
    fc_gather.end()
    for g in plane.peers:
        fc_pass(g).start()
    p_gather.mid()
    for g in range(fs):
        fc_came(g).wait_recv()
    p_gather.end()
    for g in plane.peers:
        p_pass(g).start()
    for g in range(fs):
        p_came(g).wait_recv()

    chunk = 256 if ff % 256 == 0 else 128

    def feed(i, _):
        at = pl.ds(pl.multiple_of(i * chunk, chunk), chunk)
        before = dot(h2b[core].reshape(tall, d), fcv[:, :, at].reshape(d, chunk)) + fb[:, at]
        act, slope = gelu_pair(before)
        actb[core, :, :, at] = act.astype(BF).reshape(nz, rows, chunk)
        back = dot(ctb[...].reshape(tall, 2 * he), pjv[:, :, :, :, :, at].reshape(2 * he, chunk))
        low = (back * slope).astype(BF)
        dbo[:, :, at] = low.reshape(nz, rows, chunk)
        sums[4:5, at] = jnp.sum(low.astype(F32), axis=0, keepdims=True)
        return 0

    lax.fori_loop(0, ff // chunk, feed, 0)
    swap_act = swap(2, actb.at[core], actb.at[core])
    swap_db = swap(3, dbo.at[:, :, half_at(1 - core)], dbp)
    swap_act.start()
    swap_db.start()

    def hidden_back(i, _):
        block = lax.rem(z + 1 + i, nz)
        part = dot_nt(dbo[block], fcv[...].reshape(d, ff))
        dh[block] = part.astype(BF)

        @pl.when(block == z)
        def _():
            own_dh[...] = part

        return 0

    lax.fori_loop(0, nz, hidden_back, 0)
    r_line = LineSum(dh, in_left, in_right, nz, (r_send, r_left, r_right))
    r_line.first()

    def output_part(k, i):
        w = pjv[k, i].reshape(slot, ff)
        part = dot_nt(actb[core].reshape(tall, ff), w)
        low = k * he + i * slot
        ctb[:, :, low : low + slot] = part.astype(BF).reshape(nz, rows, slot)

    swap_ct.wait_recv()
    swap_act.wait_recv()
    pieces = 2 if hf % 256 == 0 or ff % 512 else 4
    for low in range(0, ff, ff // pieces):
        cols = slice(low, low + ff // pieces)
        pg[:, :, :, :, cols] = (
            (
                dot_tn(
                    ctb[:, :, e_at(core)].reshape(tall, he),
                    actb[core, :, :, cols].reshape(tall, ff // pieces),
                )
                + dot_tn(
                    cto[...].reshape(tall, he),
                    actb[1 - core, :, :, cols].reshape(tall, ff // pieces),
                )
            )
            .astype(BF)
            .reshape(nz, fs, share, grain, ff // pieces)
        )
    p_total = PlaneSum(
        plane,
        lambda g, h: pg.at[half_z(h), g],
        lambda n, h: pr.at[n, pl.ds(0, halves(nz)[h][1])],
        (g_send, g_recv),
    )
    p_total.start()
    c_line.finish()
    swap_ct.wait_send()
    keep_out = pltpu.make_async_copy(ctb, out_part, local.at[6])
    for s in range(1, nz - 1):
        r_line.step(s)
        if s == 1:
            for k in range(2):
                for i in range(nz):
                    output_part(k, i)
            keep_out.start()
    swap_h2.wait_recv()
    swap_db.wait_recv()
    own_db = dbo[:, :, half_at(core)].reshape(tall, hf)
    other_db = dbp[...].reshape(tall, hf)
    cut = 512
    for low in range(0, d, cut):
        high = min(d, low + cut)
        fc_grad[low:high, :] = (
            dot_tn(h2b[core, :, :, low:high].reshape(tall, high - low), own_db)
            + dot_tn(h2b[1 - core, :, :, low:high].reshape(tall, high - low), other_db)
        ).astype(BF)
    p_total.mid()
    r_line.finish()

    sums[0:4, :] = jnp.zeros((4, sums.shape[1]), F32)
    dsp[core] = jnp.zeros(dsp.shape[1:], BF)

    def norm_back_chunk(i, _):
        at = pl.ds(pl.multiple_of(i * step, step), step)
        g = own_dh[at, :] + in_left[z, at, :].astype(F32) + in_right[z, at, :].astype(F32)
        xhat, rstd = norm_rows(middle[at, :])
        dm = ct[at, :].astype(F32) + norm_back(g, xhat, rstd, vec[1:2, :])
        low = dm.astype(BF)
        d_middle[at, :] = dm
        for c in range(cs):
            to = (c % 2) * he + (c // 2) * slot
            dsp[core, at, to : to + part] = low[:, c * part : (c + 1) * part]
        sums[0:1, 0:d] += jnp.sum(low.astype(F32), axis=0, keepdims=True)
        sums[1:2, 0:d] += jnp.sum(g * xhat, axis=0, keepdims=True)
        sums[2:3, 0:d] += jnp.sum(g, axis=0, keepdims=True)
        sums[3:4, 0:d] += jnp.sum(ct[at, :].astype(F32), axis=0, keepdims=True)
        return 0

    lax.fori_loop(0, rows // step, norm_back_chunk, 0)
    swap_d = swap(5, dsp.at[core], dsp.at[core])
    swap_d.start()
    back = dot(d_middle[...].astype(BF), ov[...].reshape(d, fs * lanes)).astype(BF)
    for g in range(fs):
        da[:, own_rows * g : own_rows * (g + 1)] = back[:, lanes * g : lanes * g + own_rows]
    if d < cs * width:
        da[:, d:] = jnp.zeros((rows, cs * width - d), BF)

    def d_copy(i):
        r = ranks[i]
        here = da.at[:, pl.ds(pl.multiple_of(r * width, 128), width)]
        there = d_att.at[pl.ds(pl.multiple_of(rank * rows, rows), rows)]
        return remote(here, there, d_send.at[i], d_recv.at[rank], z=r // 2, core=lax.rem(r, 2))

    for i in range(cs - 1):
        d_copy(i).start()
    d_att[pl.ds(pl.multiple_of(rank * rows, rows), rows), :] = da[
        :, pl.ds(pl.multiple_of(rank * width, 128), width)
    ]

    swap_a.wait_recv()
    swap_d.wait_recv()

    def stage_out(g):
        at = pl.ds(g * lanes, lanes)
        return pltpu.make_async_copy(stage.at[g % 2], og.at[:, :, :, at], local.at[4 + g % 2])

    for g in range(fs):
        at = slice(g * lanes, (g + 1) * lanes)
        part_sum = dot_tn(
            dsp[:, :, e_at(core)].reshape(2 * rows, he), a_pad[:, :, at].reshape(2 * rows, lanes)
        )
        part_sum = part_sum.astype(BF).reshape(nz, slot // grain, grain, lanes)
        if g >= 2:
            stage_out(g - 2).wait()
        stage[g % 2] = part_sum[:, : og.shape[1]]
        stage_out(g).start()
    for g in range(max(fs - 2, 0), fs):
        stage_out(g).wait()

    p_total.end()
    for h in range(2):
        p_sum[half_z(h)] = p_total.total(h).astype(BF)
    for i in range(1, cs):
        back = lax.rem(rank + cs - i, cs)
        to = d_att.at[pl.ds(pl.multiple_of(back * rows, rows), rows)]
        remote(to, to, d_send.at[0], d_recv.at[back], z=z).wait_recv()

    for i in range(1, nz):
        p2_copy(i).wait_send()
    for i in range(cs - 1):
        d_copy(i).wait_send()
    for g in range(fs):
        fc_pass(g).wait_send()
        p_pass(g).wait_send()
    fc_gather.sent()
    p_gather.sent()
    p_total.sent()
    keep_out.wait()
    h_line.finish()
    r_line.sent()
    for s in (swap_h2, swap_act, swap_db, swap_a, swap_d):
        s.wait_send()


def middle_part(cfg, a_own, tok, ct, ct_split, vec, fb, o_all, p1, fc):
    fs, nz, d, heads = cfg
    cs = 2 * nz
    rows, width = tok.shape[0], heads * HD
    length = rows * cs
    lanes = o_all.shape[3] // fs
    he, hf = ct_split.shape[1] // 2, fc.shape[2]
    share, grain = p1.shape[1], p1.shape[2]
    return pl.pallas_call(
        partial(middle_kernel, cfg),
        out_shape=(
            shape((rows, d), F32),
            shape((rows, d), F32),
            shape((length, width)),
            shape((nz, rows, 2 * he)),
            shape((d, hf)),
            shape((nz, share, grain, 2 * hf)),
            shape((nz,) + o_all.shape[1:]),
            shape((5, max(2 * hf, d)), F32),
        ),
        in_specs=[VMEM] * 6 + [HBM] * 3,
        out_specs=(VMEM, VMEM, VMEM, HBM, VMEM, VMEM, HBM, VMEM),
        scratch_shapes=[
            pltpu.VMEM((2, rows, fs * lanes), BF),
            pltpu.VMEM(o_all.shape, BF),
            pltpu.VMEM((fs * fc.shape[0], fc.shape[1], 2 * hf), BF),
            pltpu.VMEM((2, nz, fs, share, grain, 2 * hf), BF),
            pltpu.VMEM((nz, share, grain, 2 * hf), BF),
            pltpu.VMEM((nz, rows, 2 * he), BF),
            pltpu.VMEM((nz, rows, he), BF),
            pltpu.VMEM((2, nz, rows, d), BF),
            pltpu.VMEM((2, nz, rows, 2 * hf), BF),
            pltpu.VMEM((nz, rows, 2 * hf), BF),
            pltpu.VMEM((nz, rows, hf), BF),
            pltpu.VMEM((nz, rows, d), BF),
            pltpu.VMEM((nz, rows, d), BF),
            pltpu.VMEM((nz, rows, d), BF),
            pltpu.VMEM((rows, d), F32),
            pltpu.VMEM((rows, cs * width), BF),
            pltpu.VMEM((2, rows, 2 * he), BF),
            pltpu.VMEM((nz, fs, share, grain, 2 * hf), BF),
            pltpu.VMEM((2 * (fs - 1), nz - nz // 2, share, grain, 2 * hf), BF),
            pltpu.VMEM((2, nz) + o_all.shape[1:3] + (lanes,), BF),
        ]
        + sems(7, nz, nz, 2 * fs, (fs, 2), fs, fs, 2 * fs, (fs, 2), fs, fs)
        + sems(nz, nz, nz, nz, nz, nz, 6, 6, nz, nz, nz, cs, cs, 2 * fs, 2 * fs),
        name="middle",
        compiler_params=pltpu.CompilerParams(
            collective_id=1, has_side_effects=True, vmem_limit_bytes=62 * 2**20
        ),
    )(a_own, tok, ct, ct_split, vec, fb, o_all, p1, fc)


def last_kernel(
    cfg,
    qkv,
    att,
    lse,
    d_att,
    pos_col,
    pos_row,
    w,
    h1,
    tok,
    middle,
    d_middle,
    vec,
    sums,
    out_part,
    p_sum,
    og,
    output,
    input_grad,
    q_grad,
    p_grad,
    o_grad,
    small_grad,
    d_qkv,
    acc,
    h1v,
    qg,
    qr,
    qs,
    om,
    orc,
    osum,
    o_left,
    o_right,
    op,
    ro_left,
    ro_right,
    pz,
    other,
    partner,
    own,
    r_out,
    r_left,
    r_right,
    line,
    sm_out,
    sm_in,
    sm_f,
    ro_sems,
    ro_lsems,
    ro_rsems,
    z_send,
    z_recv,
    l_send,
    l_recv,
    local,
    q_send,
    q_recv,
    o_send,
    o_recv,
    os_send,
    os_left,
    os_right,
    m_send,
    m_recv,
    r_send,
    r_lsems,
    r_rsems,
    b_send,
    b_recv,
    s_send,
    s_recv,
    g_send,
    g_recv,
):
    fs, nz, d, heads = cfg
    cs = 2 * nz
    f, z, core = lax.axis_index("fsdp"), lax.axis_index("z"), lax.axis_index("core")
    rank = 2 * z + core
    rows = tok.shape[0]
    width = heads * HD
    lanes = w.shape[2] // fs
    grain = w.shape[1]
    own_rows, part = d // fs, d // cs
    he = out_part.shape[2] // 2
    slot = he // nz
    plane = Plane(fs)
    ranks = [lax.rem(rank + i, cs) for i in range(1, cs)]
    lanes_of = lambda g: pl.ds(pl.multiple_of(g * lanes, 128), lanes)
    runs = column_segments(cs, d, width, grain)
    block_rows = lambda b: pl.ds(pl.multiple_of(b * rows, rows), rows)
    half_z = lambda h: pl.ds(*halves(nz)[h])

    def h1_in(i):
        here = h1.at[:, lanes_of(lax.rem(f + 1 + i, fs))]
        return pltpu.make_async_copy(here, h1v.at[i % 2], local.at[4 + i % 2])

    for i in range(min(2, fs)):
        h1_in(i).start()
    om_in = pltpu.make_async_copy(og, om, local.at[2])
    op_in = pltpu.make_async_copy(out_part, op, local.at[3])
    om_in.start()
    op_in.start()
    meet(
        [dict(z=r // 2, core=lax.rem(r, 2)) for r in ranks] + [dict(fsdp=p) for p in plane.peers]
    )

    om_in.wait()
    o_total = PlaneSum(
        plane,
        lambda g, h: om.at[half_z(h), :, :, lanes_of(g)],
        lambda n, h: orc.at[n, pl.ds(0, halves(nz)[h][1])],
        (o_send, o_recv),
    )
    o_total.start()

    def z_copy(i):
        to = lax.rem(z + i, nz)
        return remote(p_sum.at[to], pz.at[z], z_send.at[to], z_recv.at[z], z=to)

    z_keep = pltpu.make_async_copy(p_sum.at[z], pz.at[z], local.at[0])
    for i in range(1, nz):
        z_copy(i).start()
    z_keep.start()

    op_in.wait()
    ro_line = LineSum(op, ro_left, ro_right, nz, (ro_sems, ro_lsems, ro_rsems))
    ro_line.first()

    def l_copy(i):
        g = plane.peers[i]
        return remote(pz.at[g], p_grad.at[f], l_send.at[i], l_recv.at[f], fsdp=g)

    l_keep = pltpu.make_async_copy(pz.at[f], p_grad.at[f], local.at[1])

    def shares_on():
        z_keep.wait()
        for i in range(1, nz):
            back = lax.rem(z + nz - i, nz)
            remote(pz.at[back], pz.at[back], z_send.at[0], z_recv.at[back], z=back).wait_recv()
        for i in range(fs - 1):
            l_copy(i).start()
        l_keep.start()

    tall = query_block(cs * rows)
    for h in range(heads):
        attend_back_head(
            h, width, tall, qkv, pos_col, pos_row, att, lse, d_att, d_qkv, acc
        )
        if h == heads - 1:
            ro_line.step(1)
            shares_on()

    slices = 3 * width // grain
    q_total = PlaneSum(
        plane,
        lambda g, h: qg.at[g, pl.ds(*halves(slices)[h])],
        lambda n, h: qr.at[n, pl.ds(0, halves(slices)[h][1])],
        (q_send, q_recv),
    )

    for i in range(fs):
        g = lax.rem(f + 1 + i, fs)
        h1_in(i).wait()
        part_sum = dot_tn(d_qkv[...], h1v[i % 2])
        qg[g] = part_sum.astype(BF).reshape(slices, grain, lanes)
        if i + 2 < fs:
            h1_in(i + 2).start()
    q_total.start()
    for s in range(2, nz - 1):
        ro_line.step(s)

    def hidden(block):
        full = dot(d_qkv[block_rows(block), :], w[...].reshape(3 * width, fs * lanes))
        return [full[:, lanes * g : lanes * g + own_rows] for g in range(fs)]

    def other_step(b, _):
        for g, piece in enumerate(hidden(2 * b + 1 - core)):
            other[b, :, own_rows * g : own_rows * (g + 1)] = piece.astype(BF)
        return 0

    lax.fori_loop(0, nz, other_step, 0)
    to_partner = remote(other, partner, m_send.at[0], m_recv.at[0], core=1 - core)
    to_partner.start()
    o_total.mid()

    to_partner.wait_recv()

    def own_step(i, _):
        b = lax.rem(z + 1 + i, nz)
        for g, piece in enumerate(hidden(2 * b + core)):
            at = slice(own_rows * g, own_rows * (g + 1))
            both = piece + partner[b, :, at].astype(F32)
            r_out[b, :, at] = both.astype(BF)

            @pl.when(b == z)
            def _():
                own[:, at] = both

        return 0

    lax.fori_loop(0, nz, own_step, 0)
    r_line = LineSum(r_out, r_left, r_right, nz, (r_send, r_lsems, r_rsems))
    r_line.first()
    q_total.mid()
    ro_line.finish()

    step = min(32, rows)

    def output_chunk(i, _):
        at = pl.ds(pl.multiple_of(i * step, step), step)
        total = (
            op[z, at, :].astype(F32)
            + ro_left[z, at, :].astype(F32)
            + ro_right[z, at, :].astype(F32)
        )
        for c in range(cs):
            low = (c % 2) * he + (c // 2) * slot
            cols = slice(c * part, (c + 1) * part)
            output[at, cols] = (
                middle[at, cols] + total[:, low : low + part] + vec[1:2, cols]
            ).astype(BF)
        return 0

    lax.fori_loop(0, rows // step, output_chunk, 0)
    o_total.end()
    for h in range(2):
        osum[half_z(h)] = o_total.total(h).astype(BF)
    o_line = LineSum(osum, o_left, o_right, nz, (os_send, os_left, os_right))
    o_line.first()
    r_line.step(1)

    q_total.end()
    for h in range(2):
        qs[pl.ds(*halves(slices)[h])] = q_total.total(h).astype(BF)

    def run_copy(n):
        dst, at, src, first, count = runs[n]
        here, there = qs.at[pl.ds(first, count)], q_grad.at[pl.ds(at, count)]
        if src == dst:
            return pltpu.make_async_copy(here, there, b_send.at[n])
        return remote(here, there, b_send.at[n], b_recv.at[n], z=dst // 2, core=dst % 2)

    for n, run in enumerate(runs):

        @pl.when(rank == run[2])
        def _():
            run_copy(n).start()

    for s in range(2, nz - 1):
        r_line.step(s)
    for s in range(1, nz - 1):
        o_line.step(s)
    r_line.finish()

    line[...] = jnp.zeros(line.shape, F32)

    def norm_back_chunk(i, _):
        at = pl.ds(pl.multiple_of(i * step, step), step)
        g = own[at, :] + r_left[z, at, :].astype(F32) + r_right[z, at, :].astype(F32)
        xhat, rstd = norm_rows(tok[at, :].astype(F32))
        input_grad[at, :] = d_middle[at, :] + norm_back(g, xhat, rstd, vec[0:1, :])
        line[0:1, 0:d] += jnp.sum(g * xhat, axis=0, keepdims=True)
        line[1:2, 0:d] += jnp.sum(g, axis=0, keepdims=True)
        return 0

    lax.fori_loop(0, rows // step, norm_back_chunk, 0)

    head_lanes = pl.ds(pl.multiple_of(rank * width, 128), width)
    line[2:3, head_lanes] = jnp.sum(d_qkv[:, 0:width].astype(F32), axis=0, keepdims=True)
    line[3:4, head_lanes] = jnp.sum(d_qkv[:, 2 * width :].astype(F32), axis=0, keepdims=True)
    line[4:8, 0:d] = sums[0:4, 0:d]
    sm_out[...] = jnp.zeros(sm_out.shape, F32)
    ff_parts = small_grad.shape[0] - 8
    hf = p_grad.shape[3] // 2
    for r in range(cs):
        sm_out[r, 0:8, 0:part] = line[0:8, r * part : (r + 1) * part]
    for k in range(2):
        for j in range(ff_parts):
            sm_out[2 * z + k, 8 + j : 9 + j, 0:part] = sums[
                4:5, k * hf + j * part : k * hf + (j + 1) * part
            ]

    def s_copy(i):
        r = ranks[i]
        here = sm_out.at[r]
        return remote(
            here, sm_in.at[rank], s_send.at[i], s_recv.at[rank], z=r // 2, core=lax.rem(r, 2)
        )

    for i in range(cs - 1):
        s_copy(i).start()
    o_line.finish()
    o_grad[...] = (
        osum[z].astype(F32) + o_left[z].astype(F32) + o_right[z].astype(F32)
    ).astype(o_grad.dtype)
    total = sm_out[rank]
    for i in range(1, cs):
        back = lax.rem(rank + cs - i, cs)
        remote(sm_in.at[back], sm_in.at[back], s_send.at[0], s_recv.at[back], z=z).wait_recv()
        total += sm_in[back]
    sm_f[f] = total

    def g_copy(i):
        return remote(sm_f.at[f], sm_f.at[f], g_send.at[i], g_recv.at[f], fsdp=plane.peers[i])

    for i in range(fs - 1):
        g_copy(i).start()
    for n, run in enumerate(runs):

        @pl.when(rank == run[0])
        def _():
            if run[0] == run[2]:
                run_copy(n).wait()
            else:
                run_copy(n).wait_recv()

    l_keep.wait()
    for g in plane.peers:
        remote(p_grad.at[g], p_grad.at[g], l_send.at[0], l_recv.at[g], fsdp=g).wait_recv()
    for g in plane.peers:
        remote(sm_f.at[g], sm_f.at[g], g_send.at[0], g_recv.at[g], fsdp=g).wait_recv()
    total = sm_f[0]
    for g in range(1, fs):
        total += sm_f[g]
    small_grad[...] = total

    for i in range(1, nz):
        z_copy(i).wait_send()
    for i in range(fs - 1):
        l_copy(i).wait_send()
        g_copy(i).wait_send()
    for s in (ro_line, r_line, o_line, o_total, q_total):
        s.sent()
    to_partner.wait_send()
    for n, run in enumerate(runs):
        if run[0] != run[2]:

            @pl.when(rank == run[2])
            def _():
                run_copy(n).wait_send()

    for i in range(cs - 1):
        s_copy(i).wait_send()


def last_part(cfg, counts, qkv, att, lse, d_att, pos, w, h1, tok, middle, d_middle, vec, sums, out_part, p_sum, og):
    fs, nz, d, heads = cfg
    cs = 2 * nz
    rows, length, width = tok.shape[0], qkv.shape[0], heads * HD
    grain, lanes = w.shape[1], w.shape[2] // fs
    q_grains, small_rows = counts
    he = out_part.shape[2] // 2
    slices = 3 * width // grain
    runs = len(column_segments(cs, d, width, grain))
    part = d // cs
    rest = 2 * (fs - 1)
    rows_low = pltpu.VMEM((nz, rows, d), BF)
    outs_low = pltpu.VMEM((nz, rows, 2 * he), BF)
    owner = (nz,) + og.shape[1:3] + (lanes,)
    return pl.pallas_call(
        partial(last_kernel, cfg),
        out_shape=(
            shape((rows, d)),
            shape((rows, d), F32),
            shape((q_grains, grain, lanes)),
            shape((fs,) + p_sum.shape[1:]),
            shape(owner[1:]),
            shape((small_rows, up(part)), F32),
        ),
        in_specs=[VMEM] * 7 + [HBM] + [VMEM] * 5 + [HBM, VMEM, HBM],
        out_specs=(VMEM,) * 6,
        scratch_shapes=[
            pltpu.VMEM((length, 3 * width), BF),
            pltpu.VMEM((length, 2 * HD), F32),
            pltpu.VMEM((2, length, lanes), BF),
            pltpu.VMEM((fs, slices, grain, lanes), BF),
            pltpu.VMEM((rest, slices - slices // 2, grain, lanes), BF),
            pltpu.VMEM((slices, grain, lanes), BF),
            pltpu.VMEM(og.shape, BF),
            pltpu.VMEM((rest, nz - nz // 2) + owner[1:], BF),
            pltpu.VMEM(owner, BF),
            pltpu.VMEM(owner, BF),
            pltpu.VMEM(owner, BF),
            outs_low,
            outs_low,
            outs_low,
            pltpu.VMEM(p_sum.shape, BF),
            rows_low,
            rows_low,
            pltpu.VMEM((rows, d), F32),
            rows_low,
            rows_low,
            rows_low,
            pltpu.VMEM((8, width * cs), F32),
            pltpu.VMEM((cs, small_rows, up(part)), F32),
            pltpu.VMEM((cs, small_rows, up(part)), F32),
            pltpu.VMEM((fs, small_rows, up(part)), F32),
        ]
        + sems(nz, nz, nz, nz, nz, fs, fs, 6, rest + 2, rest + 2, rest + 2, rest + 2)
        + sems(nz, nz, nz, 1, 1, nz, nz, nz, runs, runs, cs, cs, fs, fs),
        name="last",
        compiler_params=pltpu.CompilerParams(
            collective_id=2, has_side_effects=True, vmem_limit_bytes=62 * 2**20
        ),
    )(
        qkv,
        att,
        lse,
        d_att,
        pos[:, None],
        pos[None, :],
        w,
        h1,
        tok,
        middle,
        d_middle,
        vec,
        sums,
        out_part,
        p_sum,
        og,
    )


def body(
    tokens,
    block_order,
    cotangent,
    pre_attn_gain,
    pre_attn_bias,
    qkv_weight,
    query_bias,
    value_bias,
    out_weight,
    out_bias,
    pre_mlp_gain,
    pre_mlp_bias,
    fc_weight,
    fc_bias,
    proj_weight,
    proj_bias,
):
    fs, nz = lax.axis_size("fsdp"), lax.axis_size("z")
    cs = nz * 2
    rows, d = tokens.shape[1], tokens.shape[2]
    length = rows * cs
    heads_all = d // HD
    heads = -(-heads_all // cs)
    width = heads * HD
    part, own_rows = d // cs, d // fs
    fc_cols = fc_weight.shape[1]
    hf = up(fc_cols)

    small = jnp.stack(
        [
            pre_attn_gain,
            pre_attn_bias,
            query_bias,
            value_bias,
            out_bias,
            pre_mlp_gain,
            pre_mlp_bias,
            proj_bias,
        ]
    )
    small = jnp.concatenate([small, fc_bias.reshape(-1, part)]).astype(F32)
    small = jnp.pad(small, ((0, 0), (0, up(part) - part)))
    lanes = up(own_rows)
    wq = jnp.pad(qkv_weight.T, ((0, 0), (0, lanes - own_rows)))
    grain = math.gcd(math.gcd(wq.shape[0], HD), 8)
    wq = wq.reshape(-1, grain, lanes)
    fine = math.gcd(part, 8)
    share = -(-part // (fine * fs))
    slot = fs * share * fine
    he = nz * slot
    pj = proj_weight.T.reshape(part, 2, fc_cols)
    pj = jnp.pad(pj, ((0, slot - part), (0, 0), (0, hf - fc_cols)))
    pj = pj.reshape(fs * share, fine, 2 * hf)
    ot = jnp.pad(out_weight.T, ((0, 0), (0, lanes - own_rows))).reshape(-1, fine, lanes)
    pos = positions(block_order, length)
    fc = jnp.pad(fc_weight, ((0, 0), (0, hf - fc_cols)))
    fc = fc.reshape(-1, math.gcd(own_rows, 16), hf)
    cfg = (fs, nz, d, heads)
    h1, w, qkv, att, lse, smalls, p1, o_all, a_own = start(
        cfg, tokens[0], wq, small, pj, ot, pos
    )
    vec = lambda i: smalls[:, i, :part].reshape(d)
    gain1, pb = vec(0), vec(7)
    vecs = jnp.stack([vec(4), vec(5), vec(6)])
    fb = smalls[:, 8:, :part].reshape(cs, -1)
    fb = lax.dynamic_slice_in_dim(fb, lax.axis_index("z") * 2, 2, 0)
    fb = jnp.pad(fb, ((0, 0), (0, hf - fc_cols))).reshape(1, 2 * hf)

    ct_split = cotangent[0].reshape(rows, nz, 2, part).transpose(0, 2, 1, 3)
    ct_split = jnp.pad(ct_split, ((0, 0), (0, 0), (0, 0), (0, slot - part))).reshape(rows, 2 * he)
    middle, d_middle, d_att, out_part, fc_grad, p_sum, og, sums = middle_part(
        cfg, a_own, tokens[0], cotangent[0], ct_split, vecs, fb, o_all, p1, fc
    )
    fc_grad = lax.psum_scatter(fc_grad, "fsdp", scatter_dimension=0, tiled=True)
    fc_grad = lax.optimization_barrier(fc_grad)[:, :fc_cols]
    output, input_grad, q_grad, p_grad, out_grad, g = last_part(
        cfg,
        (wq.shape[0], small.shape[0]),
        qkv,
        att,
        lse,
        d_att,
        pos,
        w,
        h1,
        tokens[0],
        middle,
        d_middle,
        jnp.stack([gain1, pb]),
        sums,
        out_part,
        p_sum,
        og,
    )
    out_grad = out_grad.reshape(part, lanes)[:, :own_rows].T
    qkv_grad = q_grad.reshape(-1, lanes)[:, :own_rows].T
    proj_grad = p_grad.reshape(slot, 2, hf)[:part, :, :fc_cols].reshape(part, -1).T
    g = g[:, :part]
    return (
        output[None],
        input_grad[None],
        g[0],
        g[1],
        qkv_grad.astype(F32),
        g[2],
        g[3],
        out_grad.astype(F32),
        g[4],
        g[5],
        g[6],
        fc_grad.astype(F32),
        g[8:].reshape(-1),
        proj_grad.astype(F32),
        g[7],
    )


def solution(mesh):
    fs, cs = mesh.shape["fsdp"], mesh.shape["ctx"]
    split = Mesh(mesh.devices.reshape(fs, cs // 2, 2), ("fsdp", "z", "core"))
    rows = P("fsdp", CTX, None)
    weight = P("fsdp", CTX)
    vector = P(CTX)
    in_specs = (
        rows,
        P(),
        rows,
        vector,
        vector,
        weight,
        vector,
        vector,
        weight,
        vector,
        vector,
        vector,
        weight,
        vector,
        weight,
        vector,
    )
    out_specs = (
        rows,
        rows,
        vector,
        vector,
        weight,
        vector,
        vector,
        weight,
        vector,
        vector,
        vector,
        weight,
        vector,
        weight,
        vector,
    )
    return jax.shard_map(body, mesh=split, in_specs=in_specs, out_specs=out_specs, check_vma=False)
```

```python
from functools import partial
import math

import jax
import jax.numpy as jnp
from jax import lax
from jax.experimental import pallas as pl
from jax.experimental.pallas import tpu as pltpu
from jax.sharding import Mesh
from jax.sharding import PartitionSpec as P

HD = 64
EPS = 1e-05
FLOOR = -1e30
BF = jnp.bfloat16
F32 = jnp.float32
CTX = ("z", "core")
MESH = pl.DeviceIdType.MESH
VMEM = pl.BlockSpec(memory_space=pltpu.VMEM)
HBM = pl.BlockSpec(memory_space=pl.ANY)
GELU_A = math.sqrt(2.0 / math.pi)
GELU_B = 0.044715


def up(n):
    return -(-n // 128) * 128


def sems(*counts):
    return [pltpu.SemaphoreType.DMA(c if isinstance(c, tuple) else (c,)) for c in counts]


def shape(dims, kind=BF):
    return jax.ShapeDtypeStruct(dims, kind)


def dot(a, b):
    return jnp.dot(a, b, preferred_element_type=F32)


def dot_nt(a, b):
    return lax.dot_general(a, b, (((1,), (1,)), ((), ())), preferred_element_type=F32)


def dot_tn(a, b):
    return lax.dot_general(a, b, (((0,), (0,)), ((), ())), preferred_element_type=F32)


def norm_rows(rows):
    centred = rows - jnp.mean(rows, axis=-1, keepdims=True)
    rstd = lax.rsqrt(jnp.mean(centred * centred, axis=-1, keepdims=True) + EPS)
    return centred * rstd, rstd


def norm_back(upstream, xhat, rstd, gain):
    inner = upstream * gain
    return rstd * (
        inner
        - jnp.mean(inner, axis=-1, keepdims=True)
        - xhat * jnp.mean(inner * xhat, axis=-1, keepdims=True)
    )


def gelu_pair(v):
    sq = v * v
    t = jnp.tanh(GELU_A * v * (1.0 + GELU_B * sq))
    half = 0.5 * (1.0 + t)
    slope = half + 0.5 * v * (1.0 - t * t) * (GELU_A * (1.0 + 3.0 * GELU_B * sq))
    return v * half, slope


def positions(order_table, rows):
    block = rows // order_table.shape[0]
    return (order_table[:, None] * block + jnp.arange(block, dtype=jnp.int32)[None]).reshape(rows)


def remote(src, dst, send, recv, **to):
    return pltpu.make_async_remote_copy(
        src_ref=src, dst_ref=dst, send_sem=send, recv_sem=recv, device_id=to, device_id_type=MESH
    )


def column_segments(ranks, d, width, grain):
    own = 3 * d // ranks
    runs = []
    for src in range(ranks):
        for part in range(3):
            for dst in range(ranks):
                low = part * d + dst * width
                first = max(src * own, low)
                last = min((src + 1) * own, low + width, (part + 1) * d)
                if first < last:
                    at = part * width + first - low
                    runs.append(
                        (src, (first - src * own) // grain, dst, at // grain, (last - first) // grain)
                    )
    return runs


def meet(peers):
    barrier = pltpu.get_barrier_semaphore()
    for peer in peers:
        pl.semaphore_signal(barrier, inc=1, device_id=peer, device_id_type=MESH)
    pl.semaphore_wait(barrier, len(peers))


class Line:
    def __init__(self, at, size, sems):
        self.at, self.size = at, size
        self.right, self.left, self.recv = sems
        self.z = lax.axis_index("z")

    def copy(self, block, way):
        send = (self.right if way > 0 else self.left).at[block]
        at = self.at(block)
        return remote(at, at, send, self.recv.at[block], z=self.z + way)

    def start(self):
        @pl.when(self.z < self.size - 1)
        def _():
            self.copy(self.z, 1).start()

        @pl.when(self.z > 0)
        def _():
            self.copy(self.z, -1).start()

    def step(self, s, then=None):
        @pl.when(self.z >= s)
        def _():
            block = self.z - s
            self.copy(block, 1).wait_recv()

            @pl.when(self.z < self.size - 1)
            def _():
                self.copy(block, 1).start()

            if then is not None:
                then(block)

        @pl.when(self.z + s < self.size)
        def _():
            block = self.z + s
            self.copy(block, -1).wait_recv()

            @pl.when(self.z > 0)
            def _():
                self.copy(block, -1).start()

            if then is not None:
                then(block)

    def finish(self):
        for s in range(self.size):

            @pl.when((self.z >= s) & (self.z < self.size - 1))
            def _():
                self.copy(self.z - s, 1).wait_send()

            @pl.when((self.z + s < self.size) & (self.z > 0))
            def _():
                self.copy(self.z + s, -1).wait_send()


class LineSum:
    def __init__(self, parts, from_left, from_right, size, sems):
        self.parts, self.ins, self.size = parts, (from_left, from_right), size
        self.send, self.recv_left, self.recv_right = sems
        self.z = lax.axis_index("z")

    def copy(self, block, way):
        recv = self.recv_left if way > 0 else self.recv_right
        there = self.ins[0 if way > 0 else 1].at[block]
        return remote(
            self.parts.at[block], there, self.send.at[block], recv.at[block], z=self.z + way
        )

    def order(self, i):
        near = self.z < self.size // 2
        ahead = self.size - 1 - self.z
        from_low = jnp.where(i < ahead, self.size - 1 - i, i - ahead)
        from_high = jnp.where(i < self.z, i, self.size - 1 - (i - self.z))
        return jnp.where(near, from_low, from_high)

    def ready(self, block):
        @pl.when((self.z == 0) & (block > 0))
        def _():
            self.copy(block, 1).start()

        @pl.when((self.z == self.size - 1) & (block < self.size - 1))
        def _():
            self.copy(block, -1).start()

    def first(self):
        for way, edge in ((1, 0), (-1, self.size - 1)):

            @pl.when(self.z == edge)
            def _():
                for hop in range(self.size - 1, 0, -1):
                    self.copy(self.z + way * hop, way).start()

    def add_on(self, block, way):
        self.copy(block, way).wait_recv()
        came = self.ins[0 if way > 0 else 1]
        self.parts[block] = (
            self.parts[block].astype(F32) + came[block].astype(F32)
        ).astype(self.parts.dtype)
        self.copy(block, way).start()

    def step(self, s):
        right, left = self.z + self.size - 1 - s, s - (self.size - 1 - self.z)

        @pl.when((self.z > 0) & (right < self.size) & (right > self.z))
        def _():
            self.add_on(right, 1)

        @pl.when((self.z < self.size - 1) & (left >= 0) & (left < self.z))
        def _():
            self.add_on(left, -1)

    def finish(self):
        @pl.when(self.z > 0)
        def _():
            self.copy(self.z, 1).wait_recv()

        @pl.when(self.z == 0)
        def _():
            self.ins[0][self.z] = jnp.zeros(self.parts.shape[1:], self.parts.dtype)

        @pl.when(self.z < self.size - 1)
        def _():
            self.copy(self.z, -1).wait_recv()

        @pl.when(self.z == self.size - 1)
        def _():
            self.ins[1][self.z] = jnp.zeros(self.parts.shape[1:], self.parts.dtype)

    def sent(self):
        for block in range(self.size):

            @pl.when(self.z < block)
            def _():
                self.copy(block, 1).wait_send()

            @pl.when(self.z > block)
            def _():
                self.copy(block, -1).wait_send()


def halves(n):
    return ((0, n // 2), (n // 2, n - n // 2))


class Plane:
    def __init__(self, size):
        self.size, self.f = size, lax.axis_index("fsdp")
        self.square = size == 4
        f = self.f
        self.peers = [lax.rem(f + i, size) for i in range(1, size)]
        if self.square:
            self.x, self.y, self.far = f + 1 - 2 * lax.rem(f, 2), lax.rem(f + 2, 4), 3 - f
            self.peers = [self.x, self.y, self.far]


class PlaneGather:
    def __init__(self, plane, at, sems):
        self.p, self.at = plane, at
        self.send, self.recv = sems
        f = plane.f
        if plane.square:
            x, y = plane.x, plane.y
            self.early = [(f, 0, x), (f, 1, y), (f, 0, y), (f, 1, x)]
            self.late = [(x, 0, y), (y, 1, x)]
        else:
            self.early = [(f, h, g) for g in plane.peers for h in range(2)]
            self.late = []

    def copy(self, n, move):
        g, half, to = move
        at = self.at(g, half)
        return remote(at, at, self.send.at[n], self.recv.at[g, half], fsdp=to)

    def arrive(self, g, half):
        at = self.at(g, half)
        remote(at, at, self.send.at[0], self.recv.at[g, half], fsdp=g).wait_recv()

    def start(self):
        for n, move in enumerate(self.early):
            self.copy(n, move).start()

    def mid(self):
        for n, move in enumerate(self.late):
            self.arrive(move[0], move[1])
            self.copy(len(self.early) + n, move).start()

    def end(self):
        known = [(m[0], m[1]) for m in self.late]
        for g in self.p.peers:
            for half in range(2):
                if not any(g is a and half == b for a, b in known):
                    self.arrive(g, half)

    def sent(self):
        for n, move in enumerate(self.early + self.late):
            self.copy(n, move).wait_send()


class PlaneSum:
    def __init__(self, plane, at, came, sems):
        self.p, self.at, self.came = plane, at, came
        self.send, self.recv = sems
        if plane.square:
            x, y, far = plane.x, plane.y, plane.far
            self.early = [(far, 0, x, 0), (far, 1, y, 1), (x, 0, x, 2), (y, 1, y, 3)]
            self.late = [(y, 0, y, 4), (x, 1, x, 5)]
            self.mine = [[2, 4], [3, 5]]
        else:
            n = plane.size
            self.early = [
                (g, h, g, 2 * i + h) for i, g in enumerate(plane.peers) for h in range(2)
            ]
            self.late = []
            self.mine = [[2 * i + h for i in range(n - 1)] for h in range(2)]

    def copy(self, move):
        g, half, to, slot = move
        return remote(
            self.at(g, half), self.came(slot, half), self.send.at[slot], self.recv.at[slot], fsdp=to
        )

    def arrive(self, slot, half):
        there = self.came(slot, half)
        remote(
            there, there, self.send.at[slot], self.recv.at[slot], fsdp=self.p.peers[0]
        ).wait_recv()

    def start(self):
        for move in self.early:
            self.copy(move).start()

    def mid(self):
        for slot, move in enumerate(self.late):
            self.arrive(slot, move[1])
            at, came = self.at(move[0], move[1]), self.came(slot, move[1])
            at[...] = (at[...].astype(F32) + came[...].astype(F32)).astype(at.dtype)
            self.copy(move).start()

    def end(self):
        for half in range(2):
            for slot in self.mine[half]:
                self.arrive(slot, half)

    def total(self, half):
        out = self.at(self.p.f, half)[...].astype(F32)
        for slot in self.mine[half]:
            out += self.came(slot, half)[...].astype(F32)
        return out

    def sent(self):
        for move in self.early + self.late:
            self.copy(move).wait_send()


def query_block(length):
    return max(128, min(256, length, 256 * 1024 // length))


def attend_head(h, width, q_block, qkv, pos_col, pos_row, out, lse):
    rows = qkv.shape[0]
    k = qkv[:, width + h * HD : width + (h + 1) * HD]
    v = qkv[:, 2 * width + h * HD : 2 * width + (h + 1) * HD]
    for b in range(rows // q_block):
        at = slice(b * q_block, (b + 1) * q_block)
        q = qkv[at, h * HD : (h + 1) * HD] * BF(HD**-0.5)
        s = dot_nt(k, q)
        s = jnp.where(pos_col[...] <= pos_row[:, at], s, FLOOR)
        top = jnp.max(s, axis=0, keepdims=True)
        p = jnp.exp(s - top)
        total = jnp.sum(p, axis=0, keepdims=True)
        o = dot_tn(v, p.astype(BF)) * (1.0 / total)
        out[at, h * HD : (h + 1) * HD] = o.T.astype(BF)
        lse[h : h + 1, at] = top + jnp.log(total)


def attend_back_head(h, width, q_block, qkv, pos_col, pos_row, out, lse, dout, dqkv, acc):
    rows = qkv.shape[0]
    k = qkv[:, width + h * HD : width + (h + 1) * HD]
    v = qkv[:, 2 * width + h * HD : 2 * width + (h + 1) * HD]
    for b in range(rows // q_block):
        at = slice(b * q_block, (b + 1) * q_block)
        q = qkv[at, h * HD : (h + 1) * HD] * BF(HD**-0.5)
        do = dout[at, h * HD : (h + 1) * HD]
        o = out[at, h * HD : (h + 1) * HD]
        delta = jnp.sum(do.astype(F32).T * o.astype(F32).T, axis=0, keepdims=True)
        s = dot_nt(k, q)
        p = jnp.where(pos_col[...] <= pos_row[:, at], jnp.exp(s - lse[h : h + 1, at]), 0.0)
        dp = dot_nt(v, do)
        ds = (p * (dp - delta)).astype(BF)
        dq = dot_tn(k, ds) * (HD**-0.5)
        dqkv[at, h * HD : (h + 1) * HD] = dq.T.astype(BF)
        dk = dot(ds, q)
        dv = dot(p.astype(BF), do)
        if b == 0:
            acc[:, :HD] = dk
            acc[:, HD:] = dv
        else:
            acc[:, :HD] += dk
            acc[:, HD:] += dv
    dqkv[:, width + h * HD : width + (h + 1) * HD] = acc[:, :HD].astype(BF)
    dqkv[:, 2 * width + h * HD : 2 * width + (h + 1) * HD] = acc[:, HD:].astype(BF)


def start_kernel(
    cfg,
    tok,
    wq,
    small,
    pj,
    ot,
    pos_col,
    pos_row,
    h1,
    w,
    qkv,
    att,
    lse,
    smalls,
    p2,
    o_all,
    a_own,
    toks,
    vecs,
    p1,
    small_send,
    small_recv,
    q_send,
    q_recv,
    q_local,
    x_send,
    x_recv,
    t_right,
    t_left,
    t_recv,
    c_send,
    c_recv,
    p1_send,
    p1_recv,
    p2_send,
    p2_recv,
    p_local,
    a_send,
    a_recv,
    o_right,
    o_left,
    o_recv,
    ox_send,
    ox_recv,
    oc_send,
    oc_recv,
):
    fs, nz, d, heads = cfg
    cs = 2 * nz
    f, z, core = lax.axis_index("fsdp"), lax.axis_index("z"), lax.axis_index("core")
    rank = 2 * z + core
    rows, lanes = tok.shape[0], wq.shape[2]
    width = heads * HD
    grain = wq.shape[1]
    own_rows = d // fs
    part = d // cs
    lanes_of = lambda g: pl.ds(pl.multiple_of(g * lanes, 128), lanes)
    runs = column_segments(cs, d, width, grain)
    plane = Plane(fs)
    planes = plane.peers

    w[:, :, lanes_of(f)] = jnp.zeros((w.shape[0], grain, lanes), BF)
    keep_out = pltpu.make_async_copy(ot, o_all.at[rank, :, :, lanes_of(f)], p_local.at[0])
    keep_out.start()
    ranks = [lax.rem(rank + i, cs) for i in range(1, cs)]
    meet([dict(z=r // 2, core=lax.rem(r, 2)) for r in ranks] + [dict(fsdp=p) for p in planes])

    def run_copy(n):
        src, first, dst, at, count = runs[n]
        here, there = wq.at[pl.ds(first, count)], w.at[pl.ds(at, count), :, lanes_of(f)]
        if src == dst:
            return pltpu.make_async_copy(here, there, q_local.at[n])
        return remote(here, there, q_send.at[n], q_recv.at[n], z=dst // 2, core=dst % 2)

    for n, run in enumerate(runs):

        @pl.when(rank == run[0])
        def _():
            run_copy(n).start()

    def small_copy(i):
        r = ranks[i]
        to = smalls.at[rank]
        return remote(small, to, small_send.at[i], small_recv.at[rank], z=r // 2, core=lax.rem(r, 2))

    for i in range(cs - 1):
        small_copy(i).start()

    share = p1.shape[1]

    def p1_copy(i):
        here = pj.at[pl.ds(planes[i] * share, share)]
        return remote(here, p1.at[f], p1_send.at[i], p1_recv.at[f], fsdp=planes[i])

    p1[f] = pj[pl.ds(f * share, share)]
    for i in range(fs - 1):
        p1_copy(i).start()

    def ox_copy(i, block, here=None):
        at = o_all.at[2 * block + core, :, :, lanes_of(f)]
        here = at if here is None else here
        return remote(here, at, ox_send.at[i, block], ox_recv.at[f, block], fsdp=planes[i])

    def ox_arrival(g, block):
        at = o_all.at[2 * block + core, :, :, lanes_of(g)]
        return remote(at, at, ox_send.at[0, block], ox_recv.at[g, block], fsdp=g)

    def oc_copy(g, block, here=None):
        at = o_all.at[2 * block + core, :, :, lanes_of(g)]
        here = at if here is None else here
        return remote(here, at, oc_send.at[g, block], oc_recv.at[g, block], core=1 - core)

    def oc_arrival(g, block):
        at = o_all.at[2 * block + 1 - core, :, :, lanes_of(g)]
        return remote(at, at, oc_send.at[g, block], oc_recv.at[g, block], core=1 - core)

    def out_block(block, here=None):
        for i in range(fs - 1):
            ox_copy(i, block, here).start()
        oc_copy(f, block, here).start()

    out_block(z, ot)

    for n, run in enumerate(runs):

        @pl.when(rank == run[2])
        def _():
            if run[0] == run[2]:
                run_copy(n).wait()
            else:
                run_copy(n).wait_recv()

    gather = PlaneGather(
        plane, lambda g, h: w.at[pl.ds(*halves(w.shape[0])[h]), :, lanes_of(g)], (x_send, x_recv)
    )
    gather.start()

    pltpu.sync_copy(tok, toks.at[rank])
    line = Line(lambda b: toks.at[2 * b + core], nz, (t_right, t_left, t_recv))

    def pass_on(block):
        at = toks.at[2 * block + core]
        return remote(at, at, c_send.at[block], c_recv.at[block], core=1 - core)

    def arrival(block):
        at = toks.at[2 * block + 1 - core]
        return remote(at, at, c_send.at[block], c_recv.at[block], core=1 - core)

    line.start()
    pass_on(z).start()

    smalls[rank] = small[...]
    vecs[...] = jnp.zeros(vecs.shape, F32)
    for i in range(1, cs):
        back = lax.rem(rank + cs - i, cs)
        remote(small, smalls.at[back], small_send.at[i - 1], small_recv.at[back], z=z).wait_recv()
    for r in range(cs):
        vecs[:, part * r : part * (r + 1)] = smalls[r, 0:8, 0:part]
    for g in range(fs):
        h1[:, lanes * g + own_rows : lanes * (g + 1)] = jnp.zeros(
            (h1.shape[0], lanes - own_rows), BF
        )

    for s in range(1, nz):
        line.step(s, lambda b: pass_on(b).start())
        if s == 1:
            gather.mid()

    out_line = Line(
        lambda b: o_all.at[2 * b + core, :, :, lanes_of(f)], nz, (o_right, o_left, o_recv)
    )
    keep_out.wait()
    out_line.start()

    for g in planes:
        remote(p1.at[g], p1.at[g], p1_send.at[0], p1_recv.at[g], fsdp=g).wait_recv()

    def p2_copy(i):
        to = lax.rem(z + i, nz)
        return remote(p1.at[to], p2.at[z], p2_send.at[to], p2_recv.at[z], z=to)

    for i in range(1, nz):
        p2_copy(i).start()
    p2[z] = p1[z]
    for b in range(nz):
        arrival(b).wait_recv()

    step = min(32, rows)

    def norm_chunk(i, _):
        block, at = i // (rows // step), lax.rem(i, rows // step) * step
        xhat, _ = norm_rows(toks[block, pl.ds(at, step), :].astype(F32))
        h = (xhat * vecs[0:1, 0:d] + vecs[1:2, 0:d]).astype(BF)
        to = pl.ds(pl.multiple_of(i * step, step), step)
        for g in range(fs):
            h1[to, lanes * g : lanes * g + own_rows] = h[:, own_rows * g : own_rows * (g + 1)]
        return 0

    lax.fori_loop(0, cs * rows // step, norm_chunk, 0)
    out_line.step(1, out_block)
    gather.end()

    tall = min(256, cs * rows)
    head_lanes = pl.ds(pl.multiple_of(rank * width, 128), width)

    def project(i, _):
        at = pl.ds(pl.multiple_of(i * tall, tall), tall)
        full = dot_nt(h1[at, :], w[...].reshape(3 * width, fs * lanes))
        qkv[at, 0:width] = (full[:, 0:width] + vecs[2:3, head_lanes]).astype(BF)
        qkv[at, width : 2 * width] = full[:, width : 2 * width].astype(BF)
        qkv[at, 2 * width :] = (full[:, 2 * width :] + vecs[3:4, head_lanes]).astype(BF)
        return 0

    lax.fori_loop(0, cs * rows // tall, project, 0)
    for s in range(2, nz):
        out_line.step(s, out_block)
    for h in range(heads):
        attend_head(h, width, query_block(cs * rows), qkv, pos_col, pos_row, att, lse)

    def a_copy(i):
        r = ranks[i]
        here = att.at[pl.ds(pl.multiple_of(r * rows, rows), rows)]
        there = a_own.at[:, head_lanes]
        return remote(here, there, a_send.at[i], a_recv.at[rank], z=r // 2, core=lax.rem(r, 2))

    for i in range(cs - 1):
        a_copy(i).start()
    a_own[:, head_lanes] = att[pl.ds(pl.multiple_of(rank * rows, rows), rows), :]

    for g in planes:
        for b in range(nz):
            ox_arrival(g, b).wait_recv()
            oc_copy(g, b).start()
    for i in range(1, cs):
        back = lax.rem(rank + cs - i, cs)
        to = a_own.at[:, pl.ds(pl.multiple_of(back * width, 128), width)]
        remote(to, to, a_send.at[0], a_recv.at[back], z=z).wait_recv()
    for i in range(1, nz):
        back = lax.rem(z + nz - i, nz)
        remote(p2.at[back], p2.at[back], p2_send.at[0], p2_recv.at[back], z=back).wait_recv()
    for g in range(fs):
        for b in range(nz):
            oc_arrival(g, b).wait_recv()

    for n, run in enumerate(runs):
        if run[0] != run[2]:

            @pl.when(rank == run[0])
            def _():
                run_copy(n).wait_send()

    for i in range(cs - 1):
        small_copy(i).wait_send()
        a_copy(i).wait_send()
    gather.sent()
    for i in range(1, nz):
        p2_copy(i).wait_send()
    for i in range(fs - 1):
        p1_copy(i).wait_send()
        for b in range(nz):
            ox_copy(i, b).wait_send()
    for g in range(fs):
        for b in range(nz):
            oc_copy(g, b).wait_send()
    line.finish()
    out_line.finish()
    for b in range(nz):
        pass_on(b).wait_send()


def start(cfg, tok, wq, small, pj, ot, pos):
    fs, nz, d, heads = cfg
    cs = 2 * nz
    rows, lanes = tok.shape[0], wq.shape[2]
    width, length = heads * HD, rows * cs
    runs = len(column_segments(cs, d, width, wq.shape[1]))
    return pl.pallas_call(
        partial(start_kernel, cfg),
        out_shape=(
            shape((length, fs * lanes)),
            shape((3 * width // wq.shape[1], wq.shape[1], fs * lanes)),
            shape((length, 3 * width)),
            shape((length, width)),
            shape((heads, length), F32),
            shape((cs,) + small.shape, F32),
            shape((nz, pj.shape[0] // fs) + pj.shape[1:]),
            shape((cs,) + ot.shape[:2] + (fs * lanes,)),
            shape((rows, cs * width)),
        ),
        in_specs=[VMEM] * 7,
        out_specs=(VMEM,) * 7 + (HBM, VMEM),
        scratch_shapes=[
            pltpu.VMEM((cs, rows, d), BF),
            pltpu.VMEM((8, width * cs), F32),
            pltpu.VMEM((fs, pj.shape[0] // fs) + pj.shape[1:], BF),
        ]
        + sems(cs, cs, runs, runs, runs, 2 * fs, (fs, 2), nz, nz, nz, nz, nz)
        + sems(fs, fs, nz, nz, 1, cs, cs)
        + sems(nz, nz, nz, (fs, nz), (fs, nz), (fs, nz), (fs, nz)),
        name="start",
        compiler_params=pltpu.CompilerParams(
            collective_id=0, has_side_effects=True, vmem_limit_bytes=56 * 2**20
        ),
    )(tok, wq, small, pj, ot, pos[:, None], pos[None, :])


def middle_kernel(
    cfg,
    a_own,
    tok,
    ct,
    smalls,
    p2,
    o_all,
    fc,
    middle,
    d_middle,
    d_att,
    out_part,
    fc_grad,
    p_sum,
    og,
    sums,
    vec,
    fb,
    a_pad,
    ov,
    fcv,
    pjv,
    ctb,
    cto,
    h2b,
    actb,
    dbo,
    dbp,
    dh,
    in_left,
    in_right,
    own_dh,
    da,
    dsp,
    pg,
    pr,
    stage,
    local,
    p3_send,
    p3_recv,
    pc_send,
    pc_recv,
    f_send,
    f_recv,
    fc_send,
    fc_recv,
    c_right,
    c_left,
    c_recv,
    h_right,
    h_left,
    h_recv,
    e_send,
    e_recv,
    r_send,
    r_left,
    r_right,
    d_send,
    d_recv,
    g_send,
    g_recv,
):
    fs, nz, d, heads = cfg
    cs = 2 * nz
    f, z, core = lax.axis_index("fsdp"), lax.axis_index("z"), lax.axis_index("core")
    rank = 2 * z + core
    rows = tok.shape[0]
    width = heads * HD
    lanes = o_all.shape[3] // fs
    own_rows, part = d // fs, d // cs
    share, grain = p2.shape[1], p2.shape[2]
    slot = fs * share * grain
    he, hf = nz * slot, fc.shape[2]
    ff = 2 * hf
    fc_rows = fc.shape[0]
    tall = nz * rows
    step = min(32, rows)
    plane = Plane(fs)
    ranks = [lax.rem(rank + i, cs) for i in range(1, cs)]
    half_at = lambda k: pl.ds(pl.multiple_of(k * hf, 128), hf)
    e_at = lambda k: pl.ds(pl.multiple_of(k * he, 128), he)

    load_out = pltpu.make_async_copy(o_all, ov, local.at[0])
    fc_at = lambda g, k, h: fcv.at[
        pl.ds(g * fc_rows + halves(fc_rows)[h][0], halves(fc_rows)[h][1]), :, half_at(k)
    ]
    load_fc = [
        pltpu.make_async_copy(fc.at[pl.ds(*halves(fc_rows)[h])], fc_at(f, core, h), local.at[1 + h])
        for h in range(2)
    ]
    load_out.start()
    for copy in load_fc:
        copy.start()
    meet(
        [dict(z=r // 2, core=lax.rem(r, 2)) for r in ranks] + [dict(fsdp=p) for p in plane.peers]
    )

    def swap(n, here, there):
        return remote(here, there, e_send.at[n], e_recv.at[n], core=1 - core)

    half_z = lambda h: pl.ds(*halves(nz)[h])
    pjv[core, :, f] = p2[...]
    p_gather = PlaneGather(plane, lambda g, h: pjv.at[core, half_z(h), g], (p3_send, p3_recv))
    p_gather.start()

    def p_pass(g):
        at = pjv.at[core, :, g]
        return remote(at, at, pc_send.at[g], pc_recv.at[g], core=1 - core)

    def p_came(g):
        at = pjv.at[1 - core, :, g]
        return remote(at, at, pc_send.at[g], pc_recv.at[g], core=1 - core)

    p_pass(f).start()

    for copy in load_fc:
        copy.wait()
    fc_gather = PlaneGather(plane, lambda g, h: fc_at(g, core, h), (f_send, f_recv))
    fc_gather.start()

    def fc_pass(g):
        at = fcv.at[pl.ds(g * fc_rows, fc_rows), :, half_at(core)]
        return remote(at, at, fc_send.at[g], fc_recv.at[g], core=1 - core)

    def fc_came(g):
        at = fcv.at[pl.ds(g * fc_rows, fc_rows), :, half_at(1 - core)]
        return remote(at, at, fc_send.at[g], fc_recv.at[g], core=1 - core)

    fc_pass(f).start()

    ctb[z] = jnp.zeros(ctb.shape[1:], BF)
    for c in range(cs):
        to = (c % 2) * he + (c // 2) * slot
        ctb[z, :, to : to + part] = ct[:, c * part : (c + 1) * part]
    c_line = Line(lambda b: ctb.at[b], nz, (c_right, c_left, c_recv))
    c_line.start()

    for r in range(cs):
        vec[:, r * part : (r + 1) * part] = smalls[r, 4:7, 0:part]
    fb[...] = jnp.zeros(fb.shape, F32)
    for k in range(2):
        for j in range(smalls.shape[1] - 8):
            to = k * hf + j * part
            fb[:, to : to + part] = smalls[2 * z + k, 8 + j : 9 + j, 0:part]

    for g in range(fs):
        a_pad[core, :, lanes * g : lanes * g + own_rows] = a_own[
            :, own_rows * g : own_rows * (g + 1)
        ]
        a_pad[core, :, lanes * g + own_rows : lanes * (g + 1)] = jnp.zeros(
            (rows, lanes - own_rows), BF
        )
    swap_a = swap(4, a_pad.at[core], a_pad.at[core])
    swap_a.start()
    load_out.wait()
    branch = dot_nt(a_pad[core], ov[...].reshape(d, fs * lanes))
    middle[...] = tok[...].astype(F32) + branch + vec[0:1, :]

    def norm_chunk(i, _):
        at = pl.ds(pl.multiple_of(i * step, step), step)
        xhat, _ = norm_rows(middle[at, :])
        h2b[core, z, at, :] = (xhat * vec[1:2, :] + vec[2:3, :]).astype(BF)
        return 0

    lax.fori_loop(0, rows // step, norm_chunk, 0)
    h_line = Line(lambda b: h2b.at[core, b], nz, (h_right, h_left, h_recv))
    h_line.start()
    p_gather.mid()
    c_line.step(1)
    h_line.step(1)
    fc_gather.mid()
    for s in range(2, nz - 1):
        c_line.step(s)
        h_line.step(s)
    p_gather.end()
    for g in plane.peers:
        p_pass(g).start()
    fc_gather.end()
    for g in plane.peers:
        fc_pass(g).start()
    for g in range(fs):
        p_came(g).wait_recv()
    for g in range(fs):
        fc_came(g).wait_recv()

    chunk = 256 if ff % 256 == 0 else 128
    some = nz // 2
    wide = some * rows
    sums[4:5, :] = jnp.zeros((1, sums.shape[1]), F32)

    def feed(first, i):
        at = pl.ds(pl.multiple_of(i * chunk, chunk), chunk)
        blocks = pl.ds(first, some)
        w = fcv[:, :, at].reshape(d, chunk)
        before = dot(h2b[core, blocks].reshape(wide, d), w) + fb[:, at]
        act, slope = gelu_pair(before)
        actb[core, blocks, :, at] = act.astype(BF).reshape(some, rows, chunk)
        w = pjv[:, :, :, :, :, at].reshape(2 * he, chunk)
        back = dot(ctb[blocks].reshape(wide, 2 * he), w)
        low = (back * slope).astype(BF)
        dbo[blocks, :, at] = low.reshape(some, rows, chunk)
        sums[4:5, at] += jnp.sum(low.astype(F32), axis=0, keepdims=True)

    def feed_half(first):
        def one(i, _):
            feed(first, i)
            return 0

        lax.fori_loop(0, ff // chunk, one, 0)

    near = z // some * some
    feed_half(near)
    c_line.step(nz - 1)
    h_line.step(nz - 1)
    swap_ct = swap(0, ctb.at[:, :, e_at(1 - core)], cto)
    swap_h2 = swap(1, h2b.at[core], h2b.at[core])
    swap_h2.start()
    swap_ct.start()
    feed_half(some - near)
    swap_act = swap(2, actb.at[core], actb.at[core])
    swap_db = swap(3, dbo.at[:, :, half_at(1 - core)], dbp)
    swap_act.start()
    swap_db.start()

    r_line = LineSum(dh, in_left, in_right, nz, (r_send, r_left, r_right))

    def hidden_back(i, _):
        block = r_line.order(i)
        part_sum = dot_nt(dbo[block], fcv[...].reshape(d, ff))
        dh[block] = part_sum.astype(BF)

        @pl.when(block == z)
        def _():
            own_dh[...] = part_sum

        r_line.ready(block)
        return 0

    lax.fori_loop(0, nz, hidden_back, 0)

    def output_part(k, i):
        w = pjv[k, i].reshape(slot, ff)
        part = dot_nt(actb[core].reshape(tall, ff), w)
        low = k * he + i * slot
        ctb[:, :, low : low + slot] = part.astype(BF).reshape(nz, rows, slot)

    swap_ct.wait_recv()
    swap_act.wait_recv()
    pieces = 2 if hf % 256 == 0 or ff % 512 else 4
    for low in range(0, ff, ff // pieces):
        cols = slice(low, low + ff // pieces)
        pg[:, :, :, :, cols] = (
            (
                dot_tn(
                    ctb[:, :, e_at(core)].reshape(tall, he),
                    actb[core, :, :, cols].reshape(tall, ff // pieces),
                )
                + dot_tn(
                    cto[...].reshape(tall, he),
                    actb[1 - core, :, :, cols].reshape(tall, ff // pieces),
                )
            )
            .astype(BF)
            .reshape(nz, fs, share, grain, ff // pieces)
        )
    p_total = PlaneSum(
        plane,
        lambda g, h: pg.at[half_z(h), g],
        lambda n, h: pr.at[n, pl.ds(0, halves(nz)[h][1])],
        (g_send, g_recv),
    )
    p_total.start()
    c_line.finish()
    swap_ct.wait_send()
    keep_out = pltpu.make_async_copy(ctb, out_part, local.at[6])
    for s in range(1, nz - 1):
        r_line.step(s)
        if s == 1:
            for k in range(2):
                for i in range(nz):
                    output_part(k, i)
            keep_out.start()
    swap_h2.wait_recv()
    swap_db.wait_recv()
    own_db = dbo[:, :, half_at(core)].reshape(tall, hf)
    other_db = dbp[...].reshape(tall, hf)
    cut = 512
    for low in range(0, d, cut):
        high = min(d, low + cut)
        fc_grad[low:high, :] = (
            dot_tn(h2b[core, :, :, low:high].reshape(tall, high - low), own_db)
            + dot_tn(h2b[1 - core, :, :, low:high].reshape(tall, high - low), other_db)
        ).astype(BF)
    p_total.mid()
    r_line.finish()

    sums[0:4, :] = jnp.zeros((4, sums.shape[1]), F32)
    dsp[core] = jnp.zeros(dsp.shape[1:], BF)

    def norm_back_chunk(i, _):
        at = pl.ds(pl.multiple_of(i * step, step), step)
        g = own_dh[at, :] + in_left[z, at, :].astype(F32) + in_right[z, at, :].astype(F32)
        xhat, rstd = norm_rows(middle[at, :])
        dm = ct[at, :].astype(F32) + norm_back(g, xhat, rstd, vec[1:2, :])
        low = dm.astype(BF)
        d_middle[at, :] = dm
        for c in range(cs):
            to = (c % 2) * he + (c // 2) * slot
            dsp[core, at, to : to + part] = low[:, c * part : (c + 1) * part]
        sums[0:1, 0:d] += jnp.sum(low.astype(F32), axis=0, keepdims=True)
        sums[1:2, 0:d] += jnp.sum(g * xhat, axis=0, keepdims=True)
        sums[2:3, 0:d] += jnp.sum(g, axis=0, keepdims=True)
        sums[3:4, 0:d] += jnp.sum(ct[at, :].astype(F32), axis=0, keepdims=True)
        return 0

    lax.fori_loop(0, rows // step, norm_back_chunk, 0)
    swap_d = swap(5, dsp.at[core], dsp.at[core])
    swap_d.start()
    back = dot(d_middle[...].astype(BF), ov[...].reshape(d, fs * lanes)).astype(BF)
    for g in range(fs):
        da[:, own_rows * g : own_rows * (g + 1)] = back[:, lanes * g : lanes * g + own_rows]
    if d < cs * width:
        da[:, d:] = jnp.zeros((rows, cs * width - d), BF)

    def d_copy(i):
        r = ranks[i]
        here = da.at[:, pl.ds(pl.multiple_of(r * width, 128), width)]
        there = d_att.at[pl.ds(pl.multiple_of(rank * rows, rows), rows)]
        return remote(here, there, d_send.at[i], d_recv.at[rank], z=r // 2, core=lax.rem(r, 2))

    for i in range(cs - 1):
        d_copy(i).start()
    d_att[pl.ds(pl.multiple_of(rank * rows, rows), rows), :] = da[
        :, pl.ds(pl.multiple_of(rank * width, 128), width)
    ]

    swap_a.wait_recv()
    swap_d.wait_recv()

    def stage_out(g):
        at = pl.ds(g * lanes, lanes)
        return pltpu.make_async_copy(stage.at[g % 2], og.at[:, :, :, at], local.at[4 + g % 2])

    for g in range(fs):
        at = slice(g * lanes, (g + 1) * lanes)
        part_sum = dot_tn(
            dsp[:, :, e_at(core)].reshape(2 * rows, he), a_pad[:, :, at].reshape(2 * rows, lanes)
        )
        part_sum = part_sum.astype(BF).reshape(nz, slot // grain, grain, lanes)
        if g >= 2:
            stage_out(g - 2).wait()
        stage[g % 2] = part_sum[:, : og.shape[1]]
        stage_out(g).start()
    for g in range(max(fs - 2, 0), fs):
        stage_out(g).wait()

    p_total.end()
    for h in range(2):
        p_sum[half_z(h)] = p_total.total(h).astype(BF)
    for i in range(1, cs):
        back = lax.rem(rank + cs - i, cs)
        to = d_att.at[pl.ds(pl.multiple_of(back * rows, rows), rows)]
        remote(to, to, d_send.at[0], d_recv.at[back], z=z).wait_recv()

    for i in range(cs - 1):
        d_copy(i).wait_send()
    for g in range(fs):
        fc_pass(g).wait_send()
        p_pass(g).wait_send()
    fc_gather.sent()
    p_gather.sent()
    p_total.sent()
    keep_out.wait()
    h_line.finish()
    r_line.sent()
    for s in (swap_h2, swap_act, swap_db, swap_a, swap_d):
        s.wait_send()


def middle_part(cfg, a_own, tok, ct, smalls, p2, o_all, fc):
    fs, nz, d, heads = cfg
    cs = 2 * nz
    rows, width = tok.shape[0], heads * HD
    length = rows * cs
    lanes = o_all.shape[3] // fs
    share, grain = p2.shape[1], p2.shape[2]
    he, hf = nz * fs * share * grain, fc.shape[2]
    return pl.pallas_call(
        partial(middle_kernel, cfg),
        out_shape=(
            shape((rows, d), F32),
            shape((rows, d), F32),
            shape((length, width)),
            shape((nz, rows, 2 * he)),
            shape((d, hf)),
            shape((nz, share, grain, 2 * hf)),
            shape((nz,) + o_all.shape[1:]),
            shape((5, max(2 * hf, d)), F32),
        ),
        in_specs=[VMEM] * 5 + [HBM] * 2,
        out_specs=(VMEM, VMEM, VMEM, HBM, VMEM, VMEM, HBM, VMEM),
        scratch_shapes=[
            pltpu.VMEM((3, d), F32),
            pltpu.VMEM((1, 2 * hf), F32),
            pltpu.VMEM((2, rows, fs * lanes), BF),
            pltpu.VMEM(o_all.shape, BF),
            pltpu.VMEM((fs * fc.shape[0], fc.shape[1], 2 * hf), BF),
            pltpu.VMEM((2, nz, fs, share, grain, 2 * hf), BF),
            pltpu.VMEM((nz, rows, 2 * he), BF),
            pltpu.VMEM((nz, rows, he), BF),
            pltpu.VMEM((2, nz, rows, d), BF),
            pltpu.VMEM((2, nz, rows, 2 * hf), BF),
            pltpu.VMEM((nz, rows, 2 * hf), BF),
            pltpu.VMEM((nz, rows, hf), BF),
            pltpu.VMEM((nz, rows, d), BF),
            pltpu.VMEM((nz, rows, d), BF),
            pltpu.VMEM((nz, rows, d), BF),
            pltpu.VMEM((rows, d), F32),
            pltpu.VMEM((rows, cs * width), BF),
            pltpu.VMEM((2, rows, 2 * he), BF),
            pltpu.VMEM((nz, fs, share, grain, 2 * hf), BF),
            pltpu.VMEM((2 * (fs - 1), nz - nz // 2, share, grain, 2 * hf), BF),
            pltpu.VMEM((2, nz) + o_all.shape[1:3] + (lanes,), BF),
        ]
        + sems(7, 2 * fs, (fs, 2), fs, fs, 2 * fs, (fs, 2), fs, fs)
        + sems(nz, nz, nz, nz, nz, nz, 6, 6, nz, nz, nz, cs, cs, 2 * fs, 2 * fs),
        name="middle",
        compiler_params=pltpu.CompilerParams(
            collective_id=1, has_side_effects=True, vmem_limit_bytes=62 * 2**20
        ),
    )(a_own, tok, ct, smalls, p2, o_all, fc)


def last_kernel(
    cfg,
    qkv,
    att,
    lse,
    d_att,
    pos_col,
    pos_row,
    w,
    h1,
    tok,
    smalls,
    sums,
    out_part,
    p_sum,
    og,
    fg,
    out_rows,
    in_rows,
    q_grad,
    p_grad,
    o_grad,
    f_grad,
    small_grad,
    vec,
    p_all,
    q_own,
    fgv,
    fr,
    d_qkv,
    acc,
    h1v,
    qg,
    qr,
    qs,
    om,
    orc,
    osum,
    o_left,
    o_right,
    op,
    ro_left,
    ro_right,
    pz,
    other,
    partner,
    own,
    r_out,
    r_left,
    r_right,
    line,
    sm_out,
    sm_in,
    sm_f,
    ro_sems,
    ro_lsems,
    ro_rsems,
    z_send,
    z_recv,
    l_send,
    l_recv,
    local,
    q_send,
    q_recv,
    o_send,
    o_recv,
    os_send,
    os_left,
    os_right,
    f_send,
    f_recv,
    m_send,
    m_recv,
    r_send,
    r_lsems,
    r_rsems,
    b_send,
    b_recv,
    s_send,
    s_recv,
    g_send,
    g_recv,
):
    fs, nz, d, heads = cfg
    cs = 2 * nz
    f, z, core = lax.axis_index("fsdp"), lax.axis_index("z"), lax.axis_index("core")
    rank = 2 * z + core
    rows = tok.shape[0]
    width = heads * HD
    lanes = w.shape[2] // fs
    grain = w.shape[1]
    own_rows, part = d // fs, d // cs
    he = out_part.shape[2] // 2
    slot = he // nz
    hf = p_sum.shape[3] // 2
    plane = Plane(fs)
    ranks = [lax.rem(rank + i, cs) for i in range(1, cs)]
    lanes_of = lambda g: pl.ds(pl.multiple_of(g * lanes, 128), lanes)
    runs = column_segments(cs, d, width, grain)
    block_rows = lambda b: pl.ds(pl.multiple_of(b * rows, rows), rows)
    half_z = lambda h: pl.ds(*halves(nz)[h])

    def h1_in(i):
        here = h1.at[:, lanes_of(lax.rem(f + 1 + i, fs))]
        return pltpu.make_async_copy(here, h1v.at[i % 2], local.at[4 + i % 2])

    for i in range(min(2, fs)):
        h1_in(i).start()
    om_in = pltpu.make_async_copy(og, om, local.at[2])
    op_in = pltpu.make_async_copy(out_part, op, local.at[3])
    om_in.start()
    op_in.start()
    fg_in = pltpu.make_async_copy(fg, fgv, local.at[6])
    fg_in.start()
    for r in range(cs):
        vec[:, r * part : (r + 1) * part] = smalls[r, 0:1, 0:part]
    meet(
        [dict(z=r // 2, core=lax.rem(r, 2)) for r in ranks] + [dict(fsdp=p) for p in plane.peers]
    )

    om_in.wait()
    o_total = PlaneSum(
        plane,
        lambda g, h: om.at[half_z(h), :, :, lanes_of(g)],
        lambda n, h: orc.at[n, pl.ds(0, halves(nz)[h][1])],
        (o_send, o_recv),
    )
    o_total.start()

    def z_copy(i):
        to = lax.rem(z + i, nz)
        return remote(p_sum.at[to], pz.at[z], z_send.at[to], z_recv.at[z], z=to)

    z_keep = pltpu.make_async_copy(p_sum.at[z], pz.at[z], local.at[0])
    for i in range(1, nz):
        z_copy(i).start()
    z_keep.start()

    op_in.wait()
    ro_line = LineSum(op, ro_left, ro_right, nz, (ro_sems, ro_lsems, ro_rsems))
    ro_line.first()

    def l_copy(i):
        g = plane.peers[i]
        return remote(pz.at[g], p_all.at[f], l_send.at[i], l_recv.at[f], fsdp=g)

    l_keep = pltpu.make_async_copy(pz.at[f], p_all.at[f], local.at[1])

    def shares_on():
        z_keep.wait()
        for i in range(1, nz):
            back = lax.rem(z + nz - i, nz)
            remote(pz.at[back], pz.at[back], z_send.at[0], z_recv.at[back], z=back).wait_recv()
        for i in range(fs - 1):
            l_copy(i).start()
        l_keep.start()

    tall = query_block(cs * rows)
    for h in range(heads):
        attend_back_head(
            h, width, tall, qkv, pos_col, pos_row, att, lse, d_att, d_qkv, acc
        )
        if h == heads - 1:
            ro_line.step(1)
            shares_on()

    slices = 3 * width // grain
    q_total = PlaneSum(
        plane,
        lambda g, h: qg.at[g, pl.ds(*halves(slices)[h])],
        lambda n, h: qr.at[n, pl.ds(0, halves(slices)[h][1])],
        (q_send, q_recv),
    )

    for i in range(fs):
        g = lax.rem(f + 1 + i, fs)
        h1_in(i).wait()
        part_sum = dot_tn(d_qkv[...], h1v[i % 2])
        qg[g] = part_sum.astype(BF).reshape(slices, grain, lanes)
        if i + 2 < fs:
            h1_in(i + 2).start()
    q_total.start()
    fg_in.wait()
    f_rows = f_grad.shape[0]
    f_total = PlaneSum(
        plane,
        lambda g, h: fgv.at[pl.ds(g * f_rows + halves(f_rows)[h][0], halves(f_rows)[h][1])],
        lambda n, h: fr.at[n, pl.ds(0, halves(f_rows)[h][1])],
        (f_send, f_recv),
    )
    for s in range(2, nz - 1):
        ro_line.step(s)

    def hidden(block):
        full = dot(d_qkv[block_rows(block), :], w[...].reshape(3 * width, fs * lanes))
        return [full[:, lanes * g : lanes * g + own_rows] for g in range(fs)]

    def other_step(b, _):
        for g, piece in enumerate(hidden(2 * b + 1 - core)):
            other[b, :, own_rows * g : own_rows * (g + 1)] = piece.astype(BF)
        return 0

    lax.fori_loop(0, nz, other_step, 0)
    to_partner = remote(other, partner, m_send.at[0], m_recv.at[0], core=1 - core)
    to_partner.start()
    o_total.mid()

    to_partner.wait_recv()

    r_line = LineSum(r_out, r_left, r_right, nz, (r_send, r_lsems, r_rsems))

    def own_step(i, _):
        b = r_line.order(i)
        for g, piece in enumerate(hidden(2 * b + core)):
            at = slice(own_rows * g, own_rows * (g + 1))
            both = piece + partner[b, :, at].astype(F32)
            r_out[b, :, at] = both.astype(BF)

            @pl.when(b == z)
            def _():
                own[:, at] = both

        r_line.ready(b)
        return 0

    lax.fori_loop(0, nz, own_step, 0)
    q_total.mid()
    f_total.start()
    ro_line.finish()

    step = min(32, rows)

    def output_chunk(i, _):
        at = pl.ds(pl.multiple_of(i * step, step), step)
        total = (
            op[z, at, :].astype(F32)
            + ro_left[z, at, :].astype(F32)
            + ro_right[z, at, :].astype(F32)
        )
        for c in range(cs):
            low = (c % 2) * he + (c // 2) * slot
            cols = slice(c * part, (c + 1) * part)
            out_rows[at, cols] = total[:, low : low + part]
        return 0

    lax.fori_loop(0, rows // step, output_chunk, 0)
    o_total.end()
    for h in range(2):
        osum[half_z(h)] = o_total.total(h).astype(BF)
    o_line = LineSum(osum, o_left, o_right, nz, (os_send, os_left, os_right))
    o_line.first()
    r_line.step(1)

    q_total.end()
    for h in range(2):
        qs[pl.ds(*halves(slices)[h])] = q_total.total(h).astype(BF)

    def run_copy(n):
        dst, at, src, first, count = runs[n]
        here, there = qs.at[pl.ds(first, count)], q_own.at[pl.ds(at, count)]
        if src == dst:
            return pltpu.make_async_copy(here, there, b_send.at[n])
        return remote(here, there, b_send.at[n], b_recv.at[n], z=dst // 2, core=dst % 2)

    for n, run in enumerate(runs):

        @pl.when(rank == run[2])
        def _():
            run_copy(n).start()

    for s in range(2, nz - 1):
        r_line.step(s)
    for s in range(1, nz - 1):
        o_line.step(s)
    f_total.mid()

    l_keep.wait()
    for g in plane.peers:
        remote(p_all.at[g], p_all.at[g], l_send.at[0], l_recv.at[g], fsdp=g).wait_recv()
    fine = p_all.shape[2]
    whole = p_all[...].reshape(-1, fine, 2 * hf)[: part // fine].reshape(part, 2 * hf)
    ff_half = p_grad.shape[0] // 2
    for k in range(2):
        p_grad[k * ff_half : (k + 1) * ff_half, :] = whole[:, k * hf : k * hf + ff_half].T
    r_line.finish()

    line[...] = jnp.zeros(line.shape, F32)

    def norm_back_chunk(i, _):
        at = pl.ds(pl.multiple_of(i * step, step), step)
        g = own[at, :] + r_left[z, at, :].astype(F32) + r_right[z, at, :].astype(F32)
        xhat, rstd = norm_rows(tok[at, :].astype(F32))
        in_rows[at, :] = norm_back(g, xhat, rstd, vec[...])
        line[0:1, 0:d] += jnp.sum(g * xhat, axis=0, keepdims=True)
        line[1:2, 0:d] += jnp.sum(g, axis=0, keepdims=True)
        return 0

    lax.fori_loop(0, rows // step, norm_back_chunk, 0)

    head_lanes = pl.ds(pl.multiple_of(rank * width, 128), width)
    line[2:3, head_lanes] = jnp.sum(d_qkv[:, 0:width].astype(F32), axis=0, keepdims=True)
    line[3:4, head_lanes] = jnp.sum(d_qkv[:, 2 * width :].astype(F32), axis=0, keepdims=True)
    line[4:8, 0:d] = sums[0:4, 0:d]
    sm_out[...] = jnp.zeros(sm_out.shape, F32)
    ff_parts = small_grad.shape[0] - 8
    for r in range(cs):
        sm_out[r, 0:8, 0:part] = line[0:8, r * part : (r + 1) * part]
    for k in range(2):
        for j in range(ff_parts):
            sm_out[2 * z + k, 8 + j : 9 + j, 0:part] = sums[
                4:5, k * hf + j * part : k * hf + (j + 1) * part
            ]

    def s_copy(i):
        r = ranks[i]
        here = sm_out.at[r]
        return remote(
            here, sm_in.at[rank], s_send.at[i], s_recv.at[rank], z=r // 2, core=lax.rem(r, 2)
        )

    for i in range(cs - 1):
        s_copy(i).start()
    o_line.finish()
    whole = (osum[z].astype(F32) + o_left[z].astype(F32) + o_right[z].astype(F32)).astype(BF)
    o_grad[...] = whole.reshape(part, lanes)[:, :own_rows].T
    total = sm_out[rank]
    for i in range(1, cs):
        back = lax.rem(rank + cs - i, cs)
        remote(sm_in.at[back], sm_in.at[back], s_send.at[0], s_recv.at[back], z=z).wait_recv()
        total += sm_in[back]
    sm_f[f] = total

    def g_copy(i):
        return remote(sm_f.at[f], sm_f.at[f], g_send.at[i], g_recv.at[f], fsdp=plane.peers[i])

    for i in range(fs - 1):
        g_copy(i).start()
    for n, run in enumerate(runs):

        @pl.when(rank == run[0])
        def _():
            if run[0] == run[2]:
                run_copy(n).wait()
            else:
                run_copy(n).wait_recv()

    q_grad[...] = q_own[...].reshape(-1, lanes)[:, :own_rows].T
    f_total.end()
    for h in range(2):
        f_grad[pl.ds(*halves(f_rows)[h])] = f_total.total(h).astype(BF)
    for g in plane.peers:
        remote(sm_f.at[g], sm_f.at[g], g_send.at[0], g_recv.at[g], fsdp=g).wait_recv()
    total = sm_f[0]
    for g in range(1, fs):
        total += sm_f[g]
    small_grad[...] = total

    for i in range(1, nz):
        z_copy(i).wait_send()
    for i in range(fs - 1):
        l_copy(i).wait_send()
        g_copy(i).wait_send()
    for s in (ro_line, r_line, o_line, o_total, q_total, f_total):
        s.sent()
    to_partner.wait_send()
    for n, run in enumerate(runs):
        if run[0] != run[2]:

            @pl.when(rank == run[2])
            def _():
                run_copy(n).wait_send()

    for i in range(cs - 1):
        s_copy(i).wait_send()


def last_part(cfg, counts, qkv, att, lse, d_att, pos, w, h1, tok, smalls, sums, out_part, p_sum, og, fg):
    fs, nz, d, heads = cfg
    cs = 2 * nz
    rows, length, width = tok.shape[0], qkv.shape[0], heads * HD
    grain, lanes = w.shape[1], w.shape[2] // fs
    q_grains, fc_cols = counts
    small_rows = smalls.shape[1]
    f_rows = fg.shape[0] // fs
    he = out_part.shape[2] // 2
    slices = 3 * width // grain
    runs = len(column_segments(cs, d, width, grain))
    part = d // cs
    rest = 2 * (fs - 1)
    rows_low = pltpu.VMEM((nz, rows, d), BF)
    outs_low = pltpu.VMEM((nz, rows, 2 * he), BF)
    owner = (nz,) + og.shape[1:3] + (lanes,)
    return pl.pallas_call(
        partial(last_kernel, cfg),
        out_shape=(
            shape((rows, d), F32),
            shape((rows, d), F32),
            shape((d // fs, q_grains * grain)),
            shape((2 * fc_cols, part)),
            shape((d // fs, part)),
            shape((f_rows,) + fg.shape[1:]),
            shape((small_rows, up(part)), F32),
        ),
        in_specs=[VMEM] * 7 + [HBM] + [VMEM] * 3 + [HBM, VMEM, HBM, HBM],
        out_specs=(VMEM,) * 7,
        scratch_shapes=[
            pltpu.VMEM((1, d), F32),
            pltpu.VMEM((fs,) + p_sum.shape[1:], BF),
            pltpu.VMEM((q_grains, grain, lanes), BF),
            pltpu.VMEM(fg.shape, BF),
            pltpu.VMEM((rest, f_rows - f_rows // 2) + fg.shape[1:], BF),
            pltpu.VMEM((length, 3 * width), BF),
            pltpu.VMEM((length, 2 * HD), F32),
            pltpu.VMEM((2, length, lanes), BF),
            pltpu.VMEM((fs, slices, grain, lanes), BF),
            pltpu.VMEM((rest, slices - slices // 2, grain, lanes), BF),
            pltpu.VMEM((slices, grain, lanes), BF),
            pltpu.VMEM(og.shape, BF),
            pltpu.VMEM((rest, nz - nz // 2) + owner[1:], BF),
            pltpu.VMEM(owner, BF),
            pltpu.VMEM(owner, BF),
            pltpu.VMEM(owner, BF),
            outs_low,
            outs_low,
            outs_low,
            pltpu.VMEM(p_sum.shape, BF),
            rows_low,
            rows_low,
            pltpu.VMEM((rows, d), F32),
            rows_low,
            rows_low,
            rows_low,
            pltpu.VMEM((8, width * cs), F32),
            pltpu.VMEM((cs, small_rows, up(part)), F32),
            pltpu.VMEM((cs, small_rows, up(part)), F32),
            pltpu.VMEM((fs, small_rows, up(part)), F32),
        ]
        + sems(nz, nz, nz, nz, nz, fs, fs, 7, rest + 2, rest + 2, rest + 2, rest + 2)
        + sems(nz, nz, nz, rest + 2, rest + 2, 1, 1, nz, nz, nz, runs, runs, cs, cs, fs, fs),
        name="last",
        compiler_params=pltpu.CompilerParams(
            collective_id=2, has_side_effects=True, vmem_limit_bytes=62 * 2**20
        ),
    )(
        qkv,
        att,
        lse,
        d_att,
        pos[:, None],
        pos[None, :],
        w,
        h1,
        tok,
        smalls,
        sums,
        out_part,
        p_sum,
        og,
        fg,
    )


def body(
    tokens,
    block_order,
    cotangent,
    pre_attn_gain,
    pre_attn_bias,
    qkv_weight,
    query_bias,
    value_bias,
    out_weight,
    out_bias,
    pre_mlp_gain,
    pre_mlp_bias,
    fc_weight,
    fc_bias,
    proj_weight,
    proj_bias,
):
    fs, nz = lax.axis_size("fsdp"), lax.axis_size("z")
    cs = nz * 2
    rows, d = tokens.shape[1], tokens.shape[2]
    length = rows * cs
    heads_all = d // HD
    heads = -(-heads_all // cs)
    width = heads * HD
    part, own_rows = d // cs, d // fs
    fc_cols = fc_weight.shape[1]
    hf = up(fc_cols)

    small = jnp.stack(
        [
            v.astype(F32)
            for v in (
                pre_attn_gain,
                pre_attn_bias,
                query_bias,
                value_bias,
                out_bias,
                pre_mlp_gain,
                pre_mlp_bias,
                proj_bias,
            )
        ]
    )
    small = jnp.concatenate([small, fc_bias.astype(F32).reshape(-1, part)])
    small = jnp.pad(small, ((0, 0), (0, up(part) - part)))
    lanes = up(own_rows)
    wq = jnp.pad(qkv_weight.T, ((0, 0), (0, lanes - own_rows)))
    grain = math.gcd(math.gcd(wq.shape[0], HD), 8)
    wq = wq.reshape(-1, grain, lanes)
    fine = math.gcd(part, 8)
    share = -(-part // (fine * fs))
    slot = fs * share * fine
    he = nz * slot
    pj = jnp.pad(
        proj_weight.reshape(2, fc_cols, part), ((0, 0), (0, hf - fc_cols), (0, slot - part))
    )
    pj = pj.reshape(2 * hf, slot).T.reshape(fs * share, fine, 2 * hf)
    ot = jnp.pad(out_weight.T, ((0, 0), (0, lanes - own_rows))).reshape(-1, fine, lanes)
    pos = positions(block_order, length)
    fc = jnp.pad(fc_weight, ((0, 0), (0, hf - fc_cols)))
    fc = fc.reshape(-1, math.gcd(own_rows, 16), hf)
    cfg = (fs, nz, d, heads)
    h1, w, qkv, att, lse, smalls, p2, o_all, a_own = start(
        cfg, tokens[0], wq, small, pj, ot, pos
    )
    vec = lambda i: smalls[:, i, :part].reshape(d)
    middle, d_middle, d_att, out_part, fc_grad, p_sum, og, sums = middle_part(
        cfg, a_own, tokens[0], cotangent[0], smalls, p2, o_all, fc
    )
    fg = fc_grad.reshape(-1, fc.shape[1], hf)
    out_rows, in_rows, qkv_grad, proj_grad, out_grad, fc_grad, g = last_part(
        cfg,
        (wq.shape[0], fc_cols),
        qkv,
        att,
        lse,
        d_att,
        pos,
        w,
        h1,
        tokens[0],
        smalls,
        sums,
        out_part,
        p_sum,
        og,
        fg,
    )
    output = (middle + out_rows + vec(7)).astype(BF)
    input_grad = d_middle + in_rows
    fc_grad = fc_grad.reshape(own_rows, hf)[:, :fc_cols]
    g = g[:, :part]
    return (
        output[None],
        input_grad[None],
        g[0],
        g[1],
        qkv_grad.astype(F32),
        g[2],
        g[3],
        out_grad.astype(F32),
        g[4],
        g[5],
        g[6],
        fc_grad.astype(F32),
        g[8:].reshape(-1),
        proj_grad.astype(F32),
        g[7],
    )


def solution(mesh):
    fs, cs = mesh.shape["fsdp"], mesh.shape["ctx"]
    split = Mesh(mesh.devices.reshape(fs, cs // 2, 2), ("fsdp", "z", "core"))
    rows = P("fsdp", CTX, None)
    weight = P("fsdp", CTX)
    vector = P(CTX)
    in_specs = (
        rows,
        P(),
        rows,
        vector,
        vector,
        weight,
        vector,
        vector,
        weight,
        vector,
        vector,
        vector,
        weight,
        vector,
        weight,
        vector,
    )
    out_specs = (
        rows,
        rows,
        vector,
        vector,
        weight,
        vector,
        vector,
        weight,
        vector,
        vector,
        vector,
        weight,
        vector,
        weight,
        vector,
    )
    return jax.shard_map(body, mesh=split, in_specs=in_specs, out_specs=out_specs, check_vma=False)
```

```python
from functools import partial
import math

import jax
import jax.numpy as jnp
from jax import lax
from jax.experimental import pallas as pl
from jax.experimental.pallas import tpu as pltpu
from jax.sharding import Mesh
from jax.sharding import PartitionSpec as P

HD = 64
EPS = 1e-05
FLOOR = -1e30
BF = jnp.bfloat16
F32 = jnp.float32
CTX = ("z", "core")
MESH = pl.DeviceIdType.MESH
VMEM = pl.BlockSpec(memory_space=pltpu.VMEM)
HBM = pl.BlockSpec(memory_space=pl.ANY)
GELU_A = math.sqrt(2.0 / math.pi)
GELU_B = 0.044715


def up(n):
    return -(-n // 128) * 128


def sems(*counts):
    return [pltpu.SemaphoreType.DMA(c if isinstance(c, tuple) else (c,)) for c in counts]


def shape(dims, kind=BF):
    return jax.ShapeDtypeStruct(dims, kind)


def dot(a, b):
    return jnp.dot(a, b, preferred_element_type=F32)


def dot_nt(a, b):
    return lax.dot_general(a, b, (((1,), (1,)), ((), ())), preferred_element_type=F32)


def dot_tn(a, b):
    return lax.dot_general(a, b, (((0,), (0,)), ((), ())), preferred_element_type=F32)


def norm_rows(rows):
    centred = rows - jnp.mean(rows, axis=-1, keepdims=True)
    rstd = lax.rsqrt(jnp.mean(centred * centred, axis=-1, keepdims=True) + EPS)
    return centred * rstd, rstd


def norm_back(upstream, xhat, rstd, gain):
    inner = upstream * gain
    return rstd * (
        inner
        - jnp.mean(inner, axis=-1, keepdims=True)
        - xhat * jnp.mean(inner * xhat, axis=-1, keepdims=True)
    )


def gelu_pair(v):
    sq = v * v
    t = jnp.tanh(GELU_A * v * (1.0 + GELU_B * sq))
    half = 0.5 * (1.0 + t)
    slope = half + 0.5 * v * (1.0 - t * t) * (GELU_A * (1.0 + 3.0 * GELU_B * sq))
    return v * half, slope


def positions(order_table, rows):
    block = rows // order_table.shape[0]
    return (order_table[:, None] * block + jnp.arange(block, dtype=jnp.int32)[None]).reshape(rows)


def remote(src, dst, send, recv, **to):
    return pltpu.make_async_remote_copy(
        src_ref=src, dst_ref=dst, send_sem=send, recv_sem=recv, device_id=to, device_id_type=MESH
    )


def column_segments(ranks, d, width, grain):
    own = 3 * d // ranks
    runs = []
    for src in range(ranks):
        for part in range(3):
            for dst in range(ranks):
                low = part * d + dst * width
                first = max(src * own, low)
                last = min((src + 1) * own, low + width, (part + 1) * d)
                if first < last:
                    at = part * width + first - low
                    runs.append(
                        (src, (first - src * own) // grain, dst, at // grain, (last - first) // grain)
                    )
    return runs


def greet(peers):
    barrier = pltpu.get_barrier_semaphore()
    for peer in peers:
        pl.semaphore_signal(barrier, inc=1, device_id=peer, device_id_type=MESH)


def met(peers):
    pl.semaphore_wait(pltpu.get_barrier_semaphore(), len(peers))


class Line:
    def __init__(self, at, size, sems):
        self.at, self.size = at, size
        self.right, self.left, self.recv = sems
        self.z = lax.axis_index("z")

    def copy(self, block, way):
        send = (self.right if way > 0 else self.left).at[block]
        at = self.at(block)
        return remote(at, at, send, self.recv.at[block], z=self.z + way)

    def start(self):
        @pl.when(self.z < self.size - 1)
        def _():
            self.copy(self.z, 1).start()

        @pl.when(self.z > 0)
        def _():
            self.copy(self.z, -1).start()

    def step(self, s, then=None):
        @pl.when(self.z >= s)
        def _():
            block = self.z - s
            self.copy(block, 1).wait_recv()

            @pl.when(self.z < self.size - 1)
            def _():
                self.copy(block, 1).start()

            if then is not None:
                then(block)

        @pl.when(self.z + s < self.size)
        def _():
            block = self.z + s
            self.copy(block, -1).wait_recv()

            @pl.when(self.z > 0)
            def _():
                self.copy(block, -1).start()

            if then is not None:
                then(block)

    def finish(self):
        for s in range(self.size):

            @pl.when((self.z >= s) & (self.z < self.size - 1))
            def _():
                self.copy(self.z - s, 1).wait_send()

            @pl.when((self.z + s < self.size) & (self.z > 0))
            def _():
                self.copy(self.z + s, -1).wait_send()


class LineSum:
    def __init__(self, parts, came, size, sems):
        self.parts, self.came, self.size = parts, came, size
        self.send, self.recv = sems
        self.z = lax.axis_index("z")

    def copy(self, block, way):
        place = block + 1 if way > 0 else block
        there = self.came.at[place]
        return remote(
            self.parts.at[block], there, self.send.at[block], self.recv.at[place], z=self.z + way
        )

    def order(self, i):
        near = self.z < self.size // 2
        ahead = self.size - 1 - self.z
        from_low = jnp.where(i < ahead, self.size - 1 - i, i - ahead)
        from_high = jnp.where(i < self.z, i, self.size - 1 - (i - self.z))
        return jnp.where(near, from_low, from_high)

    def ready(self, block):
        @pl.when((self.z == 0) & (block > 0))
        def _():
            self.copy(block, 1).start()

        @pl.when((self.z == self.size - 1) & (block < self.size - 1))
        def _():
            self.copy(block, -1).start()

    def first(self):
        for way, edge in ((1, 0), (-1, self.size - 1)):

            @pl.when(self.z == edge)
            def _():
                for hop in range(self.size - 1, 0, -1):
                    self.copy(self.z + way * hop, way).start()

    def add_on(self, block, way):
        self.copy(block, way).wait_recv()
        came = self.came[block + 1 if way > 0 else block]
        self.parts[block] = (self.parts[block].astype(F32) + came.astype(F32)).astype(
            self.parts.dtype
        )
        self.copy(block, way).start()

    def step(self, s):
        right, left = self.z + self.size - 1 - s, s - (self.size - 1 - self.z)

        @pl.when((self.z > 0) & (right < self.size) & (right > self.z))
        def _():
            self.add_on(right, 1)

        @pl.when((self.z < self.size - 1) & (left >= 0) & (left < self.z))
        def _():
            self.add_on(left, -1)

    def finish(self):
        @pl.when(self.z > 0)
        def _():
            self.copy(self.z, 1).wait_recv()

        @pl.when(self.z == 0)
        def _():
            self.came[self.z + 1] = jnp.zeros(self.came.shape[1:], self.came.dtype)

        @pl.when(self.z < self.size - 1)
        def _():
            self.copy(self.z, -1).wait_recv()

        @pl.when(self.z == self.size - 1)
        def _():
            self.came[self.z] = jnp.zeros(self.came.shape[1:], self.came.dtype)

    def others(self, *at):
        here = (self.z,) + at
        there = (self.z + 1,) + at
        return self.came[here].astype(F32) + self.came[there].astype(F32)

    def sent(self):
        for block in range(self.size):

            @pl.when(self.z < block)
            def _():
                self.copy(block, 1).wait_send()

            @pl.when(self.z > block)
            def _():
                self.copy(block, -1).wait_send()


def halves(n):
    return ((0, n // 2), (n // 2, n - n // 2))


class Plane:
    def __init__(self, size):
        self.size, self.f = size, lax.axis_index("fsdp")
        self.square = size == 4
        f = self.f
        self.peers = [lax.rem(f + i, size) for i in range(1, size)]
        if self.square:
            self.x, self.y, self.far = f + 1 - 2 * lax.rem(f, 2), lax.rem(f + 2, 4), 3 - f
            self.peers = [self.x, self.y, self.far]


class PlaneGather:
    def __init__(self, plane, at, sems):
        self.p, self.at = plane, at
        self.send, self.recv = sems
        f = plane.f
        if plane.square:
            x, y = plane.x, plane.y
            self.early = [(f, 0, x), (f, 1, y), (f, 0, y), (f, 1, x)]
            self.late = [(x, 0, y), (y, 1, x)]
        else:
            self.early = [(f, h, g) for g in plane.peers for h in range(2)]
            self.late = []

    def copy(self, n, move):
        g, half, to = move
        at = self.at(g, half)
        return remote(at, at, self.send.at[n], self.recv.at[g, half], fsdp=to)

    def arrive(self, g, half):
        at = self.at(g, half)
        remote(at, at, self.send.at[0], self.recv.at[g, half], fsdp=g).wait_recv()

    def start(self):
        for n, move in enumerate(self.early):
            self.copy(n, move).start()

    def mid(self):
        for n, move in enumerate(self.late):
            self.arrive(move[0], move[1])
            self.copy(len(self.early) + n, move).start()

    def end(self):
        known = [(m[0], m[1]) for m in self.late]
        for g in self.p.peers:
            for half in range(2):
                if not any(g is a and half == b for a, b in known):
                    self.arrive(g, half)

    def sent(self):
        for n, move in enumerate(self.early + self.late):
            self.copy(n, move).wait_send()


class PlaneSum:
    def __init__(self, plane, at, came, sems):
        self.p, self.at, self.came = plane, at, came
        self.send, self.recv = sems
        if plane.square:
            x, y, far = plane.x, plane.y, plane.far
            self.early = [(far, 0, x, 0), (far, 1, y, 1), (x, 0, x, 2), (y, 1, y, 3)]
            self.late = [(y, 0, y, 4), (x, 1, x, 5)]
            self.mine = [[2, 4], [3, 5]]
        else:
            n = plane.size
            self.early = [
                (g, h, g, 2 * i + h) for i, g in enumerate(plane.peers) for h in range(2)
            ]
            self.late = []
            self.mine = [[2 * i + h for i in range(n - 1)] for h in range(2)]

    def copy(self, move):
        g, half, to, slot = move
        return remote(
            self.at(g, half), self.came(slot, half), self.send.at[slot], self.recv.at[slot], fsdp=to
        )

    def arrive(self, slot, half):
        there = self.came(slot, half)
        remote(
            there, there, self.send.at[slot], self.recv.at[slot], fsdp=self.p.peers[0]
        ).wait_recv()

    def start(self):
        for move in self.early:
            self.copy(move).start()

    def mid(self):
        for slot, move in enumerate(self.late):
            self.arrive(slot, move[1])
            at, came = self.at(move[0], move[1]), self.came(slot, move[1])
            at[...] = (at[...].astype(F32) + came[...].astype(F32)).astype(at.dtype)
            self.copy(move).start()

    def end(self):
        for half in range(2):
            for slot in self.mine[half]:
                self.arrive(slot, half)

    def total(self, half):
        out = self.at(self.p.f, half)[...].astype(F32)
        for slot in self.mine[half]:
            out += self.came(slot, half)[...].astype(F32)
        return out

    def sent(self):
        for move in self.early + self.late:
            self.copy(move).wait_send()


def query_block(length):
    return max(128, min(256, length, 256 * 1024 // length))


def attend_head(h, width, q_block, qkv, pos_col, pos_row, out, lse):
    rows = qkv.shape[0]
    k = qkv[:, width + h * HD : width + (h + 1) * HD]
    v = qkv[:, 2 * width + h * HD : 2 * width + (h + 1) * HD]
    for b in range(rows // q_block):
        at = slice(b * q_block, (b + 1) * q_block)
        q = qkv[at, h * HD : (h + 1) * HD] * BF(HD**-0.5)
        s = dot_nt(k, q)
        s = jnp.where(pos_col[...] <= pos_row[:, at], s, FLOOR)
        top = jnp.max(s, axis=0, keepdims=True)
        p = jnp.exp(s - top)
        total = jnp.sum(p, axis=0, keepdims=True)
        o = dot_tn(v, p.astype(BF)) * (1.0 / total)
        out[at, h * HD : (h + 1) * HD] = o.T.astype(BF)
        lse[h : h + 1, at] = top + jnp.log(total)


def attend_back_head(h, width, q_block, qkv, pos_col, pos_row, out, lse, dout, dqkv, acc):
    rows = qkv.shape[0]
    k = qkv[:, width + h * HD : width + (h + 1) * HD]
    v = qkv[:, 2 * width + h * HD : 2 * width + (h + 1) * HD]
    for b in range(rows // q_block):
        at = slice(b * q_block, (b + 1) * q_block)
        q = qkv[at, h * HD : (h + 1) * HD] * BF(HD**-0.5)
        do = dout[at, h * HD : (h + 1) * HD]
        o = out[at, h * HD : (h + 1) * HD]
        delta = jnp.sum(do.astype(F32).T * o.astype(F32).T, axis=0, keepdims=True)
        s = dot_nt(k, q)
        p = jnp.where(pos_col[...] <= pos_row[:, at], jnp.exp(s - lse[h : h + 1, at]), 0.0)
        dp = dot_nt(v, do)
        ds = (p * (dp - delta)).astype(BF)
        dq = dot_tn(k, ds) * (HD**-0.5)
        dqkv[at, h * HD : (h + 1) * HD] = dq.T.astype(BF)
        dk = dot(ds, q)
        dv = dot(p.astype(BF), do)
        if b == 0:
            acc[:, :HD] = dk
            acc[:, HD:] = dv
        else:
            acc[:, :HD] += dk
            acc[:, HD:] += dv
    dqkv[:, width + h * HD : width + (h + 1) * HD] = acc[:, :HD].astype(BF)
    dqkv[:, 2 * width + h * HD : 2 * width + (h + 1) * HD] = acc[:, HD:].astype(BF)


def start_kernel(
    cfg,
    tok,
    qkv_own,
    small,
    proj_own,
    out_own,
    block_order,
    h1_out,
    w_out,
    qkv,
    att,
    lse,
    smalls,
    p2,
    o_all,
    a_own,
    h1,
    w,
    wq,
    pj,
    ot,
    pos_col,
    pos_row,
    toks,
    vecs,
    p1,
    small_send,
    small_recv,
    q_send,
    q_recv,
    q_local,
    x_send,
    x_recv,
    t_right,
    t_left,
    t_recv,
    c_send,
    c_recv,
    p1_send,
    p1_recv,
    p2_send,
    p2_recv,
    p_local,
    a_send,
    a_recv,
    o_right,
    o_left,
    o_recv,
    ox_send,
    ox_recv,
    oc_send,
    oc_recv,
):
    fs, nz, d, heads = cfg
    cs = 2 * nz
    f, z, core = lax.axis_index("fsdp"), lax.axis_index("z"), lax.axis_index("core")
    rank = 2 * z + core
    rows, lanes = tok.shape[0], wq.shape[2]
    width = heads * HD
    grain = wq.shape[1]
    own_rows = d // fs
    part = d // cs
    lanes_of = lambda g: pl.ds(pl.multiple_of(g * lanes, 128), lanes)
    runs = column_segments(cs, d, width, grain)
    plane = Plane(fs)
    planes = plane.peers

    w[:, :, lanes_of(f)] = jnp.zeros((w.shape[0], grain, lanes), BF)
    ranks = [lax.rem(rank + i, cs) for i in range(1, cs)]
    peers = [dict(z=r // 2, core=lax.rem(r, 2)) for r in ranks] + [dict(fsdp=p) for p in planes]
    greet(peers)

    fine = ot.shape[1]
    if lanes > own_rows:
        wq[:, :, own_rows:] = jnp.zeros((wq.shape[0], grain, lanes - own_rows), BF)
        ot[:, :, own_rows:] = jnp.zeros((ot.shape[0], fine, lanes - own_rows), BF)
    wq[:, :, 0:own_rows] = qkv_own[...].T.reshape(wq.shape[0], grain, own_rows)
    ot[:, :, 0:own_rows] = out_own[...].T.reshape(ot.shape[0], fine, own_rows)
    pj[...] = jnp.zeros(pj.shape, BF)
    ff_half, hf = proj_own.shape[0] // 2, pj.shape[2] // 2
    for k in range(2):
        turned = proj_own[k * ff_half : (k + 1) * ff_half, :].T
        pj[0 : part // fine, :, k * hf : k * hf + ff_half] = turned.reshape(
            part // fine, fine, ff_half
        )
    met(peers)
    keep_out = pltpu.make_async_copy(ot, o_all.at[rank, :, :, lanes_of(f)], p_local.at[0])
    keep_out.start()

    def run_copy(n):
        src, first, dst, at, count = runs[n]
        here, there = wq.at[pl.ds(first, count)], w.at[pl.ds(at, count), :, lanes_of(f)]
        if src == dst:
            return pltpu.make_async_copy(here, there, q_local.at[n])
        return remote(here, there, q_send.at[n], q_recv.at[n], z=dst // 2, core=dst % 2)

    for n, run in enumerate(runs):

        @pl.when(rank == run[0])
        def _():
            run_copy(n).start()

    def small_copy(i):
        r = ranks[i]
        to = smalls.at[rank]
        return remote(small, to, small_send.at[i], small_recv.at[rank], z=r // 2, core=lax.rem(r, 2))

    for i in range(cs - 1):
        small_copy(i).start()

    share = p1.shape[1]

    def p1_copy(i):
        here = pj.at[pl.ds(planes[i] * share, share)]
        return remote(here, p1.at[f], p1_send.at[i], p1_recv.at[f], fsdp=planes[i])

    p1[f] = pj[pl.ds(f * share, share)]
    for i in range(fs - 1):
        p1_copy(i).start()

    def ox_copy(i, block, here=None):
        at = o_all.at[2 * block + core, :, :, lanes_of(f)]
        here = at if here is None else here
        return remote(here, at, ox_send.at[i, block], ox_recv.at[f, block], fsdp=planes[i])

    def ox_arrival(g, block):
        at = o_all.at[2 * block + core, :, :, lanes_of(g)]
        return remote(at, at, ox_send.at[0, block], ox_recv.at[g, block], fsdp=g)

    def oc_copy(g, block, here=None):
        at = o_all.at[2 * block + core, :, :, lanes_of(g)]
        here = at if here is None else here
        return remote(here, at, oc_send.at[g, block], oc_recv.at[g, block], core=1 - core)

    def oc_arrival(g, block):
        at = o_all.at[2 * block + 1 - core, :, :, lanes_of(g)]
        return remote(at, at, oc_send.at[g, block], oc_recv.at[g, block], core=1 - core)

    def out_block(block, here=None):
        for i in range(fs - 1):
            ox_copy(i, block, here).start()
        oc_copy(f, block, here).start()

    out_block(z, ot)

    for n, run in enumerate(runs):

        @pl.when(rank == run[2])
        def _():
            if run[0] == run[2]:
                run_copy(n).wait()
            else:
                run_copy(n).wait_recv()

    gather = PlaneGather(
        plane, lambda g, h: w.at[pl.ds(*halves(w.shape[0])[h]), :, lanes_of(g)], (x_send, x_recv)
    )
    gather.start()

    pltpu.sync_copy(tok, toks.at[rank])
    line = Line(lambda b: toks.at[2 * b + core], nz, (t_right, t_left, t_recv))

    def pass_on(block):
        at = toks.at[2 * block + core]
        return remote(at, at, c_send.at[block], c_recv.at[block], core=1 - core)

    def arrival(block):
        at = toks.at[2 * block + 1 - core]
        return remote(at, at, c_send.at[block], c_recv.at[block], core=1 - core)

    line.start()
    pass_on(z).start()

    smalls[rank] = small[...]
    vecs[...] = jnp.zeros(vecs.shape, F32)
    length = cs * rows
    run = length // block_order.shape[0]
    for b in range(block_order.shape[0]):
        first = block_order[b] * run
        at = slice(b * run, (b + 1) * run)
        pos_row[:, at] = first + lax.broadcasted_iota(jnp.int32, (1, run), 1)
        pos_col[at, :] = first + lax.broadcasted_iota(jnp.int32, (run, 1), 0)
    if lanes > own_rows:
        for g in range(fs):
            h1[:, lanes * g + own_rows : lanes * (g + 1)] = jnp.zeros(
                (length, lanes - own_rows), BF
            )
    for i in range(1, cs):
        back = lax.rem(rank + cs - i, cs)
        remote(small, smalls.at[back], small_send.at[i - 1], small_recv.at[back], z=z).wait_recv()
    for r in range(cs):
        vecs[:, part * r : part * (r + 1)] = smalls[r, 0:8, 0:part]

    step = min(32, rows)

    def norm_block(block):
        def chunk(i, _):
            at = pl.multiple_of(i * step, step)
            xhat, _ = norm_rows(toks[block, pl.ds(at, step), :].astype(F32))
            h = (xhat * vecs[0:1, 0:d] + vecs[1:2, 0:d]).astype(BF)
            to = pl.ds(pl.multiple_of(block * rows + i * step, step), step)
            for g in range(fs):
                h1[to, lanes * g : lanes * g + own_rows] = h[:, own_rows * g : own_rows * (g + 1)]
            return 0

        lax.fori_loop(0, rows // step, chunk, 0)

    def place(i):
        hop = (i + 1) // 2
        return jnp.where(lax.rem(i, 2) == 1, z - hop, z + hop)

    def take(i, _):
        block = place(i)

        @pl.when((block >= 0) & (block < nz))
        def _():
            @pl.when(block < z)
            def _():
                line.copy(block, 1).wait_recv()

                @pl.when(z < nz - 1)
                def _():
                    line.copy(block, 1).start()

            @pl.when(block > z)
            def _():
                line.copy(block, -1).wait_recv()

                @pl.when(z > 0)
                def _():
                    line.copy(block, -1).start()

            @pl.when(block != z)
            def _():
                pass_on(block).start()

            norm_block(2 * block + core)
            arrival(block).wait_recv()
            norm_block(2 * block + 1 - core)

        return 0

    tall = 2 * rows
    head_lanes = pl.ds(pl.multiple_of(rank * width, 128), width)

    def project(i, _):
        block = place(i)

        @pl.when((block >= 0) & (block < nz))
        def _():
            at = pl.ds(pl.multiple_of(block * tall, tall), tall)
            full = dot_nt(h1[at, :], w[...].reshape(3 * width, fs * lanes))
            qkv[at, 0:width] = (full[:, 0:width] + vecs[2:3, head_lanes]).astype(BF)
            qkv[at, width : 2 * width] = full[:, width : 2 * width].astype(BF)
            qkv[at, 2 * width :] = (full[:, 2 * width :] + vecs[3:4, head_lanes]).astype(BF)

        return 0

    lax.fori_loop(0, 3, take, 0)
    gather.mid()
    lax.fori_loop(3, 2 * nz - 3, take, 0)

    keep_out.wait()
    out_line = Line(
        lambda b: o_all.at[2 * b + core, :, :, lanes_of(f)], nz, (o_right, o_left, o_recv)
    )
    out_line.start()
    gather.end()
    lax.fori_loop(0, 2 * nz - 3, project, 0)
    lax.fori_loop(2 * nz - 3, 2 * nz - 1, take, 0)
    lax.fori_loop(2 * nz - 3, 2 * nz - 1, project, 0)
    keep_h1 = pltpu.make_async_copy(h1, h1_out, p_local.at[1])
    keep_w = pltpu.make_async_copy(w, w_out, p_local.at[2])
    keep_h1.start()
    keep_w.start()
    out_line.step(1, out_block)

    for g in planes:
        remote(p1.at[g], p1.at[g], p1_send.at[0], p1_recv.at[g], fsdp=g).wait_recv()

    def p2_copy(i):
        to = lax.rem(z + i, nz)
        return remote(p1.at[to], p2.at[z], p2_send.at[to], p2_recv.at[z], z=to)

    def a_copy(i, pair):
        r = ranks[i]
        here = att.at[pl.ds(pl.multiple_of(r * rows, rows), rows), pl.ds(pair * 128, 128)]
        there = a_own.at[:, pl.ds(pl.multiple_of(rank * width + pair * 128, 128), 128)]
        return remote(
            here, there, a_send.at[i, pair], a_recv.at[rank, pair], z=r // 2, core=lax.rem(r, 2)
        )

    for h in range(heads):
        attend_head(h, width, query_block(cs * rows), qkv, pos_col, pos_row, att, lse)
        if h + 2 < nz:
            out_line.step(h + 2, out_block)
        if h % 2 == 1:
            for i in range(cs - 1):
                a_copy(i, h // 2).start()
        if h == 0:
            for i in range(1, nz):
                p2_copy(i).start()
            p2[z] = p1[z]
    for s in range(heads + 2, nz):
        out_line.step(s, out_block)
    a_own[:, head_lanes] = att[pl.ds(pl.multiple_of(rank * rows, rows), rows), :]

    for g in planes:
        for b in range(nz):
            ox_arrival(g, b).wait_recv()
            oc_copy(g, b).start()
    for pair in range(width // 128):
        for i in range(1, cs):
            back = lax.rem(rank + cs - i, cs)
            to = a_own.at[:, pl.ds(pl.multiple_of(back * width + pair * 128, 128), 128)]
            remote(to, to, a_send.at[0, 0], a_recv.at[back, pair], z=z).wait_recv()
    for i in range(1, nz):
        back = lax.rem(z + nz - i, nz)
        remote(p2.at[back], p2.at[back], p2_send.at[0], p2_recv.at[back], z=back).wait_recv()
    for g in range(fs):
        for b in range(nz):
            oc_arrival(g, b).wait_recv()
    keep_h1.wait()
    keep_w.wait()

    for n, run in enumerate(runs):
        if run[0] != run[2]:

            @pl.when(rank == run[0])
            def _():
                run_copy(n).wait_send()

    for i in range(cs - 1):
        small_copy(i).wait_send()
        for pair in range(width // 128):
            a_copy(i, pair).wait_send()
    gather.sent()
    for i in range(1, nz):
        p2_copy(i).wait_send()
    for i in range(fs - 1):
        p1_copy(i).wait_send()
        for b in range(nz):
            ox_copy(i, b).wait_send()
    for g in range(fs):
        for b in range(nz):
            oc_copy(g, b).wait_send()
    line.finish()
    out_line.finish()
    for b in range(nz):
        pass_on(b).wait_send()


def start(cfg, tok, qkv_own, small, proj_own, out_own, block_order, hf):
    fs, nz, d, heads = cfg
    cs = 2 * nz
    rows, cols = tok.shape[0], qkv_own.shape[1]
    width, length = heads * HD, rows * cs
    part, lanes = d // cs, up(d // fs)
    grain, fine = math.gcd(math.gcd(cols, HD), 8), math.gcd(part, 8)
    share = -(-part // (fine * fs))
    runs = len(column_segments(cs, d, width, grain))
    pairs = width // 128
    smem = pl.BlockSpec(memory_space=pltpu.SMEM)
    h1 = (length, fs * lanes)
    w = (3 * width // grain, grain, fs * lanes)
    return pl.pallas_call(
        partial(start_kernel, cfg),
        out_shape=(
            shape(h1),
            shape(w),
            shape((length, 3 * width)),
            shape((length, width)),
            shape((heads, length), F32),
            shape((cs,) + small.shape, F32),
            shape((nz, share, fine, 2 * hf)),
            shape((cs, part // fine, fine, fs * lanes)),
            shape((rows, cs * width)),
        ),
        in_specs=[VMEM] * 5 + [smem],
        out_specs=(HBM, HBM) + (VMEM,) * 5 + (HBM, VMEM),
        scratch_shapes=[
            pltpu.VMEM(h1, BF),
            pltpu.VMEM(w, BF),
            pltpu.VMEM((cols // grain, grain, lanes), BF),
            pltpu.VMEM((fs * share, fine, 2 * hf), BF),
            pltpu.VMEM((part // fine, fine, lanes), BF),
            pltpu.VMEM((length, 1), jnp.int32),
            pltpu.VMEM((1, length), jnp.int32),
            pltpu.VMEM((cs, rows, d), BF),
            pltpu.VMEM((8, width * cs), F32),
            pltpu.VMEM((fs, share, fine, 2 * hf), BF),
        ]
        + sems(cs, cs, runs, runs, runs, 2 * fs, (fs, 2), nz, nz, nz, nz, nz)
        + sems(fs, fs, nz, nz, 3, (cs, pairs), (cs, pairs))
        + sems(nz, nz, nz, (fs, nz), (fs, nz), (fs, nz), (fs, nz)),
        name="start",
        compiler_params=pltpu.CompilerParams(
            collective_id=0, has_side_effects=True, vmem_limit_bytes=60 * 2**20
        ),
    )(tok, qkv_own, small, proj_own, out_own, block_order)


def middle_kernel(
    cfg,
    a_own,
    tok,
    ct,
    smalls,
    p2,
    o_all,
    fc,
    middle,
    d_middle,
    d_att,
    out_part,
    fc_grad,
    p_sum,
    og,
    sums,
    vec,
    fb,
    a_pad,
    ov,
    fcv,
    pjv,
    ctb,
    cto,
    h2b,
    actb,
    dbo,
    dbp,
    dh,
    r_in,
    own_dh,
    da,
    dsp,
    pg,
    pr,
    stage,
    local,
    p3_send,
    p3_recv,
    pc_send,
    pc_recv,
    f_send,
    f_recv,
    fc_send,
    fc_recv,
    c_right,
    c_left,
    c_recv,
    h_right,
    h_left,
    h_recv,
    e_send,
    e_recv,
    r_send,
    r_recv,
    d_send,
    d_recv,
    g_send,
    g_recv,
):
    fs, nz, d, heads = cfg
    cs = 2 * nz
    f, z, core = lax.axis_index("fsdp"), lax.axis_index("z"), lax.axis_index("core")
    rank = 2 * z + core
    rows = tok.shape[0]
    width = heads * HD
    lanes = o_all.shape[3] // fs
    own_rows, part = d // fs, d // cs
    share, grain = p2.shape[1], p2.shape[2]
    slot = fs * share * grain
    he, hf = nz * slot, fc.shape[2]
    ff = 2 * hf
    fc_rows = fc.shape[0]
    tall = nz * rows
    step = min(32, rows)
    plane = Plane(fs)
    ranks = [lax.rem(rank + i, cs) for i in range(1, cs)]
    half_at = lambda k: pl.ds(pl.multiple_of(k * hf, 128), hf)
    e_at = lambda k: pl.ds(pl.multiple_of(k * he, 128), he)

    peers = [dict(z=r // 2, core=lax.rem(r, 2)) for r in ranks]
    peers += [dict(fsdp=p) for p in plane.peers]
    greet(peers)
    load_out = pltpu.make_async_copy(o_all, ov, local.at[0])
    fc_at = lambda g, k, h: fcv.at[
        pl.ds(g * fc_rows + halves(fc_rows)[h][0], halves(fc_rows)[h][1]), :, half_at(k)
    ]
    load_fc = [
        pltpu.make_async_copy(fc.at[pl.ds(*halves(fc_rows)[h])], fc_at(f, core, h), local.at[1 + h])
        for h in range(2)
    ]
    load_out.start()
    for copy in load_fc:
        copy.start()
    ctb[z] = jnp.zeros(ctb.shape[1:], BF)
    for c in range(cs):
        to = (c % 2) * he + (c // 2) * slot
        ctb[z, :, to : to + part] = ct[:, c * part : (c + 1) * part]
    for r in range(cs):
        vec[:, r * part : (r + 1) * part] = smalls[r, 4:7, 0:part]
    fb[...] = jnp.zeros(fb.shape, F32)
    for k in range(2):
        for j in range(smalls.shape[1] - 8):
            to = k * hf + j * part
            fb[:, to : to + part] = smalls[2 * z + k, 8 + j : 9 + j, 0:part]
    for g in range(fs):
        a_pad[core, :, lanes * g : lanes * g + own_rows] = a_own[
            :, own_rows * g : own_rows * (g + 1)
        ]
        a_pad[core, :, lanes * g + own_rows : lanes * (g + 1)] = jnp.zeros(
            (rows, lanes - own_rows), BF
        )
    pjv[core, :, f] = p2[...]
    for copy in load_fc:
        copy.wait()
    met(peers)

    def swap(n, here, there):
        return remote(here, there, e_send.at[n], e_recv.at[n], core=1 - core)

    half_z = lambda h: pl.ds(*halves(nz)[h])
    p_gather = PlaneGather(plane, lambda g, h: pjv.at[core, half_z(h), g], (p3_send, p3_recv))
    p_gather.start()

    def p_pass(g):
        at = pjv.at[core, :, g]
        return remote(at, at, pc_send.at[g], pc_recv.at[g], core=1 - core)

    def p_came(g):
        at = pjv.at[1 - core, :, g]
        return remote(at, at, pc_send.at[g], pc_recv.at[g], core=1 - core)

    p_pass(f).start()

    fc_gather = PlaneGather(plane, lambda g, h: fc_at(g, core, h), (f_send, f_recv))
    fc_gather.start()

    def fc_pass(g):
        at = fcv.at[pl.ds(g * fc_rows, fc_rows), :, half_at(core)]
        return remote(at, at, fc_send.at[g], fc_recv.at[g], core=1 - core)

    def fc_came(g):
        at = fcv.at[pl.ds(g * fc_rows, fc_rows), :, half_at(1 - core)]
        return remote(at, at, fc_send.at[g], fc_recv.at[g], core=1 - core)

    fc_pass(f).start()

    c_line = Line(lambda b: ctb.at[b], nz, (c_right, c_left, c_recv))
    c_line.start()

    swap_a = swap(4, a_pad.at[core], a_pad.at[core])
    swap_a.start()
    load_out.wait()
    branch = dot_nt(a_pad[core], ov[...].reshape(d, fs * lanes))
    middle[...] = tok[...].astype(F32) + branch + vec[0:1, :]

    def norm_chunk(i, _):
        at = pl.ds(pl.multiple_of(i * step, step), step)
        xhat, _ = norm_rows(middle[at, :])
        h2b[core, z, at, :] = (xhat * vec[1:2, :] + vec[2:3, :]).astype(BF)
        return 0

    lax.fori_loop(0, rows // step, norm_chunk, 0)
    h_line = Line(lambda b: h2b.at[core, b], nz, (h_right, h_left, h_recv))
    h_line.start()
    p_gather.mid()
    c_line.step(1)
    h_line.step(1)
    fc_gather.mid()
    for s in range(2, nz - 1):
        c_line.step(s)
        h_line.step(s)
    p_gather.end()
    for g in plane.peers:
        p_pass(g).start()
    fc_gather.end()
    for g in plane.peers:
        fc_pass(g).start()
    for g in range(fs):
        p_came(g).wait_recv()
    for g in range(fs):
        fc_came(g).wait_recv()

    chunk = 256 if ff % 256 == 0 else 128
    some = nz // 2
    wide = some * rows
    sums[4:5, :] = jnp.zeros((1, sums.shape[1]), F32)

    def feed(first, i):
        at = pl.ds(pl.multiple_of(i * chunk, chunk), chunk)
        blocks = pl.ds(first, some)
        w = fcv[:, :, at].reshape(d, chunk)
        before = dot(h2b[core, blocks].reshape(wide, d), w) + fb[:, at]
        act, slope = gelu_pair(before)
        actb[core, blocks, :, at] = act.astype(BF).reshape(some, rows, chunk)
        w = pjv[:, :, :, :, :, at].reshape(2 * he, chunk)
        back = dot(ctb[blocks].reshape(wide, 2 * he), w)
        low = (back * slope).astype(BF)
        dbo[blocks, :, at] = low.reshape(some, rows, chunk)
        sums[4:5, at] += jnp.sum(low.astype(F32), axis=0, keepdims=True)

    def feed_half(first):
        def one(i, _):
            feed(first, i)
            return 0

        lax.fori_loop(0, ff // chunk, one, 0)

    near = z // some * some
    feed_half(near)
    c_line.step(nz - 1)
    h_line.step(nz - 1)
    swap_ct = swap(0, ctb.at[:, :, e_at(1 - core)], cto)
    swap_h2 = swap(1, h2b.at[core], h2b.at[core])
    swap_h2.start()
    swap_ct.start()
    feed_half(some - near)
    swap_act = swap(2, actb.at[core], actb.at[core])
    swap_db = swap(3, dbo.at[:, :, half_at(1 - core)], dbp)
    swap_act.start()
    swap_db.start()

    r_line = LineSum(dh, r_in, nz, (r_send, r_recv))

    def hidden_back(i, _):
        block = r_line.order(i)
        part_sum = dot_nt(dbo[block], fcv[...].reshape(d, ff))
        dh[block] = part_sum.astype(BF)

        @pl.when(block == z)
        def _():
            own_dh[...] = part_sum

        r_line.ready(block)
        return 0

    lax.fori_loop(0, nz, hidden_back, 0)

    def output_part(k, i):
        w = pjv[k, i].reshape(slot, ff)
        part = dot_nt(actb[core].reshape(tall, ff), w)
        low = k * he + i * slot
        ctb[:, :, low : low + slot] = part.astype(BF).reshape(nz, rows, slot)

    swap_ct.wait_recv()
    swap_act.wait_recv()
    pieces = 2 if hf % 256 == 0 or ff % 512 else 4
    for low in range(0, ff, ff // pieces):
        cols = slice(low, low + ff // pieces)
        pg[:, :, :, :, cols] = (
            (
                dot_tn(
                    ctb[:, :, e_at(core)].reshape(tall, he),
                    actb[core, :, :, cols].reshape(tall, ff // pieces),
                )
                + dot_tn(
                    cto[...].reshape(tall, he),
                    actb[1 - core, :, :, cols].reshape(tall, ff // pieces),
                )
            )
            .astype(BF)
            .reshape(nz, fs, share, grain, ff // pieces)
        )
    p_total = PlaneSum(
        plane,
        lambda g, h: pg.at[half_z(h), g],
        lambda n, h: pr.at[n, pl.ds(0, halves(nz)[h][1])],
        (g_send, g_recv),
    )
    p_total.start()
    c_line.finish()
    swap_ct.wait_send()
    keep_out = pltpu.make_async_copy(ctb, out_part, local.at[6])
    for s in range(1, nz - 1):
        r_line.step(s)
        if s == 1:
            for k in range(2):
                for i in range(nz):
                    output_part(k, i)
            keep_out.start()
    swap_h2.wait_recv()
    swap_db.wait_recv()
    own_db = dbo[:, :, half_at(core)].reshape(tall, hf)
    other_db = dbp[...].reshape(tall, hf)
    cut = 512
    for low in range(0, d, cut):
        high = min(d, low + cut)
        fc_grad[low:high, :] = (
            dot_tn(h2b[core, :, :, low:high].reshape(tall, high - low), own_db)
            + dot_tn(h2b[1 - core, :, :, low:high].reshape(tall, high - low), other_db)
        ).astype(BF)
    p_total.mid()
    r_line.finish()

    sums[0:4, :] = jnp.zeros((4, sums.shape[1]), F32)
    dsp[core] = jnp.zeros(dsp.shape[1:], BF)

    def norm_back_chunk(i, _):
        at = pl.ds(pl.multiple_of(i * step, step), step)
        g = own_dh[at, :] + r_line.others(at)
        xhat, rstd = norm_rows(middle[at, :])
        dm = ct[at, :].astype(F32) + norm_back(g, xhat, rstd, vec[1:2, :])
        low = dm.astype(BF)
        d_middle[at, :] = dm
        for c in range(cs):
            to = (c % 2) * he + (c // 2) * slot
            dsp[core, at, to : to + part] = low[:, c * part : (c + 1) * part]
        sums[0:1, 0:d] += jnp.sum(low.astype(F32), axis=0, keepdims=True)
        sums[1:2, 0:d] += jnp.sum(g * xhat, axis=0, keepdims=True)
        sums[2:3, 0:d] += jnp.sum(g, axis=0, keepdims=True)
        sums[3:4, 0:d] += jnp.sum(ct[at, :].astype(F32), axis=0, keepdims=True)
        return 0

    lax.fori_loop(0, rows // step, norm_back_chunk, 0)
    swap_d = swap(5, dsp.at[core], dsp.at[core])
    swap_d.start()
    back = dot(d_middle[...].astype(BF), ov[...].reshape(d, fs * lanes)).astype(BF)
    for g in range(fs):
        da[:, own_rows * g : own_rows * (g + 1)] = back[:, lanes * g : lanes * g + own_rows]
    if d < cs * width:
        da[:, d:] = jnp.zeros((rows, cs * width - d), BF)

    def d_copy(i):
        r = ranks[i]
        here = da.at[:, pl.ds(pl.multiple_of(r * width, 128), width)]
        there = d_att.at[pl.ds(pl.multiple_of(rank * rows, rows), rows)]
        return remote(here, there, d_send.at[i], d_recv.at[rank], z=r // 2, core=lax.rem(r, 2))

    for i in range(cs - 1):
        d_copy(i).start()
    d_att[pl.ds(pl.multiple_of(rank * rows, rows), rows), :] = da[
        :, pl.ds(pl.multiple_of(rank * width, 128), width)
    ]

    swap_a.wait_recv()
    swap_d.wait_recv()

    def stage_out(g):
        at = pl.ds(g * lanes, lanes)
        return pltpu.make_async_copy(stage.at[g % 2], og.at[:, :, :, at], local.at[4 + g % 2])

    for g in range(fs):
        at = slice(g * lanes, (g + 1) * lanes)
        part_sum = dot_tn(
            dsp[:, :, e_at(core)].reshape(2 * rows, he), a_pad[:, :, at].reshape(2 * rows, lanes)
        )
        part_sum = part_sum.astype(BF).reshape(nz, slot // grain, grain, lanes)
        if g >= 2:
            stage_out(g - 2).wait()
        stage[g % 2] = part_sum[:, : og.shape[1]]
        stage_out(g).start()
    for g in range(max(fs - 2, 0), fs):
        stage_out(g).wait()

    p_total.end()
    for h in range(2):
        p_sum[half_z(h)] = p_total.total(h).astype(BF)
    for i in range(1, cs):
        back = lax.rem(rank + cs - i, cs)
        to = d_att.at[pl.ds(pl.multiple_of(back * rows, rows), rows)]
        remote(to, to, d_send.at[0], d_recv.at[back], z=z).wait_recv()

    for i in range(cs - 1):
        d_copy(i).wait_send()
    for g in range(fs):
        fc_pass(g).wait_send()
        p_pass(g).wait_send()
    fc_gather.sent()
    p_gather.sent()
    p_total.sent()
    keep_out.wait()
    h_line.finish()
    r_line.sent()
    for s in (swap_h2, swap_act, swap_db, swap_a, swap_d):
        s.wait_send()


def middle_part(cfg, a_own, tok, ct, smalls, p2, o_all, fc):
    fs, nz, d, heads = cfg
    cs = 2 * nz
    rows, width = tok.shape[0], heads * HD
    length = rows * cs
    lanes = o_all.shape[3] // fs
    share, grain = p2.shape[1], p2.shape[2]
    he, hf = nz * fs * share * grain, fc.shape[2]
    return pl.pallas_call(
        partial(middle_kernel, cfg),
        out_shape=(
            shape((rows, d), F32),
            shape((rows, d), F32),
            shape((length, width)),
            shape((nz, rows, 2 * he)),
            shape((d, hf)),
            shape((nz, share, grain, 2 * hf)),
            shape((nz,) + o_all.shape[1:]),
            shape((5, max(2 * hf, d)), F32),
        ),
        in_specs=[VMEM] * 5 + [HBM] * 2,
        out_specs=(VMEM, VMEM, VMEM, HBM, VMEM, VMEM, HBM, VMEM),
        scratch_shapes=[
            pltpu.VMEM((3, d), F32),
            pltpu.VMEM((1, 2 * hf), F32),
            pltpu.VMEM((2, rows, fs * lanes), BF),
            pltpu.VMEM(o_all.shape, BF),
            pltpu.VMEM((fs * fc.shape[0], fc.shape[1], 2 * hf), BF),
            pltpu.VMEM((2, nz, fs, share, grain, 2 * hf), BF),
            pltpu.VMEM((nz, rows, 2 * he), BF),
            pltpu.VMEM((nz, rows, he), BF),
            pltpu.VMEM((2, nz, rows, d), BF),
            pltpu.VMEM((2, nz, rows, 2 * hf), BF),
            pltpu.VMEM((nz, rows, 2 * hf), BF),
            pltpu.VMEM((nz, rows, hf), BF),
            pltpu.VMEM((nz, rows, d), BF),
            pltpu.VMEM((nz + 1, rows, d), BF),
            pltpu.VMEM((rows, d), F32),
            pltpu.VMEM((rows, cs * width), BF),
            pltpu.VMEM((2, rows, 2 * he), BF),
            pltpu.VMEM((nz, fs, share, grain, 2 * hf), BF),
            pltpu.VMEM((2 * (fs - 1), nz - nz // 2, share, grain, 2 * hf), BF),
            pltpu.VMEM((2, nz) + o_all.shape[1:3] + (lanes,), BF),
        ]
        + sems(7, 2 * fs, (fs, 2), fs, fs, 2 * fs, (fs, 2), fs, fs)
        + sems(nz, nz, nz, nz, nz, nz, 6, 6, nz, nz + 1, cs, cs, 2 * fs, 2 * fs),
        name="middle",
        compiler_params=pltpu.CompilerParams(
            collective_id=1, has_side_effects=True, vmem_limit_bytes=62 * 2**20
        ),
    )(a_own, tok, ct, smalls, p2, o_all, fc)


def last_kernel(
    cfg,
    qkv,
    att,
    lse,
    d_att,
    block_order,
    w,
    h1,
    tok,
    smalls,
    sums,
    out_part,
    p_sum,
    og,
    fg,
    out_rows,
    in_rows,
    q_grad,
    p_grad,
    o_grad,
    f_grad,
    small_grad,
    pos_col,
    pos_row,
    vec,
    p_all,
    q_own,
    fgv,
    fr,
    d_qkv,
    acc,
    h1v,
    qg,
    qr,
    qs,
    om,
    orc,
    osum,
    o_in,
    op,
    ro_in,
    pz,
    other,
    partner,
    own,
    r_out,
    r_in,
    line,
    sm_out,
    sm_in,
    sm_f,
    z_send,
    z_recv,
    l_send,
    l_recv,
    local,
    q_send,
    q_recv,
    o_send,
    o_recv,
    os_send,
    os_recv,
    ro_send,
    ro_recv,
    f_send,
    f_recv,
    m_send,
    m_recv,
    r_send,
    r_recv,
    b_send,
    b_recv,
    s_send,
    s_recv,
    g_send,
    g_recv,
):
    fs, nz, d, heads = cfg
    cs = 2 * nz
    f, z, core = lax.axis_index("fsdp"), lax.axis_index("z"), lax.axis_index("core")
    rank = 2 * z + core
    rows = tok.shape[0]
    width = heads * HD
    lanes = w.shape[2] // fs
    grain = w.shape[1]
    own_rows, part = d // fs, d // cs
    hf = p_sum.shape[3] // 2
    he = out_part.shape[2] // 2
    slot = he // nz
    plane = Plane(fs)
    ranks = [lax.rem(rank + i, cs) for i in range(1, cs)]
    lanes_of = lambda g: pl.ds(pl.multiple_of(g * lanes, 128), lanes)
    runs = column_segments(cs, d, width, grain)
    block_rows = lambda b: pl.ds(pl.multiple_of(b * rows, rows), rows)
    half_z = lambda h: pl.ds(*halves(nz)[h])

    peers = [dict(z=r // 2, core=lax.rem(r, 2)) for r in ranks]
    peers += [dict(fsdp=p) for p in plane.peers]
    greet(peers)

    def h1_in(i):
        here = h1.at[:, lanes_of(lax.rem(f + 1 + i, fs))]
        return pltpu.make_async_copy(here, h1v.at[i % 2], local.at[4 + i % 2])

    for i in range(min(2, fs)):
        h1_in(i).start()
    om_in = pltpu.make_async_copy(og, om, local.at[2])
    op_in = pltpu.make_async_copy(out_part, op, local.at[3])
    om_in.start()
    op_in.start()
    fg_in = pltpu.make_async_copy(fg, fgv, local.at[6])
    fg_in.start()
    for r in range(cs):
        vec[:, r * part : (r + 1) * part] = smalls[r, 0:1, 0:part]
    run = cs * rows // block_order.shape[0]
    for b in range(block_order.shape[0]):
        first = block_order[b] * run
        at = slice(b * run, (b + 1) * run)
        pos_row[:, at] = first + lax.broadcasted_iota(jnp.int32, (1, run), 1)
        pos_col[at, :] = first + lax.broadcasted_iota(jnp.int32, (run, 1), 0)
    met(peers)

    om_in.wait()
    o_total = PlaneSum(
        plane,
        lambda g, h: om.at[half_z(h), :, :, lanes_of(g)],
        lambda n, h: orc.at[n, pl.ds(0, halves(nz)[h][1])],
        (o_send, o_recv),
    )
    o_total.start()

    def z_copy(i):
        to = lax.rem(z + i, nz)
        return remote(p_sum.at[to], pz.at[z], z_send.at[to], z_recv.at[z], z=to)

    z_keep = pltpu.make_async_copy(p_sum.at[z], pz.at[z], local.at[0])
    for i in range(1, nz):
        z_copy(i).start()
    z_keep.start()

    op_in.wait()
    ro_line = LineSum(op, ro_in, nz, (ro_send, ro_recv))
    ro_line.first()

    def l_copy(i):
        g = plane.peers[i]
        return remote(pz.at[g], p_all.at[f], l_send.at[i], l_recv.at[f], fsdp=g)

    l_keep = pltpu.make_async_copy(pz.at[f], p_all.at[f], local.at[1])

    def shares_on():
        z_keep.wait()
        for i in range(1, nz):
            back = lax.rem(z + nz - i, nz)
            remote(pz.at[back], pz.at[back], z_send.at[0], z_recv.at[back], z=back).wait_recv()
        for i in range(fs - 1):
            l_copy(i).start()
        l_keep.start()

    tall = query_block(cs * rows)
    for h in range(heads):
        attend_back_head(
            h, width, tall, qkv, pos_col, pos_row, att, lse, d_att, d_qkv, acc
        )
        if h == heads - 1:
            shares_on()
            ro_line.step(1)

    slices = 3 * width // grain
    q_total = PlaneSum(
        plane,
        lambda g, h: qg.at[g, pl.ds(*halves(slices)[h])],
        lambda n, h: qr.at[n, pl.ds(0, halves(slices)[h][1])],
        (q_send, q_recv),
    )

    for i in range(fs):
        g = lax.rem(f + 1 + i, fs)
        h1_in(i).wait()
        part_sum = dot_tn(d_qkv[...], h1v[i % 2])
        qg[g] = part_sum.astype(BF).reshape(slices, grain, lanes)
        if i + 2 < fs:
            h1_in(i + 2).start()
    q_total.start()
    fg_in.wait()
    f_rows = f_grad.shape[0]
    f_total = PlaneSum(
        plane,
        lambda g, h: fgv.at[pl.ds(g * f_rows + halves(f_rows)[h][0], halves(f_rows)[h][1])],
        lambda n, h: fr.at[n, pl.ds(0, halves(f_rows)[h][1])],
        (f_send, f_recv),
    )

    def hidden(block):
        full = dot(d_qkv[block_rows(block), :], w[...].reshape(3 * width, fs * lanes))
        return [full[:, lanes * g : lanes * g + own_rows] for g in range(fs)]

    def other_step(b, _):
        for g, piece in enumerate(hidden(2 * b + 1 - core)):
            other[b, :, own_rows * g : own_rows * (g + 1)] = piece.astype(BF)
        return 0

    lax.fori_loop(0, nz, other_step, 0)
    to_partner = remote(other, partner, m_send.at[0], m_recv.at[0], core=1 - core)
    to_partner.start()
    o_total.mid()

    to_partner.wait_recv()

    r_line = LineSum(r_out, r_in, nz, (r_send, r_recv))

    def own_step(i, _):
        b = r_line.order(i)
        for g, piece in enumerate(hidden(2 * b + core)):
            at = slice(own_rows * g, own_rows * (g + 1))
            both = piece + partner[b, :, at].astype(F32)
            r_out[b, :, at] = both.astype(BF)

            @pl.when(b == z)
            def _():
                own[:, at] = both

        r_line.ready(b)
        return 0

    lax.fori_loop(0, nz, own_step, 0)
    for s in range(2, nz - 1):
        ro_line.step(s)
    q_total.mid()
    r_line.step(1)
    step = min(32, rows)
    o_total.end()
    for h in range(2):
        osum[half_z(h)] = o_total.total(h).astype(BF)
    o_line = LineSum(osum, o_in, nz, (os_send, os_recv))
    for s in range(2, nz - 1):
        r_line.step(s)
    o_line.first()

    q_total.end()
    for h in range(2):
        qs[pl.ds(*halves(slices)[h])] = q_total.total(h).astype(BF)

    def run_copy(n):
        dst, at, src, first, count = runs[n]
        here, there = qs.at[pl.ds(first, count)], q_own.at[pl.ds(at, count)]
        if src == dst:
            return pltpu.make_async_copy(here, there, b_send.at[n])
        return remote(here, there, b_send.at[n], b_recv.at[n], z=dst // 2, core=dst % 2)

    for n, run in enumerate(runs):

        @pl.when(rank == run[2])
        def _():
            run_copy(n).start()

    f_total.start()

    ro_line.finish()

    def output_chunk(i, _):
        at = pl.ds(pl.multiple_of(i * step, step), step)
        total = op[z, at, :].astype(F32) + ro_line.others(at)
        for c in range(cs):
            low = (c % 2) * he + (c // 2) * slot
            out_rows[at, c * part : (c + 1) * part] = total[:, low : low + part]
        return 0

    lax.fori_loop(0, rows // step, output_chunk, 0)
    o_line.step(1)

    l_keep.wait()
    for g in plane.peers:
        remote(p_all.at[g], p_all.at[g], l_send.at[0], l_recv.at[g], fsdp=g).wait_recv()
    fine = p_all.shape[2]
    whole = p_all[...].reshape(-1, fine, 2 * hf)[: part // fine].reshape(part, 2 * hf)
    ff_half = p_grad.shape[0] // 2
    for k in range(2):
        p_grad[k * ff_half : (k + 1) * ff_half, :] = whole[:, k * hf : k * hf + ff_half].T
    for s in range(2, nz - 1):
        o_line.step(s)
    r_line.finish()

    line[...] = jnp.zeros(line.shape, F32)

    def norm_back_chunk(i, _):
        at = pl.ds(pl.multiple_of(i * step, step), step)
        g = own[at, :] + r_line.others(at)
        xhat, rstd = norm_rows(tok[at, :].astype(F32))
        in_rows[at, :] = norm_back(g, xhat, rstd, vec[...])
        line[0:1, 0:d] += jnp.sum(g * xhat, axis=0, keepdims=True)
        line[1:2, 0:d] += jnp.sum(g, axis=0, keepdims=True)
        return 0

    lax.fori_loop(0, rows // step, norm_back_chunk, 0)

    head_lanes = pl.ds(pl.multiple_of(rank * width, 128), width)
    line[2:3, head_lanes] = jnp.sum(d_qkv[:, 0:width].astype(F32), axis=0, keepdims=True)
    line[3:4, head_lanes] = jnp.sum(d_qkv[:, 2 * width :].astype(F32), axis=0, keepdims=True)
    line[4:8, 0:d] = sums[0:4, 0:d]
    sm_out[...] = jnp.zeros(sm_out.shape, F32)
    ff_parts = small_grad.shape[0] - 8
    for r in range(cs):
        sm_out[r, 0:8, 0:part] = line[0:8, r * part : (r + 1) * part]
    for k in range(2):
        for j in range(ff_parts):
            sm_out[2 * z + k, 8 + j : 9 + j, 0:part] = sums[
                4:5, k * hf + j * part : k * hf + (j + 1) * part
            ]

    def s_copy(i):
        r = ranks[i]
        here = sm_out.at[r]
        return remote(
            here, sm_in.at[rank], s_send.at[i], s_recv.at[rank], z=r // 2, core=lax.rem(r, 2)
        )

    for i in range(cs - 1):
        s_copy(i).start()
    f_total.mid()
    o_line.finish()
    whole = (osum[z].astype(F32) + o_line.others()).astype(BF)
    o_grad[...] = whole.reshape(part, lanes)[:, :own_rows].T
    total = sm_out[rank]
    for i in range(1, cs):
        back = lax.rem(rank + cs - i, cs)
        remote(sm_in.at[back], sm_in.at[back], s_send.at[0], s_recv.at[back], z=z).wait_recv()
        total += sm_in[back]
    sm_f[f] = total

    def g_copy(i):
        return remote(sm_f.at[f], sm_f.at[f], g_send.at[i], g_recv.at[f], fsdp=plane.peers[i])

    for i in range(fs - 1):
        g_copy(i).start()
    for n, run in enumerate(runs):

        @pl.when(rank == run[0])
        def _():
            if run[0] == run[2]:
                run_copy(n).wait()
            else:
                run_copy(n).wait_recv()

    q_grad[...] = q_own[...].reshape(-1, lanes)[:, :own_rows].T
    f_total.end()
    for h in range(2):
        f_grad[pl.ds(*halves(f_rows)[h])] = f_total.total(h).astype(BF)
    for g in plane.peers:
        remote(sm_f.at[g], sm_f.at[g], g_send.at[0], g_recv.at[g], fsdp=g).wait_recv()
    total = sm_f[0]
    for g in range(1, fs):
        total += sm_f[g]
    small_grad[...] = total

    for i in range(1, nz):
        z_copy(i).wait_send()
    for i in range(fs - 1):
        l_copy(i).wait_send()
        g_copy(i).wait_send()
    for s in (r_line, o_line, ro_line, o_total, q_total, f_total):
        s.sent()
    to_partner.wait_send()
    for n, run in enumerate(runs):
        if run[0] != run[2]:

            @pl.when(rank == run[2])
            def _():
                run_copy(n).wait_send()

    for i in range(cs - 1):
        s_copy(i).wait_send()


def last_part(cfg, counts, qkv, att, lse, d_att, block_order, w, h1, tok, smalls, sums, out_part, p_sum, og, fg):
    fs, nz, d, heads = cfg
    cs = 2 * nz
    rows, length, width = tok.shape[0], qkv.shape[0], heads * HD
    grain, lanes = w.shape[1], w.shape[2] // fs
    q_grains, fc_cols = counts
    small_rows = smalls.shape[1]
    f_rows = fg.shape[0] // fs
    slices = 3 * width // grain
    runs = len(column_segments(cs, d, width, grain))
    part = d // cs
    rest = 2 * (fs - 1)
    rows_low = pltpu.VMEM((nz, rows, d), BF)
    smem = pl.BlockSpec(memory_space=pltpu.SMEM)
    owner = (nz,) + og.shape[1:3] + (lanes,)
    return pl.pallas_call(
        partial(last_kernel, cfg),
        out_shape=(
            shape((rows, d), F32),
            shape((rows, d), F32),
            shape((d // fs, q_grains * grain)),
            shape((2 * fc_cols, part)),
            shape((d // fs, part)),
            shape((f_rows,) + fg.shape[1:]),
            shape((small_rows, up(part)), F32),
        ),
        in_specs=[VMEM] * 4 + [smem, VMEM, HBM] + [VMEM] * 3 + [HBM, VMEM, HBM, HBM],
        out_specs=(VMEM,) * 7,
        scratch_shapes=[
            pltpu.VMEM((length, 1), jnp.int32),
            pltpu.VMEM((1, length), jnp.int32),
            pltpu.VMEM((1, d), F32),
            pltpu.VMEM((fs,) + p_sum.shape[1:], BF),
            pltpu.VMEM((q_grains, grain, lanes), BF),
            pltpu.VMEM(fg.shape, BF),
            pltpu.VMEM((rest, f_rows - f_rows // 2) + fg.shape[1:], BF),
            pltpu.VMEM((length, 3 * width), BF),
            pltpu.VMEM((length, 2 * HD), F32),
            pltpu.VMEM((2, length, lanes), BF),
            pltpu.VMEM((fs, slices, grain, lanes), BF),
            pltpu.VMEM((rest, slices - slices // 2, grain, lanes), BF),
            pltpu.VMEM((slices, grain, lanes), BF),
            pltpu.VMEM(og.shape, BF),
            pltpu.VMEM((rest, nz - nz // 2) + owner[1:], BF),
            pltpu.VMEM(owner, BF),
            pltpu.VMEM((nz + 1,) + owner[1:], BF),
            pltpu.VMEM(out_part.shape, BF),
            pltpu.VMEM((nz + 1,) + out_part.shape[1:], BF),
            pltpu.VMEM(p_sum.shape, BF),
            rows_low,
            rows_low,
            pltpu.VMEM((rows, d), F32),
            rows_low,
            pltpu.VMEM((nz + 1, rows, d), BF),
            pltpu.VMEM((8, width * cs), F32),
            pltpu.VMEM((cs, small_rows, up(part)), F32),
            pltpu.VMEM((cs, small_rows, up(part)), F32),
            pltpu.VMEM((fs, small_rows, up(part)), F32),
        ]
        + sems(nz, nz, fs, fs, 7, rest + 2, rest + 2, rest + 2, rest + 2, nz, nz + 1)
        + sems(nz, nz + 1)
        + sems(rest + 2, rest + 2, 1, 1, nz, nz + 1, runs, runs, cs, cs, fs, fs),
        name="last",
        compiler_params=pltpu.CompilerParams(
            collective_id=2, has_side_effects=True, vmem_limit_bytes=62 * 2**20
        ),
    )(
        qkv,
        att,
        lse,
        d_att,
        block_order,
        w,
        h1,
        tok,
        smalls,
        sums,
        out_part,
        p_sum,
        og,
        fg,
    )


def body(
    tokens,
    block_order,
    cotangent,
    pre_attn_gain,
    pre_attn_bias,
    qkv_weight,
    query_bias,
    value_bias,
    out_weight,
    out_bias,
    pre_mlp_gain,
    pre_mlp_bias,
    fc_weight,
    fc_bias,
    proj_weight,
    proj_bias,
):
    fs, nz = lax.axis_size("fsdp"), lax.axis_size("z")
    cs = nz * 2
    rows, d = tokens.shape[1], tokens.shape[2]
    length = rows * cs
    heads_all = d // HD
    heads = -(-heads_all // cs)
    width = heads * HD
    part, own_rows = d // cs, d // fs
    fc_cols = fc_weight.shape[1]
    hf = up(fc_cols)

    rows_of = lambda v: jnp.pad(
        v.astype(F32).reshape(-1, part), ((0, 0), (0, up(part) - part))
    )
    small = jnp.concatenate(
        [
            rows_of(v)
            for v in (
                pre_attn_gain,
                pre_attn_bias,
                query_bias,
                value_bias,
                out_bias,
                pre_mlp_gain,
                pre_mlp_bias,
                proj_bias,
                fc_bias,
            )
        ]
    )
    fc = jnp.pad(fc_weight, ((0, 0), (0, hf - fc_cols)))
    fc = fc.reshape(-1, math.gcd(own_rows, 16), hf)
    cfg = (fs, nz, d, heads)
    h1, w, qkv, att, lse, smalls, p2, o_all, a_own = start(
        cfg, tokens[0], qkv_weight, small, proj_weight, out_weight, block_order, hf
    )
    vec = lambda i: smalls[:, i, :part].reshape(d)
    middle, d_middle, d_att, out_part, fc_grad, p_sum, og, sums = middle_part(
        cfg, a_own, tokens[0], cotangent[0], smalls, p2, o_all, fc
    )
    fg = fc_grad.reshape(-1, fc.shape[1], hf)
    out_rows, in_rows, qkv_grad, proj_grad, out_grad, fc_grad, g = last_part(
        cfg,
        (qkv_weight.shape[1] // w.shape[1], fc_cols),
        qkv,
        att,
        lse,
        d_att,
        block_order,
        w,
        h1,
        tokens[0],
        smalls,
        sums,
        out_part,
        p_sum,
        og,
        fg,
    )
    output = (middle + out_rows + vec(7)).astype(BF)
    input_grad = d_middle + in_rows
    fc_grad = fc_grad.reshape(own_rows, hf)[:, :fc_cols]
    g = g[:, :part]
    return (
        output[None],
        input_grad[None],
        g[0],
        g[1],
        qkv_grad.astype(F32),
        g[2],
        g[3],
        out_grad.astype(F32),
        g[4],
        g[5],
        g[6],
        fc_grad.astype(F32),
        g[8:].reshape(-1),
        proj_grad.astype(F32),
        g[7],
    )


def solution(mesh):
    fs, cs = mesh.shape["fsdp"], mesh.shape["ctx"]
    split = Mesh(mesh.devices.reshape(fs, cs // 2, 2), ("fsdp", "z", "core"))
    rows = P("fsdp", CTX, None)
    weight = P("fsdp", CTX)
    vector = P(CTX)
    in_specs = (
        rows,
        P(),
        rows,
        vector,
        vector,
        weight,
        vector,
        vector,
        weight,
        vector,
        vector,
        vector,
        weight,
        vector,
        weight,
        vector,
    )
    out_specs = (
        rows,
        rows,
        vector,
        vector,
        weight,
        vector,
        vector,
        weight,
        vector,
        vector,
        vector,
        weight,
        vector,
        weight,
        vector,
    )
    return jax.shard_map(body, mesh=split, in_specs=in_specs, out_specs=out_specs, check_vma=False)
```

```python
from functools import partial
import math

import jax
import jax.numpy as jnp
from jax import lax
from jax.experimental import pallas as pl
from jax.experimental.pallas import tpu as pltpu
from jax.sharding import Mesh
from jax.sharding import PartitionSpec as P

HD = 64
EPS = 1e-05
FLOOR = -1e30
BF = jnp.bfloat16
F32 = jnp.float32
CTX = ("z", "core")
MESH = pl.DeviceIdType.MESH
VMEM = pl.BlockSpec(memory_space=pltpu.VMEM)
HBM = pl.BlockSpec(memory_space=pl.ANY)
GELU_A = math.sqrt(2.0 / math.pi)
GELU_B = 0.044715


def up(n):
    return -(-n // 128) * 128


def sems(*counts):
    return [pltpu.SemaphoreType.DMA(c if isinstance(c, tuple) else (c,)) for c in counts]


def shape(dims, kind=BF):
    return jax.ShapeDtypeStruct(dims, kind)


def dot(a, b):
    return jnp.dot(a, b, preferred_element_type=F32)


def dot_nt(a, b):
    return lax.dot_general(a, b, (((1,), (1,)), ((), ())), preferred_element_type=F32)


def dot_tn(a, b):
    return lax.dot_general(a, b, (((0,), (0,)), ((), ())), preferred_element_type=F32)


def norm_rows(rows):
    centred = rows - jnp.mean(rows, axis=-1, keepdims=True)
    rstd = lax.rsqrt(jnp.mean(centred * centred, axis=-1, keepdims=True) + EPS)
    return centred * rstd, rstd


def norm_back(upstream, xhat, rstd, gain):
    inner = upstream * gain
    return rstd * (
        inner
        - jnp.mean(inner, axis=-1, keepdims=True)
        - xhat * jnp.mean(inner * xhat, axis=-1, keepdims=True)
    )


def gelu_pair(v):
    sq = v * v
    t = jnp.tanh(GELU_A * v * (1.0 + GELU_B * sq))
    half = 0.5 * (1.0 + t)
    slope = half + 0.5 * v * (1.0 - t * t) * (GELU_A * (1.0 + 3.0 * GELU_B * sq))
    return v * half, slope


def positions(order_table, rows):
    block = rows // order_table.shape[0]
    return (order_table[:, None] * block + jnp.arange(block, dtype=jnp.int32)[None]).reshape(rows)


def remote(src, dst, send, recv, **to):
    return pltpu.make_async_remote_copy(
        src_ref=src, dst_ref=dst, send_sem=send, recv_sem=recv, device_id=to, device_id_type=MESH
    )


def column_segments(ranks, d, width, grain):
    own = 3 * d // ranks
    runs = []
    for src in range(ranks):
        for part in range(3):
            for dst in range(ranks):
                low = part * d + dst * width
                first = max(src * own, low)
                last = min((src + 1) * own, low + width, (part + 1) * d)
                if first < last:
                    at = part * width + first - low
                    runs.append(
                        (src, (first - src * own) // grain, dst, at // grain, (last - first) // grain)
                    )
    return runs


def greet(peers):
    barrier = pltpu.get_barrier_semaphore()
    for peer in peers:
        pl.semaphore_signal(barrier, inc=1, device_id=peer, device_id_type=MESH)


def met(peers):
    pl.semaphore_wait(pltpu.get_barrier_semaphore(), len(peers))


class Line:
    def __init__(self, at, size, sems):
        self.at, self.size = at, size
        self.right, self.left, self.recv = sems
        self.z = lax.axis_index("z")

    def copy(self, block, way):
        send = (self.right if way > 0 else self.left).at[block]
        at = self.at(block)
        return remote(at, at, send, self.recv.at[block], z=self.z + way)

    def start(self):
        @pl.when(self.z < self.size - 1)
        def _():
            self.copy(self.z, 1).start()

        @pl.when(self.z > 0)
        def _():
            self.copy(self.z, -1).start()

    def step(self, s, then=None):
        @pl.when(self.z >= s)
        def _():
            block = self.z - s
            self.copy(block, 1).wait_recv()

            @pl.when(self.z < self.size - 1)
            def _():
                self.copy(block, 1).start()

            if then is not None:
                then(block)

        @pl.when(self.z + s < self.size)
        def _():
            block = self.z + s
            self.copy(block, -1).wait_recv()

            @pl.when(self.z > 0)
            def _():
                self.copy(block, -1).start()

            if then is not None:
                then(block)

    def finish(self):
        for s in range(self.size):

            @pl.when((self.z >= s) & (self.z < self.size - 1))
            def _():
                self.copy(self.z - s, 1).wait_send()

            @pl.when((self.z + s < self.size) & (self.z > 0))
            def _():
                self.copy(self.z + s, -1).wait_send()


class LineSum:
    def __init__(self, parts, came, size, sems):
        self.parts = parts if callable(parts) else (lambda block: parts.at[block])
        self.came, self.size = came, size
        self.send, self.recv = sems
        self.z = lax.axis_index("z")

    def copy(self, block, way):
        place = block + 1 if way > 0 else block
        there = self.came.at[place]
        return remote(
            self.parts(block), there, self.send.at[block], self.recv.at[place], z=self.z + way
        )

    def order(self, i):
        near = self.z < self.size // 2
        ahead = self.size - 1 - self.z
        from_low = jnp.where(i < ahead, self.size - 1 - i, i - ahead)
        from_high = jnp.where(i < self.z, i, self.size - 1 - (i - self.z))
        return jnp.where(near, from_low, from_high)

    def ready(self, block):
        @pl.when((self.z == 0) & (block > 0))
        def _():
            self.copy(block, 1).start()

        @pl.when((self.z == self.size - 1) & (block < self.size - 1))
        def _():
            self.copy(block, -1).start()

    def first(self, hops=None):
        for way, edge in ((1, 0), (-1, self.size - 1)):

            @pl.when(self.z == edge)
            def _():
                for hop in range(self.size - 1, 0, -1) if hops is None else hops:
                    self.copy(self.z + way * hop, way).start()

    def add_on(self, block, way):
        self.copy(block, way).wait_recv()
        came = self.came[block + 1 if way > 0 else block]
        part = self.parts(block)
        part[...] = (part[...].astype(F32) + came.astype(F32)).astype(part.dtype)
        self.copy(block, way).start()

    def step(self, s):
        right, left = self.z + self.size - 1 - s, s - (self.size - 1 - self.z)

        @pl.when((self.z > 0) & (right < self.size) & (right > self.z))
        def _():
            self.add_on(right, 1)

        @pl.when((self.z < self.size - 1) & (left >= 0) & (left < self.z))
        def _():
            self.add_on(left, -1)

    def finish(self):
        @pl.when(self.z > 0)
        def _():
            self.copy(self.z, 1).wait_recv()

        @pl.when(self.z == 0)
        def _():
            self.came[self.z + 1] = jnp.zeros(self.came.shape[1:], self.came.dtype)

        @pl.when(self.z < self.size - 1)
        def _():
            self.copy(self.z, -1).wait_recv()

        @pl.when(self.z == self.size - 1)
        def _():
            self.came[self.z] = jnp.zeros(self.came.shape[1:], self.came.dtype)

    def others(self, *at):
        here = (self.z,) + at
        there = (self.z + 1,) + at
        return self.came[here].astype(F32) + self.came[there].astype(F32)

    def sent(self):
        for block in range(self.size):

            @pl.when(self.z < block)
            def _():
                self.copy(block, 1).wait_send()

            @pl.when(self.z > block)
            def _():
                self.copy(block, -1).wait_send()


def halves(n):
    return ((0, n // 2), (n // 2, n - n // 2))


class Plane:
    def __init__(self, size):
        self.size, self.f = size, lax.axis_index("fsdp")
        self.square = size == 4
        f = self.f
        self.peers = [lax.rem(f + i, size) for i in range(1, size)]
        if self.square:
            self.x, self.y, self.far = f + 1 - 2 * lax.rem(f, 2), lax.rem(f + 2, 4), 3 - f
            self.peers = [self.x, self.y, self.far]


class PlaneGather:
    def __init__(self, plane, at, sems):
        self.p, self.at = plane, at
        self.send, self.recv = sems
        f = plane.f
        if plane.square:
            x, y = plane.x, plane.y
            self.early = [(f, 0, x), (f, 1, y), (f, 0, y), (f, 1, x)]
            self.late = [(x, 0, y), (y, 1, x)]
        else:
            self.early = [(f, h, g) for g in plane.peers for h in range(2)]
            self.late = []

    def copy(self, n, move):
        g, half, to = move
        at = self.at(g, half)
        return remote(at, at, self.send.at[n], self.recv.at[g, half], fsdp=to)

    def arrive(self, g, half):
        at = self.at(g, half)
        remote(at, at, self.send.at[0], self.recv.at[g, half], fsdp=g).wait_recv()

    def start(self):
        for n, move in enumerate(self.early):
            self.copy(n, move).start()

    def mid(self):
        for n, move in enumerate(self.late):
            self.arrive(move[0], move[1])
            self.copy(len(self.early) + n, move).start()

    def end(self):
        known = [(m[0], m[1]) for m in self.late]
        for g in self.p.peers:
            for half in range(2):
                if not any(g is a and half == b for a, b in known):
                    self.arrive(g, half)

    def sent(self):
        for n, move in enumerate(self.early + self.late):
            self.copy(n, move).wait_send()


class PlaneSum:
    def __init__(self, plane, at, came, sems):
        self.p, self.at, self.came = plane, at, came
        self.send, self.recv = sems
        if plane.square:
            x, y, far = plane.x, plane.y, plane.far
            self.early = [(far, 0, x, 0), (far, 1, y, 1), (x, 0, x, 2), (y, 1, y, 3)]
            self.late = [(y, 0, y, 4), (x, 1, x, 5)]
            self.mine = [[2, 4], [3, 5]]
        else:
            n = plane.size
            self.early = [
                (g, h, g, 2 * i + h) for i, g in enumerate(plane.peers) for h in range(2)
            ]
            self.late = []
            self.mine = [[2 * i + h for i in range(n - 1)] for h in range(2)]

    def copy(self, move):
        g, half, to, slot = move
        return remote(
            self.at(g, half), self.came(slot, half), self.send.at[slot], self.recv.at[slot], fsdp=to
        )

    def arrive(self, slot, half):
        there = self.came(slot, half)
        remote(
            there, there, self.send.at[slot], self.recv.at[slot], fsdp=self.p.peers[0]
        ).wait_recv()

    def start(self):
        for move in self.early:
            self.copy(move).start()

    def mid(self):
        for slot, move in enumerate(self.late):
            self.arrive(slot, move[1])
            at, came = self.at(move[0], move[1]), self.came(slot, move[1])
            at[...] = (at[...].astype(F32) + came[...].astype(F32)).astype(at.dtype)
            self.copy(move).start()

    def end(self):
        for half in range(2):
            for slot in self.mine[half]:
                self.arrive(slot, half)

    def total(self, half):
        out = self.at(self.p.f, half)[...].astype(F32)
        for slot in self.mine[half]:
            out += self.came(slot, half)[...].astype(F32)
        return out

    def sent(self):
        for move in self.early + self.late:
            self.copy(move).wait_send()


def query_block(length):
    return max(128, min(256, length, 256 * 1024 // length))


def attend_head(h, width, q_block, qkv, pos_col, pos_row, out, lse):
    rows = qkv.shape[0]
    k = qkv[:, width + h * HD : width + (h + 1) * HD]
    v = qkv[:, 2 * width + h * HD : 2 * width + (h + 1) * HD]
    for b in range(rows // q_block):
        at = slice(b * q_block, (b + 1) * q_block)
        q = qkv[at, h * HD : (h + 1) * HD] * BF(HD**-0.5)
        s = dot_nt(k, q)
        s = jnp.where(pos_col[...] <= pos_row[:, at], s, FLOOR)
        top = jnp.max(s, axis=0, keepdims=True)
        p = jnp.exp(s - top)
        total = jnp.sum(p, axis=0, keepdims=True)
        o = dot_tn(v, p.astype(BF)) * (1.0 / total)
        out[at, h * HD : (h + 1) * HD] = o.T.astype(BF)
        lse[h : h + 1, at] = top + jnp.log(total)


def attend_back_head(h, width, q_block, qkv, pos_col, pos_row, out, lse, dout, dqkv, acc):
    rows = qkv.shape[0]
    k = qkv[:, width + h * HD : width + (h + 1) * HD]
    v = qkv[:, 2 * width + h * HD : 2 * width + (h + 1) * HD]
    for b in range(rows // q_block):
        at = slice(b * q_block, (b + 1) * q_block)
        q = qkv[at, h * HD : (h + 1) * HD] * BF(HD**-0.5)
        do = dout[at, h * HD : (h + 1) * HD]
        o = out[at, h * HD : (h + 1) * HD]
        delta = jnp.sum(do.astype(F32).T * o.astype(F32).T, axis=0, keepdims=True)
        s = dot_nt(k, q)
        p = jnp.where(pos_col[...] <= pos_row[:, at], jnp.exp(s - lse[h : h + 1, at]), 0.0)
        dp = dot_nt(v, do)
        ds = (p * (dp - delta)).astype(BF)
        dq = dot_tn(k, ds) * (HD**-0.5)
        dqkv[at, h * HD : (h + 1) * HD] = dq.T.astype(BF)
        dk = dot(ds, q)
        dv = dot(p.astype(BF), do)
        if b == 0:
            acc[:, :HD] = dk
            acc[:, HD:] = dv
        else:
            acc[:, :HD] += dk
            acc[:, HD:] += dv
    dqkv[:, width + h * HD : width + (h + 1) * HD] = acc[:, :HD].astype(BF)
    dqkv[:, 2 * width + h * HD : 2 * width + (h + 1) * HD] = acc[:, HD:].astype(BF)


def start_kernel(
    cfg,
    tok_cols,
    qkv_own,
    proj_cols,
    out_own,
    block_order,
    gain_one,
    shift_one,
    query_shift,
    value_shift,
    out_shift,
    gain_two,
    shift_two,
    proj_shift,
    fc_shift,
    h1_out,
    w_out,
    qkv,
    att,
    lse,
    smalls,
    p2,
    o_all,
    a_own,
    tok,
    h1,
    w,
    wq,
    pj,
    ot,
    pos_col,
    pos_row,
    toks,
    vecs,
    small,
    p1,
    small_send,
    small_recv,
    q_send,
    q_recv,
    q_local,
    x_send,
    x_recv,
    t_right,
    t_left,
    t_recv,
    c_send,
    c_recv,
    p1_send,
    p1_recv,
    p2_send,
    p2_recv,
    p_local,
    a_send,
    a_recv,
    o_right,
    o_left,
    o_recv,
    ox_send,
    ox_recv,
    oc_send,
    oc_recv,
):
    fs, nz, d, heads = cfg
    cs = 2 * nz
    f, z, core = lax.axis_index("fsdp"), lax.axis_index("z"), lax.axis_index("core")
    rank = 2 * z + core
    rows, lanes = tok_cols.shape[1], wq.shape[2]
    width = heads * HD
    grain = wq.shape[1]
    own_rows = d // fs
    part = d // cs
    lanes_of = lambda g: pl.ds(pl.multiple_of(g * lanes, 128), lanes)
    runs = column_segments(cs, d, width, grain)
    plane = Plane(fs)
    planes = plane.peers

    w[:, :, lanes_of(f)] = jnp.zeros((w.shape[0], grain, lanes), BF)
    ranks = [lax.rem(rank + i, cs) for i in range(1, cs)]
    peers = [dict(z=r // 2, core=lax.rem(r, 2)) for r in ranks] + [dict(fsdp=p) for p in planes]
    greet(peers)

    fine = ot.shape[1]
    if lanes > own_rows:
        wq[:, :, own_rows:] = jnp.zeros((wq.shape[0], grain, lanes - own_rows), BF)
        ot[:, :, own_rows:] = jnp.zeros((ot.shape[0], fine, lanes - own_rows), BF)
    wq[:, :, 0:own_rows] = qkv_own[...].T.reshape(wq.shape[0], grain, own_rows)
    ot[:, :, 0:own_rows] = out_own[...].T.reshape(ot.shape[0], fine, own_rows)
    pj[...] = jnp.zeros(pj.shape, BF)
    ff_half, hf = proj_cols.shape[1] // 2, pj.shape[2] // 2
    for k in range(2):
        pj[0 : part // fine, :, k * hf : k * hf + ff_half] = proj_cols[
            :, k * ff_half : (k + 1) * ff_half
        ].reshape(part // fine, fine, ff_half)
    tok[...] = tok_cols[...].T
    toks[rank] = tok[...]
    small[...] = jnp.zeros(small.shape, F32)
    for n, v in enumerate(
        (
            gain_one,
            shift_one,
            query_shift,
            value_shift,
            out_shift,
            gain_two,
            shift_two,
            proj_shift,
        )
    ):
        small[n : n + 1, 0:part] = v[...].astype(F32).reshape(1, part)
    fc_line = fc_shift[...].astype(F32).reshape(1, fc_shift.shape[0])
    for j in range(small.shape[0] - 8):
        small[8 + j : 9 + j, 0:part] = fc_line[:, j * part : (j + 1) * part]
    met(peers)
    keep_out = pltpu.make_async_copy(ot, o_all.at[rank, :, :, lanes_of(f)], p_local.at[0])
    keep_out.start()

    def run_copy(n):
        src, first, dst, at, count = runs[n]
        here, there = wq.at[pl.ds(first, count)], w.at[pl.ds(at, count), :, lanes_of(f)]
        if src == dst:
            return pltpu.make_async_copy(here, there, q_local.at[n])
        return remote(here, there, q_send.at[n], q_recv.at[n], z=dst // 2, core=dst % 2)

    for n, run in enumerate(runs):

        @pl.when(rank == run[0])
        def _():
            run_copy(n).start()

    def small_copy(i):
        r = ranks[i]
        to = smalls.at[rank]
        return remote(small, to, small_send.at[i], small_recv.at[rank], z=r // 2, core=lax.rem(r, 2))

    for i in range(cs - 1):
        small_copy(i).start()

    share = p1.shape[1]

    def p1_copy(i):
        here = pj.at[pl.ds(planes[i] * share, share)]
        return remote(here, p1.at[f], p1_send.at[i], p1_recv.at[f], fsdp=planes[i])

    p1[f] = pj[pl.ds(f * share, share)]
    for i in range(fs - 1):
        p1_copy(i).start()

    def ox_copy(i, block, here=None):
        at = o_all.at[2 * block + core, :, :, lanes_of(f)]
        here = at if here is None else here
        return remote(here, at, ox_send.at[i, block], ox_recv.at[f, block], fsdp=planes[i])

    def ox_arrival(g, block):
        at = o_all.at[2 * block + core, :, :, lanes_of(g)]
        return remote(at, at, ox_send.at[0, block], ox_recv.at[g, block], fsdp=g)

    def oc_copy(g, block, here=None):
        at = o_all.at[2 * block + core, :, :, lanes_of(g)]
        here = at if here is None else here
        return remote(here, at, oc_send.at[g, block], oc_recv.at[g, block], core=1 - core)

    def oc_arrival(g, block):
        at = o_all.at[2 * block + 1 - core, :, :, lanes_of(g)]
        return remote(at, at, oc_send.at[g, block], oc_recv.at[g, block], core=1 - core)

    def out_block(block, here=None):
        for i in range(fs - 1):
            ox_copy(i, block, here).start()
        oc_copy(f, block, here).start()

    out_block(z, ot)

    for n, run in enumerate(runs):

        @pl.when(rank == run[2])
        def _():
            if run[0] == run[2]:
                run_copy(n).wait()
            else:
                run_copy(n).wait_recv()

    gather = PlaneGather(
        plane, lambda g, h: w.at[pl.ds(*halves(w.shape[0])[h]), :, lanes_of(g)], (x_send, x_recv)
    )
    gather.start()

    line = Line(lambda b: toks.at[2 * b + core], nz, (t_right, t_left, t_recv))

    def pass_on(block):
        at = toks.at[2 * block + core]
        return remote(at, at, c_send.at[block], c_recv.at[block], core=1 - core)

    def arrival(block):
        at = toks.at[2 * block + 1 - core]
        return remote(at, at, c_send.at[block], c_recv.at[block], core=1 - core)

    line.start()
    pass_on(z).start()

    smalls[rank] = small[...]
    vecs[...] = jnp.zeros(vecs.shape, F32)
    length = cs * rows
    run = length // block_order.shape[0]
    for b in range(block_order.shape[0]):
        first = block_order[b] * run
        at = slice(b * run, (b + 1) * run)
        pos_row[:, at] = first + lax.broadcasted_iota(jnp.int32, (1, run), 1)
        pos_col[at, :] = first + lax.broadcasted_iota(jnp.int32, (run, 1), 0)
    if lanes > own_rows:
        for g in range(fs):
            h1[:, lanes * g + own_rows : lanes * (g + 1)] = jnp.zeros(
                (length, lanes - own_rows), BF
            )
    for i in range(1, cs):
        back = lax.rem(rank + cs - i, cs)
        remote(small, smalls.at[back], small_send.at[i - 1], small_recv.at[back], z=z).wait_recv()
    for r in range(cs):
        vecs[:, part * r : part * (r + 1)] = smalls[r, 0:8, 0:part]

    step = min(32, rows)

    def norm_block(block):
        def chunk(i, _):
            at = pl.multiple_of(i * step, step)
            xhat, _ = norm_rows(toks[block, pl.ds(at, step), :].astype(F32))
            h = (xhat * vecs[0:1, 0:d] + vecs[1:2, 0:d]).astype(BF)
            to = pl.ds(pl.multiple_of(block * rows + i * step, step), step)
            for g in range(fs):
                h1[to, lanes * g : lanes * g + own_rows] = h[:, own_rows * g : own_rows * (g + 1)]
            return 0

        lax.fori_loop(0, rows // step, chunk, 0)

    def place(i):
        hop = (i + 1) // 2
        return jnp.where(lax.rem(i, 2) == 1, z - hop, z + hop)

    def take(i, _):
        block = place(i)

        @pl.when((block >= 0) & (block < nz))
        def _():
            @pl.when(block < z)
            def _():
                line.copy(block, 1).wait_recv()

                @pl.when(z < nz - 1)
                def _():
                    line.copy(block, 1).start()

            @pl.when(block > z)
            def _():
                line.copy(block, -1).wait_recv()

                @pl.when(z > 0)
                def _():
                    line.copy(block, -1).start()

            @pl.when(block != z)
            def _():
                pass_on(block).start()

            norm_block(2 * block + core)
            arrival(block).wait_recv()
            norm_block(2 * block + 1 - core)

        return 0

    tall = 2 * rows
    head_lanes = pl.ds(pl.multiple_of(rank * width, 128), width)

    def project(i, _):
        block = place(i)

        @pl.when((block >= 0) & (block < nz))
        def _():
            at = pl.ds(pl.multiple_of(block * tall, tall), tall)
            full = dot_nt(h1[at, :], w[...].reshape(3 * width, fs * lanes))
            qkv[at, 0:width] = (full[:, 0:width] + vecs[2:3, head_lanes]).astype(BF)
            qkv[at, width : 2 * width] = full[:, width : 2 * width].astype(BF)
            qkv[at, 2 * width :] = (full[:, 2 * width :] + vecs[3:4, head_lanes]).astype(BF)

        return 0

    lax.fori_loop(0, 3, take, 0)
    gather.mid()
    lax.fori_loop(3, 2 * nz - 3, take, 0)

    keep_out.wait()
    out_line = Line(
        lambda b: o_all.at[2 * b + core, :, :, lanes_of(f)], nz, (o_right, o_left, o_recv)
    )
    out_line.start()
    gather.end()
    lax.fori_loop(0, 2 * nz - 3, project, 0)
    lax.fori_loop(2 * nz - 3, 2 * nz - 1, take, 0)
    lax.fori_loop(2 * nz - 3, 2 * nz - 1, project, 0)
    keep_h1 = pltpu.make_async_copy(h1, h1_out, p_local.at[1])
    keep_w = pltpu.make_async_copy(w, w_out, p_local.at[2])
    keep_h1.start()
    keep_w.start()
    out_line.step(1, out_block)

    for g in planes:
        remote(p1.at[g], p1.at[g], p1_send.at[0], p1_recv.at[g], fsdp=g).wait_recv()

    def p2_copy(i):
        to = lax.rem(z + i, nz)
        return remote(p1.at[to], p2.at[z], p2_send.at[to], p2_recv.at[z], z=to)

    def a_copy(i, pair):
        r = ranks[i]
        here = att.at[pl.ds(pl.multiple_of(r * rows, rows), rows), pl.ds(pair * 128, 128)]
        there = a_own.at[:, pl.ds(pl.multiple_of(rank * width + pair * 128, 128), 128)]
        return remote(
            here, there, a_send.at[i, pair], a_recv.at[rank, pair], z=r // 2, core=lax.rem(r, 2)
        )

    for h in range(heads):
        attend_head(h, width, query_block(cs * rows), qkv, pos_col, pos_row, att, lse)
        if h + 2 < nz:
            out_line.step(h + 2, out_block)
        if h % 2 == 1:
            for i in range(cs - 1):
                a_copy(i, h // 2).start()
        if h == 0:
            for i in range(1, nz):
                p2_copy(i).start()
            p2[z] = p1[z]
    for s in range(heads + 2, nz):
        out_line.step(s, out_block)
    a_own[:, head_lanes] = att[pl.ds(pl.multiple_of(rank * rows, rows), rows), :]

    for g in planes:
        for b in range(nz):
            ox_arrival(g, b).wait_recv()
            oc_copy(g, b).start()
    for pair in range(width // 128):
        for i in range(1, cs):
            back = lax.rem(rank + cs - i, cs)
            to = a_own.at[:, pl.ds(pl.multiple_of(back * width + pair * 128, 128), 128)]
            remote(to, to, a_send.at[0, 0], a_recv.at[back, pair], z=z).wait_recv()
    for i in range(1, nz):
        back = lax.rem(z + nz - i, nz)
        remote(p2.at[back], p2.at[back], p2_send.at[0], p2_recv.at[back], z=back).wait_recv()
    for g in range(fs):
        for b in range(nz):
            oc_arrival(g, b).wait_recv()
    keep_h1.wait()
    keep_w.wait()

    for n, run in enumerate(runs):
        if run[0] != run[2]:

            @pl.when(rank == run[0])
            def _():
                run_copy(n).wait_send()

    for i in range(cs - 1):
        small_copy(i).wait_send()
        for pair in range(width // 128):
            a_copy(i, pair).wait_send()
    gather.sent()
    for i in range(1, nz):
        p2_copy(i).wait_send()
    for i in range(fs - 1):
        p1_copy(i).wait_send()
        for b in range(nz):
            ox_copy(i, b).wait_send()
    for g in range(fs):
        for b in range(nz):
            oc_copy(g, b).wait_send()
    line.finish()
    out_line.finish()
    for b in range(nz):
        pass_on(b).wait_send()


def start(cfg, tok_cols, qkv_own, proj_cols, out_own, block_order, vectors, hf):
    fs, nz, d, heads = cfg
    cs = 2 * nz
    rows, cols = tok_cols.shape[1], qkv_own.shape[1]
    width, length = heads * HD, rows * cs
    part, lanes = d // cs, up(d // fs)
    grain, fine = math.gcd(math.gcd(cols, HD), 8), math.gcd(part, 8)
    share = -(-part // (fine * fs))
    runs = len(column_segments(cs, d, width, grain))
    pairs = width // 128
    small = (8 + vectors[8].shape[0] // part, up(part))
    smem = pl.BlockSpec(memory_space=pltpu.SMEM)
    h1 = (length, fs * lanes)
    w = (3 * width // grain, grain, fs * lanes)
    return pl.pallas_call(
        partial(start_kernel, cfg),
        out_shape=(
            shape(h1),
            shape(w),
            shape((length, 3 * width)),
            shape((length, width)),
            shape((heads, length), F32),
            shape((cs,) + small, F32),
            shape((nz, share, fine, 2 * hf)),
            shape((cs, part // fine, fine, fs * lanes)),
            shape((rows, cs * width)),
            shape((rows, d)),
        ),
        in_specs=[VMEM] * 4 + [smem] + [VMEM] * 9,
        out_specs=(HBM, HBM) + (VMEM,) * 5 + (HBM, VMEM, VMEM),
        scratch_shapes=[
            pltpu.VMEM(h1, BF),
            pltpu.VMEM(w, BF),
            pltpu.VMEM((cols // grain, grain, lanes), BF),
            pltpu.VMEM((fs * share, fine, 2 * hf), BF),
            pltpu.VMEM((part // fine, fine, lanes), BF),
            pltpu.VMEM((length, 1), jnp.int32),
            pltpu.VMEM((1, length), jnp.int32),
            pltpu.VMEM((cs, rows, d), BF),
            pltpu.VMEM((8, width * cs), F32),
            pltpu.VMEM(small, F32),
            pltpu.VMEM((fs, share, fine, 2 * hf), BF),
        ]
        + sems(cs, cs, runs, runs, runs, 2 * fs, (fs, 2), nz, nz, nz, nz, nz)
        + sems(fs, fs, nz, nz, 3, (cs, pairs), (cs, pairs))
        + sems(nz, nz, nz, (fs, nz), (fs, nz), (fs, nz), (fs, nz)),
        name="start",
        compiler_params=pltpu.CompilerParams(
            collective_id=0, has_side_effects=True, vmem_limit_bytes=60 * 2**20
        ),
    )(tok_cols, qkv_own, proj_cols, out_own, block_order, *vectors)


def middle_kernel(
    cfg,
    a_own,
    tok,
    ct_cols,
    smalls,
    p2,
    fc,
    o_all,
    middle,
    d_middle,
    d_att,
    out_part,
    fc_grad,
    p_sum,
    og,
    sums,
    vec,
    fb,
    ct,
    a_pad,
    ov,
    fcv,
    pjv,
    ctb,
    cto,
    h2b,
    actb,
    dbo,
    dbp,
    dh,
    r_in,
    own_dh,
    da,
    dsp,
    pg,
    pr,
    stage,
    local,
    p3_send,
    p3_recv,
    pc_send,
    pc_recv,
    f_send,
    f_recv,
    fc_send,
    fc_recv,
    c_right,
    c_left,
    c_recv,
    h_right,
    h_left,
    h_recv,
    e_send,
    e_recv,
    r_send,
    r_recv,
    d_send,
    d_recv,
    g_send,
    g_recv,
):
    fs, nz, d, heads = cfg
    cs = 2 * nz
    f, z, core = lax.axis_index("fsdp"), lax.axis_index("z"), lax.axis_index("core")
    rank = 2 * z + core
    rows = tok.shape[0]
    width = heads * HD
    lanes = o_all.shape[3] // fs
    own_rows, part = d // fs, d // cs
    share, grain = p2.shape[1], p2.shape[2]
    slot = fs * share * grain
    he, hf = nz * slot, pjv.shape[5] // 2
    ff = 2 * hf
    fc_grain, fc_cols = fcv.shape[1], fc.shape[1]
    fc_rows = fc.shape[0] // fc_grain
    tall = nz * rows
    step = min(32, rows)
    plane = Plane(fs)
    ranks = [lax.rem(rank + i, cs) for i in range(1, cs)]
    half_at = lambda k: pl.ds(pl.multiple_of(k * hf, 128), hf)
    e_at = lambda k: pl.ds(pl.multiple_of(k * he, 128), he)

    peers = [dict(z=r // 2, core=lax.rem(r, 2)) for r in ranks]
    peers += [dict(fsdp=p) for p in plane.peers]
    greet(peers)
    load_out = pltpu.make_async_copy(o_all, ov, local.at[0])
    fc_at = lambda g, k, h: fcv.at[
        pl.ds(g * fc_rows + halves(fc_rows)[h][0], halves(fc_rows)[h][1]), :, half_at(k)
    ]
    load_out.start()
    for k in range(2):

        @pl.when(core == k)
        def _():
            at = pl.ds(f * fc_rows, fc_rows)
            if hf > fc_cols:
                fcv[at, :, k * hf + fc_cols : (k + 1) * hf] = jnp.zeros(
                    (fc_rows, fc_grain, hf - fc_cols), BF
                )
            fcv[at, :, k * hf : k * hf + fc_cols] = fc[...].reshape(fc_rows, fc_grain, fc_cols)

    ct[...] = ct_cols[...].T
    ctb[z] = jnp.zeros(ctb.shape[1:], BF)
    for c in range(cs):
        to = (c % 2) * he + (c // 2) * slot
        ctb[z, :, to : to + part] = ct[:, c * part : (c + 1) * part]
    for r in range(cs):
        vec[:, r * part : (r + 1) * part] = smalls[r, 4:7, 0:part]
    fb[...] = jnp.zeros(fb.shape, F32)
    for k in range(2):
        for j in range(smalls.shape[1] - 8):
            to = k * hf + j * part
            fb[:, to : to + part] = smalls[2 * z + k, 8 + j : 9 + j, 0:part]
    for g in range(fs):
        a_pad[core, :, lanes * g : lanes * g + own_rows] = a_own[
            :, own_rows * g : own_rows * (g + 1)
        ]
        a_pad[core, :, lanes * g + own_rows : lanes * (g + 1)] = jnp.zeros(
            (rows, lanes - own_rows), BF
        )
    pjv[core, :, f] = p2[...]
    met(peers)

    def swap(n, here, there):
        return remote(here, there, e_send.at[n], e_recv.at[n], core=1 - core)

    half_z = lambda h: pl.ds(*halves(nz)[h])
    p_gather = PlaneGather(plane, lambda g, h: pjv.at[core, half_z(h), g], (p3_send, p3_recv))
    p_gather.start()

    def p_pass(g):
        at = pjv.at[core, :, g]
        return remote(at, at, pc_send.at[g], pc_recv.at[g], core=1 - core)

    def p_came(g):
        at = pjv.at[1 - core, :, g]
        return remote(at, at, pc_send.at[g], pc_recv.at[g], core=1 - core)

    p_pass(f).start()

    fc_gather = PlaneGather(plane, lambda g, h: fc_at(g, core, h), (f_send, f_recv))
    fc_gather.start()

    def fc_pass(g):
        at = fcv.at[pl.ds(g * fc_rows, fc_rows), :, half_at(core)]
        return remote(at, at, fc_send.at[g], fc_recv.at[g], core=1 - core)

    def fc_came(g):
        at = fcv.at[pl.ds(g * fc_rows, fc_rows), :, half_at(1 - core)]
        return remote(at, at, fc_send.at[g], fc_recv.at[g], core=1 - core)

    fc_pass(f).start()

    c_line = Line(lambda b: ctb.at[b], nz, (c_right, c_left, c_recv))
    c_line.start()

    swap_a = swap(4, a_pad.at[core], a_pad.at[core])
    swap_a.start()
    load_out.wait()
    branch = dot_nt(a_pad[core], ov[...].reshape(d, fs * lanes))
    middle[...] = tok[...].astype(F32) + branch + vec[0:1, :]

    def norm_chunk(i, _):
        at = pl.ds(pl.multiple_of(i * step, step), step)
        xhat, _ = norm_rows(middle[at, :])
        h2b[core, z, at, :] = (xhat * vec[1:2, :] + vec[2:3, :]).astype(BF)
        return 0

    lax.fori_loop(0, rows // step, norm_chunk, 0)
    h_line = Line(lambda b: h2b.at[core, b], nz, (h_right, h_left, h_recv))
    h_line.start()
    p_gather.mid()
    c_line.step(1)
    h_line.step(1)
    fc_gather.mid()
    for s in range(2, nz - 1):
        c_line.step(s)
        h_line.step(s)
    p_gather.end()
    for g in plane.peers:
        p_pass(g).start()
    fc_gather.end()
    for g in plane.peers:
        fc_pass(g).start()
    for g in range(fs):
        p_came(g).wait_recv()
    for g in range(fs):
        fc_came(g).wait_recv()

    chunk = 256 if ff % 256 == 0 else 128
    some = nz // 2
    wide = some * rows
    sums[4:5, :] = jnp.zeros((1, sums.shape[1]), F32)

    def feed(first, i):
        at = pl.ds(pl.multiple_of(i * chunk, chunk), chunk)
        blocks = pl.ds(first, some)
        w = fcv[:, :, at].reshape(d, chunk)
        before = dot(h2b[core, blocks].reshape(wide, d), w) + fb[:, at]
        act, slope = gelu_pair(before)
        actb[core, blocks, :, at] = act.astype(BF).reshape(some, rows, chunk)
        w = pjv[:, :, :, :, :, at].reshape(2 * he, chunk)
        back = dot(ctb[blocks].reshape(wide, 2 * he), w)
        low = (back * slope).astype(BF)
        dbo[blocks, :, at] = low.reshape(some, rows, chunk)
        sums[4:5, at] += jnp.sum(low.astype(F32), axis=0, keepdims=True)

    def feed_half(first):
        def one(i, _):
            feed(first, i)
            return 0

        lax.fori_loop(0, ff // chunk, one, 0)

    near = z // some * some
    feed_half(near)
    c_line.step(nz - 1)
    h_line.step(nz - 1)
    swap_ct = swap(0, ctb.at[:, :, e_at(1 - core)], cto)
    swap_h2 = swap(1, h2b.at[core], h2b.at[core])
    swap_h2.start()
    swap_ct.start()
    feed_half(some - near)
    swap_act = swap(2, actb.at[core], actb.at[core])
    swap_db = swap(3, dbo.at[:, :, half_at(1 - core)], dbp)
    swap_act.start()
    swap_db.start()

    r_line = LineSum(dh, r_in, nz, (r_send, r_recv))

    def hidden_back(i, _):
        block = r_line.order(i)
        part_sum = dot_nt(dbo[block], fcv[...].reshape(d, ff))
        dh[block] = part_sum.astype(BF)

        @pl.when(block == z)
        def _():
            own_dh[...] = part_sum

        r_line.ready(block)
        return 0

    lax.fori_loop(0, nz, hidden_back, 0)

    def output_part(k, i):
        w = pjv[k, i].reshape(slot, ff)
        part = dot_nt(actb[core].reshape(tall, ff), w)
        low = (2 * i + k) * (d // cs)
        ctb[:, :, low : low + d // cs] = part[:, : d // cs].astype(BF).reshape(nz, rows, d // cs)

    swap_ct.wait_recv()
    swap_act.wait_recv()
    pieces = 2 if hf % 256 == 0 or ff % 512 else 4
    for low in range(0, ff, ff // pieces):
        cols = slice(low, low + ff // pieces)
        pg[:, :, :, :, cols] = (
            (
                dot_tn(
                    ctb[:, :, e_at(core)].reshape(tall, he),
                    actb[core, :, :, cols].reshape(tall, ff // pieces),
                )
                + dot_tn(
                    cto[...].reshape(tall, he),
                    actb[1 - core, :, :, cols].reshape(tall, ff // pieces),
                )
            )
            .astype(BF)
            .reshape(nz, fs, share, grain, ff // pieces)
        )
    p_total = PlaneSum(
        plane,
        lambda g, h: pg.at[half_z(h), g],
        lambda n, h: pr.at[n, pl.ds(0, halves(nz)[h][1])],
        (g_send, g_recv),
    )
    p_total.start()
    c_line.finish()
    swap_ct.wait_send()
    keep_out = pltpu.make_async_copy(ctb.at[:, :, pl.ds(0, up(d))], out_part, local.at[6])
    for s in range(1, nz - 1):
        r_line.step(s)
        if s == 1:
            for k in range(2):
                for i in range(nz):
                    output_part(k, i)
            keep_out.start()
    swap_h2.wait_recv()
    swap_db.wait_recv()
    own_db = dbo[:, :, half_at(core)].reshape(tall, hf)
    other_db = dbp[...].reshape(tall, hf)
    cut = 512
    for low in range(0, d, cut):
        high = min(d, low + cut)
        fc_grad[low:high, :] = (
            dot_tn(h2b[core, :, :, low:high].reshape(tall, high - low), own_db)
            + dot_tn(h2b[1 - core, :, :, low:high].reshape(tall, high - low), other_db)
        ).astype(BF)
    p_total.mid()
    r_line.finish()

    sums[0:4, :] = jnp.zeros((4, sums.shape[1]), F32)
    dsp[core] = jnp.zeros(dsp.shape[1:], BF)

    def norm_back_chunk(i, _):
        at = pl.ds(pl.multiple_of(i * step, step), step)
        g = own_dh[at, :] + r_line.others(at)
        xhat, rstd = norm_rows(middle[at, :])
        dm = ct[at, :].astype(F32) + norm_back(g, xhat, rstd, vec[1:2, :])
        low = dm.astype(BF)
        d_middle[at, :] = dm
        for c in range(cs):
            to = (c % 2) * he + (c // 2) * slot
            dsp[core, at, to : to + part] = low[:, c * part : (c + 1) * part]
        sums[0:1, 0:d] += jnp.sum(low.astype(F32), axis=0, keepdims=True)
        sums[1:2, 0:d] += jnp.sum(g * xhat, axis=0, keepdims=True)
        sums[2:3, 0:d] += jnp.sum(g, axis=0, keepdims=True)
        sums[3:4, 0:d] += jnp.sum(ct[at, :].astype(F32), axis=0, keepdims=True)
        return 0

    lax.fori_loop(0, rows // step, norm_back_chunk, 0)
    swap_d = swap(5, dsp.at[core], dsp.at[core])
    swap_d.start()
    back = dot(d_middle[...].astype(BF), ov[...].reshape(d, fs * lanes)).astype(BF)
    for g in range(fs):
        da[:, own_rows * g : own_rows * (g + 1)] = back[:, lanes * g : lanes * g + own_rows]
    if d < cs * width:
        da[:, d:] = jnp.zeros((rows, cs * width - d), BF)

    def d_copy(i):
        r = ranks[i]
        here = da.at[:, pl.ds(pl.multiple_of(r * width, 128), width)]
        there = d_att.at[pl.ds(pl.multiple_of(rank * rows, rows), rows)]
        return remote(here, there, d_send.at[i], d_recv.at[rank], z=r // 2, core=lax.rem(r, 2))

    for i in range(cs - 1):
        d_copy(i).start()
    d_att[pl.ds(pl.multiple_of(rank * rows, rows), rows), :] = da[
        :, pl.ds(pl.multiple_of(rank * width, 128), width)
    ]

    swap_a.wait_recv()
    swap_d.wait_recv()

    def stage_out(g):
        at = pl.ds(g * lanes, lanes)
        return pltpu.make_async_copy(stage.at[g % 2], og.at[:, :, :, at], local.at[4 + g % 2])

    for g in range(fs):
        at = slice(g * lanes, (g + 1) * lanes)
        part_sum = dot_tn(
            dsp[:, :, e_at(core)].reshape(2 * rows, he), a_pad[:, :, at].reshape(2 * rows, lanes)
        )
        part_sum = part_sum.astype(BF).reshape(nz, slot // grain, grain, lanes)
        if g >= 2:
            stage_out(g - 2).wait()
        stage[g % 2] = part_sum[:, : og.shape[1]]
        stage_out(g).start()
    for g in range(max(fs - 2, 0), fs):
        stage_out(g).wait()

    p_total.end()
    for h in range(2):
        p_sum[half_z(h)] = p_total.total(h).astype(BF)
    for i in range(1, cs):
        back = lax.rem(rank + cs - i, cs)
        to = d_att.at[pl.ds(pl.multiple_of(back * rows, rows), rows)]
        remote(to, to, d_send.at[0], d_recv.at[back], z=z).wait_recv()

    for i in range(cs - 1):
        d_copy(i).wait_send()
    for g in range(fs):
        fc_pass(g).wait_send()
        p_pass(g).wait_send()
    fc_gather.sent()
    p_gather.sent()
    p_total.sent()
    keep_out.wait()
    h_line.finish()
    r_line.sent()
    for s in (swap_h2, swap_act, swap_db, swap_a, swap_d):
        s.wait_send()


def middle_part(cfg, a_own, tok, ct_cols, smalls, p2, fc, o_all):
    fs, nz, d, heads = cfg
    cs = 2 * nz
    rows, width = tok.shape[0], heads * HD
    length = rows * cs
    lanes = o_all.shape[3] // fs
    share, grain = p2.shape[1], p2.shape[2]
    he, hf = nz * fs * share * grain, p2.shape[3] // 2
    fc_grain = math.gcd(d // fs, 16)
    return pl.pallas_call(
        partial(middle_kernel, cfg),
        out_shape=(
            shape((rows, d), F32),
            shape((rows, d), F32),
            shape((length, width)),
            shape((nz, rows, up(d))),
            shape((d, hf)),
            shape((nz, share, grain, 2 * hf)),
            shape((nz,) + o_all.shape[1:]),
            shape((5, max(2 * hf, d)), F32),
        ),
        in_specs=[VMEM] * 6 + [HBM],
        out_specs=(VMEM, VMEM, VMEM, HBM, VMEM, VMEM, HBM, VMEM),
        scratch_shapes=[
            pltpu.VMEM((3, d), F32),
            pltpu.VMEM((1, 2 * hf), F32),
            pltpu.VMEM((rows, d), BF),
            pltpu.VMEM((2, rows, fs * lanes), BF),
            pltpu.VMEM(o_all.shape, BF),
            pltpu.VMEM((d // fc_grain, fc_grain, 2 * hf), BF),
            pltpu.VMEM((2, nz, fs, share, grain, 2 * hf), BF),
            pltpu.VMEM((nz, rows, 2 * he), BF),
            pltpu.VMEM((nz, rows, he), BF),
            pltpu.VMEM((2, nz, rows, d), BF),
            pltpu.VMEM((2, nz, rows, 2 * hf), BF),
            pltpu.VMEM((nz, rows, 2 * hf), BF),
            pltpu.VMEM((nz, rows, hf), BF),
            pltpu.VMEM((nz, rows, d), BF),
            pltpu.VMEM((nz + 1, rows, d), BF),
            pltpu.VMEM((rows, d), F32),
            pltpu.VMEM((rows, cs * width), BF),
            pltpu.VMEM((2, rows, 2 * he), BF),
            pltpu.VMEM((nz, fs, share, grain, 2 * hf), BF),
            pltpu.VMEM((2 * (fs - 1), nz - nz // 2, share, grain, 2 * hf), BF),
            pltpu.VMEM((2, nz) + o_all.shape[1:3] + (lanes,), BF),
        ]
        + sems(7, 2 * fs, (fs, 2), fs, fs, 2 * fs, (fs, 2), fs, fs)
        + sems(nz, nz, nz, nz, nz, nz, 6, 6, nz, nz + 1, cs, cs, 2 * fs, 2 * fs),
        name="middle",
        compiler_params=pltpu.CompilerParams(
            collective_id=1, has_side_effects=True, vmem_limit_bytes=62 * 2**20
        ),
    )(a_own, tok, ct_cols, smalls, p2, fc, o_all)


def last_kernel(
    cfg,
    qkv,
    att,
    lse,
    d_att,
    block_order,
    w_in,
    h1,
    tok,
    smalls,
    sums,
    middle_in,
    d_middle_in,
    out_part,
    p_sum,
    og,
    fg,
    output,
    input_grad,
    q_grad,
    p_grad,
    o_grad,
    f_grad,
    small_grad,
    w,
    middle,
    d_middle,
    out_rows,
    in_rows,
    pos_col,
    pos_row,
    vec,
    p_all,
    q_own,
    fgv,
    fr,
    d_qkv,
    acc,
    h1v,
    qg,
    qr,
    qs,
    om,
    orc,
    osum,
    o_in,
    op,
    ro_in,
    pz,
    other,
    partner,
    own,
    r_out,
    r_in,
    line,
    sm_out,
    sm_in,
    sm_f,
    z_send,
    z_recv,
    l_send,
    l_recv,
    local,
    q_send,
    q_recv,
    o_send,
    o_recv,
    os_send,
    os_recv,
    ro_send,
    ro_recv,
    f_send,
    f_recv,
    m_send,
    m_recv,
    r_send,
    r_recv,
    b_send,
    b_recv,
    s_send,
    s_recv,
    g_send,
    g_recv,
):
    fs, nz, d, heads = cfg
    cs = 2 * nz
    f, z, core = lax.axis_index("fsdp"), lax.axis_index("z"), lax.axis_index("core")
    rank = 2 * z + core
    rows = tok.shape[0]
    width = heads * HD
    lanes = w.shape[2] // fs
    grain = w.shape[1]
    own_rows, part = d // fs, d // cs
    hf = p_sum.shape[3] // 2
    plane = Plane(fs)
    ranks = [lax.rem(rank + i, cs) for i in range(1, cs)]
    lanes_of = lambda g: pl.ds(pl.multiple_of(g * lanes, 128), lanes)
    runs = column_segments(cs, d, width, grain)
    block_rows = lambda b: pl.ds(pl.multiple_of(b * rows, rows), rows)
    half_z = lambda h: pl.ds(*halves(nz)[h])

    peers = [dict(z=r // 2, core=lax.rem(r, 2)) for r in ranks]
    peers += [dict(fsdp=p) for p in plane.peers]
    greet(peers)

    def h1_in(i):
        here = h1.at[:, lanes_of(lax.rem(f + 1 + i, fs))]
        return pltpu.make_async_copy(here, h1v.at[i % 2], local.at[4 + i % 2])

    for i in range(min(2, fs)):
        h1_in(i).start()
    om_in = pltpu.make_async_copy(og, om, local.at[2])
    op_in = pltpu.make_async_copy(out_part, op, local.at[3])
    om_in.start()
    op_in.start()
    fg_in = pltpu.make_async_copy(fg, fgv, local.at[6])
    fg_in.start()
    late = [
        pltpu.make_async_copy(a, b, local.at[7 + n])
        for n, (a, b) in enumerate(((w_in, w), (middle_in, middle), (d_middle_in, d_middle)))
    ]
    for copy in late:
        copy.start()
    for r in range(cs):
        cols = slice(r * part, (r + 1) * part)
        vec[0:1, cols] = smalls[r, 0:1, 0:part]
        vec[1:2, cols] = smalls[r, 7:8, 0:part]
    run = cs * rows // block_order.shape[0]
    for b in range(block_order.shape[0]):
        first = block_order[b] * run
        at = slice(b * run, (b + 1) * run)
        pos_row[:, at] = first + lax.broadcasted_iota(jnp.int32, (1, run), 1)
        pos_col[at, :] = first + lax.broadcasted_iota(jnp.int32, (run, 1), 0)
    met(peers)

    om_in.wait()
    o_total = PlaneSum(
        plane,
        lambda g, h: om.at[half_z(h), :, :, lanes_of(g)],
        lambda n, h: orc.at[n, pl.ds(0, halves(nz)[h][1])],
        (o_send, o_recv),
    )
    o_total.start()

    def z_copy(i):
        to = lax.rem(z + i, nz)
        return remote(p_sum.at[to], pz.at[z], z_send.at[to], z_recv.at[z], z=to)

    z_keep = pltpu.make_async_copy(p_sum.at[z], pz.at[z], local.at[0])
    for i in range(1, nz):
        z_copy(i).start()
    z_keep.start()

    op_in.wait()
    ro_line = LineSum(op, ro_in, nz, (ro_send, ro_recv))
    ro_line.first()

    def l_copy(i):
        g = plane.peers[i]
        return remote(pz.at[g], p_all.at[f], l_send.at[i], l_recv.at[f], fsdp=g)

    l_keep = pltpu.make_async_copy(pz.at[f], p_all.at[f], local.at[1])

    def shares_on():
        z_keep.wait()
        for i in range(1, nz):
            back = lax.rem(z + nz - i, nz)
            remote(pz.at[back], pz.at[back], z_send.at[0], z_recv.at[back], z=back).wait_recv()
        for i in range(fs - 1):
            l_copy(i).start()
        l_keep.start()

    tall = query_block(cs * rows)
    for h in range(heads):
        attend_back_head(
            h, width, tall, qkv, pos_col, pos_row, att, lse, d_att, d_qkv, acc
        )
        if h == heads - 1:
            shares_on()
            ro_line.step(1)

    slices = 3 * width // grain
    q_total = PlaneSum(
        plane,
        lambda g, h: qg.at[g, pl.ds(*halves(slices)[h])],
        lambda n, h: qr.at[n, pl.ds(0, halves(slices)[h][1])],
        (q_send, q_recv),
    )

    for i in range(fs):
        g = lax.rem(f + 1 + i, fs)
        h1_in(i).wait()
        part_sum = dot_tn(d_qkv[...], h1v[i % 2])
        qg[g] = part_sum.astype(BF).reshape(slices, grain, lanes)
        if i + 2 < fs:
            h1_in(i + 2).start()
    q_total.start()
    fg_in.wait()
    f_rows = f_grad.shape[0] // fgv.shape[1]
    f_total = PlaneSum(
        plane,
        lambda g, h: fgv.at[pl.ds(g * f_rows + halves(f_rows)[h][0], halves(f_rows)[h][1])],
        lambda n, h: fr.at[n, pl.ds(0, halves(f_rows)[h][1])],
        (f_send, f_recv),
    )

    def hidden(block):
        full = dot(d_qkv[block_rows(block), :], w[...].reshape(3 * width, fs * lanes))
        return [full[:, lanes * g : lanes * g + own_rows] for g in range(fs)]

    def other_step(b, _):
        for g, piece in enumerate(hidden(2 * b + 1 - core)):
            other[b, :, own_rows * g : own_rows * (g + 1)] = piece.astype(BF)
        return 0

    for copy in late:
        copy.wait()
    lax.fori_loop(0, nz, other_step, 0)
    to_partner = remote(other, partner, m_send.at[0], m_recv.at[0], core=1 - core)
    to_partner.start()
    o_total.mid()

    to_partner.wait_recv()

    r_line = LineSum(r_out, r_in, nz, (r_send, r_recv))

    def own_step(i, _):
        b = r_line.order(i)
        for g, piece in enumerate(hidden(2 * b + core)):
            at = slice(own_rows * g, own_rows * (g + 1))
            both = piece + partner[b, :, at].astype(F32)
            r_out[b, :, at] = both.astype(BF)

            @pl.when(b == z)
            def _():
                own[:, at] = both

        r_line.ready(b)
        return 0

    lax.fori_loop(0, nz, own_step, 0)
    for s in range(2, nz - 1):
        ro_line.step(s)
    q_total.mid()
    r_line.step(1)
    step = min(32, rows)
    o_total.end()
    for h in range(2):
        osum[half_z(h)] = o_total.total(h).astype(BF)
    o_line = LineSum(osum, o_in, nz, (os_send, os_recv))
    for s in range(2, nz - 1):
        r_line.step(s)
    o_line.first()

    q_total.end()
    for h in range(2):
        qs[pl.ds(*halves(slices)[h])] = q_total.total(h).astype(BF)

    def run_copy(n):
        dst, at, src, first, count = runs[n]
        here, there = qs.at[pl.ds(first, count)], q_own.at[pl.ds(at, count)]
        if src == dst:
            return pltpu.make_async_copy(here, there, b_send.at[n])
        return remote(here, there, b_send.at[n], b_recv.at[n], z=dst // 2, core=dst % 2)

    for n, run in enumerate(runs):

        @pl.when(rank == run[2])
        def _():
            run_copy(n).start()

    f_total.start()

    ro_line.finish()

    def output_chunk(i, _):
        at = pl.ds(pl.multiple_of(i * step, step), step)
        total = op[z, at, :].astype(F32) + ro_line.others(at)
        out_rows[at, :] = middle[at, :] + total[:, 0:d] + vec[1:2, :]
        return 0

    lax.fori_loop(0, rows // step, output_chunk, 0)
    output[...] = out_rows[...].T.astype(BF)
    o_line.step(1)

    l_keep.wait()
    for g in plane.peers:
        remote(p_all.at[g], p_all.at[g], l_send.at[0], l_recv.at[g], fsdp=g).wait_recv()
    fine = p_all.shape[2]
    whole = p_all[...].reshape(-1, fine, 2 * hf)[: part // fine].reshape(part, 2 * hf)
    ff_half = p_grad.shape[1] // 2
    for k in range(2):
        p_grad[:, k * ff_half : (k + 1) * ff_half] = whole[:, k * hf : k * hf + ff_half].astype(F32)
    for s in range(2, nz - 1):
        o_line.step(s)
    r_line.finish()

    line[...] = jnp.zeros(line.shape, F32)

    def norm_back_chunk(i, _):
        at = pl.ds(pl.multiple_of(i * step, step), step)
        g = own[at, :] + r_line.others(at)
        xhat, rstd = norm_rows(tok[at, :].astype(F32))
        in_rows[at, :] = d_middle[at, :] + norm_back(g, xhat, rstd, vec[0:1, :])
        line[0:1, 0:d] += jnp.sum(g * xhat, axis=0, keepdims=True)
        line[1:2, 0:d] += jnp.sum(g, axis=0, keepdims=True)
        return 0

    lax.fori_loop(0, rows // step, norm_back_chunk, 0)

    input_grad[...] = in_rows[...].T

    head_lanes = pl.ds(pl.multiple_of(rank * width, 128), width)
    line[2:3, head_lanes] = jnp.sum(d_qkv[:, 0:width].astype(F32), axis=0, keepdims=True)
    line[3:4, head_lanes] = jnp.sum(d_qkv[:, 2 * width :].astype(F32), axis=0, keepdims=True)
    line[4:8, 0:d] = sums[0:4, 0:d]
    sm_out[...] = jnp.zeros(sm_out.shape, F32)
    ff_parts = small_grad.shape[0] - 8
    for r in range(cs):
        sm_out[r, 0:8, 0:part] = line[0:8, r * part : (r + 1) * part]
    for k in range(2):
        for j in range(ff_parts):
            sm_out[2 * z + k, 8 + j : 9 + j, 0:part] = sums[
                4:5, k * hf + j * part : k * hf + (j + 1) * part
            ]

    def s_copy(i):
        r = ranks[i]
        here = sm_out.at[r]
        return remote(
            here, sm_in.at[rank], s_send.at[i], s_recv.at[rank], z=r // 2, core=lax.rem(r, 2)
        )

    for i in range(cs - 1):
        s_copy(i).start()
    f_total.mid()
    o_line.finish()
    whole = (osum[z].astype(F32) + o_line.others()).reshape(part, lanes)
    o_grad[...] = whole[:, :own_rows].T
    total = sm_out[rank]
    for i in range(1, cs):
        back = lax.rem(rank + cs - i, cs)
        remote(sm_in.at[back], sm_in.at[back], s_send.at[0], s_recv.at[back], z=z).wait_recv()
        total += sm_in[back]
    sm_f[f] = total

    def g_copy(i):
        return remote(sm_f.at[f], sm_f.at[f], g_send.at[i], g_recv.at[f], fsdp=plane.peers[i])

    for i in range(fs - 1):
        g_copy(i).start()
    for n, run in enumerate(runs):

        @pl.when(rank == run[0])
        def _():
            if run[0] == run[2]:
                run_copy(n).wait()
            else:
                run_copy(n).wait_recv()

    q_grad[...] = q_own[...].reshape(-1, lanes)[:, :own_rows].T.astype(F32)
    f_total.end()
    for h in range(2):
        low, count = (n * fgv.shape[1] for n in halves(f_rows)[h])
        whole = f_total.total(h).reshape(count, fgv.shape[2])
        f_grad[low : low + count, :] = whole[:, : f_grad.shape[1]]
    for g in plane.peers:
        remote(sm_f.at[g], sm_f.at[g], g_send.at[0], g_recv.at[g], fsdp=g).wait_recv()
    total = sm_f[0]
    for g in range(1, fs):
        total += sm_f[g]
    small_grad[...] = total

    for i in range(1, nz):
        z_copy(i).wait_send()
    for i in range(fs - 1):
        l_copy(i).wait_send()
        g_copy(i).wait_send()
    for s in (r_line, o_line, ro_line, o_total, q_total, f_total):
        s.sent()
    to_partner.wait_send()
    for n, run in enumerate(runs):
        if run[0] != run[2]:

            @pl.when(rank == run[2])
            def _():
                run_copy(n).wait_send()

    for i in range(cs - 1):
        s_copy(i).wait_send()


def last_part(cfg, counts, qkv, att, lse, d_att, block_order, w, h1, tok, smalls, sums, middle, d_middle, out_part, p_sum, og, fg):
    fs, nz, d, heads = cfg
    cs = 2 * nz
    rows, length, width = tok.shape[0], qkv.shape[0], heads * HD
    grain, lanes = w.shape[1], w.shape[2] // fs
    q_grains, fc_cols = counts
    small_rows = smalls.shape[1]
    f_rows = fg.shape[0] // fs
    slices = 3 * width // grain
    runs = len(column_segments(cs, d, width, grain))
    part = d // cs
    rest = 2 * (fs - 1)
    rows_low = pltpu.VMEM((nz, rows, d), BF)
    smem = pl.BlockSpec(memory_space=pltpu.SMEM)
    owner = (nz,) + og.shape[1:3] + (lanes,)
    return pl.pallas_call(
        partial(last_kernel, cfg),
        out_shape=(
            shape((d, rows)),
            shape((d, rows), F32),
            shape((d // fs, q_grains * grain), F32),
            shape((part, 2 * fc_cols), F32),
            shape((d // fs, part), F32),
            shape((d // fs, fc_cols), F32),
            shape((small_rows, up(part)), F32),
        ),
        in_specs=[VMEM] * 4 + [smem, HBM, HBM] + [VMEM] * 3 + [HBM] * 2 + [HBM, VMEM, HBM, HBM],
        out_specs=(VMEM,) * 7,
        scratch_shapes=[
            pltpu.VMEM(w.shape, BF),
            pltpu.VMEM((rows, d), F32),
            pltpu.VMEM((rows, d), F32),
            pltpu.VMEM((rows, d), F32),
            pltpu.VMEM((rows, d), F32),
            pltpu.VMEM((length, 1), jnp.int32),
            pltpu.VMEM((1, length), jnp.int32),
            pltpu.VMEM((2, d), F32),
            pltpu.VMEM((fs,) + p_sum.shape[1:], BF),
            pltpu.VMEM((q_grains, grain, lanes), BF),
            pltpu.VMEM(fg.shape, BF),
            pltpu.VMEM((rest, f_rows - f_rows // 2) + fg.shape[1:], BF),
            pltpu.VMEM((length, 3 * width), BF),
            pltpu.VMEM((length, 2 * HD), F32),
            pltpu.VMEM((2, length, lanes), BF),
            pltpu.VMEM((fs, slices, grain, lanes), BF),
            pltpu.VMEM((rest, slices - slices // 2, grain, lanes), BF),
            pltpu.VMEM((slices, grain, lanes), BF),
            pltpu.VMEM(og.shape, BF),
            pltpu.VMEM((rest, nz - nz // 2) + owner[1:], BF),
            pltpu.VMEM(owner, BF),
            pltpu.VMEM((nz + 1,) + owner[1:], BF),
            pltpu.VMEM(out_part.shape, BF),
            pltpu.VMEM((nz + 1,) + out_part.shape[1:], BF),
            pltpu.VMEM(p_sum.shape, BF),
            rows_low,
            rows_low,
            pltpu.VMEM((rows, d), F32),
            rows_low,
            pltpu.VMEM((nz + 1, rows, d), BF),
            pltpu.VMEM((8, width * cs), F32),
            pltpu.VMEM((cs, small_rows, up(part)), F32),
            pltpu.VMEM((cs, small_rows, up(part)), F32),
            pltpu.VMEM((fs, small_rows, up(part)), F32),
        ]
        + sems(nz, nz, fs, fs, 10, rest + 2, rest + 2, rest + 2, rest + 2, nz, nz + 1)
        + sems(nz, nz + 1)
        + sems(rest + 2, rest + 2, 1, 1, nz, nz + 1, runs, runs, cs, cs, fs, fs),
        name="last",
        compiler_params=pltpu.CompilerParams(
            collective_id=2, has_side_effects=True, vmem_limit_bytes=62 * 2**20
        ),
    )(
        qkv,
        att,
        lse,
        d_att,
        block_order,
        w,
        h1,
        tok,
        smalls,
        sums,
        middle,
        d_middle,
        out_part,
        p_sum,
        og,
        fg,
    )


def finish_kernel(*refs):
    vectors, refs = refs[0], refs[1:]
    big = 6
    ins, outs, smalls = refs[:big], refs[big : 2 * big], refs[2 * big : 2 * big + 9]
    held, line, came, left = refs[2 * big + 9 : 3 * big + 9], refs[-3], refs[-2], refs[-1]
    reads = [pltpu.make_async_copy(ins[n], held[n], came.at[n]) for n in range(big)]
    writes = [pltpu.make_async_copy(held[n], outs[n], left.at[n]) for n in range(big)]
    for read in reads:
        read.start()
    part = smalls[0].shape[0]
    for n in range(8):
        smalls[n][...] = vectors[n : n + 1, 0:part].reshape(part)
    for n in range(vectors.shape[0] - 8):
        line[:, n * part : (n + 1) * part] = vectors[8 + n : 9 + n, 0:part]
    smalls[8][...] = line[...].reshape(line.shape[1])
    for read, write in zip(reads, writes):
        read.wait()
        write.start()
    for write in writes:
        write.wait()


def finish(vectors, part, arrays):
    kinds = [shape(a.shape, a.dtype) for a in arrays]
    long = (vectors.shape[0] - 8) * part
    smalls = [shape((part,), F32)] * 8 + [shape((long,), F32)]
    return pl.pallas_call(
        finish_kernel,
        out_shape=kinds + smalls,
        in_specs=[VMEM] + [HBM] * len(arrays),
        out_specs=[HBM] * len(arrays) + [VMEM] * 9,
        scratch_shapes=[pltpu.VMEM(a.shape, a.dtype) for a in arrays]
        + [pltpu.VMEM((1, long), F32)]
        + sems(len(arrays), len(arrays)),
        name="finish",
        compiler_params=pltpu.CompilerParams(vmem_limit_bytes=62 * 2**20),
    )(vectors, *arrays)


def body(
    tokens,
    block_order,
    cotangent,
    pre_attn_gain,
    pre_attn_bias,
    qkv_weight,
    query_bias,
    value_bias,
    out_weight,
    out_bias,
    pre_mlp_gain,
    pre_mlp_bias,
    fc_weight,
    fc_bias,
    proj_weight,
    proj_bias,
):
    fs, nz = lax.axis_size("fsdp"), lax.axis_size("z")
    cs = nz * 2
    rows, d = tokens.shape[1], tokens.shape[2]
    length = rows * cs
    heads_all = d // HD
    heads = -(-heads_all // cs)
    width = heads * HD
    part, own_rows = d // cs, d // fs
    fc_cols = fc_weight.shape[1]
    hf = up(fc_cols)

    cfg = (fs, nz, d, heads)
    h1, w, qkv, att, lse, smalls, p2, o_all, a_own, tok = start(
        cfg,
        tokens[0].T,
        qkv_weight,
        proj_weight.T,
        out_weight,
        block_order,
        (
            pre_attn_gain,
            pre_attn_bias,
            query_bias,
            value_bias,
            out_bias,
            pre_mlp_gain,
            pre_mlp_bias,
            proj_bias,
            fc_bias,
        ),
        hf,
    )
    middle, d_middle, d_att, out_part, fc_grad, p_sum, og, sums = middle_part(
        cfg, a_own, tok, cotangent[0].T, smalls, p2, fc_weight, o_all
    )
    fg = fc_grad.reshape(-1, math.gcd(own_rows, 16), hf)
    output, input_grad, qkv_grad, proj_grad, out_grad, fc_grad, g = last_part(
        cfg,
        (qkv_weight.shape[1] // w.shape[1], fc_cols),
        qkv,
        att,
        lse,
        d_att,
        block_order,
        w,
        h1,
        tok,
        smalls,
        sums,
        middle,
        d_middle,
        out_part,
        p_sum,
        og,
        fg,
    )
    output, input_grad, qkv_grad, proj_grad, out_grad, fc_grad, *g = finish(
        g, part, (output, input_grad, qkv_grad, proj_grad, out_grad, fc_grad)
    )
    return (
        output.T[None],
        input_grad.T[None],
        g[0],
        g[1],
        qkv_grad,
        g[2],
        g[3],
        out_grad,
        g[4],
        g[5],
        g[6],
        fc_grad,
        g[8],
        proj_grad.T,
        g[7],
    )


def solution(mesh):
    fs, cs = mesh.shape["fsdp"], mesh.shape["ctx"]
    split = Mesh(mesh.devices.reshape(fs, cs // 2, 2), ("fsdp", "z", "core"))
    rows = P("fsdp", CTX, None)
    weight = P("fsdp", CTX)
    vector = P(CTX)
    in_specs = (
        rows,
        P(),
        rows,
        vector,
        vector,
        weight,
        vector,
        vector,
        weight,
        vector,
        vector,
        vector,
        weight,
        vector,
        weight,
        vector,
    )
    out_specs = (
        rows,
        rows,
        vector,
        vector,
        weight,
        vector,
        vector,
        weight,
        vector,
        vector,
        vector,
        weight,
        vector,
        weight,
        vector,
    )
    return jax.shard_map(body, mesh=split, in_specs=in_specs, out_specs=out_specs, check_vma=False)
```

```python
from functools import partial
import math

import jax
import jax.numpy as jnp
from jax import lax
from jax.experimental import pallas as pl
from jax.experimental.pallas import tpu as pltpu
from jax.sharding import Mesh
from jax.sharding import PartitionSpec as P

HD = 64
EPS = 1e-05
FLOOR = -1e30
BF = jnp.bfloat16
F32 = jnp.float32
CTX = ("z", "core")
MESH = pl.DeviceIdType.MESH
VMEM = pl.BlockSpec(memory_space=pltpu.VMEM)
HBM = pl.BlockSpec(memory_space=pl.ANY)
GELU_A = math.sqrt(2.0 / math.pi)
GELU_B = 0.044715


def up(n):
    return -(-n // 128) * 128


def sems(*counts):
    return [pltpu.SemaphoreType.DMA(c if isinstance(c, tuple) else (c,)) for c in counts]


def shape(dims, kind=BF):
    return jax.ShapeDtypeStruct(dims, kind)


def dot(a, b):
    return jnp.dot(a, b, preferred_element_type=F32)


def dot_nt(a, b):
    return lax.dot_general(a, b, (((1,), (1,)), ((), ())), preferred_element_type=F32)


def dot_tn(a, b):
    return lax.dot_general(a, b, (((0,), (0,)), ((), ())), preferred_element_type=F32)


def norm_rows(rows):
    centred = rows - jnp.mean(rows, axis=-1, keepdims=True)
    rstd = lax.rsqrt(jnp.mean(centred * centred, axis=-1, keepdims=True) + EPS)
    return centred * rstd, rstd


def norm_back(upstream, xhat, rstd, gain):
    inner = upstream * gain
    return rstd * (
        inner
        - jnp.mean(inner, axis=-1, keepdims=True)
        - xhat * jnp.mean(inner * xhat, axis=-1, keepdims=True)
    )


def gelu_pair(v):
    sq = v * v
    t = jnp.tanh(GELU_A * v * (1.0 + GELU_B * sq))
    half = 0.5 * (1.0 + t)
    slope = half + 0.5 * v * (1.0 - t * t) * (GELU_A * (1.0 + 3.0 * GELU_B * sq))
    return v * half, slope


def positions(order_table, rows):
    block = rows // order_table.shape[0]
    return (order_table[:, None] * block + jnp.arange(block, dtype=jnp.int32)[None]).reshape(rows)


def remote(src, dst, send, recv, **to):
    return pltpu.make_async_remote_copy(
        src_ref=src, dst_ref=dst, send_sem=send, recv_sem=recv, device_id=to, device_id_type=MESH
    )


def column_segments(ranks, d, width, grain):
    own = 3 * d // ranks
    runs = []
    for src in range(ranks):
        for part in range(3):
            for dst in range(ranks):
                low = part * d + dst * width
                first = max(src * own, low)
                last = min((src + 1) * own, low + width, (part + 1) * d)
                if first < last:
                    at = part * width + first - low
                    runs.append(
                        (src, (first - src * own) // grain, dst, at // grain, (last - first) // grain)
                    )
    return runs


def greet(peers):
    barrier = pltpu.get_barrier_semaphore()
    for peer in peers:
        pl.semaphore_signal(barrier, inc=1, device_id=peer, device_id_type=MESH)


def met(peers):
    pl.semaphore_wait(pltpu.get_barrier_semaphore(), len(peers))


class Line:
    def __init__(self, at, size, sems):
        self.at, self.size = at, size
        self.right, self.left, self.recv = sems
        self.z = lax.axis_index("z")

    def copy(self, block, way):
        send = (self.right if way > 0 else self.left).at[block]
        at = self.at(block)
        return remote(at, at, send, self.recv.at[block], z=self.z + way)

    def start(self):
        @pl.when(self.z < self.size - 1)
        def _():
            self.copy(self.z, 1).start()

        @pl.when(self.z > 0)
        def _():
            self.copy(self.z, -1).start()

    def step(self, s, then=None):
        @pl.when(self.z >= s)
        def _():
            block = self.z - s
            self.copy(block, 1).wait_recv()

            @pl.when(self.z < self.size - 1)
            def _():
                self.copy(block, 1).start()

            if then is not None:
                then(block)

        @pl.when(self.z + s < self.size)
        def _():
            block = self.z + s
            self.copy(block, -1).wait_recv()

            @pl.when(self.z > 0)
            def _():
                self.copy(block, -1).start()

            if then is not None:
                then(block)

    def finish(self):
        for s in range(self.size):

            @pl.when((self.z >= s) & (self.z < self.size - 1))
            def _():
                self.copy(self.z - s, 1).wait_send()

            @pl.when((self.z + s < self.size) & (self.z > 0))
            def _():
                self.copy(self.z + s, -1).wait_send()


class LineSum:
    def __init__(self, parts, came, size, sems):
        self.parts = parts if callable(parts) else (lambda block: parts.at[block])
        self.came, self.size = came, size
        self.send, self.recv = sems
        self.z = lax.axis_index("z")

    def copy(self, block, way):
        place = block + 1 if way > 0 else block
        there = self.came.at[place]
        return remote(
            self.parts(block), there, self.send.at[block], self.recv.at[place], z=self.z + way
        )

    def order(self, i):
        near = self.z < self.size // 2
        ahead = self.size - 1 - self.z
        from_low = jnp.where(i < ahead, self.size - 1 - i, i - ahead)
        from_high = jnp.where(i < self.z, i, self.size - 1 - (i - self.z))
        return jnp.where(near, from_low, from_high)

    def ready(self, block):
        @pl.when((self.z == 0) & (block > 0))
        def _():
            self.copy(block, 1).start()

        @pl.when((self.z == self.size - 1) & (block < self.size - 1))
        def _():
            self.copy(block, -1).start()

    def first(self, hops=None):
        for way, edge in ((1, 0), (-1, self.size - 1)):

            @pl.when(self.z == edge)
            def _():
                for hop in range(self.size - 1, 0, -1) if hops is None else hops:
                    self.copy(self.z + way * hop, way).start()

    def add_on(self, block, way):
        self.copy(block, way).wait_recv()
        came = self.came[block + 1 if way > 0 else block]
        part = self.parts(block)
        part[...] = (part[...].astype(F32) + came.astype(F32)).astype(part.dtype)
        self.copy(block, way).start()

    def step(self, s):
        right, left = self.z + self.size - 1 - s, s - (self.size - 1 - self.z)

        @pl.when((self.z > 0) & (right < self.size) & (right > self.z))
        def _():
            self.add_on(right, 1)

        @pl.when((self.z < self.size - 1) & (left >= 0) & (left < self.z))
        def _():
            self.add_on(left, -1)

    def finish(self):
        @pl.when(self.z > 0)
        def _():
            self.copy(self.z, 1).wait_recv()

        @pl.when(self.z == 0)
        def _():
            self.came[self.z + 1] = jnp.zeros(self.came.shape[1:], self.came.dtype)

        @pl.when(self.z < self.size - 1)
        def _():
            self.copy(self.z, -1).wait_recv()

        @pl.when(self.z == self.size - 1)
        def _():
            self.came[self.z] = jnp.zeros(self.came.shape[1:], self.came.dtype)

    def others(self, *at):
        here = (self.z,) + at
        there = (self.z + 1,) + at
        return self.came[here].astype(F32) + self.came[there].astype(F32)

    def sent(self):
        for block in range(self.size):

            @pl.when(self.z < block)
            def _():
                self.copy(block, 1).wait_send()

            @pl.when(self.z > block)
            def _():
                self.copy(block, -1).wait_send()


def halves(n):
    return ((0, n // 2), (n // 2, n - n // 2))


class Plane:
    def __init__(self, size):
        self.size, self.f = size, lax.axis_index("fsdp")
        self.square = size == 4
        f = self.f
        self.peers = [lax.rem(f + i, size) for i in range(1, size)]
        if self.square:
            self.x, self.y, self.far = f + 1 - 2 * lax.rem(f, 2), lax.rem(f + 2, 4), 3 - f
            self.peers = [self.x, self.y, self.far]


class PlaneGather:
    def __init__(self, plane, at, sems):
        self.p, self.at = plane, at
        self.send, self.recv = sems
        f = plane.f
        if plane.square:
            x, y = plane.x, plane.y
            self.early = [(f, 0, x), (f, 1, y), (f, 0, y), (f, 1, x)]
            self.late = [(x, 0, y), (y, 1, x)]
        else:
            self.early = [(f, h, g) for g in plane.peers for h in range(2)]
            self.late = []

    def copy(self, n, move):
        g, half, to = move
        at = self.at(g, half)
        return remote(at, at, self.send.at[n], self.recv.at[g, half], fsdp=to)

    def arrive(self, g, half):
        at = self.at(g, half)
        remote(at, at, self.send.at[0], self.recv.at[g, half], fsdp=g).wait_recv()

    def start(self):
        for n, move in enumerate(self.early):
            self.copy(n, move).start()

    def mid(self):
        for n, move in enumerate(self.late):
            self.arrive(move[0], move[1])
            self.copy(len(self.early) + n, move).start()

    def end(self, then=None, stages=(0, 1)):
        known = [(m[0], m[1]) for m in self.late]
        peers = self.p.peers
        groups = (peers[:2], peers[2:]) if self.p.square else (peers, [])
        for stage in stages:
            for g in groups[stage]:
                for half in range(2):
                    if not any(g is a and half == b for a, b in known):
                        self.arrive(g, half)
                if then is not None:
                    then(g)

    def sent(self):
        for n, move in enumerate(self.early + self.late):
            self.copy(n, move).wait_send()


class PlaneSum:
    def __init__(self, plane, at, came, sems):
        self.p, self.at, self.came = plane, at, came
        self.send, self.recv = sems
        if plane.square:
            x, y, far = plane.x, plane.y, plane.far
            self.early = [(far, 0, x, 0), (far, 1, y, 1), (x, 0, x, 2), (y, 1, y, 3)]
            self.late = [(y, 0, y, 4), (x, 1, x, 5)]
            self.mine = [[2, 4], [3, 5]]
        else:
            n = plane.size
            self.early = [
                (g, h, g, 2 * i + h) for i, g in enumerate(plane.peers) for h in range(2)
            ]
            self.late = []
            self.mine = [[2 * i + h for i in range(n - 1)] for h in range(2)]

    def copy(self, move):
        g, half, to, slot = move
        return remote(
            self.at(g, half), self.came(slot, half), self.send.at[slot], self.recv.at[slot], fsdp=to
        )

    def arrive(self, slot, half):
        there = self.came(slot, half)
        remote(
            there, there, self.send.at[slot], self.recv.at[slot], fsdp=self.p.peers[0]
        ).wait_recv()

    def start(self):
        for move in self.early:
            self.copy(move).start()

    def mid(self):
        for slot, move in enumerate(self.late):
            self.arrive(slot, move[1])
            at, came = self.at(move[0], move[1]), self.came(slot, move[1])
            at[...] = (at[...].astype(F32) + came[...].astype(F32)).astype(at.dtype)
            self.copy(move).start()

    def end(self):
        for half in range(2):
            for slot in self.mine[half]:
                self.arrive(slot, half)

    def total(self, half):
        out = self.at(self.p.f, half)[...].astype(F32)
        for slot in self.mine[half]:
            out += self.came(slot, half)[...].astype(F32)
        return out

    def sent(self):
        for move in self.early + self.late:
            self.copy(move).wait_send()


def query_block(length):
    return max(128, min(256, length, 256 * 1024 // length))


def attend_head(h, width, q_block, qkv, pos_col, pos_row, out, lse):
    rows = qkv.shape[0]
    k = qkv[:, width + h * HD : width + (h + 1) * HD]
    v = qkv[:, 2 * width + h * HD : 2 * width + (h + 1) * HD]
    for b in range(rows // q_block):
        at = slice(b * q_block, (b + 1) * q_block)
        q = qkv[at, h * HD : (h + 1) * HD] * BF(HD**-0.5)
        s = dot_nt(k, q)
        s = jnp.where(pos_col[...] <= pos_row[:, at], s, FLOOR)
        top = jnp.max(s, axis=0, keepdims=True)
        p = jnp.exp(s - top)
        total = jnp.sum(p, axis=0, keepdims=True)
        o = dot_tn(v, p.astype(BF)) * (1.0 / total)
        out[at, h * HD : (h + 1) * HD] = o.T.astype(BF)
        lse[h : h + 1, at] = top + jnp.log(total)


def attend_back_head(h, width, q_block, qkv, pos_col, pos_row, out, lse, dout, dqkv, acc):
    rows = qkv.shape[0]
    k = qkv[:, width + h * HD : width + (h + 1) * HD]
    v = qkv[:, 2 * width + h * HD : 2 * width + (h + 1) * HD]
    for b in range(rows // q_block):
        at = slice(b * q_block, (b + 1) * q_block)
        q = qkv[at, h * HD : (h + 1) * HD] * BF(HD**-0.5)
        do = dout[at, h * HD : (h + 1) * HD]
        o = out[at, h * HD : (h + 1) * HD]
        delta = jnp.sum(do.astype(F32).T * o.astype(F32).T, axis=0, keepdims=True)
        s = dot_nt(k, q)
        p = jnp.where(pos_col[...] <= pos_row[:, at], jnp.exp(s - lse[h : h + 1, at]), 0.0)
        dp = dot_nt(v, do)
        ds = (p * (dp - delta)).astype(BF)
        dq = dot_tn(k, ds) * (HD**-0.5)
        dqkv[at, h * HD : (h + 1) * HD] = dq.T.astype(BF)
        dk = dot(ds, q)
        dv = dot(p.astype(BF), do)
        if b == 0:
            acc[:, :HD] = dk
            acc[:, HD:] = dv
        else:
            acc[:, :HD] += dk
            acc[:, HD:] += dv
    dqkv[:, width + h * HD : width + (h + 1) * HD] = acc[:, :HD].astype(BF)
    dqkv[:, 2 * width + h * HD : 2 * width + (h + 1) * HD] = acc[:, HD:].astype(BF)


def start_kernel(
    cfg,
    tok_cols,
    qkv_own,
    proj_cols,
    out_own,
    block_order,
    gain_one,
    shift_one,
    query_shift,
    value_shift,
    out_shift,
    gain_two,
    shift_two,
    proj_shift,
    fc_shift,
    h1_out,
    w_out,
    qkv,
    att,
    lse,
    smalls,
    p2,
    o_all,
    a_own,
    tok,
    h1,
    w,
    wq,
    pj,
    ot,
    pos_col,
    pos_row,
    toks,
    vecs,
    small,
    p1,
    small_send,
    small_recv,
    q_send,
    q_recv,
    q_local,
    x_send,
    x_recv,
    t_right,
    t_left,
    t_recv,
    c_send,
    c_recv,
    p1_send,
    p1_recv,
    p2_send,
    p2_recv,
    p_local,
    a_send,
    a_recv,
    o_right,
    o_left,
    o_recv,
    ox_send,
    ox_recv,
    oc_send,
    oc_recv,
):
    fs, nz, d, heads = cfg
    cs = 2 * nz
    f, z, core = lax.axis_index("fsdp"), lax.axis_index("z"), lax.axis_index("core")
    rank = 2 * z + core
    rows, lanes = tok_cols.shape[1], wq.shape[2]
    width = heads * HD
    grain = wq.shape[1]
    own_rows = d // fs
    part = d // cs
    lanes_of = lambda g: pl.ds(pl.multiple_of(g * lanes, 128), lanes)
    runs = column_segments(cs, d, width, grain)
    plane = Plane(fs)
    planes = plane.peers

    w[:, :, lanes_of(f)] = jnp.zeros((w.shape[0], grain, lanes), BF)
    ranks = [lax.rem(rank + i, cs) for i in range(1, cs)]
    peers = [dict(z=r // 2, core=lax.rem(r, 2)) for r in ranks] + [dict(fsdp=p) for p in planes]
    greet(peers)

    fine = ot.shape[1]
    if lanes > own_rows:
        wq[:, :, own_rows:] = jnp.zeros((wq.shape[0], grain, lanes - own_rows), BF)
        ot[:, :, own_rows:] = jnp.zeros((ot.shape[0], fine, lanes - own_rows), BF)
    wq[:, :, 0:own_rows] = qkv_own[...].T.reshape(wq.shape[0], grain, own_rows)
    ot[:, :, 0:own_rows] = out_own[...].T.reshape(ot.shape[0], fine, own_rows)
    pj[...] = jnp.zeros(pj.shape, BF)
    ff_half, hf = proj_cols.shape[1] // 2, pj.shape[2] // 2
    for k in range(2):
        pj[0 : part // fine, :, k * hf : k * hf + ff_half] = proj_cols[
            :, k * ff_half : (k + 1) * ff_half
        ].reshape(part // fine, fine, ff_half)
    tok[...] = tok_cols[...].T
    toks[rank] = tok[...]
    small[...] = jnp.zeros(small.shape, F32)
    for n, v in enumerate(
        (
            gain_one,
            shift_one,
            query_shift,
            value_shift,
            out_shift,
            gain_two,
            shift_two,
            proj_shift,
        )
    ):
        small[n : n + 1, 0:part] = v[...].astype(F32).reshape(1, part)
    fc_line = fc_shift[...].astype(F32).reshape(1, fc_shift.shape[0])
    for j in range(small.shape[0] - 8):
        small[8 + j : 9 + j, 0:part] = fc_line[:, j * part : (j + 1) * part]
    met(peers)
    keep_out = pltpu.make_async_copy(ot, o_all.at[rank, :, :, lanes_of(f)], p_local.at[0])
    keep_out.start()

    def run_copy(n):
        src, first, dst, at, count = runs[n]
        here, there = wq.at[pl.ds(first, count)], w.at[pl.ds(at, count), :, lanes_of(f)]
        if src == dst:
            return pltpu.make_async_copy(here, there, q_local.at[n])
        return remote(here, there, q_send.at[n], q_recv.at[n], z=dst // 2, core=dst % 2)

    for n, run in enumerate(runs):

        @pl.when(rank == run[0])
        def _():
            run_copy(n).start()

    def small_copy(i):
        r = ranks[i]
        to = smalls.at[rank]
        return remote(small, to, small_send.at[i], small_recv.at[rank], z=r // 2, core=lax.rem(r, 2))

    for i in range(cs - 1):
        small_copy(i).start()

    share = p1.shape[1]

    def p1_copy(i):
        here = pj.at[pl.ds(planes[i] * share, share)]
        return remote(here, p1.at[f], p1_send.at[i], p1_recv.at[f], fsdp=planes[i])

    p1[f] = pj[pl.ds(f * share, share)]
    for i in range(fs - 1):
        p1_copy(i).start()

    def ox_copy(i, block, here=None):
        at = o_all.at[2 * block + core, :, :, lanes_of(f)]
        here = at if here is None else here
        return remote(here, at, ox_send.at[i, block], ox_recv.at[f, block], fsdp=planes[i])

    def ox_arrival(g, block):
        at = o_all.at[2 * block + core, :, :, lanes_of(g)]
        return remote(at, at, ox_send.at[0, block], ox_recv.at[g, block], fsdp=g)

    def oc_copy(g, block, here=None):
        at = o_all.at[2 * block + core, :, :, lanes_of(g)]
        here = at if here is None else here
        return remote(here, at, oc_send.at[g, block], oc_recv.at[g, block], core=1 - core)

    def oc_arrival(g, block):
        at = o_all.at[2 * block + 1 - core, :, :, lanes_of(g)]
        return remote(at, at, oc_send.at[g, block], oc_recv.at[g, block], core=1 - core)

    def out_block(block, here=None):
        for i in range(fs - 1):
            ox_copy(i, block, here).start()
        oc_copy(f, block, here).start()

    out_block(z, ot)

    for n, run in enumerate(runs):

        @pl.when(rank == run[2])
        def _():
            if run[0] == run[2]:
                run_copy(n).wait()
            else:
                run_copy(n).wait_recv()

    gather = PlaneGather(
        plane, lambda g, h: w.at[pl.ds(*halves(w.shape[0])[h]), :, lanes_of(g)], (x_send, x_recv)
    )
    gather.start()

    line = Line(lambda b: toks.at[2 * b + core], nz, (t_right, t_left, t_recv))

    def pass_on(block):
        at = toks.at[2 * block + core]
        return remote(at, at, c_send.at[block], c_recv.at[block], core=1 - core)

    def arrival(block):
        at = toks.at[2 * block + 1 - core]
        return remote(at, at, c_send.at[block], c_recv.at[block], core=1 - core)

    line.start()
    pass_on(z).start()

    smalls[rank] = small[...]
    vecs[...] = jnp.zeros(vecs.shape, F32)
    length = cs * rows
    run = length // block_order.shape[0]
    for b in range(block_order.shape[0]):
        first = block_order[b] * run
        at = slice(b * run, (b + 1) * run)
        pos_row[:, at] = first + lax.broadcasted_iota(jnp.int32, (1, run), 1)
        pos_col[at, :] = first + lax.broadcasted_iota(jnp.int32, (run, 1), 0)
    if lanes > own_rows:
        for g in range(fs):
            h1[:, lanes * g + own_rows : lanes * (g + 1)] = jnp.zeros(
                (length, lanes - own_rows), BF
            )
    for i in range(1, cs):
        back = lax.rem(rank + cs - i, cs)
        remote(small, smalls.at[back], small_send.at[i - 1], small_recv.at[back], z=z).wait_recv()
    for r in range(cs):
        vecs[:, part * r : part * (r + 1)] = smalls[r, 0:8, 0:part]

    step = min(32, rows)

    def norm_block(block):
        def chunk(i, _):
            at = pl.multiple_of(i * step, step)
            xhat, _ = norm_rows(toks[block, pl.ds(at, step), :].astype(F32))
            h = (xhat * vecs[0:1, 0:d] + vecs[1:2, 0:d]).astype(BF)
            to = pl.ds(pl.multiple_of(block * rows + i * step, step), step)
            for g in range(fs):
                h1[to, lanes * g : lanes * g + own_rows] = h[:, own_rows * g : own_rows * (g + 1)]
            return 0

        lax.fori_loop(0, rows // step, chunk, 0)

    def place(i):
        hop = (i + 1) // 2
        return jnp.where(lax.rem(i, 2) == 1, z - hop, z + hop)

    def take(i, _):
        block = place(i)

        @pl.when((block >= 0) & (block < nz))
        def _():
            @pl.when(block < z)
            def _():
                line.copy(block, 1).wait_recv()

                @pl.when(z < nz - 1)
                def _():
                    line.copy(block, 1).start()

            @pl.when(block > z)
            def _():
                line.copy(block, -1).wait_recv()

                @pl.when(z > 0)
                def _():
                    line.copy(block, -1).start()

            @pl.when(block != z)
            def _():
                pass_on(block).start()

            norm_block(2 * block + core)
            arrival(block).wait_recv()
            norm_block(2 * block + 1 - core)

        return 0

    tall = 2 * rows
    head_lanes = pl.ds(pl.multiple_of(rank * width, 128), width)

    def project(i, _):
        block = place(i)

        @pl.when((block >= 0) & (block < nz))
        def _():
            at = pl.ds(pl.multiple_of(block * tall, tall), tall)
            full = dot_nt(h1[at, :], w[...].reshape(3 * width, fs * lanes))
            qkv[at, 0:width] = (full[:, 0:width] + vecs[2:3, head_lanes]).astype(BF)
            qkv[at, width : 2 * width] = full[:, width : 2 * width].astype(BF)
            qkv[at, 2 * width :] = (full[:, 2 * width :] + vecs[3:4, head_lanes]).astype(BF)

        return 0

    lax.fori_loop(0, 3, take, 0)
    gather.mid()
    lax.fori_loop(3, 2 * nz - 3, take, 0)

    keep_out.wait()
    out_line = Line(
        lambda b: o_all.at[2 * b + core, :, :, lanes_of(f)], nz, (o_right, o_left, o_recv)
    )
    out_line.start()
    gather.end()
    lax.fori_loop(0, 2 * nz - 3, project, 0)
    lax.fori_loop(2 * nz - 3, 2 * nz - 1, take, 0)
    lax.fori_loop(2 * nz - 3, 2 * nz - 1, project, 0)
    keep_h1 = pltpu.make_async_copy(h1, h1_out, p_local.at[1])
    keep_w = pltpu.make_async_copy(w, w_out, p_local.at[2])
    keep_h1.start()
    keep_w.start()
    out_line.step(1, out_block)

    for g in planes:
        remote(p1.at[g], p1.at[g], p1_send.at[0], p1_recv.at[g], fsdp=g).wait_recv()

    def p2_copy(i):
        to = lax.rem(z + i, nz)
        return remote(p1.at[to], p2.at[z], p2_send.at[to], p2_recv.at[z], z=to)

    def a_copy(i, pair):
        r = ranks[i]
        here = att.at[pl.ds(pl.multiple_of(r * rows, rows), rows), pl.ds(pair * 128, 128)]
        there = a_own.at[:, pl.ds(pl.multiple_of(rank * width + pair * 128, 128), 128)]
        return remote(
            here, there, a_send.at[i, pair], a_recv.at[rank, pair], z=r // 2, core=lax.rem(r, 2)
        )

    for h in range(heads):
        attend_head(h, width, query_block(cs * rows), qkv, pos_col, pos_row, att, lse)
        if h + 2 < nz:
            out_line.step(h + 2, out_block)
        if h % 2 == 1:
            for i in range(cs - 1):
                a_copy(i, h // 2).start()
        if h == 0:
            for i in range(1, nz):
                p2_copy(i).start()
            p2[z] = p1[z]
    for s in range(heads + 2, nz):
        out_line.step(s, out_block)
    a_own[:, head_lanes] = att[pl.ds(pl.multiple_of(rank * rows, rows), rows), :]

    for g in planes:
        for b in range(nz):
            ox_arrival(g, b).wait_recv()
            oc_copy(g, b).start()
    for pair in range(width // 128):
        for i in range(1, cs):
            back = lax.rem(rank + cs - i, cs)
            to = a_own.at[:, pl.ds(pl.multiple_of(back * width + pair * 128, 128), 128)]
            remote(to, to, a_send.at[0, 0], a_recv.at[back, pair], z=z).wait_recv()
    for i in range(1, nz):
        back = lax.rem(z + nz - i, nz)
        remote(p2.at[back], p2.at[back], p2_send.at[0], p2_recv.at[back], z=back).wait_recv()
    for g in range(fs):
        for b in range(nz):
            oc_arrival(g, b).wait_recv()
    keep_h1.wait()
    keep_w.wait()

    for n, run in enumerate(runs):
        if run[0] != run[2]:

            @pl.when(rank == run[0])
            def _():
                run_copy(n).wait_send()

    for i in range(cs - 1):
        small_copy(i).wait_send()
        for pair in range(width // 128):
            a_copy(i, pair).wait_send()
    gather.sent()
    for i in range(1, nz):
        p2_copy(i).wait_send()
    for i in range(fs - 1):
        p1_copy(i).wait_send()
        for b in range(nz):
            ox_copy(i, b).wait_send()
    for g in range(fs):
        for b in range(nz):
            oc_copy(g, b).wait_send()
    line.finish()
    out_line.finish()
    for b in range(nz):
        pass_on(b).wait_send()


def start(cfg, tok_cols, qkv_own, proj_cols, out_own, block_order, vectors, hf):
    fs, nz, d, heads = cfg
    cs = 2 * nz
    rows, cols = tok_cols.shape[1], qkv_own.shape[1]
    width, length = heads * HD, rows * cs
    part, lanes = d // cs, up(d // fs)
    grain, fine = math.gcd(math.gcd(cols, HD), 8), math.gcd(part, 8)
    share = -(-part // (fine * fs))
    runs = len(column_segments(cs, d, width, grain))
    pairs = width // 128
    small = (8 + vectors[8].shape[0] // part, up(part))
    smem = pl.BlockSpec(memory_space=pltpu.SMEM)
    h1 = (length, fs * lanes)
    w = (3 * width // grain, grain, fs * lanes)
    return pl.pallas_call(
        partial(start_kernel, cfg),
        out_shape=(
            shape(h1),
            shape(w),
            shape((length, 3 * width)),
            shape((length, width)),
            shape((heads, length), F32),
            shape((cs,) + small, F32),
            shape((nz, share, fine, 2 * hf)),
            shape((cs, part // fine, fine, fs * lanes)),
            shape((rows, cs * width)),
            shape((rows, d)),
        ),
        in_specs=[VMEM] * 4 + [smem] + [VMEM] * 9,
        out_specs=(HBM, HBM) + (VMEM,) * 5 + (HBM, VMEM, VMEM),
        scratch_shapes=[
            pltpu.VMEM(h1, BF),
            pltpu.VMEM(w, BF),
            pltpu.VMEM((cols // grain, grain, lanes), BF),
            pltpu.VMEM((fs * share, fine, 2 * hf), BF),
            pltpu.VMEM((part // fine, fine, lanes), BF),
            pltpu.VMEM((length, 1), jnp.int32),
            pltpu.VMEM((1, length), jnp.int32),
            pltpu.VMEM((cs, rows, d), BF),
            pltpu.VMEM((8, width * cs), F32),
            pltpu.VMEM(small, F32),
            pltpu.VMEM((fs, share, fine, 2 * hf), BF),
        ]
        + sems(cs, cs, runs, runs, runs, 2 * fs, (fs, 2), nz, nz, nz, nz, nz)
        + sems(fs, fs, nz, nz, 3, (cs, pairs), (cs, pairs))
        + sems(nz, nz, nz, (fs, nz), (fs, nz), (fs, nz), (fs, nz)),
        name="start",
        compiler_params=pltpu.CompilerParams(
            collective_id=0, has_side_effects=True, vmem_limit_bytes=60 * 2**20
        ),
    )(tok_cols, qkv_own, proj_cols, out_own, block_order, *vectors)


def middle_kernel(
    cfg,
    a_own,
    tok,
    ct_cols,
    smalls,
    p2,
    fc,
    o_all,
    middle,
    d_middle,
    d_att,
    out_part,
    fc_grad,
    p_sum,
    og,
    sums,
    vec,
    fb,
    ct,
    a_pad,
    ov,
    fcv,
    pjv,
    ctb,
    cto,
    h2b,
    actb,
    dbo,
    dbp,
    dh,
    r_in,
    own_dh,
    da,
    dsp,
    pg,
    pr,
    stage,
    local,
    p3_send,
    p3_recv,
    pc_send,
    pc_recv,
    f_send,
    f_recv,
    fc_send,
    fc_recv,
    c_right,
    c_left,
    c_recv,
    h_right,
    h_left,
    h_recv,
    e_send,
    e_recv,
    r_send,
    r_recv,
    d_send,
    d_recv,
    g_send,
    g_recv,
):
    fs, nz, d, heads = cfg
    cs = 2 * nz
    f, z, core = lax.axis_index("fsdp"), lax.axis_index("z"), lax.axis_index("core")
    rank = 2 * z + core
    rows = tok.shape[0]
    width = heads * HD
    lanes = o_all.shape[3] // fs
    own_rows, part = d // fs, d // cs
    share, grain = p2.shape[1], p2.shape[2]
    slot = fs * share * grain
    he, hf = nz * slot, pjv.shape[5] // 2
    ff = 2 * hf
    fc_grain, fc_cols = fcv.shape[1], fc.shape[1]
    fc_rows = fc.shape[0] // fc_grain
    tall = nz * rows
    step = min(32, rows)
    plane = Plane(fs)
    ranks = [lax.rem(rank + i, cs) for i in range(1, cs)]
    half_at = lambda k: pl.ds(pl.multiple_of(k * hf, 128), hf)
    e_at = lambda k: pl.ds(pl.multiple_of(k * he, 128), he)

    peers = [dict(z=r // 2, core=lax.rem(r, 2)) for r in ranks]
    peers += [dict(fsdp=p) for p in plane.peers]
    greet(peers)
    load_out = pltpu.make_async_copy(o_all, ov, local.at[0])
    fc_at = lambda g, k, h: fcv.at[
        pl.ds(g * fc_rows + halves(fc_rows)[h][0], halves(fc_rows)[h][1]), :, half_at(k)
    ]
    load_out.start()
    for k in range(2):

        @pl.when(core == k)
        def _():
            at = pl.ds(f * fc_rows, fc_rows)
            if hf > fc_cols:
                fcv[at, :, k * hf + fc_cols : (k + 1) * hf] = jnp.zeros(
                    (fc_rows, fc_grain, hf - fc_cols), BF
                )
            fcv[at, :, k * hf : k * hf + fc_cols] = fc[...].reshape(fc_rows, fc_grain, fc_cols)

    ct[...] = ct_cols[...].T
    ctb[z] = jnp.zeros(ctb.shape[1:], BF)
    for c in range(cs):
        to = (c % 2) * he + (c // 2) * slot
        ctb[z, :, to : to + part] = ct[:, c * part : (c + 1) * part]
    for r in range(cs):
        vec[:, r * part : (r + 1) * part] = smalls[r, 4:7, 0:part]
    fb[...] = jnp.zeros(fb.shape, F32)
    for k in range(2):
        for j in range(smalls.shape[1] - 8):
            to = k * hf + j * part
            fb[:, to : to + part] = smalls[2 * z + k, 8 + j : 9 + j, 0:part]
    for g in range(fs):
        a_pad[core, :, lanes * g : lanes * g + own_rows] = a_own[
            :, own_rows * g : own_rows * (g + 1)
        ]
        a_pad[core, :, lanes * g + own_rows : lanes * (g + 1)] = jnp.zeros(
            (rows, lanes - own_rows), BF
        )
    pjv[core, :, f] = p2[...]
    met(peers)

    def swap(n, here, there):
        return remote(here, there, e_send.at[n], e_recv.at[n], core=1 - core)

    half_z = lambda h: pl.ds(*halves(nz)[h])
    p_gather = PlaneGather(plane, lambda g, h: pjv.at[core, half_z(h), g], (p3_send, p3_recv))

    def p_pass(g):
        at = pjv.at[core, :, g]
        return remote(at, at, pc_send.at[g], pc_recv.at[g], core=1 - core)

    def p_came(g):
        at = pjv.at[1 - core, :, g]
        return remote(at, at, pc_send.at[g], pc_recv.at[g], core=1 - core)

    fc_gather = PlaneGather(plane, lambda g, h: fc_at(g, core, h), (f_send, f_recv))
    fc_gather.start()

    def fc_pass(g):
        at = fcv.at[pl.ds(g * fc_rows, fc_rows), :, half_at(core)]
        return remote(at, at, fc_send.at[g], fc_recv.at[g], core=1 - core)

    def fc_came(g):
        at = fcv.at[pl.ds(g * fc_rows, fc_rows), :, half_at(1 - core)]
        return remote(at, at, fc_send.at[g], fc_recv.at[g], core=1 - core)

    fc_pass(f).start()

    c_line = Line(lambda b: ctb.at[b], nz, (c_right, c_left, c_recv))
    c_line.start()

    swap_a = swap(4, a_pad.at[core], a_pad.at[core])
    swap_a.start()
    load_out.wait()
    branch = dot_nt(a_pad[core], ov[...].reshape(d, fs * lanes))
    middle[...] = tok[...].astype(F32) + branch + vec[0:1, :]

    def norm_chunk(i, _):
        at = pl.ds(pl.multiple_of(i * step, step), step)
        xhat, _ = norm_rows(middle[at, :])
        h2b[core, z, at, :] = (xhat * vec[1:2, :] + vec[2:3, :]).astype(BF)
        return 0

    lax.fori_loop(0, rows // step, norm_chunk, 0)
    h_line = Line(lambda b: h2b.at[core, b], nz, (h_right, h_left, h_recv))
    h_line.start()
    fc_gather.mid()
    p_gather.start()
    p_pass(f).start()
    on = lambda g: fc_pass(g).start()
    h_line.step(1)
    fc_gather.end(on, (0,))
    for s in range(2, nz - 1):
        h_line.step(s)
    c_line.step(1)
    fc_gather.end(on, (1,))
    for g in range(fs):
        fc_came(g).wait_recv()

    chunk = 256 if ff % 256 == 0 else 128
    some = nz // 2
    wide = some * rows
    sums[4:5, :] = jnp.zeros((1, sums.shape[1]), F32)

    def by_columns(one):
        def step_columns(i, _):
            one(pl.ds(pl.multiple_of(i * chunk, chunk), chunk))
            return 0

        lax.fori_loop(0, ff // chunk, step_columns, 0)

    def feed(first):
        blocks = pl.ds(first, some)

        def one(at):
            w = fcv[:, :, at].reshape(d, chunk)
            before = dot(h2b[core, blocks].reshape(wide, d), w) + fb[:, at]
            act, slope = gelu_pair(before)
            actb[core, blocks, :, at] = act.astype(BF).reshape(some, rows, chunk)
            dbo[blocks, :, at] = slope.astype(BF).reshape(some, rows, chunk)

        by_columns(one)

    def feed_back(first):
        blocks = pl.ds(first, some)

        def one(at):
            w = pjv[:, :, :, :, :, at].reshape(2 * he, chunk)
            back = dot(ctb[blocks].reshape(wide, 2 * he), w)
            slope = dbo[blocks, :, at].reshape(wide, chunk).astype(F32)
            low = (back * slope).astype(BF)
            dbo[blocks, :, at] = low.reshape(some, rows, chunk)
            sums[4:5, at] += jnp.sum(low.astype(F32), axis=0, keepdims=True)

        by_columns(one)

    near = z // some * some
    feed(near)
    p_gather.mid()
    for s in range(2, nz - 1):
        c_line.step(s)
    h_line.step(nz - 1)
    swap_h2 = swap(1, h2b.at[core], h2b.at[core])
    feed(some - near)
    on = lambda g: p_pass(g).start()
    p_gather.end(on)
    for g in range(fs):
        p_came(g).wait_recv()
    swap_h2.start()
    feed_back(near)
    c_line.step(nz - 1)
    feed_back(some - near)
    swap_ct = swap(0, ctb.at[:, :, e_at(1 - core)], cto)
    swap_ct.start()
    swap_act = swap(2, actb.at[core], actb.at[core])
    swap_db = swap(3, dbo.at[:, :, half_at(1 - core)], dbp)
    swap_act.start()
    swap_db.start()

    r_line = LineSum(dh, r_in, nz, (r_send, r_recv))

    def hidden_back(i, _):
        block = r_line.order(i)
        part_sum = dot_nt(dbo[block], fcv[...].reshape(d, ff))
        dh[block] = part_sum.astype(BF)

        @pl.when(block == z)
        def _():
            own_dh[...] = part_sum

        r_line.ready(block)
        return 0

    lax.fori_loop(0, nz, hidden_back, 0)

    def output_part(k, i):
        w = pjv[k, i].reshape(slot, ff)
        part = dot_nt(actb[core].reshape(tall, ff), w)
        low = (2 * i + k) * (d // cs)
        ctb[:, :, low : low + d // cs] = part[:, : d // cs].astype(BF).reshape(nz, rows, d // cs)

    swap_ct.wait_recv()
    swap_act.wait_recv()
    pieces = 2 if hf % 256 == 0 or ff % 512 else 4
    for low in range(0, ff, ff // pieces):
        cols = slice(low, low + ff // pieces)
        pg[:, :, :, :, cols] = (
            (
                dot_tn(
                    ctb[:, :, e_at(core)].reshape(tall, he),
                    actb[core, :, :, cols].reshape(tall, ff // pieces),
                )
                + dot_tn(
                    cto[...].reshape(tall, he),
                    actb[1 - core, :, :, cols].reshape(tall, ff // pieces),
                )
            )
            .astype(BF)
            .reshape(nz, fs, share, grain, ff // pieces)
        )
    p_total = PlaneSum(
        plane,
        lambda g, h: pg.at[half_z(h), g],
        lambda n, h: pr.at[n, pl.ds(0, halves(nz)[h][1])],
        (g_send, g_recv),
    )
    p_total.start()
    c_line.finish()
    swap_ct.wait_send()
    keep_out = pltpu.make_async_copy(ctb.at[:, :, pl.ds(0, up(d))], out_part, local.at[6])
    for s in range(1, nz - 1):
        r_line.step(s)
        if s == 1:
            for k in range(2):
                for i in range(nz):
                    output_part(k, i)
            keep_out.start()
    swap_h2.wait_recv()
    swap_db.wait_recv()
    own_db = dbo[:, :, half_at(core)].reshape(tall, hf)
    other_db = dbp[...].reshape(tall, hf)
    cut = 512
    for low in range(0, d, cut):
        high = min(d, low + cut)
        fc_grad[low:high, :] = (
            dot_tn(h2b[core, :, :, low:high].reshape(tall, high - low), own_db)
            + dot_tn(h2b[1 - core, :, :, low:high].reshape(tall, high - low), other_db)
        ).astype(BF)
    p_total.mid()
    r_line.finish()

    sums[0:4, :] = jnp.zeros((4, sums.shape[1]), F32)
    dsp[core] = jnp.zeros(dsp.shape[1:], BF)

    def norm_back_chunk(i, _):
        at = pl.ds(pl.multiple_of(i * step, step), step)
        g = own_dh[at, :] + r_line.others(at)
        xhat, rstd = norm_rows(middle[at, :])
        dm = ct[at, :].astype(F32) + norm_back(g, xhat, rstd, vec[1:2, :])
        low = dm.astype(BF)
        d_middle[at, :] = dm
        for c in range(cs):
            to = (c % 2) * he + (c // 2) * slot
            dsp[core, at, to : to + part] = low[:, c * part : (c + 1) * part]
        sums[0:1, 0:d] += jnp.sum(low.astype(F32), axis=0, keepdims=True)
        sums[1:2, 0:d] += jnp.sum(g * xhat, axis=0, keepdims=True)
        sums[2:3, 0:d] += jnp.sum(g, axis=0, keepdims=True)
        sums[3:4, 0:d] += jnp.sum(ct[at, :].astype(F32), axis=0, keepdims=True)
        return 0

    lax.fori_loop(0, rows // step, norm_back_chunk, 0)
    swap_d = swap(5, dsp.at[core], dsp.at[core])
    swap_d.start()
    back = dot(d_middle[...].astype(BF), ov[...].reshape(d, fs * lanes)).astype(BF)
    for g in range(fs):
        da[:, own_rows * g : own_rows * (g + 1)] = back[:, lanes * g : lanes * g + own_rows]
    if d < cs * width:
        da[:, d:] = jnp.zeros((rows, cs * width - d), BF)

    def d_copy(i):
        r = ranks[i]
        here = da.at[:, pl.ds(pl.multiple_of(r * width, 128), width)]
        there = d_att.at[pl.ds(pl.multiple_of(rank * rows, rows), rows)]
        return remote(here, there, d_send.at[i], d_recv.at[rank], z=r // 2, core=lax.rem(r, 2))

    for i in range(cs - 1):
        d_copy(i).start()
    d_att[pl.ds(pl.multiple_of(rank * rows, rows), rows), :] = da[
        :, pl.ds(pl.multiple_of(rank * width, 128), width)
    ]

    swap_a.wait_recv()
    swap_d.wait_recv()

    def stage_out(g):
        at = pl.ds(g * lanes, lanes)
        return pltpu.make_async_copy(stage.at[g % 2], og.at[:, :, :, at], local.at[4 + g % 2])

    for g in range(fs):
        at = slice(g * lanes, (g + 1) * lanes)
        part_sum = dot_tn(
            dsp[:, :, e_at(core)].reshape(2 * rows, he), a_pad[:, :, at].reshape(2 * rows, lanes)
        )
        part_sum = part_sum.astype(BF).reshape(nz, slot // grain, grain, lanes)
        if g >= 2:
            stage_out(g - 2).wait()
        stage[g % 2] = part_sum[:, : og.shape[1]]
        stage_out(g).start()
    for g in range(max(fs - 2, 0), fs):
        stage_out(g).wait()

    p_total.end()
    for h in range(2):
        p_sum[half_z(h)] = p_total.total(h).astype(BF)
    for i in range(1, cs):
        back = lax.rem(rank + cs - i, cs)
        to = d_att.at[pl.ds(pl.multiple_of(back * rows, rows), rows)]
        remote(to, to, d_send.at[0], d_recv.at[back], z=z).wait_recv()

    for i in range(cs - 1):
        d_copy(i).wait_send()
    for g in range(fs):
        fc_pass(g).wait_send()
        p_pass(g).wait_send()
    fc_gather.sent()
    p_gather.sent()
    p_total.sent()
    keep_out.wait()
    h_line.finish()
    r_line.sent()
    for s in (swap_h2, swap_act, swap_db, swap_a, swap_d):
        s.wait_send()


def middle_part(cfg, a_own, tok, ct_cols, smalls, p2, fc, o_all):
    fs, nz, d, heads = cfg
    cs = 2 * nz
    rows, width = tok.shape[0], heads * HD
    length = rows * cs
    lanes = o_all.shape[3] // fs
    share, grain = p2.shape[1], p2.shape[2]
    he, hf = nz * fs * share * grain, p2.shape[3] // 2
    fc_grain = math.gcd(d // fs, 16)
    return pl.pallas_call(
        partial(middle_kernel, cfg),
        out_shape=(
            shape((rows, d), F32),
            shape((rows, d), F32),
            shape((length, width)),
            shape((nz, rows, up(d))),
            shape((d, hf)),
            shape((nz, share, grain, 2 * hf)),
            shape((nz,) + o_all.shape[1:]),
            shape((5, max(2 * hf, d)), F32),
        ),
        in_specs=[VMEM] * 6 + [HBM],
        out_specs=(VMEM, VMEM, VMEM, HBM, VMEM, VMEM, HBM, VMEM),
        scratch_shapes=[
            pltpu.VMEM((3, d), F32),
            pltpu.VMEM((1, 2 * hf), F32),
            pltpu.VMEM((rows, d), BF),
            pltpu.VMEM((2, rows, fs * lanes), BF),
            pltpu.VMEM(o_all.shape, BF),
            pltpu.VMEM((d // fc_grain, fc_grain, 2 * hf), BF),
            pltpu.VMEM((2, nz, fs, share, grain, 2 * hf), BF),
            pltpu.VMEM((nz, rows, 2 * he), BF),
            pltpu.VMEM((nz, rows, he), BF),
            pltpu.VMEM((2, nz, rows, d), BF),
            pltpu.VMEM((2, nz, rows, 2 * hf), BF),
            pltpu.VMEM((nz, rows, 2 * hf), BF),
            pltpu.VMEM((nz, rows, hf), BF),
            pltpu.VMEM((nz, rows, d), BF),
            pltpu.VMEM((nz + 1, rows, d), BF),
            pltpu.VMEM((rows, d), F32),
            pltpu.VMEM((rows, cs * width), BF),
            pltpu.VMEM((2, rows, 2 * he), BF),
            pltpu.VMEM((nz, fs, share, grain, 2 * hf), BF),
            pltpu.VMEM((2 * (fs - 1), nz - nz // 2, share, grain, 2 * hf), BF),
            pltpu.VMEM((2, nz) + o_all.shape[1:3] + (lanes,), BF),
        ]
        + sems(7, 2 * fs, (fs, 2), fs, fs, 2 * fs, (fs, 2), fs, fs)
        + sems(nz, nz, nz, nz, nz, nz, 6, 6, nz, nz + 1, cs, cs, 2 * fs, 2 * fs),
        name="middle",
        compiler_params=pltpu.CompilerParams(
            collective_id=1, has_side_effects=True, vmem_limit_bytes=62 * 2**20
        ),
    )(a_own, tok, ct_cols, smalls, p2, fc, o_all)


def last_kernel(
    cfg,
    qkv,
    att,
    lse,
    d_att,
    block_order,
    w_in,
    h1,
    tok,
    smalls,
    sums,
    middle_in,
    d_middle_in,
    out_part,
    p_sum,
    og,
    fg,
    output,
    input_grad,
    q_grad,
    p_grad,
    o_grad,
    f_grad,
    small_grad,
    w,
    middle,
    d_middle,
    out_rows,
    in_rows,
    pos_col,
    pos_row,
    vec,
    p_all,
    q_own,
    fgv,
    fr,
    d_qkv,
    acc,
    h1v,
    qg,
    qr,
    qs,
    om,
    orc,
    osum,
    o_in,
    op,
    ro_in,
    pz,
    other,
    partner,
    own,
    r_out,
    r_in,
    line,
    sm_out,
    sm_in,
    sm_f,
    z_send,
    z_recv,
    l_send,
    l_recv,
    local,
    q_send,
    q_recv,
    o_send,
    o_recv,
    os_send,
    os_recv,
    ro_send,
    ro_recv,
    f_send,
    f_recv,
    m_send,
    m_recv,
    r_send,
    r_recv,
    b_send,
    b_recv,
    s_send,
    s_recv,
    g_send,
    g_recv,
):
    fs, nz, d, heads = cfg
    cs = 2 * nz
    f, z, core = lax.axis_index("fsdp"), lax.axis_index("z"), lax.axis_index("core")
    rank = 2 * z + core
    rows = tok.shape[0]
    width = heads * HD
    lanes = w.shape[2] // fs
    grain = w.shape[1]
    own_rows, part = d // fs, d // cs
    hf = p_sum.shape[3] // 2
    plane = Plane(fs)
    ranks = [lax.rem(rank + i, cs) for i in range(1, cs)]
    lanes_of = lambda g: pl.ds(pl.multiple_of(g * lanes, 128), lanes)
    runs = column_segments(cs, d, width, grain)
    block_rows = lambda b: pl.ds(pl.multiple_of(b * rows, rows), rows)
    half_z = lambda h: pl.ds(*halves(nz)[h])

    peers = [dict(z=r // 2, core=lax.rem(r, 2)) for r in ranks]
    peers += [dict(fsdp=p) for p in plane.peers]
    greet(peers)

    def h1_in(i):
        here = h1.at[:, lanes_of(lax.rem(f + 1 + i, fs))]
        return pltpu.make_async_copy(here, h1v.at[i % 2], local.at[4 + i % 2])

    for i in range(min(2, fs)):
        h1_in(i).start()
    om_in = pltpu.make_async_copy(og, om, local.at[2])
    op_in = pltpu.make_async_copy(out_part, op, local.at[3])
    om_in.start()
    op_in.start()
    fg_in = pltpu.make_async_copy(fg, fgv, local.at[6])
    fg_in.start()
    late = [
        pltpu.make_async_copy(a, b, local.at[7 + n])
        for n, (a, b) in enumerate(((w_in, w), (middle_in, middle), (d_middle_in, d_middle)))
    ]
    for copy in late:
        copy.start()
    for r in range(cs):
        cols = slice(r * part, (r + 1) * part)
        vec[0:1, cols] = smalls[r, 0:1, 0:part]
        vec[1:2, cols] = smalls[r, 7:8, 0:part]
    run = cs * rows // block_order.shape[0]
    for b in range(block_order.shape[0]):
        first = block_order[b] * run
        at = slice(b * run, (b + 1) * run)
        pos_row[:, at] = first + lax.broadcasted_iota(jnp.int32, (1, run), 1)
        pos_col[at, :] = first + lax.broadcasted_iota(jnp.int32, (run, 1), 0)
    met(peers)

    om_in.wait()
    o_total = PlaneSum(
        plane,
        lambda g, h: om.at[half_z(h), :, :, lanes_of(g)],
        lambda n, h: orc.at[n, pl.ds(0, halves(nz)[h][1])],
        (o_send, o_recv),
    )
    o_total.start()

    def z_copy(i):
        to = lax.rem(z + i, nz)
        return remote(p_sum.at[to], pz.at[z], z_send.at[to], z_recv.at[z], z=to)

    z_keep = pltpu.make_async_copy(p_sum.at[z], pz.at[z], local.at[0])
    for i in range(1, nz):
        z_copy(i).start()
    z_keep.start()

    op_in.wait()
    ro_line = LineSum(op, ro_in, nz, (ro_send, ro_recv))
    ro_line.first()

    def l_copy(i):
        g = plane.peers[i]
        return remote(pz.at[g], p_all.at[f], l_send.at[i], l_recv.at[f], fsdp=g)

    l_keep = pltpu.make_async_copy(pz.at[f], p_all.at[f], local.at[1])

    def shares_on():
        z_keep.wait()
        for i in range(1, nz):
            back = lax.rem(z + nz - i, nz)
            remote(pz.at[back], pz.at[back], z_send.at[0], z_recv.at[back], z=back).wait_recv()
        for i in range(fs - 1):
            l_copy(i).start()
        l_keep.start()

    tall = query_block(cs * rows)
    for h in range(heads):
        attend_back_head(
            h, width, tall, qkv, pos_col, pos_row, att, lse, d_att, d_qkv, acc
        )
        if h == heads - 1:
            shares_on()
            ro_line.step(1)

    slices = 3 * width // grain
    q_total = PlaneSum(
        plane,
        lambda g, h: qg.at[g, pl.ds(*halves(slices)[h])],
        lambda n, h: qr.at[n, pl.ds(0, halves(slices)[h][1])],
        (q_send, q_recv),
    )

    for i in range(fs):
        g = lax.rem(f + 1 + i, fs)
        h1_in(i).wait()
        part_sum = dot_tn(d_qkv[...], h1v[i % 2])
        qg[g] = part_sum.astype(BF).reshape(slices, grain, lanes)
        if i + 2 < fs:
            h1_in(i + 2).start()
    q_total.start()
    fg_in.wait()
    f_rows = f_grad.shape[0] // fgv.shape[1]
    f_total = PlaneSum(
        plane,
        lambda g, h: fgv.at[pl.ds(g * f_rows + halves(f_rows)[h][0], halves(f_rows)[h][1])],
        lambda n, h: fr.at[n, pl.ds(0, halves(f_rows)[h][1])],
        (f_send, f_recv),
    )

    def hidden(block):
        full = dot(d_qkv[block_rows(block), :], w[...].reshape(3 * width, fs * lanes))
        return [full[:, lanes * g : lanes * g + own_rows] for g in range(fs)]

    def other_step(b, _):
        for g, piece in enumerate(hidden(2 * b + 1 - core)):
            other[b, :, own_rows * g : own_rows * (g + 1)] = piece.astype(BF)
        return 0

    for copy in late:
        copy.wait()
    lax.fori_loop(0, nz, other_step, 0)
    to_partner = remote(other, partner, m_send.at[0], m_recv.at[0], core=1 - core)
    to_partner.start()
    o_total.mid()

    to_partner.wait_recv()

    r_line = LineSum(r_out, r_in, nz, (r_send, r_recv))

    def own_step(i, _):
        b = r_line.order(i)
        for g, piece in enumerate(hidden(2 * b + core)):
            at = slice(own_rows * g, own_rows * (g + 1))
            both = piece + partner[b, :, at].astype(F32)
            r_out[b, :, at] = both.astype(BF)

            @pl.when(b == z)
            def _():
                own[:, at] = both

        r_line.ready(b)
        return 0

    lax.fori_loop(0, nz, own_step, 0)
    for s in range(2, nz - 1):
        ro_line.step(s)
    q_total.mid()
    r_line.step(1)
    step = min(32, rows)
    o_total.end()
    for h in range(2):
        osum[half_z(h)] = o_total.total(h).astype(BF)
    o_line = LineSum(osum, o_in, nz, (os_send, os_recv))
    for s in range(2, nz - 1):
        r_line.step(s)
    o_line.first()

    q_total.end()
    for h in range(2):
        qs[pl.ds(*halves(slices)[h])] = q_total.total(h).astype(BF)

    def run_copy(n):
        dst, at, src, first, count = runs[n]
        here, there = qs.at[pl.ds(first, count)], q_own.at[pl.ds(at, count)]
        if src == dst:
            return pltpu.make_async_copy(here, there, b_send.at[n])
        return remote(here, there, b_send.at[n], b_recv.at[n], z=dst // 2, core=dst % 2)

    for n, run in enumerate(runs):

        @pl.when(rank == run[2])
        def _():
            run_copy(n).start()

    f_total.start()

    ro_line.finish()

    def output_chunk(i, _):
        at = pl.ds(pl.multiple_of(i * step, step), step)
        total = op[z, at, :].astype(F32) + ro_line.others(at)
        out_rows[at, :] = middle[at, :] + total[:, 0:d] + vec[1:2, :]
        return 0

    lax.fori_loop(0, rows // step, output_chunk, 0)
    output[...] = out_rows[...].T.astype(BF)
    o_line.step(1)

    l_keep.wait()
    for g in plane.peers:
        remote(p_all.at[g], p_all.at[g], l_send.at[0], l_recv.at[g], fsdp=g).wait_recv()
    fine = p_all.shape[2]
    whole = p_all[...].reshape(-1, fine, 2 * hf)[: part // fine].reshape(part, 2 * hf)
    ff_half = p_grad.shape[1] // 2
    for k in range(2):
        p_grad[:, k * ff_half : (k + 1) * ff_half] = whole[:, k * hf : k * hf + ff_half].astype(F32)
    for s in range(2, nz - 1):
        o_line.step(s)
    r_line.finish()

    line[...] = jnp.zeros(line.shape, F32)

    def norm_back_chunk(i, _):
        at = pl.ds(pl.multiple_of(i * step, step), step)
        g = own[at, :] + r_line.others(at)
        xhat, rstd = norm_rows(tok[at, :].astype(F32))
        in_rows[at, :] = d_middle[at, :] + norm_back(g, xhat, rstd, vec[0:1, :])
        line[0:1, 0:d] += jnp.sum(g * xhat, axis=0, keepdims=True)
        line[1:2, 0:d] += jnp.sum(g, axis=0, keepdims=True)
        return 0

    lax.fori_loop(0, rows // step, norm_back_chunk, 0)

    input_grad[...] = in_rows[...].T

    head_lanes = pl.ds(pl.multiple_of(rank * width, 128), width)
    line[2:3, head_lanes] = jnp.sum(d_qkv[:, 0:width].astype(F32), axis=0, keepdims=True)
    line[3:4, head_lanes] = jnp.sum(d_qkv[:, 2 * width :].astype(F32), axis=0, keepdims=True)
    line[4:8, 0:d] = sums[0:4, 0:d]
    sm_out[...] = jnp.zeros(sm_out.shape, F32)
    ff_parts = small_grad.shape[0] - 8
    for r in range(cs):
        sm_out[r, 0:8, 0:part] = line[0:8, r * part : (r + 1) * part]
    for k in range(2):
        for j in range(ff_parts):
            sm_out[2 * z + k, 8 + j : 9 + j, 0:part] = sums[
                4:5, k * hf + j * part : k * hf + (j + 1) * part
            ]

    def s_copy(i):
        r = ranks[i]
        here = sm_out.at[r]
        return remote(
            here, sm_in.at[rank], s_send.at[i], s_recv.at[rank], z=r // 2, core=lax.rem(r, 2)
        )

    for i in range(cs - 1):
        s_copy(i).start()
    f_total.mid()
    o_line.finish()
    whole = (osum[z].astype(F32) + o_line.others()).reshape(part, lanes)
    o_grad[...] = whole[:, :own_rows].T
    total = sm_out[rank]
    for i in range(1, cs):
        back = lax.rem(rank + cs - i, cs)
        remote(sm_in.at[back], sm_in.at[back], s_send.at[0], s_recv.at[back], z=z).wait_recv()
        total += sm_in[back]
    sm_f[f] = total

    def g_copy(i):
        return remote(sm_f.at[f], sm_f.at[f], g_send.at[i], g_recv.at[f], fsdp=plane.peers[i])

    for i in range(fs - 1):
        g_copy(i).start()
    for n, run in enumerate(runs):

        @pl.when(rank == run[0])
        def _():
            if run[0] == run[2]:
                run_copy(n).wait()
            else:
                run_copy(n).wait_recv()

    q_grad[...] = q_own[...].reshape(-1, lanes)[:, :own_rows].T.astype(F32)
    f_total.end()
    for h in range(2):
        low, count = (n * fgv.shape[1] for n in halves(f_rows)[h])
        whole = f_total.total(h).reshape(count, fgv.shape[2])
        f_grad[low : low + count, :] = whole[:, : f_grad.shape[1]]
    for g in plane.peers:
        remote(sm_f.at[g], sm_f.at[g], g_send.at[0], g_recv.at[g], fsdp=g).wait_recv()
    total = sm_f[0]
    for g in range(1, fs):
        total += sm_f[g]
    small_grad[...] = total

    for i in range(1, nz):
        z_copy(i).wait_send()
    for i in range(fs - 1):
        l_copy(i).wait_send()
        g_copy(i).wait_send()
    for s in (r_line, o_line, ro_line, o_total, q_total, f_total):
        s.sent()
    to_partner.wait_send()
    for n, run in enumerate(runs):
        if run[0] != run[2]:

            @pl.when(rank == run[2])
            def _():
                run_copy(n).wait_send()

    for i in range(cs - 1):
        s_copy(i).wait_send()


def last_part(cfg, counts, qkv, att, lse, d_att, block_order, w, h1, tok, smalls, sums, middle, d_middle, out_part, p_sum, og, fg):
    fs, nz, d, heads = cfg
    cs = 2 * nz
    rows, length, width = tok.shape[0], qkv.shape[0], heads * HD
    grain, lanes = w.shape[1], w.shape[2] // fs
    q_grains, fc_cols = counts
    small_rows = smalls.shape[1]
    f_rows = fg.shape[0] // fs
    slices = 3 * width // grain
    runs = len(column_segments(cs, d, width, grain))
    part = d // cs
    rest = 2 * (fs - 1)
    rows_low = pltpu.VMEM((nz, rows, d), BF)
    smem = pl.BlockSpec(memory_space=pltpu.SMEM)
    owner = (nz,) + og.shape[1:3] + (lanes,)
    return pl.pallas_call(
        partial(last_kernel, cfg),
        out_shape=(
            shape((d, rows)),
            shape((d, rows), F32),
            shape((d // fs, q_grains * grain), F32),
            shape((part, 2 * fc_cols), F32),
            shape((d // fs, part), F32),
            shape((d // fs, fc_cols), F32),
            shape((small_rows, up(part)), F32),
        ),
        in_specs=[VMEM] * 4 + [smem, HBM, HBM] + [VMEM] * 3 + [HBM] * 2 + [HBM, VMEM, HBM, HBM],
        out_specs=(VMEM,) * 7,
        scratch_shapes=[
            pltpu.VMEM(w.shape, BF),
            pltpu.VMEM((rows, d), F32),
            pltpu.VMEM((rows, d), F32),
            pltpu.VMEM((rows, d), F32),
            pltpu.VMEM((rows, d), F32),
            pltpu.VMEM((length, 1), jnp.int32),
            pltpu.VMEM((1, length), jnp.int32),
            pltpu.VMEM((2, d), F32),
            pltpu.VMEM((fs,) + p_sum.shape[1:], BF),
            pltpu.VMEM((q_grains, grain, lanes), BF),
            pltpu.VMEM(fg.shape, BF),
            pltpu.VMEM((rest, f_rows - f_rows // 2) + fg.shape[1:], BF),
            pltpu.VMEM((length, 3 * width), BF),
            pltpu.VMEM((length, 2 * HD), F32),
            pltpu.VMEM((2, length, lanes), BF),
            pltpu.VMEM((fs, slices, grain, lanes), BF),
            pltpu.VMEM((rest, slices - slices // 2, grain, lanes), BF),
            pltpu.VMEM((slices, grain, lanes), BF),
            pltpu.VMEM(og.shape, BF),
            pltpu.VMEM((rest, nz - nz // 2) + owner[1:], BF),
            pltpu.VMEM(owner, BF),
            pltpu.VMEM((nz + 1,) + owner[1:], BF),
            pltpu.VMEM(out_part.shape, BF),
            pltpu.VMEM((nz + 1,) + out_part.shape[1:], BF),
            pltpu.VMEM(p_sum.shape, BF),
            rows_low,
            rows_low,
            pltpu.VMEM((rows, d), F32),
            rows_low,
            pltpu.VMEM((nz + 1, rows, d), BF),
            pltpu.VMEM((8, width * cs), F32),
            pltpu.VMEM((cs, small_rows, up(part)), F32),
            pltpu.VMEM((cs, small_rows, up(part)), F32),
            pltpu.VMEM((fs, small_rows, up(part)), F32),
        ]
        + sems(nz, nz, fs, fs, 10, rest + 2, rest + 2, rest + 2, rest + 2, nz, nz + 1)
        + sems(nz, nz + 1)
        + sems(rest + 2, rest + 2, 1, 1, nz, nz + 1, runs, runs, cs, cs, fs, fs),
        name="last",
        compiler_params=pltpu.CompilerParams(
            collective_id=2, has_side_effects=True, vmem_limit_bytes=62 * 2**20
        ),
    )(
        qkv,
        att,
        lse,
        d_att,
        block_order,
        w,
        h1,
        tok,
        smalls,
        sums,
        middle,
        d_middle,
        out_part,
        p_sum,
        og,
        fg,
    )


def finish_kernel(*refs):
    vectors, refs = refs[0], refs[1:]
    big = 6
    ins, outs, smalls = refs[:big], refs[big : 2 * big], refs[2 * big : 2 * big + 9]
    held, line, came, left = refs[2 * big + 9 : 3 * big + 9], refs[-3], refs[-2], refs[-1]
    reads = [pltpu.make_async_copy(ins[n], held[n], came.at[n]) for n in range(big)]
    writes = [pltpu.make_async_copy(held[n], outs[n], left.at[n]) for n in range(big)]
    for read in reads:
        read.start()
    part = smalls[0].shape[0]
    for n in range(8):
        smalls[n][...] = vectors[n : n + 1, 0:part].reshape(part)
    for n in range(vectors.shape[0] - 8):
        line[:, n * part : (n + 1) * part] = vectors[8 + n : 9 + n, 0:part]
    smalls[8][...] = line[...].reshape(line.shape[1])
    for read, write in zip(reads, writes):
        read.wait()
        write.start()
    for write in writes:
        write.wait()


def finish(vectors, part, arrays):
    kinds = [shape(a.shape, a.dtype) for a in arrays]
    long = (vectors.shape[0] - 8) * part
    smalls = [shape((part,), F32)] * 8 + [shape((long,), F32)]
    return pl.pallas_call(
        finish_kernel,
        out_shape=kinds + smalls,
        in_specs=[VMEM] + [HBM] * len(arrays),
        out_specs=[HBM] * len(arrays) + [VMEM] * 9,
        scratch_shapes=[pltpu.VMEM(a.shape, a.dtype) for a in arrays]
        + [pltpu.VMEM((1, long), F32)]
        + sems(len(arrays), len(arrays)),
        name="finish",
        compiler_params=pltpu.CompilerParams(vmem_limit_bytes=62 * 2**20),
    )(vectors, *arrays)


def body(
    tokens,
    block_order,
    cotangent,
    pre_attn_gain,
    pre_attn_bias,
    qkv_weight,
    query_bias,
    value_bias,
    out_weight,
    out_bias,
    pre_mlp_gain,
    pre_mlp_bias,
    fc_weight,
    fc_bias,
    proj_weight,
    proj_bias,
):
    fs, nz = lax.axis_size("fsdp"), lax.axis_size("z")
    cs = nz * 2
    rows, d = tokens.shape[1], tokens.shape[2]
    length = rows * cs
    heads_all = d // HD
    heads = -(-heads_all // cs)
    width = heads * HD
    part, own_rows = d // cs, d // fs
    fc_cols = fc_weight.shape[1]
    hf = up(fc_cols)

    cfg = (fs, nz, d, heads)
    h1, w, qkv, att, lse, smalls, p2, o_all, a_own, tok = start(
        cfg,
        tokens[0].T,
        qkv_weight,
        proj_weight.T,
        out_weight,
        block_order,
        (
            pre_attn_gain,
            pre_attn_bias,
            query_bias,
            value_bias,
            out_bias,
            pre_mlp_gain,
            pre_mlp_bias,
            proj_bias,
            fc_bias,
        ),
        hf,
    )
    middle, d_middle, d_att, out_part, fc_grad, p_sum, og, sums = middle_part(
        cfg, a_own, tok, cotangent[0].T, smalls, p2, fc_weight, o_all
    )
    fg = fc_grad.reshape(-1, math.gcd(own_rows, 16), hf)
    output, input_grad, qkv_grad, proj_grad, out_grad, fc_grad, g = last_part(
        cfg,
        (qkv_weight.shape[1] // w.shape[1], fc_cols),
        qkv,
        att,
        lse,
        d_att,
        block_order,
        w,
        h1,
        tok,
        smalls,
        sums,
        middle,
        d_middle,
        out_part,
        p_sum,
        og,
        fg,
    )
    output, input_grad, qkv_grad, proj_grad, out_grad, fc_grad, *g = finish(
        g, part, (output, input_grad, qkv_grad, proj_grad, out_grad, fc_grad)
    )
    return (
        output.T[None],
        input_grad.T[None],
        g[0],
        g[1],
        qkv_grad,
        g[2],
        g[3],
        out_grad,
        g[4],
        g[5],
        g[6],
        fc_grad,
        g[8],
        proj_grad.T,
        g[7],
    )


def solution(mesh):
    fs, cs = mesh.shape["fsdp"], mesh.shape["ctx"]
    split = Mesh(mesh.devices.reshape(fs, cs // 2, 2), ("fsdp", "z", "core"))
    rows = P("fsdp", CTX, None)
    weight = P("fsdp", CTX)
    vector = P(CTX)
    in_specs = (
        rows,
        P(),
        rows,
        vector,
        vector,
        weight,
        vector,
        vector,
        weight,
        vector,
        vector,
        vector,
        weight,
        vector,
        weight,
        vector,
    )
    out_specs = (
        rows,
        rows,
        vector,
        vector,
        weight,
        vector,
        vector,
        weight,
        vector,
        vector,
        vector,
        weight,
        vector,
        weight,
        vector,
    )
    return jax.shard_map(body, mesh=split, in_specs=in_specs, out_specs=out_specs, check_vma=False)
```

```python
from functools import partial
import math

import jax
import jax.numpy as jnp
from jax import lax
from jax.experimental import pallas as pl
from jax.experimental.pallas import tpu as pltpu
from jax.sharding import Mesh
from jax.sharding import PartitionSpec as P

HD = 64
EPS = 1e-05
FLOOR = -1e30
BF = jnp.bfloat16
F32 = jnp.float32
CTX = ("z", "core")
MESH = pl.DeviceIdType.MESH
VMEM = pl.BlockSpec(memory_space=pltpu.VMEM)
HBM = pl.BlockSpec(memory_space=pl.ANY)
GELU_A = math.sqrt(2.0 / math.pi)
GELU_B = 0.044715


def up(n):
    return -(-n // 128) * 128


def sems(*counts):
    return [pltpu.SemaphoreType.DMA(c if isinstance(c, tuple) else (c,)) for c in counts]


def shape(dims, kind=BF):
    return jax.ShapeDtypeStruct(dims, kind)


def dot(a, b):
    return jnp.dot(a, b, preferred_element_type=F32)


def dot_nt(a, b):
    return lax.dot_general(a, b, (((1,), (1,)), ((), ())), preferred_element_type=F32)


def dot_tn(a, b):
    return lax.dot_general(a, b, (((0,), (0,)), ((), ())), preferred_element_type=F32)


def norm_rows(rows):
    centred = rows - jnp.mean(rows, axis=-1, keepdims=True)
    rstd = lax.rsqrt(jnp.mean(centred * centred, axis=-1, keepdims=True) + EPS)
    return centred * rstd, rstd


def norm_back(upstream, xhat, rstd, gain):
    inner = upstream * gain
    return rstd * (
        inner
        - jnp.mean(inner, axis=-1, keepdims=True)
        - xhat * jnp.mean(inner * xhat, axis=-1, keepdims=True)
    )


def gelu_pair(v):
    sq = v * v
    t = jnp.tanh(GELU_A * v * (1.0 + GELU_B * sq))
    half = 0.5 * (1.0 + t)
    slope = half + 0.5 * v * (1.0 - t * t) * (GELU_A * (1.0 + 3.0 * GELU_B * sq))
    return v * half, slope


def positions(order_table, rows):
    block = rows // order_table.shape[0]
    return (order_table[:, None] * block + jnp.arange(block, dtype=jnp.int32)[None]).reshape(rows)


def remote(src, dst, send, recv, **to):
    return pltpu.make_async_remote_copy(
        src_ref=src, dst_ref=dst, send_sem=send, recv_sem=recv, device_id=to, device_id_type=MESH
    )


def column_segments(ranks, d, width, grain):
    own = 3 * d // ranks
    runs = []
    for src in range(ranks):
        for part in range(3):
            for dst in range(ranks):
                low = part * d + dst * width
                first = max(src * own, low)
                last = min((src + 1) * own, low + width, (part + 1) * d)
                if first < last:
                    at = part * width + first - low
                    runs.append(
                        (src, (first - src * own) // grain, dst, at // grain, (last - first) // grain)
                    )
    return runs


def column_grain(d, ranks):
    return math.gcd(math.gcd(3 * d // ranks, HD), 8)


def greet(peers):
    barrier = pltpu.get_barrier_semaphore()
    for peer in peers:
        pl.semaphore_signal(barrier, inc=1, device_id=peer, device_id_type=MESH)


def met(peers):
    pl.semaphore_wait(pltpu.get_barrier_semaphore(), len(peers))


class Line:
    def __init__(self, at, size, sems):
        self.at, self.size = at, size
        self.right, self.left, self.recv = sems
        self.z = lax.axis_index("z")

    def copy(self, block, way):
        send = (self.right if way > 0 else self.left).at[block]
        at = self.at(block)
        return remote(at, at, send, self.recv.at[block], z=self.z + way)

    def start(self):
        @pl.when(self.z < self.size - 1)
        def _():
            self.copy(self.z, 1).start()

        @pl.when(self.z > 0)
        def _():
            self.copy(self.z, -1).start()

    def step(self, s, then=None):
        @pl.when(self.z >= s)
        def _():
            block = self.z - s
            self.copy(block, 1).wait_recv()

            @pl.when(self.z < self.size - 1)
            def _():
                self.copy(block, 1).start()

            if then is not None:
                then(block)

        @pl.when(self.z + s < self.size)
        def _():
            block = self.z + s
            self.copy(block, -1).wait_recv()

            @pl.when(self.z > 0)
            def _():
                self.copy(block, -1).start()

            if then is not None:
                then(block)

    def finish(self):
        for s in range(self.size):

            @pl.when((self.z >= s) & (self.z < self.size - 1))
            def _():
                self.copy(self.z - s, 1).wait_send()

            @pl.when((self.z + s < self.size) & (self.z > 0))
            def _():
                self.copy(self.z + s, -1).wait_send()


class LineSum:
    def __init__(self, parts, came, size, sems):
        self.parts = parts if callable(parts) else (lambda block: parts.at[block])
        self.came, self.size = came, size
        self.send, self.recv = sems
        self.z = lax.axis_index("z")

    def copy(self, block, way):
        place = block + 1 if way > 0 else block
        there = self.came.at[place]
        return remote(
            self.parts(block), there, self.send.at[block], self.recv.at[place], z=self.z + way
        )

    def order(self, i):
        near = self.z < self.size // 2
        ahead = self.size - 1 - self.z
        from_low = jnp.where(i < ahead, self.size - 1 - i, i - ahead)
        from_high = jnp.where(i < self.z, i, self.size - 1 - (i - self.z))
        return jnp.where(near, from_low, from_high)

    def ready(self, block):
        @pl.when((self.z == 0) & (block > 0))
        def _():
            self.copy(block, 1).start()

        @pl.when((self.z == self.size - 1) & (block < self.size - 1))
        def _():
            self.copy(block, -1).start()

    def first(self, hops=None):
        for way, edge in ((1, 0), (-1, self.size - 1)):

            @pl.when(self.z == edge)
            def _():
                for hop in range(self.size - 1, 0, -1) if hops is None else hops:
                    self.copy(self.z + way * hop, way).start()

    def add_on(self, block, way):
        self.copy(block, way).wait_recv()
        came = self.came[block + 1 if way > 0 else block]
        part = self.parts(block)
        part[...] = (part[...].astype(F32) + came.astype(F32)).astype(part.dtype)
        self.copy(block, way).start()

    def step(self, s):
        right, left = self.z + self.size - 1 - s, s - (self.size - 1 - self.z)

        @pl.when((self.z > 0) & (right < self.size) & (right > self.z))
        def _():
            self.add_on(right, 1)

        @pl.when((self.z < self.size - 1) & (left >= 0) & (left < self.z))
        def _():
            self.add_on(left, -1)

    def finish(self):
        @pl.when(self.z > 0)
        def _():
            self.copy(self.z, 1).wait_recv()

        @pl.when(self.z == 0)
        def _():
            self.came[self.z + 1] = jnp.zeros(self.came.shape[1:], self.came.dtype)

        @pl.when(self.z < self.size - 1)
        def _():
            self.copy(self.z, -1).wait_recv()

        @pl.when(self.z == self.size - 1)
        def _():
            self.came[self.z] = jnp.zeros(self.came.shape[1:], self.came.dtype)

    def others(self, *at):
        here = (self.z,) + at
        there = (self.z + 1,) + at
        return self.came[here].astype(F32) + self.came[there].astype(F32)

    def sent(self):
        for block in range(self.size):

            @pl.when(self.z < block)
            def _():
                self.copy(block, 1).wait_send()

            @pl.when(self.z > block)
            def _():
                self.copy(block, -1).wait_send()


def halves(n):
    return ((0, n // 2), (n // 2, n - n // 2))


class Plane:
    def __init__(self, size):
        self.size, self.f = size, lax.axis_index("fsdp")
        self.square = size == 4
        f = self.f
        self.peers = [lax.rem(f + i, size) for i in range(1, size)]
        if self.square:
            self.x, self.y, self.far = f + 1 - 2 * lax.rem(f, 2), lax.rem(f + 2, 4), 3 - f
            self.peers = [self.x, self.y, self.far]


class PlaneGather:
    def __init__(self, plane, at, sems):
        self.p, self.at = plane, at
        self.send, self.recv = sems
        f = plane.f
        if plane.square:
            x, y = plane.x, plane.y
            self.early = [(f, 0, x), (f, 1, y), (f, 0, y), (f, 1, x)]
            self.late = [(x, 0, y), (y, 1, x)]
        else:
            self.early = [(f, h, g) for g in plane.peers for h in range(2)]
            self.late = []

    def copy(self, n, move):
        g, half, to = move
        at = self.at(g, half)
        return remote(at, at, self.send.at[n], self.recv.at[g, half], fsdp=to)

    def arrive(self, g, half):
        at = self.at(g, half)
        remote(at, at, self.send.at[0], self.recv.at[g, half], fsdp=g).wait_recv()

    def start(self):
        for n, move in enumerate(self.early):
            self.copy(n, move).start()

    def mid(self):
        for n, move in enumerate(self.late):
            self.arrive(move[0], move[1])
            self.copy(len(self.early) + n, move).start()

    def end(self, then=None, stages=(0, 1)):
        known = [(m[0], m[1]) for m in self.late]
        peers = self.p.peers
        groups = (peers[:2], peers[2:]) if self.p.square else (peers, [])
        for stage in stages:
            for g in groups[stage]:
                for half in range(2):
                    if not any(g is a and half == b for a, b in known):
                        self.arrive(g, half)
                if then is not None:
                    then(g)

    def sent(self):
        for n, move in enumerate(self.early + self.late):
            self.copy(n, move).wait_send()


class PlaneSum:
    def __init__(self, plane, at, came, sems):
        self.p, self.at, self.came = plane, at, came
        self.send, self.recv = sems
        if plane.square:
            x, y, far = plane.x, plane.y, plane.far
            self.early = [(far, 0, x, 0), (far, 1, y, 1), (x, 0, x, 2), (y, 1, y, 3)]
            self.late = [(y, 0, y, 4), (x, 1, x, 5)]
            self.mine = [[2, 4], [3, 5]]
        else:
            n = plane.size
            self.early = [
                (g, h, g, 2 * i + h) for i, g in enumerate(plane.peers) for h in range(2)
            ]
            self.late = []
            self.mine = [[2 * i + h for i in range(n - 1)] for h in range(2)]

    def copy(self, move):
        g, half, to, slot = move
        return remote(
            self.at(g, half), self.came(slot, half), self.send.at[slot], self.recv.at[slot], fsdp=to
        )

    def arrive(self, slot, half):
        there = self.came(slot, half)
        remote(
            there, there, self.send.at[slot], self.recv.at[slot], fsdp=self.p.peers[0]
        ).wait_recv()

    def start(self):
        for move in self.early:
            self.copy(move).start()

    def mid(self):
        for slot, move in enumerate(self.late):
            self.arrive(slot, move[1])
            at, came = self.at(move[0], move[1]), self.came(slot, move[1])
            at[...] = (at[...].astype(F32) + came[...].astype(F32)).astype(at.dtype)
            self.copy(move).start()

    def end(self):
        for half in range(2):
            for slot in self.mine[half]:
                self.arrive(slot, half)

    def total(self, half):
        out = self.at(self.p.f, half)[...].astype(F32)
        for slot in self.mine[half]:
            out += self.came(slot, half)[...].astype(F32)
        return out

    def sent(self):
        for move in self.early + self.late:
            self.copy(move).wait_send()


def query_block(length):
    return max(128, min(256, length, 256 * 1024 // length))


def attend_head(h, width, q_block, qkv, pos_col, pos_row, out, lse):
    rows = qkv.shape[0]
    k = qkv[:, width + h * HD : width + (h + 1) * HD]
    v = qkv[:, 2 * width + h * HD : 2 * width + (h + 1) * HD]
    for b in range(rows // q_block):
        at = slice(b * q_block, (b + 1) * q_block)
        q = qkv[at, h * HD : (h + 1) * HD] * BF(HD**-0.5)
        s = dot_nt(k, q)
        s = jnp.where(pos_col[...] <= pos_row[:, at], s, FLOOR)
        top = jnp.max(s, axis=0, keepdims=True)
        p = jnp.exp(s - top)
        total = jnp.sum(p, axis=0, keepdims=True)
        o = dot_tn(v, p.astype(BF)) * (1.0 / total)
        out[at, h * HD : (h + 1) * HD] = o.T.astype(BF)
        lse[h : h + 1, at] = top + jnp.log(total)


def attend_back_head(h, width, q_block, qkv, pos_col, pos_row, out, lse, dout, dqkv, acc):
    rows = qkv.shape[0]
    k = qkv[:, width + h * HD : width + (h + 1) * HD]
    v = qkv[:, 2 * width + h * HD : 2 * width + (h + 1) * HD]
    for b in range(rows // q_block):
        at = slice(b * q_block, (b + 1) * q_block)
        q = qkv[at, h * HD : (h + 1) * HD] * BF(HD**-0.5)
        do = dout[at, h * HD : (h + 1) * HD]
        o = out[at, h * HD : (h + 1) * HD]
        delta = jnp.sum(do.astype(F32).T * o.astype(F32).T, axis=0, keepdims=True)
        s = dot_nt(k, q)
        p = jnp.where(pos_col[...] <= pos_row[:, at], jnp.exp(s - lse[h : h + 1, at]), 0.0)
        dp = dot_nt(v, do)
        ds = (p * (dp - delta)).astype(BF)
        dq = dot_tn(k, ds) * (HD**-0.5)
        dqkv[at, h * HD : (h + 1) * HD] = dq.T.astype(BF)
        dk = dot(ds, q)
        dv = dot(p.astype(BF), do)
        if b == 0:
            acc[:, :HD] = dk
            acc[:, HD:] = dv
        else:
            acc[:, :HD] += dk
            acc[:, HD:] += dv
    dqkv[:, width + h * HD : width + (h + 1) * HD] = acc[:, :HD].astype(BF)
    dqkv[:, 2 * width + h * HD : 2 * width + (h + 1) * HD] = acc[:, HD:].astype(BF)


def start_kernel(
    cfg,
    tok_cols,
    qkv_own,
    proj_cols,
    out_own,
    block_order,
    gain_one,
    shift_one,
    query_shift,
    value_shift,
    out_shift,
    gain_two,
    shift_two,
    proj_shift,
    fc_shift,
    h1_out,
    w_out,
    qkv,
    att,
    lse,
    smalls,
    p2,
    o_all,
    a_own,
    tok,
    h1,
    w,
    landed,
    wq,
    pj,
    ot,
    pos_col,
    pos_row,
    toks,
    vecs,
    small,
    p1,
    small_send,
    small_recv,
    q_send,
    q_recv,
    q_local,
    x_send,
    x_recv,
    t_right,
    t_left,
    t_recv,
    c_send,
    c_recv,
    p1_send,
    p1_recv,
    p2_send,
    p2_recv,
    p_local,
    a_send,
    a_recv,
    o_right,
    o_left,
    o_recv,
    ox_send,
    ox_recv,
    oc_send,
    oc_recv,
):
    fs, nz, d, heads = cfg
    cs = 2 * nz
    f, z, core = lax.axis_index("fsdp"), lax.axis_index("z"), lax.axis_index("core")
    rank = 2 * z + core
    rows, lanes = tok_cols.shape[1], wq.shape[2]
    width = heads * HD
    grain = wq.shape[1]
    own_rows = d // fs
    part = d // cs
    lanes_of = lambda g: pl.ds(pl.multiple_of(g * lanes, 128), lanes)
    runs = column_segments(cs, d, width, grain)
    plane = Plane(fs)
    planes = plane.peers

    landed[...] = jnp.zeros(landed.shape, BF)
    ranks = [lax.rem(rank + i, cs) for i in range(1, cs)]
    peers = [dict(z=r // 2, core=lax.rem(r, 2)) for r in ranks] + [dict(fsdp=p) for p in planes]
    greet(peers)

    fine = ot.shape[1]
    if lanes > own_rows:
        wq[:, :, own_rows:] = jnp.zeros((wq.shape[0], grain, lanes - own_rows), BF)
        ot[:, :, own_rows:] = jnp.zeros((ot.shape[0], fine, lanes - own_rows), BF)
    wq[:, :, 0:own_rows] = qkv_own[...].T.reshape(wq.shape[0], grain, own_rows)
    ot[:, :, 0:own_rows] = out_own[...].T.reshape(ot.shape[0], fine, own_rows)
    pj[...] = jnp.zeros(pj.shape, BF)
    ff_half, hf = proj_cols.shape[1] // 2, pj.shape[2] // 2
    for k in range(2):
        pj[0 : part // fine, :, k * hf : k * hf + ff_half] = proj_cols[
            :, k * ff_half : (k + 1) * ff_half
        ].reshape(part // fine, fine, ff_half)
    tok[...] = tok_cols[...].T
    toks[rank] = tok[...]
    small[...] = jnp.zeros(small.shape, F32)
    for n, v in enumerate(
        (
            gain_one,
            shift_one,
            query_shift,
            value_shift,
            out_shift,
            gain_two,
            shift_two,
            proj_shift,
        )
    ):
        small[n : n + 1, 0:part] = v[...].astype(F32).reshape(1, part)
    fc_line = fc_shift[...].astype(F32).reshape(1, fc_shift.shape[0])
    for j in range(small.shape[0] - 8):
        small[8 + j : 9 + j, 0:part] = fc_line[:, j * part : (j + 1) * part]
    met(peers)
    keep_out = pltpu.make_async_copy(ot, o_all.at[rank, :, :, lanes_of(f)], p_local.at[0])
    keep_out.start()

    def run_copy(n):
        src, first, dst, at, count = runs[n]
        here, there = wq.at[pl.ds(first, count)], landed.at[pl.ds(at, count)]
        if src == dst:
            return pltpu.make_async_copy(here, there, q_local.at[n])
        return remote(here, there, q_send.at[n], q_recv.at[n], z=dst // 2, core=dst % 2)

    for n, run in enumerate(runs):

        @pl.when(rank == run[0])
        def _():
            run_copy(n).start()

    def small_copy(i):
        r = ranks[i]
        to = smalls.at[rank]
        return remote(small, to, small_send.at[i], small_recv.at[rank], z=r // 2, core=lax.rem(r, 2))

    for i in range(cs - 1):
        small_copy(i).start()

    share = p1.shape[1]

    def p1_copy(i):
        here = pj.at[pl.ds(planes[i] * share, share)]
        return remote(here, p1.at[f], p1_send.at[i], p1_recv.at[f], fsdp=planes[i])


    def ox_copy(i, block, here=None):
        at = o_all.at[2 * block + core, :, :, lanes_of(f)]
        here = at if here is None else here
        return remote(here, at, ox_send.at[i, block], ox_recv.at[f, block], fsdp=planes[i])

    def ox_arrival(g, block):
        at = o_all.at[2 * block + core, :, :, lanes_of(g)]
        return remote(at, at, ox_send.at[0, block], ox_recv.at[g, block], fsdp=g)

    def oc_copy(g, block, here=None):
        at = o_all.at[2 * block + core, :, :, lanes_of(g)]
        here = at if here is None else here
        return remote(here, at, oc_send.at[g, block], oc_recv.at[g, block], core=1 - core)

    def oc_arrival(g, block):
        at = o_all.at[2 * block + 1 - core, :, :, lanes_of(g)]
        return remote(at, at, oc_send.at[g, block], oc_recv.at[g, block], core=1 - core)

    def out_block(block, here=None):
        for i in range(fs - 1):
            ox_copy(i, block, here).start()
        oc_copy(f, block, here).start()

    out_block(z, ot)

    for n, run in enumerate(runs):

        @pl.when(rank == run[2])
        def _():
            if run[0] == run[2]:
                run_copy(n).wait()
            else:
                run_copy(n).wait_recv()

    share_w = w.shape[0] // fs
    turned = landed[...].reshape(3 * width, lanes)[:, :own_rows].T
    w[pl.ds(f * share_w, share_w)] = turned.reshape(share_w, w.shape[1], 3 * width)
    w_at = lambda g, h: w.at[pl.ds(g * share_w + halves(share_w)[h][0], halves(share_w)[h][1])]
    gather = PlaneGather(plane, w_at, (x_send, x_recv))
    gather.start()

    line = Line(lambda b: toks.at[2 * b + core], nz, (t_right, t_left, t_recv))

    def pass_on(block):
        at = toks.at[2 * block + core]
        return remote(at, at, c_send.at[block], c_recv.at[block], core=1 - core)

    def arrival(block):
        at = toks.at[2 * block + 1 - core]
        return remote(at, at, c_send.at[block], c_recv.at[block], core=1 - core)

    line.start()
    pass_on(z).start()

    smalls[rank] = small[...]
    vecs[...] = jnp.zeros(vecs.shape, F32)
    length = cs * rows
    run = length // block_order.shape[0]
    for b in range(block_order.shape[0]):
        first = block_order[b] * run
        at = slice(b * run, (b + 1) * run)
        pos_row[:, at] = first + lax.broadcasted_iota(jnp.int32, (1, run), 1)
        pos_col[at, :] = first + lax.broadcasted_iota(jnp.int32, (run, 1), 0)
    if h1.shape[1] > d:
        h1[:, d:] = jnp.zeros((length, h1.shape[1] - d), BF)
    for i in range(1, cs):
        back = lax.rem(rank + cs - i, cs)
        remote(small, smalls.at[back], small_send.at[i - 1], small_recv.at[back], z=z).wait_recv()
    for r in range(cs):
        vecs[:, part * r : part * (r + 1)] = smalls[r, 0:8, 0:part]

    step = min(32, rows)

    def norm_block(block):
        def chunk(i, _):
            at = pl.multiple_of(i * step, step)
            xhat, _ = norm_rows(toks[block, pl.ds(at, step), :].astype(F32))
            h = (xhat * vecs[0:1, 0:d] + vecs[1:2, 0:d]).astype(BF)
            to = pl.ds(pl.multiple_of(block * rows + i * step, step), step)
            h1[to, 0:d] = h
            return 0

        lax.fori_loop(0, rows // step, chunk, 0)

    def place(i):
        hop = (i + 1) // 2
        return jnp.where(lax.rem(i, 2) == 1, z - hop, z + hop)

    def take(i, _):
        block = place(i)

        @pl.when((block >= 0) & (block < nz))
        def _():
            @pl.when(block < z)
            def _():
                line.copy(block, 1).wait_recv()

                @pl.when(z < nz - 1)
                def _():
                    line.copy(block, 1).start()

            @pl.when(block > z)
            def _():
                line.copy(block, -1).wait_recv()

                @pl.when(z > 0)
                def _():
                    line.copy(block, -1).start()

            @pl.when(block != z)
            def _():
                pass_on(block).start()

            norm_block(2 * block + core)
            arrival(block).wait_recv()
            norm_block(2 * block + 1 - core)

        return 0

    tall = 2 * rows
    head_lanes = pl.ds(pl.multiple_of(rank * width, 128), width)

    def project(i, _):
        block = place(i)

        @pl.when((block >= 0) & (block < nz))
        def _():
            at = pl.ds(pl.multiple_of(block * tall, tall), tall)
            full = dot(h1[at, 0:d], w[...].reshape(d, 3 * width))
            qkv[at, 0:width] = (full[:, 0:width] + vecs[2:3, head_lanes]).astype(BF)
            qkv[at, width : 2 * width] = full[:, width : 2 * width].astype(BF)
            qkv[at, 2 * width :] = (full[:, 2 * width :] + vecs[3:4, head_lanes]).astype(BF)

        return 0

    lax.fori_loop(0, 3, take, 0)
    gather.mid()
    p1[f] = pj[pl.ds(f * share, share)]
    for i in range(fs - 1):
        p1_copy(i).start()
    lax.fori_loop(3, 2 * nz - 3, take, 0)

    keep_out.wait()
    out_line = Line(
        lambda b: o_all.at[2 * b + core, :, :, lanes_of(f)], nz, (o_right, o_left, o_recv)
    )
    out_line.start()
    gather.end()
    lax.fori_loop(0, 2 * nz - 3, project, 0)
    lax.fori_loop(2 * nz - 3, 2 * nz - 1, take, 0)
    lax.fori_loop(2 * nz - 3, 2 * nz - 1, project, 0)
    keep_h1 = pltpu.make_async_copy(h1, h1_out, p_local.at[1])
    keep_w = pltpu.make_async_copy(w, w_out, p_local.at[2])
    keep_h1.start()
    keep_w.start()
    out_line.step(1, out_block)

    for g in planes:
        remote(p1.at[g], p1.at[g], p1_send.at[0], p1_recv.at[g], fsdp=g).wait_recv()

    def p2_copy(i):
        to = lax.rem(z + i, nz)
        return remote(p1.at[to], p2.at[z], p2_send.at[to], p2_recv.at[z], z=to)

    def a_copy(i, pair):
        r = ranks[i]
        here = att.at[pl.ds(pl.multiple_of(r * rows, rows), rows), pl.ds(pair * 128, 128)]
        there = a_own.at[:, pl.ds(pl.multiple_of(rank * width + pair * 128, 128), 128)]
        return remote(
            here, there, a_send.at[i, pair], a_recv.at[rank, pair], z=r // 2, core=lax.rem(r, 2)
        )

    for h in range(heads):
        attend_head(h, width, query_block(cs * rows), qkv, pos_col, pos_row, att, lse)
        if h + 2 < nz:
            out_line.step(h + 2, out_block)
        if h % 2 == 1:
            for i in range(cs - 1):
                a_copy(i, h // 2).start()
        if h == 0:
            for i in range(1, nz):
                p2_copy(i).start()
            p2[z] = p1[z]
    for s in range(heads + 2, nz):
        out_line.step(s, out_block)
    a_own[:, head_lanes] = att[pl.ds(pl.multiple_of(rank * rows, rows), rows), :]

    for g in planes:
        for b in range(nz):
            ox_arrival(g, b).wait_recv()
            oc_copy(g, b).start()
    for pair in range(width // 128):
        for i in range(1, cs):
            back = lax.rem(rank + cs - i, cs)
            to = a_own.at[:, pl.ds(pl.multiple_of(back * width + pair * 128, 128), 128)]
            remote(to, to, a_send.at[0, 0], a_recv.at[back, pair], z=z).wait_recv()
    for i in range(1, nz):
        back = lax.rem(z + nz - i, nz)
        remote(p2.at[back], p2.at[back], p2_send.at[0], p2_recv.at[back], z=back).wait_recv()
    for g in range(fs):
        for b in range(nz):
            oc_arrival(g, b).wait_recv()
    keep_h1.wait()
    keep_w.wait()

    for n, run in enumerate(runs):
        if run[0] != run[2]:

            @pl.when(rank == run[0])
            def _():
                run_copy(n).wait_send()

    for i in range(cs - 1):
        small_copy(i).wait_send()
        for pair in range(width // 128):
            a_copy(i, pair).wait_send()
    gather.sent()
    for i in range(1, nz):
        p2_copy(i).wait_send()
    for i in range(fs - 1):
        p1_copy(i).wait_send()
        for b in range(nz):
            ox_copy(i, b).wait_send()
    for g in range(fs):
        for b in range(nz):
            oc_copy(g, b).wait_send()
    line.finish()
    out_line.finish()
    for b in range(nz):
        pass_on(b).wait_send()


def start(cfg, tok_cols, qkv_own, proj_cols, out_own, block_order, vectors, hf):
    fs, nz, d, heads = cfg
    cs = 2 * nz
    rows, cols = tok_cols.shape[1], qkv_own.shape[1]
    width, length = heads * HD, rows * cs
    part, lanes = d // cs, up(d // fs)
    grain, fine = column_grain(d, cs), math.gcd(part, 8)
    rows_grain = math.gcd(d // fs, 16)
    share = -(-part // (fine * fs))
    runs = len(column_segments(cs, d, width, grain))
    pairs = width // 128
    small = (8 + vectors[8].shape[0] // part, up(part))
    smem = pl.BlockSpec(memory_space=pltpu.SMEM)
    h1 = (length, up(d))
    w = (d // rows_grain, rows_grain, 3 * width)
    return pl.pallas_call(
        partial(start_kernel, cfg),
        out_shape=(
            shape(h1),
            shape(w),
            shape((length, 3 * width)),
            shape((length, width)),
            shape((heads, length), F32),
            shape((cs,) + small, F32),
            shape((nz, share, fine, 2 * hf)),
            shape((cs, part // fine, fine, fs * lanes)),
            shape((rows, cs * width)),
            shape((rows, d)),
        ),
        in_specs=[VMEM] * 4 + [smem] + [VMEM] * 9,
        out_specs=(HBM, HBM) + (VMEM,) * 5 + (HBM, VMEM, VMEM),
        scratch_shapes=[
            pltpu.VMEM(h1, BF),
            pltpu.VMEM(w, BF),
            pltpu.VMEM((3 * width // grain, grain, lanes), BF),
            pltpu.VMEM((cols // grain, grain, lanes), BF),
            pltpu.VMEM((fs * share, fine, 2 * hf), BF),
            pltpu.VMEM((part // fine, fine, lanes), BF),
            pltpu.VMEM((length, 1), jnp.int32),
            pltpu.VMEM((1, length), jnp.int32),
            pltpu.VMEM((cs, rows, d), BF),
            pltpu.VMEM((8, width * cs), F32),
            pltpu.VMEM(small, F32),
            pltpu.VMEM((fs, share, fine, 2 * hf), BF),
        ]
        + sems(cs, cs, runs, runs, runs, 2 * fs, (fs, 2), nz, nz, nz, nz, nz)
        + sems(fs, fs, nz, nz, 3, (cs, pairs), (cs, pairs))
        + sems(nz, nz, nz, (fs, nz), (fs, nz), (fs, nz), (fs, nz)),
        name="start",
        compiler_params=pltpu.CompilerParams(
            collective_id=0, has_side_effects=True, vmem_limit_bytes=60 * 2**20
        ),
    )(tok_cols, qkv_own, proj_cols, out_own, block_order, *vectors)


def middle_kernel(
    cfg,
    a_own,
    tok,
    ct_cols,
    smalls,
    p2,
    fc,
    o_all,
    middle,
    d_middle,
    d_att,
    out_part,
    fc_grad,
    p_sum,
    og,
    sums,
    vec,
    fb,
    ct,
    a_pad,
    ov,
    fcv,
    pjv,
    ctb,
    cto,
    h2b,
    actb,
    dbo,
    dbp,
    dh,
    r_in,
    own_dh,
    da,
    dsp,
    pg,
    pr,
    stage,
    local,
    p3_send,
    p3_recv,
    pc_send,
    pc_recv,
    f_send,
    f_recv,
    fc_send,
    fc_recv,
    c_right,
    c_left,
    c_recv,
    h_right,
    h_left,
    h_recv,
    e_send,
    e_recv,
    r_send,
    r_recv,
    d_send,
    d_recv,
    g_send,
    g_recv,
):
    fs, nz, d, heads = cfg
    cs = 2 * nz
    f, z, core = lax.axis_index("fsdp"), lax.axis_index("z"), lax.axis_index("core")
    rank = 2 * z + core
    rows = tok.shape[0]
    width = heads * HD
    lanes = o_all.shape[3] // fs
    own_rows, part = d // fs, d // cs
    share, grain = p2.shape[1], p2.shape[2]
    slot = fs * share * grain
    he, hf = nz * slot, pjv.shape[5] // 2
    ff = 2 * hf
    fc_grain, fc_cols = fcv.shape[1], fc.shape[1]
    fc_rows = fc.shape[0] // fc_grain
    tall = nz * rows
    step = min(32, rows)
    plane = Plane(fs)
    ranks = [lax.rem(rank + i, cs) for i in range(1, cs)]
    half_at = lambda k: pl.ds(pl.multiple_of(k * hf, 128), hf)
    e_at = lambda k: pl.ds(pl.multiple_of(k * he, 128), he)

    peers = [dict(z=r // 2, core=lax.rem(r, 2)) for r in ranks]
    peers += [dict(fsdp=p) for p in plane.peers]
    greet(peers)
    load_out = pltpu.make_async_copy(o_all, ov, local.at[0])
    fc_at = lambda g, k, h: fcv.at[
        pl.ds(g * fc_rows + halves(fc_rows)[h][0], halves(fc_rows)[h][1]), :, half_at(k)
    ]
    load_out.start()
    for k in range(2):

        @pl.when(core == k)
        def _():
            at = pl.ds(f * fc_rows, fc_rows)
            if hf > fc_cols:
                fcv[at, :, k * hf + fc_cols : (k + 1) * hf] = jnp.zeros(
                    (fc_rows, fc_grain, hf - fc_cols), BF
                )
            fcv[at, :, k * hf : k * hf + fc_cols] = fc[...].reshape(fc_rows, fc_grain, fc_cols)

    ct[...] = ct_cols[...].T
    ctb[z] = jnp.zeros(ctb.shape[1:], BF)
    for c in range(cs):
        to = (c % 2) * he + (c // 2) * slot
        ctb[z, :, to : to + part] = ct[:, c * part : (c + 1) * part]
    for r in range(cs):
        vec[:, r * part : (r + 1) * part] = smalls[r, 4:7, 0:part]
    fb[...] = jnp.zeros(fb.shape, F32)
    for k in range(2):
        for j in range(smalls.shape[1] - 8):
            to = k * hf + j * part
            fb[:, to : to + part] = smalls[2 * z + k, 8 + j : 9 + j, 0:part]
    for g in range(fs):
        a_pad[core, :, lanes * g : lanes * g + own_rows] = a_own[
            :, own_rows * g : own_rows * (g + 1)
        ]
        a_pad[core, :, lanes * g + own_rows : lanes * (g + 1)] = jnp.zeros(
            (rows, lanes - own_rows), BF
        )
    pjv[core, :, f] = p2[...]
    met(peers)

    def swap(n, here, there):
        return remote(here, there, e_send.at[n], e_recv.at[n], core=1 - core)

    half_z = lambda h: pl.ds(*halves(nz)[h])
    p_gather = PlaneGather(plane, lambda g, h: pjv.at[core, half_z(h), g], (p3_send, p3_recv))

    def p_pass(g):
        at = pjv.at[core, :, g]
        return remote(at, at, pc_send.at[g], pc_recv.at[g], core=1 - core)

    def p_came(g):
        at = pjv.at[1 - core, :, g]
        return remote(at, at, pc_send.at[g], pc_recv.at[g], core=1 - core)

    fc_gather = PlaneGather(plane, lambda g, h: fc_at(g, core, h), (f_send, f_recv))
    fc_gather.start()

    def fc_pass(g):
        at = fcv.at[pl.ds(g * fc_rows, fc_rows), :, half_at(core)]
        return remote(at, at, fc_send.at[g], fc_recv.at[g], core=1 - core)

    def fc_came(g):
        at = fcv.at[pl.ds(g * fc_rows, fc_rows), :, half_at(1 - core)]
        return remote(at, at, fc_send.at[g], fc_recv.at[g], core=1 - core)

    fc_pass(f).start()

    c_line = Line(lambda b: ctb.at[b], nz, (c_right, c_left, c_recv))
    c_line.start()

    swap_a = swap(4, a_pad.at[core], a_pad.at[core])
    swap_a.start()
    load_out.wait()
    branch = dot_nt(a_pad[core], ov[...].reshape(d, fs * lanes))
    middle[...] = tok[...].astype(F32) + branch + vec[0:1, :]

    def norm_chunk(i, _):
        at = pl.ds(pl.multiple_of(i * step, step), step)
        xhat, _ = norm_rows(middle[at, :])
        h2b[core, z, at, :] = (xhat * vec[1:2, :] + vec[2:3, :]).astype(BF)
        return 0

    lax.fori_loop(0, rows // step, norm_chunk, 0)
    h_line = Line(lambda b: h2b.at[core, b], nz, (h_right, h_left, h_recv))
    h_line.start()
    fc_gather.mid()
    p_gather.start()
    p_pass(f).start()
    on = lambda g: fc_pass(g).start()
    h_line.step(1)
    fc_gather.end(on, (0,))
    for s in range(2, nz - 1):
        h_line.step(s)
    c_line.step(1)
    fc_gather.end(on, (1,))
    for g in range(fs):
        fc_came(g).wait_recv()

    chunk = 256 if ff % 256 == 0 else 128
    some = nz // 2
    wide = some * rows
    sums[4:5, :] = jnp.zeros((1, sums.shape[1]), F32)

    def by_columns(one):
        def step_columns(i, _):
            one(pl.ds(pl.multiple_of(i * chunk, chunk), chunk))
            return 0

        lax.fori_loop(0, ff // chunk, step_columns, 0)

    def feed(first):
        blocks = pl.ds(first, some)

        def one(at):
            w = fcv[:, :, at].reshape(d, chunk)
            before = dot(h2b[core, blocks].reshape(wide, d), w) + fb[:, at]
            act, slope = gelu_pair(before)
            actb[core, blocks, :, at] = act.astype(BF).reshape(some, rows, chunk)
            dbo[blocks, :, at] = slope.astype(BF).reshape(some, rows, chunk)

        by_columns(one)

    def feed_back(first):
        blocks = pl.ds(first, some)

        def one(at):
            w = pjv[:, :, :, :, :, at].reshape(2 * he, chunk)
            back = dot(ctb[blocks].reshape(wide, 2 * he), w)
            slope = dbo[blocks, :, at].reshape(wide, chunk).astype(F32)
            low = (back * slope).astype(BF)
            dbo[blocks, :, at] = low.reshape(some, rows, chunk)
            sums[4:5, at] += jnp.sum(low.astype(F32), axis=0, keepdims=True)

        by_columns(one)

    near = z // some * some
    feed(near)
    p_gather.mid()
    for s in range(2, nz - 1):
        c_line.step(s)
    h_line.step(nz - 1)
    swap_h2 = swap(1, h2b.at[core], h2b.at[core])
    feed(some - near)
    on = lambda g: p_pass(g).start()
    p_gather.end(on)
    for g in range(fs):
        p_came(g).wait_recv()
    swap_h2.start()
    feed_back(near)
    c_line.step(nz - 1)
    feed_back(some - near)
    swap_ct = swap(0, ctb.at[:, :, e_at(1 - core)], cto)
    swap_ct.start()
    swap_act = swap(2, actb.at[core], actb.at[core])
    swap_db = swap(3, dbo.at[:, :, half_at(1 - core)], dbp)
    swap_act.start()
    swap_db.start()

    r_line = LineSum(dh, r_in, nz, (r_send, r_recv))

    def hidden_back(i, _):
        block = r_line.order(i)
        part_sum = dot_nt(dbo[block], fcv[...].reshape(d, ff))
        dh[block] = part_sum.astype(BF)

        @pl.when(block == z)
        def _():
            own_dh[...] = part_sum

        r_line.ready(block)
        return 0

    lax.fori_loop(0, nz, hidden_back, 0)

    def output_part(k, i):
        w = pjv[k, i].reshape(slot, ff)
        part = dot_nt(actb[core].reshape(tall, ff), w)
        low = (2 * i + k) * (d // cs)
        ctb[:, :, low : low + d // cs] = part[:, : d // cs].astype(BF).reshape(nz, rows, d // cs)

    swap_ct.wait_recv()
    swap_act.wait_recv()
    pieces = 2 if hf % 256 == 0 or ff % 512 else 4
    for low in range(0, ff, ff // pieces):
        cols = slice(low, low + ff // pieces)
        pg[:, :, :, :, cols] = (
            (
                dot_tn(
                    ctb[:, :, e_at(core)].reshape(tall, he),
                    actb[core, :, :, cols].reshape(tall, ff // pieces),
                )
                + dot_tn(
                    cto[...].reshape(tall, he),
                    actb[1 - core, :, :, cols].reshape(tall, ff // pieces),
                )
            )
            .astype(BF)
            .reshape(nz, fs, share, grain, ff // pieces)
        )
    p_total = PlaneSum(
        plane,
        lambda g, h: pg.at[half_z(h), g],
        lambda n, h: pr.at[n, pl.ds(0, halves(nz)[h][1])],
        (g_send, g_recv),
    )
    p_total.start()
    c_line.finish()
    swap_ct.wait_send()
    keep_out = pltpu.make_async_copy(ctb.at[:, :, pl.ds(0, up(d))], out_part, local.at[6])
    for s in range(1, nz - 1):
        r_line.step(s)
        if s == 1:
            for k in range(2):
                for i in range(nz):
                    output_part(k, i)
            keep_out.start()
    swap_h2.wait_recv()
    swap_db.wait_recv()
    own_db = dbo[:, :, half_at(core)].reshape(tall, hf)
    other_db = dbp[...].reshape(tall, hf)
    cut = 512
    for low in range(0, d, cut):
        high = min(d, low + cut)
        fc_grad[low:high, :] = (
            dot_tn(h2b[core, :, :, low:high].reshape(tall, high - low), own_db)
            + dot_tn(h2b[1 - core, :, :, low:high].reshape(tall, high - low), other_db)
        ).astype(BF)
    p_total.mid()
    r_line.finish()

    sums[0:4, :] = jnp.zeros((4, sums.shape[1]), F32)
    dsp[core] = jnp.zeros(dsp.shape[1:], BF)

    def norm_back_chunk(i, _):
        at = pl.ds(pl.multiple_of(i * step, step), step)
        g = own_dh[at, :] + r_line.others(at)
        xhat, rstd = norm_rows(middle[at, :])
        dm = ct[at, :].astype(F32) + norm_back(g, xhat, rstd, vec[1:2, :])
        low = dm.astype(BF)
        d_middle[at, :] = dm
        for c in range(cs):
            to = (c % 2) * he + (c // 2) * slot
            dsp[core, at, to : to + part] = low[:, c * part : (c + 1) * part]
        sums[0:1, 0:d] += jnp.sum(low.astype(F32), axis=0, keepdims=True)
        sums[1:2, 0:d] += jnp.sum(g * xhat, axis=0, keepdims=True)
        sums[2:3, 0:d] += jnp.sum(g, axis=0, keepdims=True)
        sums[3:4, 0:d] += jnp.sum(ct[at, :].astype(F32), axis=0, keepdims=True)
        return 0

    lax.fori_loop(0, rows // step, norm_back_chunk, 0)
    swap_d = swap(5, dsp.at[core], dsp.at[core])
    swap_d.start()
    back = dot(d_middle[...].astype(BF), ov[...].reshape(d, fs * lanes)).astype(BF)
    for g in range(fs):
        da[:, own_rows * g : own_rows * (g + 1)] = back[:, lanes * g : lanes * g + own_rows]
    if d < cs * width:
        da[:, d:] = jnp.zeros((rows, cs * width - d), BF)

    def d_copy(i):
        r = ranks[i]
        here = da.at[:, pl.ds(pl.multiple_of(r * width, 128), width)]
        there = d_att.at[pl.ds(pl.multiple_of(rank * rows, rows), rows)]
        return remote(here, there, d_send.at[i], d_recv.at[rank], z=r // 2, core=lax.rem(r, 2))

    for i in range(cs - 1):
        d_copy(i).start()
    d_att[pl.ds(pl.multiple_of(rank * rows, rows), rows), :] = da[
        :, pl.ds(pl.multiple_of(rank * width, 128), width)
    ]

    swap_a.wait_recv()
    swap_d.wait_recv()

    def stage_out(g):
        at = pl.ds(g * lanes, lanes)
        return pltpu.make_async_copy(stage.at[g % 2], og.at[:, :, :, at], local.at[4 + g % 2])

    for g in range(fs):
        at = slice(g * lanes, (g + 1) * lanes)
        part_sum = dot_tn(
            dsp[:, :, e_at(core)].reshape(2 * rows, he), a_pad[:, :, at].reshape(2 * rows, lanes)
        )
        part_sum = part_sum.astype(BF).reshape(nz, slot // grain, grain, lanes)
        if g >= 2:
            stage_out(g - 2).wait()
        stage[g % 2] = part_sum[:, : og.shape[1]]
        stage_out(g).start()
    for g in range(max(fs - 2, 0), fs):
        stage_out(g).wait()

    p_total.end()
    for h in range(2):
        p_sum[half_z(h)] = p_total.total(h).astype(BF)
    for i in range(1, cs):
        back = lax.rem(rank + cs - i, cs)
        to = d_att.at[pl.ds(pl.multiple_of(back * rows, rows), rows)]
        remote(to, to, d_send.at[0], d_recv.at[back], z=z).wait_recv()

    for i in range(cs - 1):
        d_copy(i).wait_send()
    for g in range(fs):
        fc_pass(g).wait_send()
        p_pass(g).wait_send()
    fc_gather.sent()
    p_gather.sent()
    p_total.sent()
    keep_out.wait()
    h_line.finish()
    r_line.sent()
    for s in (swap_h2, swap_act, swap_db, swap_a, swap_d):
        s.wait_send()


def middle_part(cfg, a_own, tok, ct_cols, smalls, p2, fc, o_all):
    fs, nz, d, heads = cfg
    cs = 2 * nz
    rows, width = tok.shape[0], heads * HD
    length = rows * cs
    lanes = o_all.shape[3] // fs
    share, grain = p2.shape[1], p2.shape[2]
    he, hf = nz * fs * share * grain, p2.shape[3] // 2
    fc_grain = math.gcd(d // fs, 16)
    return pl.pallas_call(
        partial(middle_kernel, cfg),
        out_shape=(
            shape((rows, d), F32),
            shape((rows, d), F32),
            shape((length, width)),
            shape((nz, rows, up(d))),
            shape((d, hf)),
            shape((nz, share, grain, 2 * hf)),
            shape((nz,) + o_all.shape[1:]),
            shape((5, max(2 * hf, d)), F32),
        ),
        in_specs=[VMEM] * 6 + [HBM],
        out_specs=(VMEM, VMEM, VMEM, HBM, VMEM, VMEM, HBM, VMEM),
        scratch_shapes=[
            pltpu.VMEM((3, d), F32),
            pltpu.VMEM((1, 2 * hf), F32),
            pltpu.VMEM((rows, d), BF),
            pltpu.VMEM((2, rows, fs * lanes), BF),
            pltpu.VMEM(o_all.shape, BF),
            pltpu.VMEM((d // fc_grain, fc_grain, 2 * hf), BF),
            pltpu.VMEM((2, nz, fs, share, grain, 2 * hf), BF),
            pltpu.VMEM((nz, rows, 2 * he), BF),
            pltpu.VMEM((nz, rows, he), BF),
            pltpu.VMEM((2, nz, rows, d), BF),
            pltpu.VMEM((2, nz, rows, 2 * hf), BF),
            pltpu.VMEM((nz, rows, 2 * hf), BF),
            pltpu.VMEM((nz, rows, hf), BF),
            pltpu.VMEM((nz, rows, d), BF),
            pltpu.VMEM((nz + 1, rows, d), BF),
            pltpu.VMEM((rows, d), F32),
            pltpu.VMEM((rows, cs * width), BF),
            pltpu.VMEM((2, rows, 2 * he), BF),
            pltpu.VMEM((nz, fs, share, grain, 2 * hf), BF),
            pltpu.VMEM((2 * (fs - 1), nz - nz // 2, share, grain, 2 * hf), BF),
            pltpu.VMEM((2, nz) + o_all.shape[1:3] + (lanes,), BF),
        ]
        + sems(7, 2 * fs, (fs, 2), fs, fs, 2 * fs, (fs, 2), fs, fs)
        + sems(nz, nz, nz, nz, nz, nz, 6, 6, nz, nz + 1, cs, cs, 2 * fs, 2 * fs),
        name="middle",
        compiler_params=pltpu.CompilerParams(
            collective_id=1, has_side_effects=True, vmem_limit_bytes=62 * 2**20
        ),
    )(a_own, tok, ct_cols, smalls, p2, fc, o_all)


def last_kernel(
    cfg,
    qkv,
    att,
    lse,
    d_att,
    block_order,
    w_in,
    h1,
    tok,
    smalls,
    sums,
    middle_in,
    d_middle_in,
    out_part,
    p_sum,
    og,
    fg,
    output,
    input_grad,
    q_grad,
    p_grad,
    o_grad,
    f_grad,
    small_grad,
    w,
    middle,
    d_middle,
    out_rows,
    in_rows,
    pos_col,
    pos_row,
    vec,
    p_all,
    q_own,
    fgv,
    fr,
    d_qkv,
    acc,
    h1v,
    qg,
    qr,
    qs,
    om,
    orc,
    osum,
    o_in,
    op,
    ro_in,
    pz,
    other,
    partner,
    own,
    r_out,
    r_in,
    line,
    sm_out,
    sm_in,
    sm_f,
    z_send,
    z_recv,
    l_send,
    l_recv,
    local,
    q_send,
    q_recv,
    o_send,
    o_recv,
    os_send,
    os_recv,
    ro_send,
    ro_recv,
    f_send,
    f_recv,
    m_send,
    m_recv,
    r_send,
    r_recv,
    b_send,
    b_recv,
    s_send,
    s_recv,
    g_send,
    g_recv,
):
    fs, nz, d, heads = cfg
    cs = 2 * nz
    f, z, core = lax.axis_index("fsdp"), lax.axis_index("z"), lax.axis_index("core")
    rank = 2 * z + core
    rows = tok.shape[0]
    width = heads * HD
    own_rows, part = d // fs, d // cs
    lanes, grain = up(own_rows), column_grain(d, cs)
    hf = p_sum.shape[3] // 2
    plane = Plane(fs)
    ranks = [lax.rem(rank + i, cs) for i in range(1, cs)]
    lanes_of = lambda g: pl.ds(pl.multiple_of(g * lanes, 128), lanes)
    runs = column_segments(cs, d, width, grain)
    block_rows = lambda b: pl.ds(pl.multiple_of(b * rows, rows), rows)
    half_z = lambda h: pl.ds(*halves(nz)[h])

    peers = [dict(z=r // 2, core=lax.rem(r, 2)) for r in ranks]
    peers += [dict(fsdp=p) for p in plane.peers]
    greet(peers)

    cut = h1v.shape[2]
    lows = list(range(0, h1.shape[1], cut))

    def h1_in(i):
        size = min(cut, h1.shape[1] - lows[i])
        here, there = h1.at[:, pl.ds(lows[i], size)], h1v.at[i % 2, :, pl.ds(0, size)]
        return pltpu.make_async_copy(here, there, local.at[4 + i % 2])

    for i in range(min(2, len(lows))):
        h1_in(i).start()
    om_in = pltpu.make_async_copy(og, om, local.at[2])
    op_in = pltpu.make_async_copy(out_part, op, local.at[3])
    om_in.start()
    op_in.start()
    fg_in = pltpu.make_async_copy(fg, fgv, local.at[6])
    fg_in.start()
    late = [
        pltpu.make_async_copy(a, b, local.at[7 + n])
        for n, (a, b) in enumerate(((w_in, w), (middle_in, middle), (d_middle_in, d_middle)))
    ]
    for copy in late:
        copy.start()
    for r in range(cs):
        cols = slice(r * part, (r + 1) * part)
        vec[0:1, cols] = smalls[r, 0:1, 0:part]
        vec[1:2, cols] = smalls[r, 7:8, 0:part]
    run = cs * rows // block_order.shape[0]
    for b in range(block_order.shape[0]):
        first = block_order[b] * run
        at = slice(b * run, (b + 1) * run)
        pos_row[:, at] = first + lax.broadcasted_iota(jnp.int32, (1, run), 1)
        pos_col[at, :] = first + lax.broadcasted_iota(jnp.int32, (run, 1), 0)
    met(peers)

    om_in.wait()
    o_total = PlaneSum(
        plane,
        lambda g, h: om.at[half_z(h), :, :, lanes_of(g)],
        lambda n, h: orc.at[n, pl.ds(0, halves(nz)[h][1])],
        (o_send, o_recv),
    )
    o_total.start()

    def z_copy(i):
        to = lax.rem(z + i, nz)
        return remote(p_sum.at[to], pz.at[z], z_send.at[to], z_recv.at[z], z=to)

    z_keep = pltpu.make_async_copy(p_sum.at[z], pz.at[z], local.at[0])
    for i in range(1, nz):
        z_copy(i).start()
    z_keep.start()

    op_in.wait()
    ro_line = LineSum(op, ro_in, nz, (ro_send, ro_recv))
    ro_line.first()

    def l_copy(i):
        g = plane.peers[i]
        return remote(pz.at[g], p_all.at[f], l_send.at[i], l_recv.at[f], fsdp=g)

    l_keep = pltpu.make_async_copy(pz.at[f], p_all.at[f], local.at[1])

    def shares_on():
        z_keep.wait()
        for i in range(1, nz):
            back = lax.rem(z + nz - i, nz)
            remote(pz.at[back], pz.at[back], z_send.at[0], z_recv.at[back], z=back).wait_recv()
        for i in range(fs - 1):
            l_copy(i).start()
        l_keep.start()

    tall = query_block(cs * rows)
    for h in range(heads):
        attend_back_head(
            h, width, tall, qkv, pos_col, pos_row, att, lse, d_att, d_qkv, acc
        )
        if h == heads - 1:
            shares_on()
            ro_line.step(1)

    slices = 3 * width // grain
    q_share, q_rows = qg.shape[0] // fs, qg.shape[1]
    q_total = PlaneSum(
        plane,
        lambda g, h: qg.at[pl.ds(g * q_share + halves(q_share)[h][0], halves(q_share)[h][1])],
        lambda n, h: qr.at[n, pl.ds(0, halves(q_share)[h][1])],
        (q_send, q_recv),
    )
    for i, low in enumerate(lows):
        size = min(cut, d - low)
        h1_in(i).wait()
        part_sum = dot_tn(h1v[i % 2, :, 0:size], d_qkv[...])
        qg[low // q_rows : (low + size) // q_rows] = part_sum.astype(BF).reshape(
            size // q_rows, q_rows, 3 * width
        )
        if i + 2 < len(lows):
            h1_in(i + 2).start()
    q_total.start()
    fg_in.wait()
    f_rows = f_grad.shape[0] // fgv.shape[1]
    f_total = PlaneSum(
        plane,
        lambda g, h: fgv.at[pl.ds(g * f_rows + halves(f_rows)[h][0], halves(f_rows)[h][1])],
        lambda n, h: fr.at[n, pl.ds(0, halves(f_rows)[h][1])],
        (f_send, f_recv),
    )

    def hidden(block):
        return dot_nt(d_qkv[block_rows(block), :], w[...].reshape(d, 3 * width))

    def other_step(b, _):
        other[b] = hidden(2 * b + 1 - core).astype(BF)
        return 0

    for copy in late:
        copy.wait()
    lax.fori_loop(0, nz, other_step, 0)
    to_partner = remote(other, partner, m_send.at[0], m_recv.at[0], core=1 - core)
    to_partner.start()
    o_total.mid()

    to_partner.wait_recv()

    r_line = LineSum(r_out, r_in, nz, (r_send, r_recv))

    def own_step(i, _):
        b = r_line.order(i)
        both = hidden(2 * b + core) + partner[b].astype(F32)
        r_out[b] = both.astype(BF)

        @pl.when(b == z)
        def _():
            own[...] = both

        r_line.ready(b)
        return 0

    lax.fori_loop(0, nz, own_step, 0)
    for s in range(2, nz - 1):
        ro_line.step(s)
    q_total.mid()
    r_line.step(1)
    step = min(32, rows)
    o_total.end()
    for h in range(2):
        osum[half_z(h)] = o_total.total(h).astype(BF)
    o_line = LineSum(osum, o_in, nz, (os_send, os_recv))
    for s in range(2, nz - 1):
        r_line.step(s)
    o_line.first()

    q_total.end()
    for h in range(2):
        low, count = (n * q_rows for n in halves(q_share)[h])
        turned = q_total.total(h).astype(BF).reshape(count, 3 * width).T
        qs[:, :, low : low + count] = turned.reshape(slices, grain, count)
    if lanes > own_rows:
        qs[:, :, own_rows:] = jnp.zeros((slices, grain, lanes - own_rows), BF)

    def run_copy(n):
        dst, at, src, first, count = runs[n]
        here, there = qs.at[pl.ds(first, count)], q_own.at[pl.ds(at, count)]
        if src == dst:
            return pltpu.make_async_copy(here, there, b_send.at[n])
        return remote(here, there, b_send.at[n], b_recv.at[n], z=dst // 2, core=dst % 2)

    for n, run in enumerate(runs):

        @pl.when(rank == run[2])
        def _():
            run_copy(n).start()

    f_total.start()

    ro_line.finish()

    def output_chunk(i, _):
        at = pl.ds(pl.multiple_of(i * step, step), step)
        total = op[z, at, :].astype(F32) + ro_line.others(at)
        out_rows[at, :] = middle[at, :] + total[:, 0:d] + vec[1:2, :]
        return 0

    lax.fori_loop(0, rows // step, output_chunk, 0)
    output[...] = out_rows[...].T.astype(BF)
    o_line.step(1)

    l_keep.wait()
    for g in plane.peers:
        remote(p_all.at[g], p_all.at[g], l_send.at[0], l_recv.at[g], fsdp=g).wait_recv()
    fine = p_all.shape[2]
    whole = p_all[...].reshape(-1, fine, 2 * hf)[: part // fine].reshape(part, 2 * hf)
    ff_half = p_grad.shape[1] // 2
    for k in range(2):
        p_grad[:, k * ff_half : (k + 1) * ff_half] = whole[:, k * hf : k * hf + ff_half].astype(F32)
    for s in range(2, nz - 1):
        o_line.step(s)
    r_line.finish()

    line[...] = jnp.zeros(line.shape, F32)

    def norm_back_chunk(i, _):
        at = pl.ds(pl.multiple_of(i * step, step), step)
        g = own[at, :] + r_line.others(at)
        xhat, rstd = norm_rows(tok[at, :].astype(F32))
        in_rows[at, :] = d_middle[at, :] + norm_back(g, xhat, rstd, vec[0:1, :])
        line[0:1, 0:d] += jnp.sum(g * xhat, axis=0, keepdims=True)
        line[1:2, 0:d] += jnp.sum(g, axis=0, keepdims=True)
        return 0

    lax.fori_loop(0, rows // step, norm_back_chunk, 0)

    input_grad[...] = in_rows[...].T

    head_lanes = pl.ds(pl.multiple_of(rank * width, 128), width)
    line[2:3, head_lanes] = jnp.sum(d_qkv[:, 0:width].astype(F32), axis=0, keepdims=True)
    line[3:4, head_lanes] = jnp.sum(d_qkv[:, 2 * width :].astype(F32), axis=0, keepdims=True)
    line[4:8, 0:d] = sums[0:4, 0:d]
    sm_out[...] = jnp.zeros(sm_out.shape, F32)
    ff_parts = small_grad.shape[0] - 8
    for r in range(cs):
        sm_out[r, 0:8, 0:part] = line[0:8, r * part : (r + 1) * part]
    for k in range(2):
        for j in range(ff_parts):
            sm_out[2 * z + k, 8 + j : 9 + j, 0:part] = sums[
                4:5, k * hf + j * part : k * hf + (j + 1) * part
            ]

    def s_copy(i):
        r = ranks[i]
        here = sm_out.at[r]
        return remote(
            here, sm_in.at[rank], s_send.at[i], s_recv.at[rank], z=r // 2, core=lax.rem(r, 2)
        )

    for i in range(cs - 1):
        s_copy(i).start()
    f_total.mid()
    o_line.finish()
    whole = (osum[z].astype(F32) + o_line.others()).reshape(part, lanes)
    o_grad[...] = whole[:, :own_rows].T
    total = sm_out[rank]
    for i in range(1, cs):
        back = lax.rem(rank + cs - i, cs)
        remote(sm_in.at[back], sm_in.at[back], s_send.at[0], s_recv.at[back], z=z).wait_recv()
        total += sm_in[back]
    sm_f[f] = total

    def g_copy(i):
        return remote(sm_f.at[f], sm_f.at[f], g_send.at[i], g_recv.at[f], fsdp=plane.peers[i])

    for i in range(fs - 1):
        g_copy(i).start()
    for n, run in enumerate(runs):

        @pl.when(rank == run[0])
        def _():
            if run[0] == run[2]:
                run_copy(n).wait()
            else:
                run_copy(n).wait_recv()

    q_grad[...] = q_own[...].reshape(-1, lanes)[:, :own_rows].T.astype(F32)
    f_total.end()
    for h in range(2):
        low, count = (n * fgv.shape[1] for n in halves(f_rows)[h])
        whole = f_total.total(h).reshape(count, fgv.shape[2])
        f_grad[low : low + count, :] = whole[:, : f_grad.shape[1]]
    for g in plane.peers:
        remote(sm_f.at[g], sm_f.at[g], g_send.at[0], g_recv.at[g], fsdp=g).wait_recv()
    total = sm_f[0]
    for g in range(1, fs):
        total += sm_f[g]
    small_grad[...] = total

    for i in range(1, nz):
        z_copy(i).wait_send()
    for i in range(fs - 1):
        l_copy(i).wait_send()
        g_copy(i).wait_send()
    for s in (r_line, o_line, ro_line, o_total, q_total, f_total):
        s.sent()
    to_partner.wait_send()
    for n, run in enumerate(runs):
        if run[0] != run[2]:

            @pl.when(rank == run[2])
            def _():
                run_copy(n).wait_send()

    for i in range(cs - 1):
        s_copy(i).wait_send()


def last_part(cfg, counts, qkv, att, lse, d_att, block_order, w, h1, tok, smalls, sums, middle, d_middle, out_part, p_sum, og, fg):
    fs, nz, d, heads = cfg
    cs = 2 * nz
    rows, length, width = tok.shape[0], qkv.shape[0], heads * HD
    grain, lanes = column_grain(d, cs), up(d // fs)
    w_share, w_rows = w.shape[0] // fs, w.shape[1]
    q_grains, fc_cols = counts
    small_rows = smalls.shape[1]
    f_rows = fg.shape[0] // fs
    slices = 3 * width // grain
    runs = len(column_segments(cs, d, width, grain))
    part = d // cs
    rest = 2 * (fs - 1)
    rows_low = pltpu.VMEM((nz, rows, d), BF)
    smem = pl.BlockSpec(memory_space=pltpu.SMEM)
    owner = (nz,) + og.shape[1:3] + (lanes,)
    return pl.pallas_call(
        partial(last_kernel, cfg),
        out_shape=(
            shape((d, rows)),
            shape((d, rows), F32),
            shape((d // fs, q_grains * grain), F32),
            shape((part, 2 * fc_cols), F32),
            shape((d // fs, part), F32),
            shape((d // fs, fc_cols), F32),
            shape((small_rows, up(part)), F32),
        ),
        in_specs=[VMEM] * 4 + [smem, HBM, HBM] + [VMEM] * 3 + [HBM] * 2 + [HBM, VMEM, HBM, HBM],
        out_specs=(VMEM,) * 7,
        scratch_shapes=[
            pltpu.VMEM(w.shape, BF),
            pltpu.VMEM((rows, d), F32),
            pltpu.VMEM((rows, d), F32),
            pltpu.VMEM((rows, d), F32),
            pltpu.VMEM((rows, d), F32),
            pltpu.VMEM((length, 1), jnp.int32),
            pltpu.VMEM((1, length), jnp.int32),
            pltpu.VMEM((2, d), F32),
            pltpu.VMEM((fs,) + p_sum.shape[1:], BF),
            pltpu.VMEM((q_grains, grain, lanes), BF),
            pltpu.VMEM(fg.shape, BF),
            pltpu.VMEM((rest, f_rows - f_rows // 2) + fg.shape[1:], BF),
            pltpu.VMEM((length, 3 * width), BF),
            pltpu.VMEM((length, 2 * HD), F32),
            pltpu.VMEM((2, length, 512), BF),
            pltpu.VMEM(w.shape, BF),
            pltpu.VMEM((rest, w_share - w_share // 2, w_rows, 3 * width), BF),
            pltpu.VMEM((slices, grain, lanes), BF),
            pltpu.VMEM(og.shape, BF),
            pltpu.VMEM((rest, nz - nz // 2) + owner[1:], BF),
            pltpu.VMEM(owner, BF),
            pltpu.VMEM((nz + 1,) + owner[1:], BF),
            pltpu.VMEM(out_part.shape, BF),
            pltpu.VMEM((nz + 1,) + out_part.shape[1:], BF),
            pltpu.VMEM(p_sum.shape, BF),
            rows_low,
            rows_low,
            pltpu.VMEM((rows, d), F32),
            rows_low,
            pltpu.VMEM((nz + 1, rows, d), BF),
            pltpu.VMEM((8, width * cs), F32),
            pltpu.VMEM((cs, small_rows, up(part)), F32),
            pltpu.VMEM((cs, small_rows, up(part)), F32),
            pltpu.VMEM((fs, small_rows, up(part)), F32),
        ]
        + sems(nz, nz, fs, fs, 10, rest + 2, rest + 2, rest + 2, rest + 2, nz, nz + 1)
        + sems(nz, nz + 1)
        + sems(rest + 2, rest + 2, 1, 1, nz, nz + 1, runs, runs, cs, cs, fs, fs),
        name="last",
        compiler_params=pltpu.CompilerParams(
            collective_id=2, has_side_effects=True, vmem_limit_bytes=62 * 2**20
        ),
    )(
        qkv,
        att,
        lse,
        d_att,
        block_order,
        w,
        h1,
        tok,
        smalls,
        sums,
        middle,
        d_middle,
        out_part,
        p_sum,
        og,
        fg,
    )


def finish_kernel(*refs):
    vectors, refs = refs[0], refs[1:]
    big = 6
    ins, outs, smalls = refs[:big], refs[big : 2 * big], refs[2 * big : 2 * big + 9]
    held, line, came, left = refs[2 * big + 9 : 3 * big + 9], refs[-3], refs[-2], refs[-1]
    reads = [pltpu.make_async_copy(ins[n], held[n], came.at[n]) for n in range(big)]
    writes = [pltpu.make_async_copy(held[n], outs[n], left.at[n]) for n in range(big)]
    for read in reads:
        read.start()
    part = smalls[0].shape[0]
    for n in range(8):
        smalls[n][...] = vectors[n : n + 1, 0:part].reshape(part)
    for n in range(vectors.shape[0] - 8):
        line[:, n * part : (n + 1) * part] = vectors[8 + n : 9 + n, 0:part]
    smalls[8][...] = line[...].reshape(line.shape[1])
    for read, write in zip(reads, writes):
        read.wait()
        write.start()
    for write in writes:
        write.wait()


def finish(vectors, part, arrays):
    kinds = [shape(a.shape, a.dtype) for a in arrays]
    long = (vectors.shape[0] - 8) * part
    smalls = [shape((part,), F32)] * 8 + [shape((long,), F32)]
    return pl.pallas_call(
        finish_kernel,
        out_shape=kinds + smalls,
        in_specs=[VMEM] + [HBM] * len(arrays),
        out_specs=[HBM] * len(arrays) + [VMEM] * 9,
        scratch_shapes=[pltpu.VMEM(a.shape, a.dtype) for a in arrays]
        + [pltpu.VMEM((1, long), F32)]
        + sems(len(arrays), len(arrays)),
        name="finish",
        compiler_params=pltpu.CompilerParams(vmem_limit_bytes=62 * 2**20),
    )(vectors, *arrays)


def body(
    tokens,
    block_order,
    cotangent,
    pre_attn_gain,
    pre_attn_bias,
    qkv_weight,
    query_bias,
    value_bias,
    out_weight,
    out_bias,
    pre_mlp_gain,
    pre_mlp_bias,
    fc_weight,
    fc_bias,
    proj_weight,
    proj_bias,
):
    fs, nz = lax.axis_size("fsdp"), lax.axis_size("z")
    cs = nz * 2
    rows, d = tokens.shape[1], tokens.shape[2]
    length = rows * cs
    heads_all = d // HD
    heads = -(-heads_all // cs)
    width = heads * HD
    part, own_rows = d // cs, d // fs
    fc_cols = fc_weight.shape[1]
    hf = up(fc_cols)

    cfg = (fs, nz, d, heads)
    h1, w, qkv, att, lse, smalls, p2, o_all, a_own, tok = start(
        cfg,
        tokens[0].T,
        qkv_weight,
        proj_weight.T,
        out_weight,
        block_order,
        (
            pre_attn_gain,
            pre_attn_bias,
            query_bias,
            value_bias,
            out_bias,
            pre_mlp_gain,
            pre_mlp_bias,
            proj_bias,
            fc_bias,
        ),
        hf,
    )
    middle, d_middle, d_att, out_part, fc_grad, p_sum, og, sums = middle_part(
        cfg, a_own, tok, cotangent[0].T, smalls, p2, fc_weight, o_all
    )
    fg = fc_grad.reshape(-1, math.gcd(own_rows, 16), hf)
    output, input_grad, qkv_grad, proj_grad, out_grad, fc_grad, g = last_part(
        cfg,
        (qkv_weight.shape[1] // column_grain(d, cs), fc_cols),
        qkv,
        att,
        lse,
        d_att,
        block_order,
        w,
        h1,
        tok,
        smalls,
        sums,
        middle,
        d_middle,
        out_part,
        p_sum,
        og,
        fg,
    )
    output, input_grad, qkv_grad, proj_grad, out_grad, fc_grad, *g = finish(
        g, part, (output, input_grad, qkv_grad, proj_grad, out_grad, fc_grad)
    )
    return (
        output.T[None],
        input_grad.T[None],
        g[0],
        g[1],
        qkv_grad,
        g[2],
        g[3],
        out_grad,
        g[4],
        g[5],
        g[6],
        fc_grad,
        g[8],
        proj_grad.T,
        g[7],
    )


def solution(mesh):
    fs, cs = mesh.shape["fsdp"], mesh.shape["ctx"]
    split = Mesh(mesh.devices.reshape(fs, cs // 2, 2), ("fsdp", "z", "core"))
    rows = P("fsdp", CTX, None)
    weight = P("fsdp", CTX)
    vector = P(CTX)
    in_specs = (
        rows,
        P(),
        rows,
        vector,
        vector,
        weight,
        vector,
        vector,
        weight,
        vector,
        vector,
        vector,
        weight,
        vector,
        weight,
        vector,
    )
    out_specs = (
        rows,
        rows,
        vector,
        vector,
        weight,
        vector,
        vector,
        weight,
        vector,
        vector,
        vector,
        weight,
        vector,
        weight,
        vector,
    )
    return jax.shard_map(body, mesh=split, in_specs=in_specs, out_specs=out_specs, check_vma=False)
```
